32 devices in a mesh: case: 2 (over y), dom: 8 (over z, x), sub: 2 (over core).
Axes of the slice: x: 2, y: 2, z: 4, core: 2. Of those that a mesh axis runs over, the one named last changes fastest.
Arguments:
- states: float32 [19, 65536], P(None, ('case', 'dom', 'sub')), parts along dimension 1, may hold values from -0.9 to 2, as said below
- send_node: int32 [32, 4, 512], P(('case', 'dom', 'sub')), parts along dimension 0, may hold values from 0 to 2047
- send_count: int32 [32, 4], P(('case', 'dom', 'sub')), parts along dimension 0, may hold values from 1 to 512, as said below
- recv_row: int32 [32, 4, 512], P(('case', 'dom', 'sub')), parts along dimension 0, may hold values from 0 to 1023
- columns: int32 [128, 8], P(('case', 'dom'), 'sub'), parts along dimension 0, may hold values from 0 to 11
- tile_values: float32 [128, 8, 128, 128], P(('case', 'dom'), 'sub'), parts along dimension 0, may hold values from -0.109375 to 0.109375
- diagonal: float32 [16384], P(('case', 'dom')), parts along dimension 0, may hold values from 2.5 to 4
Outputs:
- new_states: float32 [19, 65536], P(None, ('case', 'dom', 'sub')), parts along dimension 1
- potential: float32 [16384], P(('case', 'dom')), parts along dimension 0
- residual: float32 [16384], P(('case', 'dom')), parts along dimension 0
The draws below stay inside these ranges and needn't reach their ends.
There are 2 independent parts, one for each index of `case`. The reference program is written for one: setup_inputs(seed, part) draws one part's arguments, and reference() takes and returns one part's arrays. A program takes and returns all parts, laid end to end along the dimension named above; each array names one. Nothing has to cross between parts.
Inputs may be any that keep to these rules, and one draw needn't show every extreme that they name: `states`: row 0 lies in -0.9 to 0.4, rows 1 to 13 in 0.001 to 0.999, rows 14 to 18 are positive. `send_count`: every device has one peer with exactly 512 live slots.
All inputs are finite; a program needn't handle non-finite values.
Results may differ from the reference program's by a relative error of at most 0.0001.
Values sent between devices are 32-bit elements; how exact they have to be, the bound alone decides.
No kernel may reach another device: no remote copies, remote signals or barrier semaphores. Data moves between devices by JAX's collectives and lax.ppermute only.
A program may use at most 64 MiB of HBM per device.

```python
import jax
import jax.numpy as jnp
from jax import lax

HN_DEV = 2048
TILES_DEV = 8
BLOCK = 128
SLOTS = 8
HALO = 2
PEERS = 4
SWEEPS = 3
STEPS = 2
CAP = 512
HEART = 32768
TORSO = 8192
N_DOM = 8
N_SUB = 2


def draw_states(key, part):
    key = jax.random.fold_in(key, 11)
    first, second, third = jax.random.split(key, 3)
    volt_draw = jax.random.uniform(first, (1, HEART), jnp.float32, 0.0, 1.0)
    gate_draw = jax.random.uniform(second, (13, HEART), jnp.float32, 0.0, 1.0)
    conc_draw = jax.random.uniform(third, (5, HEART), jnp.float32, 0.0, 1.0)
    voltage = -0.9 + 1.3 * volt_draw
    gating = 0.02 + 0.96 * gate_draw
    lower = jnp.array([0.05, 1.0, 0.2, 0.5, 0.1], jnp.float32)[:, None]
    upper = jnp.array([0.2, 1.6, 1.0, 2.0, 1.0], jnp.float32)[:, None]
    concentration = jnp.exp(jnp.log(lower) + conc_draw * jnp.log(upper / lower))
    return jnp.concatenate([voltage, gating, concentration], axis=0)


def draw_send_count(key, part):
    key = jax.random.fold_in(key, 23)
    first, second = jax.random.split(key, 2)
    senders = N_DOM * N_SUB
    counts = jax.random.randint(first, (senders, PEERS), 1, CAP + 1)
    offset_ids = jnp.arange(PEERS, dtype=jnp.int32)
    chosen = jax.random.randint(second, (senders,), 0, PEERS)
    counts = jnp.where(offset_ids[None, :] == chosen[:, None], CAP, counts)
    return counts.astype(jnp.int32)


def plant(result, stream_key, smallest, largest):
    longest = result.shape.index(max(result.shape))
    spots = []
    for shift in (0, 1):
        where = [jax.random.randint(jax.random.fold_in(stream_key, axis), (), 0, length) for axis, length in enumerate(result.shape)]
        where[longest] = (where[longest] + shift) % result.shape[longest]
        spots.append(tuple(where))
    return result.at[spots[0]].set(smallest).at[spots[1]].set(largest)


def block_levels(key, dims, shards, smallest, largest):
    def one(position, blocks):
        heights = jax.random.uniform(jax.random.fold_in(jax.random.fold_in(key, 6), position), (blocks,), jnp.float32, smallest / len(shards), largest / len(shards))
        return jnp.repeat(jnp.exp(heights), dims[position] // blocks).reshape((-1,) + (1,) * (len(dims) - position - 1))

    loudness = one(*shards[0])
    for cut in shards[1:]:
        loudness = loudness * one(*cut)
    return loudness


def noise(key, shape, width, reach, cuts=(), held_as=jnp.bfloat16):
    loudness = block_levels(key, shape, cuts, -0.22, 0.18) if cuts else 1.0
    entries = jax.random.normal(key, shape, jnp.float32) * width * loudness
    return jnp.minimum(jnp.maximum(entries, -reach), reach).astype(held_as)


def setup_inputs(seed: int = 0, part: int = 0) -> dict:
    key_of = jax.random.split(jax.random.key(seed), 8)
    part_splits = jax.random.split(jax.random.fold_in(key_of[7], part), 8)
    states = draw_states(jax.random.fold_in(jax.random.fold_in(key_of[7], part), 71), part)
    send_node = plant(jax.random.randint(part_splits[1], (N_DOM * N_SUB, PEERS, CAP), 0, HN_DEV), jax.random.fold_in(part_splits[1], 1), 0, HN_DEV - 1).astype(jnp.int32)
    send_count = draw_send_count(jax.random.fold_in(jax.random.fold_in(key_of[7], part), 71), part)
    recv_row = plant(jax.random.randint(part_splits[3], (N_DOM * N_SUB, PEERS, CAP), 0, TILES_DEV * BLOCK), jax.random.fold_in(part_splits[3], 1), 0, (TILES_DEV * BLOCK) - 1).astype(jnp.int32)
    columns = plant(jax.random.randint(part_splits[4], (N_DOM * TILES_DEV, SLOTS), 0, TILES_DEV + 2 * HALO), jax.random.fold_in(part_splits[4], 1), 0, (TILES_DEV + 2 * HALO) - 1).astype(jnp.int32)
    tile_values = noise(part_splits[5], (N_DOM * TILES_DEV, SLOTS, BLOCK, BLOCK), (3 * SLOTS * BLOCK) ** -0.5, 0.109375, ((0, 8), (1, 2)), jnp.float32)
    diagonal = jnp.clip(2.5 + 1.5 * jax.random.uniform(part_splits[6], (TORSO,), jnp.float32) ** block_levels(part_splits[6], (TORSO,), ((0, 8),), -0.2, 0.2), 2.5, 4.0)
    return {"states": states, "send_node": send_node, "send_count": send_count, "recv_row": recv_row, "columns": columns, "tile_values": tile_values, "diagonal": diagonal}


TIME_STEP = 0.02
NERNST_SCALE = 0.267
SODIUM_OUT = 1.4
POTASSIUM_OUT = 0.054
CALCIUM_OUT = 2000.0
COND_SODIUM = 8.0
COND_CALCIUM = 1.0
COND_TRANSIENT = 0.3
COND_RAPID = 0.2
COND_SLOW = 0.3
COND_INWARD = 2.0
COND_RELEASE = 3.0
MEMBRANE_RATE = 2.0
TORSO_COUPLING = 0.5
FEEDBACK_RATE = 5.0
CHEB_THETA = 1.0
CHEB_DELTA = 0.5
GATE_MIDPOINT = [-0.56, -0.70, -0.70, -0.08, -0.20, -0.30, 0.20, -0.28, -0.26, -0.88, 0.05, -0.80, -0.50]
GATE_STEEPNESS = [0.09, -0.07, -0.07, 0.07, -0.07, -0.09, 0.06, -0.05, 0.07, -0.24, 0.14, -0.10, 0.08]
TIME_BASE = [0.02, 0.3, 1.0, 0.1, 2.0, 0.5, 0.1, 1.0, 1.0, 0.5, 1.0, 0.05, 0.2]
TIME_PEAK = [0.1, 1.0, 3.0, 0.5, 5.0, 2.0, 0.3, 5.0, 3.0, 2.0, 4.0, 0.1, 1.0]


def ionic(states):
    voltage = states[0]
    gating = states[1:14]
    sodium = states[14]
    potassium = states[15]
    calcium = states[16]
    reticulum = states[17]
    subspace = states[18]
    midpoint = jnp.array(GATE_MIDPOINT, jnp.float32)[:, None]
    steepness = jnp.array(GATE_STEEPNESS, jnp.float32)[:, None]
    time_base = jnp.array(TIME_BASE, jnp.float32)[:, None]
    time_peak = jnp.array(TIME_PEAK, jnp.float32)[:, None]
    shifted = voltage[None, :] - midpoint
    steady = jax.nn.sigmoid(shifted / steepness)
    time_const = time_base + time_peak * jnp.exp(-jnp.square(shifted / 0.3))
    gating = steady + (gating - steady) * jnp.exp(-TIME_STEP / time_const)
    sodium_rev = NERNST_SCALE * jnp.log(SODIUM_OUT / sodium)
    potassium_rev = NERNST_SCALE * jnp.log(POTASSIUM_OUT / potassium)
    calcium_rev = 0.5 * NERNST_SCALE * jnp.log(CALCIUM_OUT / subspace)
    sodium_flow = COND_SODIUM * gating[0] ** 3 * gating[1] * gating[2] * (voltage - sodium_rev)
    calcium_flow = COND_CALCIUM * gating[3] * gating[4] * gating[5] * (voltage - calcium_rev)
    potassium_cond = (COND_TRANSIENT * gating[6] * gating[7] + COND_RAPID * gating[8] * gating[9]
                      + COND_SLOW * gating[10] ** 2 + COND_INWARD * gating[11])
    potassium_flow = potassium_cond * (voltage - potassium_rev)
    current = sodium_flow + calcium_flow + potassium_flow
    release = COND_RELEASE * gating[12] * (reticulum - subspace) / (reticulum + subspace)
    sodium = sodium * jnp.exp(-0.5 * TIME_STEP * sodium_flow)
    potassium = potassium * jnp.exp(-0.5 * TIME_STEP * potassium_flow)
    calcium = calcium * jnp.exp(-0.5 * TIME_STEP * calcium_flow)
    subspace = subspace * jnp.exp(TIME_STEP * (release - 0.5 * calcium_flow))
    reticulum = reticulum * jnp.exp(-TIME_STEP * release)
    voltage = voltage - TIME_STEP * MEMBRANE_RATE * current
    stacked = jnp.concatenate([voltage[None], gating, sodium[None], potassium[None], calcium[None],
                               reticulum[None], subspace[None]], axis=0)
    return stacked, current


def coupling_maps(send_node, send_count, recv_row):
    senders = N_DOM * N_SUB
    sender_ids = jnp.arange(senders, dtype=jnp.int32)
    sender_dom = sender_ids // N_SUB
    sender_sub = sender_ids % N_SUB
    offsets = jnp.array([0, 1, N_DOM - 1, N_DOM // 2], jnp.int32)[:PEERS]
    peer_dom = (sender_dom[:, None] + offsets[None, :]) % N_DOM
    receiver = peer_dom * N_SUB + sender_sub[:, None]
    land_row = recv_row[receiver, jnp.arange(PEERS, dtype=jnp.int32)[None, :]]
    torso_row = peer_dom[:, :, None] * (TILES_DEV * BLOCK) + land_row
    slot_live = jnp.arange(CAP, dtype=jnp.int32)[None, None, :] < send_count[:, :, None]
    heart_node = sender_ids[:, None, None] * HN_DEV + send_node
    return slot_live.reshape(-1), torso_row.reshape(-1).astype(jnp.int32), heart_node.reshape(-1).astype(jnp.int32)


def apply_operator(field, columns, tile_values, diagonal):
    padded = jnp.pad(field, HALO * BLOCK).reshape(-1, BLOCK)

    def partition_product(index):
        window = lax.dynamic_slice_in_dim(padded, index * TILES_DEV, TILES_DEV + 2 * HALO, 0)
        column_part = lax.dynamic_slice_in_dim(columns, index * TILES_DEV, TILES_DEV, 0)
        tile_part = lax.dynamic_slice_in_dim(tile_values, index * TILES_DEV, TILES_DEV, 0)
        picked = window[column_part]
        return jnp.einsum("rkab,rkb->ra", tile_part, picked, precision=lax.Precision.HIGHEST)

    products = lax.map(partition_product, jnp.arange(N_DOM, dtype=jnp.int32))
    return diagonal * field + products.reshape(-1)


def reference(states, send_node, send_count, recv_row, columns, tile_values, diagonal):
    slot_live, torso_row, heart_node = coupling_maps(send_node, send_count, recv_row)
    sigma = CHEB_THETA / CHEB_DELTA
    estimate = jnp.zeros((TORSO,), jnp.float32)
    residual = estimate
    for time_step in range(STEPS):
        states, current = ionic(states)
        outgoing = jnp.where(slot_live, current[heart_node], 0.0)
        forcing = TORSO_COUPLING * jnp.zeros((TORSO,), jnp.float32).at[torso_row].add(outgoing)
        estimate = jnp.zeros((TORSO,), jnp.float32)
        residual = forcing
        ratio = 1.0 / sigma
        direction = residual / (CHEB_THETA * diagonal)
        for sweep_idx in range(SWEEPS):
            estimate = estimate + direction
            residual = residual - apply_operator(direction, columns, tile_values, diagonal)
            if sweep_idx + 1 < SWEEPS:
                ratio_next = 1.0 / (2.0 * sigma - ratio)
                direction = ratio_next * ratio * direction + (2.0 * ratio_next / CHEB_DELTA) * (residual / diagonal)
                ratio = ratio_next
        returned = jnp.where(slot_live, estimate[torso_row], 0.0)
        feedback = jnp.zeros((HEART,), jnp.float32).at[heart_node].add(returned)
        states = states.at[0].add(TIME_STEP * FEEDBACK_RATE * feedback)
    return states, estimate, residual
```

```python
import functools

import jax
import jax.numpy as jnp
from jax import lax
from jax.experimental import pallas as pl
from jax.experimental.pallas import tpu as pltpu
from jax.sharding import PartitionSpec as P

HALO = 2
SWEEPS = 3
LANES = 128

TIME_STEP = 0.02
NERNST_SCALE = 0.267
SODIUM_OUT = 1.4
POTASSIUM_OUT = 0.054
CALCIUM_OUT = 2000.0
COND_SODIUM = 8.0
COND_CALCIUM = 1.0
COND_TRANSIENT = 0.3
COND_RAPID = 0.2
COND_SLOW = 0.3
COND_INWARD = 2.0
COND_RELEASE = 3.0
MEMBRANE_RATE = 2.0
TORSO_COUPLING = 0.5
FEEDBACK_RATE = 5.0
CHEB_THETA = 1.0
CHEB_DELTA = 0.5
GATE_MIDPOINT = [-0.56, -0.7, -0.7, -0.08, -0.2, -0.3, 0.2, -0.28, -0.26, -0.88, 0.05, -0.8, -0.5]
GATE_STEEPNESS = [0.09, -0.07, -0.07, 0.07, -0.07, -0.09, 0.06, -0.05, 0.07, -0.24, 0.14, -0.1, 0.08]
TIME_BASE = [0.02, 0.3, 1.0, 0.1, 2.0, 0.5, 0.1, 1.0, 1.0, 0.5, 1.0, 0.05, 0.2]
TIME_PEAK = [0.1, 1.0, 3.0, 0.5, 5.0, 2.0, 0.3, 5.0, 3.0, 2.0, 4.0, 0.1, 1.0]

SIGMA = CHEB_THETA / CHEB_DELTA
KEEP, PULL = [], []
_ratio = 1.0 / SIGMA
for _ in range(SWEEPS - 1):
    _next = 1.0 / (2.0 * SIGMA - _ratio)
    KEEP.append(_next * _ratio)
    PULL.append(2.0 * _next / CHEB_DELTA)
    _ratio = _next

VMEM = pl.BlockSpec(memory_space=pltpu.VMEM)
SMEM = pl.BlockSpec(memory_space=pltpu.SMEM)
F32 = jnp.float32


def call(kernel, outs, scratch=(), limit=16, cost=4_000_000):
    return functools.partial(
        pl.pallas_call,
        kernel,
        out_shape=outs,
        out_specs=jax.tree.map(lambda _: VMEM, outs),
        scratch_shapes=list(scratch),
        compiler_params=pltpu.CompilerParams(vmem_limit_bytes=limit << 20),
        cost_estimate=pl.CostEstimate(flops=cost, bytes_accessed=1 << 18, transcendentals=0),
    )


def ionic_rows(rows):
    voltage, gating = rows[0], rows[1:14]
    sodium, potassium, calcium, reticulum, subspace = rows[14:19]
    moved = []
    for i, gate in enumerate(gating):
        shifted = voltage - GATE_MIDPOINT[i]
        steady = jax.nn.sigmoid(shifted / GATE_STEEPNESS[i])
        time_const = TIME_BASE[i] + TIME_PEAK[i] * jnp.exp(-jnp.square(shifted / 0.3))
        moved.append(steady + (gate - steady) * jnp.exp(-TIME_STEP / time_const))
    g = moved
    sodium_rev = NERNST_SCALE * jnp.log(SODIUM_OUT / sodium)
    potassium_rev = NERNST_SCALE * jnp.log(POTASSIUM_OUT / potassium)
    calcium_rev = 0.5 * NERNST_SCALE * jnp.log(CALCIUM_OUT / subspace)
    sodium_flow = COND_SODIUM * (g[0] * g[0] * g[0]) * g[1] * g[2] * (voltage - sodium_rev)
    calcium_flow = COND_CALCIUM * g[3] * g[4] * g[5] * (voltage - calcium_rev)
    potassium_cond = (
        COND_TRANSIENT * g[6] * g[7]
        + COND_RAPID * g[8] * g[9]
        + COND_SLOW * (g[10] * g[10])
        + COND_INWARD * g[11]
    )
    potassium_flow = potassium_cond * (voltage - potassium_rev)
    current = sodium_flow + calcium_flow + potassium_flow
    release = COND_RELEASE * g[12] * (reticulum - subspace) / (reticulum + subspace)
    sodium = sodium * jnp.exp(-0.5 * TIME_STEP * sodium_flow)
    potassium = potassium * jnp.exp(-0.5 * TIME_STEP * potassium_flow)
    calcium = calcium * jnp.exp(-0.5 * TIME_STEP * calcium_flow)
    subspace = subspace * jnp.exp(TIME_STEP * (release - 0.5 * calcium_flow))
    reticulum = reticulum * jnp.exp(-TIME_STEP * release)
    voltage = voltage - TIME_STEP * MEMBRANE_RATE * current
    return [voltage, *moved, sodium, potassium, calcium, reticulum, subspace], current


def pairs_of(index):
    chunks = [index[:, k : k + LANES] for k in range(0, index.shape[1], LANES)]
    return [jnp.concatenate(chunks[k : k + 2], axis=0) for k in range(0, len(chunks), 2)]


def gather(source, rows, index):
    peers = index.shape[0]
    out = []
    for pair in pairs_of(index):
        high, low = pair >> 7, pair & (LANES - 1)
        total = jnp.zeros(pair.shape, F32)
        for h in range(rows):
            picked = jnp.take_along_axis(source(h), low, axis=1)
            total = jnp.where(high == h, picked, total)
        out += [total[:peers], total[peers:]]
    return jnp.concatenate(out, axis=1)


def scatter(values, index, rows):
    slots = values.shape[1]
    high, low = index >> 7, index & (LANES - 1)
    first = values.astype(jnp.bfloat16).astype(F32)
    rest = values - first
    second = rest.astype(jnp.bfloat16).astype(F32)
    third = rest - second
    mine = lax.broadcasted_iota(jnp.int32, (rows, slots), 0) == high
    left = jnp.concatenate([jnp.where(mine, part, 0.0) for part in (first, second, third)], axis=0)
    spread = lax.broadcasted_iota(jnp.int32, (LANES, slots), 0) == low
    right = jnp.where(spread, 1.0, 0.0).astype(jnp.bfloat16)
    sums = lax.dot_general(
        left.astype(jnp.bfloat16), right, (((1,), (1,)), ((), ())), preferred_element_type=F32
    )
    return sums[:rows] + sums[rows : 2 * rows] + sums[2 * rows :]


def spread_current(current, nodes, maps, chain, torso, shares_ref, place_ref):
    slots = maps.shape[1]
    peers = maps.shape[0]
    outgoing = gather(
        lambda h: jnp.broadcast_to(current[h : h + 1], (2 * peers, LANES)), current.shape[0], nodes
    )
    shares_ref[...] = jnp.zeros_like(shares_ref)
    for o in range(peers):
        share = scatter(outgoing[o : o + 1], jnp.where(nodes[o : o + 1] < 0, -1, maps[o : o + 1]), torso)
        at = pl.ds(pl.multiple_of(place_ref[o] * torso, 8), torso)
        shares_ref[at, :] = shares_ref[at, :] + share
    del slots


def feedback_of(estimates, nodes, maps, heart):
    peers = nodes.shape[0]
    torso = estimates[0].shape[0]

    def source(h):
        rows = [estimate[h : h + 1] for estimate in estimates]
        return jnp.concatenate(rows * 2, axis=0)

    live = jnp.where(nodes < 0, -1, maps)
    returned = gather(source, torso, live)
    total = jnp.zeros((heart, LANES), F32)
    for o in range(peers):
        total = total + scatter(returned[o : o + 1], nodes[o : o + 1], heart)
    return total


def product(own_ref, other_ref, own_cols, other_cols, window_ref, out_ref):
    tiles, slots = own_ref.shape[0], own_ref.shape[1]
    eye = lax.broadcasted_iota(jnp.int32, (LANES, LANES), 0) == lax.broadcasted_iota(
        jnp.int32, (LANES, LANES), 1
    )

    def row(t, carry):
        total = None
        for ref, cols in ((own_ref, own_cols), (other_ref, other_cols)):
            for k in range(slots):
                term = ref[t, k] * window_ref[pl.ds(cols[t, k], 1), :]
                total = term if total is None else total + term
        column = jnp.sum(total, axis=1, keepdims=True)
        out_ref[pl.ds(t, 1), :] = jnp.sum(jnp.where(eye, column, 0.0), axis=0, keepdims=True)
        return carry

    lax.fori_loop(0, tiles, row, 0)


def first_ionic(states_ref, out_ref, current_ref):
    chunks = out_ref.shape[1]
    for k in range(chunks):
        out_ref[:, k, :] = states_ref[:, k * LANES : (k + 1) * LANES]
    rows, current = ionic_rows([out_ref[i] for i in range(out_ref.shape[0])])
    for i, row in enumerate(rows):
        out_ref[i] = row
    current_ref[...] = current


def first_shares(chain, torso, place_ref, current_ref, nodes_ref, maps_ref, shares_ref):
    spread_current(
        current_ref[...], nodes_ref[...], maps_ref[...], chain, torso, shares_ref, place_ref
    )


def next_shares(
    chain, torso, place_ref, states_ref, e0, e1, e2, e3, nodes_ref, maps_ref, out_ref, shares_ref
):
    nodes, maps = nodes_ref[...], maps_ref[...]
    feedback = feedback_of([e[...] for e in (e0, e1, e2, e3)], nodes, maps, states_ref.shape[1])
    rows = [states_ref[i] for i in range(states_ref.shape[0])]
    rows[0] = rows[0] + TIME_STEP * FEEDBACK_RATE * feedback
    rows, current = ionic_rows(rows)
    for i, row in enumerate(rows):
        out_ref[i] = row
    spread_current(current, nodes, maps, chain, torso, shares_ref, place_ref)


def last_feedback(states_ref, e0, e1, e2, e3, nodes_ref, maps_ref, out_ref, dense_ref):
    nodes, maps = nodes_ref[...], maps_ref[...]
    feedback = feedback_of([e[...] for e in (e0, e1, e2, e3)], nodes, maps, states_ref.shape[1])
    dense_ref[...] = states_ref[...]
    dense_ref[0] = states_ref[0] + TIME_STEP * FEEDBACK_RATE * feedback
    for k in range(states_ref.shape[1]):
        out_ref[:, k * LANES : (k + 1) * LANES] = dense_ref[:, k, :]


def sweep_one(
    chain, place_ref, own_cols, other_cols, own_ref, other_ref, forcing_ref, diag_ref,
    residual_ref, direction_ref, estimate_ref, window_ref, product_ref,
):
    torso = residual_ref.shape[0]
    here = place_ref[0]
    before = forcing_ref[pl.ds(pl.multiple_of(jnp.maximum(here - 1, 0) * torso, 8), torso), :]
    after = forcing_ref[pl.ds(pl.multiple_of(jnp.minimum(here + 1, chain - 1) * torso, 8), torso), :]
    own = forcing_ref[pl.ds(pl.multiple_of(here * torso, 8), torso), :]
    before = jnp.where(here > 0, before[torso - HALO :], 0.0)
    after = jnp.where(here < chain - 1, after[:HALO], 0.0)
    diag = diag_ref[HALO : HALO + torso]
    residual = TORSO_COUPLING * own
    direction = residual / (CHEB_THETA * diag)
    window_ref[0:HALO] = TORSO_COUPLING * before / (CHEB_THETA * diag_ref[0:HALO])
    window_ref[HALO : HALO + torso] = direction
    window_ref[HALO + torso : 2 * HALO + torso] = (
        TORSO_COUPLING * after / (CHEB_THETA * diag_ref[HALO + torso : 2 * HALO + torso])
    )
    product(own_ref, other_ref, own_cols, other_cols, window_ref, product_ref)
    residual = residual - (diag * direction + product_ref[...])
    estimate = direction
    direction = KEEP[0] * direction + PULL[0] * (residual / diag)
    residual_ref[...] = residual
    direction_ref[...] = direction
    estimate_ref[...] = estimate + direction


def sweep_two(
    own_cols, other_cols, own_ref, other_ref, before_ref, after_ref, direction_in, residual_in,
    estimate_in, diag_ref, residual_ref, direction_ref, estimate_ref, window_ref, product_ref,
):
    torso = residual_ref.shape[0]
    diag = diag_ref[HALO : HALO + torso]
    direction = direction_in[...]
    window_ref[0:HALO] = before_ref[...]
    window_ref[HALO : HALO + torso] = direction
    window_ref[HALO + torso : 2 * HALO + torso] = after_ref[...]
    product(own_ref, other_ref, own_cols, other_cols, window_ref, product_ref)
    residual = residual_in[...] - (diag * direction + product_ref[...])
    direction = KEEP[1] * direction + PULL[1] * (residual / diag)
    residual_ref[...] = residual
    direction_ref[...] = direction
    estimate_ref[...] = estimate_in[...] + direction


def last_residual(
    own_cols, other_cols, own_ref, other_ref, before_ref, after_ref, direction_in, residual_in,
    diag_ref, residual_ref, window_ref, product_ref,
):
    torso = residual_ref.shape[0]
    diag = diag_ref[HALO : HALO + torso]
    direction = direction_in[...]
    window_ref[0:HALO] = before_ref[...]
    window_ref[HALO : HALO + torso] = direction
    window_ref[HALO + torso : 2 * HALO + torso] = after_ref[...]
    product(own_ref, other_ref, own_cols, other_cols, window_ref, product_ref)
    residual_ref[...] = residual_in[...] - (diag * direction + product_ref[...])


def on_device(states, send_node, send_count, recv_row, columns, tile_values, diagonal):
    chain = lax.axis_size("dom")
    here = lax.axis_index("dom")
    peers, slots = send_node.shape[1:]
    node_count = states.shape[1]
    heart = node_count // LANES
    torso = diagonal.shape[0] // LANES
    offsets = [0, 1, chain - 1, chain // 2]
    place = ((here + jnp.array(offsets, jnp.int32)) % chain).astype(jnp.int32)

    def from_peer(value, offset):
        return lax.ppermute(value, "dom", [((i + offset) % chain, i) for i in range(chain)])

    def from_neighbour(value, offset):
        pairs = [(i + offset, i) for i in range(chain) if 0 <= i + offset < chain]
        return lax.ppermute(value, "dom", pairs)

    def shape(*dims):
        return jax.ShapeDtypeStruct(dims, F32)

    edge = HALO * LANES
    flip = [(0, 1), (1, 0)]
    rows_out = recv_row[0].astype(F32)
    got_after = from_peer(jnp.concatenate([rows_out[1], diagonal[:edge]]), 1)
    got_before = from_peer(jnp.concatenate([rows_out[2], diagonal[-edge:]]), chain - 1)
    got_far = from_peer(rows_out[3], chain // 2)
    other_tiles = lax.ppermute(tile_values, "sub", flip)
    other_cols = lax.ppermute(columns, "sub", flip)
    maps = jnp.stack([rows_out[0], got_after[:slots], got_before[:slots], got_far]).astype(jnp.int32)
    diag = jnp.concatenate([got_before[slots:], diagonal, got_after[slots:]]).reshape(-1, LANES)
    live = jnp.arange(slots, dtype=jnp.int32)[None, :] < send_count[0][:, None]
    nodes = jnp.where(live, send_node[0], -1)

    dense = shape(states.shape[0], heart, LANES)
    field = shape(torso, LANES)
    part = shape(chain * torso, LANES)
    work = (pltpu.VMEM((torso + 2 * HALO + 4, LANES), F32), pltpu.VMEM((torso, LANES), F32))

    states, current = call(first_ionic, (dense, shape(heart, LANES)))(in_specs=[VMEM])(states)
    shares = call(functools.partial(first_shares, chain, torso), part)(
        in_specs=[SMEM] + [VMEM] * 3
    )(place, current, nodes, maps)
    for time_step in range(2):
        last = time_step == 1
        forcing = lax.psum(shares, ("dom", "sub"))
        residual, direction, estimate = call(
            functools.partial(sweep_one, chain), (field,) * 3, work
        )(in_specs=[SMEM] * 3 + [VMEM] * 4)(
            place, columns, other_cols, tile_values, other_tiles, forcing, diag
        )
        before = from_neighbour(direction[-HALO:], -1)
        after = from_neighbour(direction[:HALO], 1)
        residual, direction, estimate = call(sweep_two, (field,) * 3, work)(
            in_specs=[SMEM] * 2 + [VMEM] * 8
        )(
            columns, other_cols, tile_values, other_tiles, before, after, direction, residual,
            estimate, diag,
        )
        estimates = [estimate] + [from_peer(estimate, offset) for offset in offsets[1:]]
        if not last:
            states, shares = call(
                functools.partial(next_shares, chain, torso), (dense, part)
            )(in_specs=[SMEM] + [VMEM] * 7)(place, states, *estimates, nodes, maps)
            continue
        before = from_neighbour(direction[-HALO:], -1)
        after = from_neighbour(direction[:HALO], 1)
        residual = call(last_residual, field, work)(in_specs=[SMEM] * 2 + [VMEM] * 7)(
            columns, other_cols, tile_values, other_tiles, before, after, direction, residual, diag
        )
        new_states = call(
            last_feedback, shape(19, node_count), (pltpu.VMEM(dense.shape, F32),)
        )(in_specs=[VMEM] * 7)(states, *estimates, nodes, maps)
    return new_states, estimate.reshape(-1), residual.reshape(-1)


def solution(mesh):
    placed = (
        P(None, ("case", "dom", "sub")),
        P(("case", "dom", "sub"), None, None),
        P(("case", "dom", "sub"), None),
        P(("case", "dom", "sub"), None, None),
        P(("case", "dom"), "sub"),
        P(("case", "dom"), "sub", None, None),
        P(("case", "dom")),
    )
    return jax.shard_map(
        on_device,
        mesh=mesh,
        in_specs=placed,
        out_specs=(P(None, ("case", "dom", "sub")), P(("case", "dom")), P(("case", "dom"))),
        check_vma=False,
    )
```

```python
import functools

import jax
import jax.numpy as jnp
from jax import lax
from jax.experimental import pallas as pl
from jax.experimental.pallas import tpu as pltpu
from jax.sharding import PartitionSpec as P

HALO = 2
SWEEPS = 3
LANES = 128

TIME_STEP = 0.02
NERNST_SCALE = 0.267
SODIUM_OUT = 1.4
POTASSIUM_OUT = 0.054
CALCIUM_OUT = 2000.0
COND_SODIUM = 8.0
COND_CALCIUM = 1.0
COND_TRANSIENT = 0.3
COND_RAPID = 0.2
COND_SLOW = 0.3
COND_INWARD = 2.0
COND_RELEASE = 3.0
MEMBRANE_RATE = 2.0
TORSO_COUPLING = 0.5
FEEDBACK_RATE = 5.0
CHEB_THETA = 1.0
CHEB_DELTA = 0.5
GATE_MIDPOINT = [-0.56, -0.7, -0.7, -0.08, -0.2, -0.3, 0.2, -0.28, -0.26, -0.88, 0.05, -0.8, -0.5]
GATE_STEEPNESS = [0.09, -0.07, -0.07, 0.07, -0.07, -0.09, 0.06, -0.05, 0.07, -0.24, 0.14, -0.1, 0.08]
TIME_BASE = [0.02, 0.3, 1.0, 0.1, 2.0, 0.5, 0.1, 1.0, 1.0, 0.5, 1.0, 0.05, 0.2]
TIME_PEAK = [0.1, 1.0, 3.0, 0.5, 5.0, 2.0, 0.3, 5.0, 3.0, 2.0, 4.0, 0.1, 1.0]

SIGMA = CHEB_THETA / CHEB_DELTA
KEEP, PULL = [], []
_ratio = 1.0 / SIGMA
for _ in range(SWEEPS - 1):
    _next = 1.0 / (2.0 * SIGMA - _ratio)
    KEEP.append(_next * _ratio)
    PULL.append(2.0 * _next / CHEB_DELTA)
    _ratio = _next

VMEM = pl.BlockSpec(memory_space=pltpu.VMEM)
SMEM = pl.BlockSpec(memory_space=pltpu.SMEM)
F32 = jnp.float32


def call(kernel, outs, scratch=(), limit=16, cost=4_000_000):
    return functools.partial(
        pl.pallas_call,
        kernel,
        out_shape=outs,
        out_specs=jax.tree.map(lambda _: VMEM, outs),
        scratch_shapes=list(scratch),
        compiler_params=pltpu.CompilerParams(vmem_limit_bytes=limit << 20),
        cost_estimate=pl.CostEstimate(flops=cost, bytes_accessed=1 << 18, transcendentals=0),
    )


def ionic_rows(rows):
    voltage, gating = rows[0], rows[1:14]
    sodium, potassium, calcium, reticulum, subspace = rows[14:19]
    moved = []
    for i, gate in enumerate(gating):
        shifted = voltage - GATE_MIDPOINT[i]
        steady = jax.nn.sigmoid(shifted / GATE_STEEPNESS[i])
        time_const = TIME_BASE[i] + TIME_PEAK[i] * jnp.exp(-jnp.square(shifted / 0.3))
        moved.append(steady + (gate - steady) * jnp.exp(-TIME_STEP / time_const))
    g = moved
    sodium_rev = NERNST_SCALE * jnp.log(SODIUM_OUT / sodium)
    potassium_rev = NERNST_SCALE * jnp.log(POTASSIUM_OUT / potassium)
    calcium_rev = 0.5 * NERNST_SCALE * jnp.log(CALCIUM_OUT / subspace)
    sodium_flow = COND_SODIUM * (g[0] * g[0] * g[0]) * g[1] * g[2] * (voltage - sodium_rev)
    calcium_flow = COND_CALCIUM * g[3] * g[4] * g[5] * (voltage - calcium_rev)
    potassium_cond = (
        COND_TRANSIENT * g[6] * g[7]
        + COND_RAPID * g[8] * g[9]
        + COND_SLOW * (g[10] * g[10])
        + COND_INWARD * g[11]
    )
    potassium_flow = potassium_cond * (voltage - potassium_rev)
    current = sodium_flow + calcium_flow + potassium_flow
    release = COND_RELEASE * g[12] * (reticulum - subspace) / (reticulum + subspace)
    sodium = sodium * jnp.exp(-0.5 * TIME_STEP * sodium_flow)
    potassium = potassium * jnp.exp(-0.5 * TIME_STEP * potassium_flow)
    calcium = calcium * jnp.exp(-0.5 * TIME_STEP * calcium_flow)
    subspace = subspace * jnp.exp(TIME_STEP * (release - 0.5 * calcium_flow))
    reticulum = reticulum * jnp.exp(-TIME_STEP * release)
    voltage = voltage - TIME_STEP * MEMBRANE_RATE * current
    return [voltage, *moved, sodium, potassium, calcium, reticulum, subspace], current


def pairs_of(index):
    chunks = [index[:, k : k + LANES] for k in range(0, index.shape[1], LANES)]
    return [jnp.concatenate(chunks[k : k + 2], axis=0) for k in range(0, len(chunks), 2)]


def gather(source, rows, index):
    peers = index.shape[0]
    out = []
    for pair in pairs_of(index):
        high, low = pair >> 7, pair & (LANES - 1)
        total = jnp.zeros(pair.shape, F32)
        for h in range(rows):
            picked = jnp.take_along_axis(source(h), low, axis=1)
            total = jnp.where(high == h, picked, total)
        out += [total[:peers], total[peers:]]
    return jnp.concatenate(out, axis=1)


def scatter(values, index, rows):
    slots = values.shape[1]
    high, low = index >> 7, index & (LANES - 1)
    first = values.astype(jnp.bfloat16).astype(F32)
    rest = values - first
    second = rest.astype(jnp.bfloat16).astype(F32)
    third = rest - second
    mine = lax.broadcasted_iota(jnp.int32, (rows, slots), 0) == high
    left = jnp.concatenate([jnp.where(mine, part, 0.0) for part in (first, second, third)], axis=0)
    spread = lax.broadcasted_iota(jnp.int32, (LANES, slots), 0) == low
    right = jnp.where(spread, 1.0, 0.0).astype(jnp.bfloat16)
    sums = lax.dot_general(
        left.astype(jnp.bfloat16), right, (((1,), (1,)), ((), ())), preferred_element_type=F32
    )
    return sums[:rows] + sums[rows : 2 * rows] + sums[2 * rows :]


def spread_current(current, nodes, maps, chain, torso, shares_ref, blocks_ref):
    peers = maps.shape[0]
    copies = blocks_ref.shape[0] // chain
    outgoing = gather(
        lambda h: jnp.broadcast_to(current[h : h + 1], (2 * peers, LANES)), current.shape[0], nodes
    )
    shares_ref[...] = jnp.zeros_like(shares_ref)
    here = lax.axis_index("dom")
    for o, offset in enumerate(peer_offsets(chain)):
        share = scatter(outgoing[o : o + 1], maps[o : o + 1], torso)
        at = pl.ds(pl.multiple_of((lax.rem(here + offset, chain) + 1) * torso, 8), torso)
        shares_ref[at, :] = shares_ref[at, :] + share

    def block(q, carry):
        before, own, after = (
            shares_ref[pl.ds(pl.multiple_of((q + k) * torso, 8), torso), :] for k in range(3)
        )
        filler = jnp.zeros((torso - 2 * HALO, LANES), F32)
        rims = jnp.concatenate([before[torso - HALO :], after[:HALO], filler], axis=0)
        for k in range(copies):
            blocks_ref[q * copies + k, 0:torso] = own
            blocks_ref[q * copies + k, torso : 2 * torso] = rims
        return carry

    lax.fori_loop(0, chain, block, 0)


def peer_offsets(chain):
    return [0, 1, chain - 1, chain // 2]


def feedback_of(estimates, nodes, maps, heart):
    peers = nodes.shape[0]
    torso = estimates[0].shape[0]

    def source(h):
        rows = [estimate[h : h + 1] for estimate in estimates]
        return jnp.concatenate(rows * 2, axis=0)

    returned = gather(source, torso, maps)
    total = jnp.zeros((heart, LANES), F32)
    for o in range(peers):
        total = total + scatter(returned[o : o + 1], nodes[o : o + 1], heart)
    return total


def product(own_ref, other_ref, own_cols, other_cols, window_ref, out_ref):
    tiles, slots = own_ref.shape[0], own_ref.shape[1]
    eye = lax.broadcasted_iota(jnp.int32, (LANES, LANES), 0) == lax.broadcasted_iota(
        jnp.int32, (LANES, LANES), 1
    )
    for t in range(tiles):
        total = None
        for ref, cols in ((own_ref, own_cols), (other_ref, other_cols)):
            for k in range(slots):
                term = ref[t, k] * window_ref[pl.ds(cols[k, t], 1), :]
                total = term if total is None else total + term
        column = jnp.sum(total, axis=1, keepdims=True)
        out_ref[t : t + 1, :] = jnp.sum(jnp.where(eye, column, 0.0), axis=0, keepdims=True)


def prepare(count_ref, node_ref, row_ref, diag_ref, nodes_ref, prev_ref, next_ref, far_ref):
    peers, slots = nodes_ref.shape
    torso = diag_ref.shape[0]
    slot = lax.broadcasted_iota(jnp.int32, (1, slots), 1)
    for o in range(peers):
        nodes_ref[o : o + 1] = jnp.where(slot < count_ref[0, o], node_ref[0, o : o + 1], -1)
    rows = [row_ref[0, o : o + 1].astype(F32) for o in range(peers)]
    prev_ref[:, 0:slots] = rows[1]
    next_ref[:, 0:slots] = rows[2]
    far_ref[...] = rows[3]
    for k in range(HALO):
        at = slice(slots + k * LANES, slots + (k + 1) * LANES)
        prev_ref[:, at] = diag_ref[k : k + 1]
        next_ref[:, at] = diag_ref[torso - HALO + k : torso - HALO + k + 1]


def first_ionic(states_ref, out_ref, current_ref):
    chunks = out_ref.shape[1]
    for k in range(chunks):
        out_ref[:, k, :] = states_ref[:, k * LANES : (k + 1) * LANES]
    rows, current = ionic_rows([out_ref[i] for i in range(out_ref.shape[0])])
    for i, row in enumerate(rows):
        out_ref[i] = row
    current_ref[...] = current


def first_shares(
    chain, current_ref, nodes_ref, row_ref, after_ref, before_ref, far_ref, diag_ref,
    maps_ref, wide_ref, blocks_ref, shares_ref,
):
    nodes = nodes_ref[...]
    slots = nodes.shape[1]
    torso = diag_ref.shape[0]
    rows = [after_ref[:, 0:slots], before_ref[:, 0:slots], far_ref[...]]
    rows = [row_ref[0, 0:1]] + [row.astype(jnp.int32) for row in rows]
    maps = jnp.where(nodes < 0, -1, jnp.concatenate(rows, axis=0))
    maps_ref[...] = maps
    wide_ref[HALO : HALO + torso] = diag_ref[...]
    for k in range(HALO):
        at = slice(slots + k * LANES, slots + (k + 1) * LANES)
        wide_ref[k : k + 1] = before_ref[:, at]
        wide_ref[HALO + torso + k : HALO + torso + k + 1] = after_ref[:, at]
    spread_current(current_ref[...], nodes, maps, chain, torso, shares_ref, blocks_ref)


def next_shares(
    chain, states_ref, e0, e1, e2, e3, nodes_ref, maps_ref, out_ref, blocks_ref, shares_ref
):
    nodes, maps = nodes_ref[...], maps_ref[...]
    torso = e0.shape[0]
    feedback = feedback_of([e[...] for e in (e0, e1, e2, e3)], nodes, maps, states_ref.shape[1])
    rows = [states_ref[i] for i in range(states_ref.shape[0])]
    rows[0] = rows[0] + TIME_STEP * FEEDBACK_RATE * feedback
    rows, current = ionic_rows(rows)
    for i, row in enumerate(rows):
        out_ref[i] = row
    spread_current(current, nodes, maps, chain, torso, shares_ref, blocks_ref)


def last_feedback(states_ref, e0, e1, e2, e3, nodes_ref, maps_ref, out_ref, dense_ref):
    nodes, maps = nodes_ref[...], maps_ref[...]
    torso = e0.shape[0]
    estimates = [e0[...], e1[0:torso], e2[0:torso], e3[...]]
    feedback = feedback_of(estimates, nodes, maps, states_ref.shape[1])
    dense_ref[...] = states_ref[...]
    dense_ref[0] = states_ref[0] + TIME_STEP * FEEDBACK_RATE * feedback
    for k in range(states_ref.shape[1]):
        out_ref[:, k * LANES : (k + 1) * LANES] = dense_ref[:, k, :]


def sweep_one(
    own_cols, other_cols, own_ref, other_ref, parts_ref, diag_ref,
    residual_ref, direction_ref, estimate_ref, window_ref, product_ref,
):
    torso = residual_ref.shape[0]
    forcing = TORSO_COUPLING * jnp.sum(parts_ref[...], axis=0)
    diag = diag_ref[HALO : HALO + torso]
    residual = forcing[0:torso]
    direction = residual / (CHEB_THETA * diag)
    before, after = forcing[torso : torso + HALO], forcing[torso + HALO : torso + 2 * HALO]
    window_ref[0:HALO] = before / (CHEB_THETA * diag_ref[0:HALO])
    window_ref[HALO : HALO + torso] = direction
    window_ref[HALO + torso : 2 * HALO + torso] = (
        after / (CHEB_THETA * diag_ref[HALO + torso : 2 * HALO + torso])
    )
    product(own_ref, other_ref, own_cols, other_cols, window_ref, product_ref)
    residual = residual - (diag * direction + product_ref[...])
    estimate = direction
    direction = KEEP[0] * direction + PULL[0] * (residual / diag)
    residual_ref[...] = residual
    direction_ref[...] = direction
    estimate_ref[...] = estimate + direction


def sweep_two(
    own_cols, other_cols, own_ref, other_ref, before_ref, after_ref, direction_in, residual_in,
    estimate_in, diag_ref, residual_ref, direction_ref, estimate_ref, prev_ref, next_ref,
    window_ref, product_ref,
):
    torso = residual_ref.shape[0]
    diag = diag_ref[HALO : HALO + torso]
    direction = direction_in[...]
    window_ref[0:HALO] = before_ref[...]
    window_ref[HALO : HALO + torso] = direction
    window_ref[HALO + torso : 2 * HALO + torso] = after_ref[...]
    product(own_ref, other_ref, own_cols, other_cols, window_ref, product_ref)
    residual = residual_in[...] - (diag * direction + product_ref[...])
    direction = KEEP[1] * direction + PULL[1] * (residual / diag)
    estimate = estimate_in[...] + direction
    residual_ref[...] = residual
    direction_ref[...] = direction
    estimate_ref[...] = estimate
    prev_ref[0:torso] = estimate
    prev_ref[torso : torso + HALO] = direction[0:HALO]
    next_ref[0:torso] = estimate
    next_ref[torso : torso + HALO] = direction[torso - HALO : torso]


def last_residual(
    chain, own_cols, other_cols, own_ref, other_ref, after_ref, before_ref, direction_in,
    residual_in, diag_ref, residual_ref, window_ref, product_ref,
):
    torso = residual_ref.shape[0]
    here = lax.axis_index("dom")
    diag = diag_ref[HALO : HALO + torso]
    direction = direction_in[...]
    window_ref[0:HALO] = jnp.where(here > 0, before_ref[torso : torso + HALO], 0.0)
    window_ref[HALO : HALO + torso] = direction
    window_ref[HALO + torso : 2 * HALO + torso] = jnp.where(
        here < chain - 1, after_ref[torso : torso + HALO], 0.0
    )
    product(own_ref, other_ref, own_cols, other_cols, window_ref, product_ref)
    residual_ref[...] = residual_in[...] - (diag * direction + product_ref[...])


def on_device(states, send_node, send_count, recv_row, columns, tile_values, diagonal):
    chain = lax.axis_size("dom")
    pair = lax.axis_size("sub")
    slots = send_node.shape[2]
    node_count = states.shape[1]
    heart = node_count // LANES
    torso = diagonal.shape[0] // LANES
    _, _, _, far = peer_offsets(chain)

    def from_peer(value, offset):
        return lax.ppermute(value, "dom", [((i + offset) % chain, i) for i in range(chain)])

    def from_neighbour(value, offset):
        pairs = [(i + offset, i) for i in range(chain) if 0 <= i + offset < chain]
        return lax.ppermute(value, "dom", pairs)

    def shape(*dims, dtype=F32):
        return jax.ShapeDtypeStruct(dims, dtype)

    dense = shape(states.shape[0], heart, LANES)
    field = shape(torso, LANES)
    wide = shape(torso + 2 * HALO, LANES)
    packed = shape(torso + HALO, LANES)
    table = shape(*send_node.shape[1:], dtype=jnp.int32)
    blocks = shape(chain * pair, 2 * torso, LANES)
    rim = shape(1, slots + HALO * LANES)
    shares = (pltpu.VMEM(((chain + 2) * torso, LANES), F32),)
    work = (pltpu.VMEM(wide.shape, F32), pltpu.VMEM(field.shape, F32))

    flip = [(0, 1), (1, 0)]
    diagonal = diagonal.reshape(torso, LANES)
    columns = columns.T
    nodes, to_prev, to_next, to_far = call(prepare, (table, rim, rim, shape(1, slots)))(
        in_specs=[SMEM] + [VMEM] * 3
    )(send_count, send_node, recv_row, diagonal)
    got_after = from_peer(to_prev, 1)
    got_before = from_peer(to_next, chain - 1)
    got_far = from_peer(to_far, far)
    other_tiles = lax.ppermute(tile_values, "sub", flip)
    other_cols = lax.ppermute(columns, "sub", flip)

    states, current = call(first_ionic, (dense, shape(heart, LANES)))(in_specs=[VMEM])(states)
    maps, diag, parts = call(
        functools.partial(first_shares, chain), (table, wide, blocks), shares
    )(in_specs=[VMEM] * 7)(current, nodes, recv_row, got_after, got_before, got_far, diagonal)
    for time_step in range(2):
        parts = lax.all_to_all(parts, ("dom", "sub"), split_axis=0, concat_axis=0, tiled=True)
        residual, direction, estimate = call(sweep_one, (field,) * 3, work)(
            in_specs=[SMEM] * 2 + [VMEM] * 4
        )(columns, other_cols, tile_values, other_tiles, parts, diag)
        before = from_neighbour(direction[-HALO:], -1)
        after = from_neighbour(direction[:HALO], 1)
        residual, direction, estimate, to_prev, to_next = call(
            sweep_two, (field,) * 3 + (packed,) * 2, work
        )(in_specs=[SMEM] * 2 + [VMEM] * 8)(
            columns, other_cols, tile_values, other_tiles, before, after, direction, residual,
            estimate, diag,
        )
        got_far = from_peer(estimate, far)
        if time_step == 0:
            got_after, got_before = from_peer(estimate, 1), from_peer(estimate, chain - 1)
            states, parts = call(
                functools.partial(next_shares, chain), (dense, blocks), shares
            )(in_specs=[VMEM] * 7)(states, estimate, got_after, got_before, got_far, nodes, maps)
            continue
        got_after, got_before = from_peer(to_prev, 1), from_peer(to_next, chain - 1)
        residual = call(functools.partial(last_residual, chain), field, work)(
            in_specs=[SMEM] * 2 + [VMEM] * 7
        )(
            columns, other_cols, tile_values, other_tiles, got_after, got_before, direction,
            residual, diag,
        )
        new_states = call(
            last_feedback, shape(*dense.shape[:1], node_count), (pltpu.VMEM(dense.shape, F32),)
        )(in_specs=[VMEM] * 7)(states, estimate, got_after, got_before, got_far, nodes, maps)
    return new_states, estimate.reshape(-1), residual.reshape(-1)


def solution(mesh):
    placed = (
        P(None, ("case", "dom", "sub")),
        P(("case", "dom", "sub"), None, None),
        P(("case", "dom", "sub"), None),
        P(("case", "dom", "sub"), None, None),
        P(("case", "dom"), "sub"),
        P(("case", "dom"), "sub", None, None),
        P(("case", "dom")),
    )
    return jax.shard_map(
        on_device,
        mesh=mesh,
        in_specs=placed,
        out_specs=(P(None, ("case", "dom", "sub")), P(("case", "dom")), P(("case", "dom"))),
        check_vma=False,
    )
```

```python
import functools

import jax
import jax.numpy as jnp
from jax import lax
from jax.experimental import pallas as pl
from jax.experimental.pallas import tpu as pltpu
from jax.sharding import PartitionSpec as P

HALO = 2
SWEEPS = 3
LANES = 128

TIME_STEP = 0.02
NERNST_SCALE = 0.267
SODIUM_OUT = 1.4
POTASSIUM_OUT = 0.054
CALCIUM_OUT = 2000.0
COND_SODIUM = 8.0
COND_CALCIUM = 1.0
COND_TRANSIENT = 0.3
COND_RAPID = 0.2
COND_SLOW = 0.3
COND_INWARD = 2.0
COND_RELEASE = 3.0
MEMBRANE_RATE = 2.0
TORSO_COUPLING = 0.5
FEEDBACK_RATE = 5.0
CHEB_THETA = 1.0
CHEB_DELTA = 0.5
GATE_MIDPOINT = [-0.56, -0.7, -0.7, -0.08, -0.2, -0.3, 0.2, -0.28, -0.26, -0.88, 0.05, -0.8, -0.5]
GATE_STEEPNESS = [0.09, -0.07, -0.07, 0.07, -0.07, -0.09, 0.06, -0.05, 0.07, -0.24, 0.14, -0.1, 0.08]
TIME_BASE = [0.02, 0.3, 1.0, 0.1, 2.0, 0.5, 0.1, 1.0, 1.0, 0.5, 1.0, 0.05, 0.2]
TIME_PEAK = [0.1, 1.0, 3.0, 0.5, 5.0, 2.0, 0.3, 5.0, 3.0, 2.0, 4.0, 0.1, 1.0]

SIGMA = CHEB_THETA / CHEB_DELTA
KEEP, PULL = [], []
_ratio = 1.0 / SIGMA
for _ in range(SWEEPS - 1):
    _next = 1.0 / (2.0 * SIGMA - _ratio)
    KEEP.append(_next * _ratio)
    PULL.append(2.0 * _next / CHEB_DELTA)
    _ratio = _next

VMEM = pl.BlockSpec(memory_space=pltpu.VMEM)
SMEM = pl.BlockSpec(memory_space=pltpu.SMEM)
HBM = pl.BlockSpec(memory_space=pltpu.HBM)
F32 = jnp.float32


def call(kernel, outs, scratch=(), limit=16, cost=4_000_000):
    return functools.partial(
        pl.pallas_call,
        kernel,
        out_shape=outs,
        out_specs=jax.tree.map(lambda _: VMEM, outs),
        scratch_shapes=list(scratch),
        compiler_params=pltpu.CompilerParams(vmem_limit_bytes=limit << 20),
        cost_estimate=pl.CostEstimate(flops=cost, bytes_accessed=1 << 18, transcendentals=0),
    )


def ionic_rows(rows):
    voltage, gating = rows[0], rows[1:14]
    sodium, potassium, calcium, reticulum, subspace = rows[14:19]
    moved = []
    for i, gate in enumerate(gating):
        shifted = voltage - GATE_MIDPOINT[i]
        steady = jax.nn.sigmoid(shifted / GATE_STEEPNESS[i])
        time_const = TIME_BASE[i] + TIME_PEAK[i] * jnp.exp(-jnp.square(shifted / 0.3))
        moved.append(steady + (gate - steady) * jnp.exp(-TIME_STEP / time_const))
    g = moved
    sodium_rev = NERNST_SCALE * jnp.log(SODIUM_OUT / sodium)
    potassium_rev = NERNST_SCALE * jnp.log(POTASSIUM_OUT / potassium)
    calcium_rev = 0.5 * NERNST_SCALE * jnp.log(CALCIUM_OUT / subspace)
    sodium_flow = COND_SODIUM * (g[0] * g[0] * g[0]) * g[1] * g[2] * (voltage - sodium_rev)
    calcium_flow = COND_CALCIUM * g[3] * g[4] * g[5] * (voltage - calcium_rev)
    potassium_cond = (
        COND_TRANSIENT * g[6] * g[7]
        + COND_RAPID * g[8] * g[9]
        + COND_SLOW * (g[10] * g[10])
        + COND_INWARD * g[11]
    )
    potassium_flow = potassium_cond * (voltage - potassium_rev)
    current = sodium_flow + calcium_flow + potassium_flow
    release = COND_RELEASE * g[12] * (reticulum - subspace) / (reticulum + subspace)
    sodium = sodium * jnp.exp(-0.5 * TIME_STEP * sodium_flow)
    potassium = potassium * jnp.exp(-0.5 * TIME_STEP * potassium_flow)
    calcium = calcium * jnp.exp(-0.5 * TIME_STEP * calcium_flow)
    subspace = subspace * jnp.exp(TIME_STEP * (release - 0.5 * calcium_flow))
    reticulum = reticulum * jnp.exp(-TIME_STEP * release)
    voltage = voltage - TIME_STEP * MEMBRANE_RATE * current
    return [voltage, *moved, sodium, potassium, calcium, reticulum, subspace], current


def pairs_of(index):
    chunks = [index[:, k : k + LANES] for k in range(0, index.shape[1], LANES)]
    return [jnp.concatenate(chunks[k : k + 2], axis=0) for k in range(0, len(chunks), 2)]


def gather(source, rows, index):
    peers = index.shape[0]
    out = []
    for pair in pairs_of(index):
        high, low = pair >> 7, pair & (LANES - 1)
        total = jnp.zeros(pair.shape, F32)
        for h in range(rows):
            picked = jnp.take_along_axis(source(h), low, axis=1)
            total = jnp.where(high == h, picked, total)
        out += [total[:peers], total[peers:]]
    return jnp.concatenate(out, axis=1)


def scatter(values, index, rows):
    slots = values.shape[1]
    high, low = index >> 7, index & (LANES - 1)
    first = values.astype(jnp.bfloat16).astype(F32)
    rest = values - first
    second = rest.astype(jnp.bfloat16).astype(F32)
    third = rest - second
    mine = lax.broadcasted_iota(jnp.int32, (rows, slots), 0) == high
    left = jnp.concatenate([jnp.where(mine, part, 0.0) for part in (first, second, third)], axis=0)
    spread = lax.broadcasted_iota(jnp.int32, (LANES, slots), 0) == low
    right = jnp.where(spread, 1.0, 0.0).astype(jnp.bfloat16)
    sums = lax.dot_general(
        left.astype(jnp.bfloat16), right, (((1,), (1,)), ((), ())), preferred_element_type=F32
    )
    return sums[:rows] + sums[rows : 2 * rows] + sums[2 * rows :]


def pick_current(current, nodes):
    rows, peers = current.shape[0], nodes.shape[0]
    return gather(
        lambda h: jnp.broadcast_to(current[h : h + 1], (2 * peers, LANES)), rows, nodes
    )


def spread_current(outgoing, maps, diag, chain, shares_ref, blocks_ref):
    torso = diag.shape[0]
    shares_ref[...] = jnp.zeros_like(shares_ref)
    here = lax.axis_index("dom")
    for o, offset in enumerate(peer_offsets(chain)):
        share = scatter(outgoing[o : o + 1], maps[o : o + 1], torso)
        at = pl.ds(pl.multiple_of((lax.rem(here + offset, chain) + 1) * torso, 8), torso)
        shares_ref[at, :] = shares_ref[at, :] + share

    def block(q, carry):
        before, own, after = (
            shares_ref[pl.ds(pl.multiple_of((q + k) * torso, 8), torso), :] for k in range(3)
        )
        blocks_ref[q, 0:torso] = own
        blocks_ref[q, torso : torso + 2 * HALO] = jnp.concatenate(
            [before[torso - HALO :], after[:HALO]], axis=0
        )
        blocks_ref[q, torso + 2 * HALO :] = jnp.concatenate(
            [
                jnp.where(q == lax.rem(here + 1, chain), diag[torso - HALO :], 0.0),
                jnp.where(q == lax.rem(here + chain - 1, chain), diag[:HALO], 0.0),
            ],
            axis=0,
        )
        return carry

    lax.fori_loop(0, chain, block, 0)


def peer_offsets(chain):
    return [0, 1, chain - 1, chain // 2]


def feedback_of(estimates, nodes, maps, heart):
    peers = nodes.shape[0]
    torso = estimates[0].shape[0]

    def source(h):
        rows = [estimate[h : h + 1] for estimate in estimates]
        return jnp.concatenate(rows * 2, axis=0)

    returned = gather(source, torso, maps)
    total = jnp.zeros((heart, LANES), F32)
    for o in range(peers):
        total = total + scatter(returned[o : o + 1], nodes[o : o + 1], heart)
    return total


def product(own_ref, other_ref, own_cols, other_cols, window_ref, out_ref):
    tiles, slots = own_ref.shape[0], own_ref.shape[1]
    eye = lax.broadcasted_iota(jnp.int32, (LANES, LANES), 0) == lax.broadcasted_iota(
        jnp.int32, (LANES, LANES), 1
    )
    for t in range(tiles):
        total = None
        for ref, cols in ((own_ref, own_cols), (other_ref, other_cols)):
            for k in range(slots):
                term = ref[t, k] * window_ref[pl.ds(cols[k, t], 1), :]
                total = term if total is None else total + term
        column = jnp.sum(total, axis=1, keepdims=True)
        out_ref[t : t + 1, :] = jnp.sum(jnp.where(eye, column, 0.0), axis=0, keepdims=True)


def fetch(pairs, sems):
    copies = [pltpu.make_async_copy(a, b, sems.at[i]) for i, (a, b) in enumerate(pairs)]
    for copy in copies:
        copy.start()
    return copies


def begin(
    count_hbm, node_hbm, row_hbm, diag_hbm, states_hbm, tiles_hbm, cols_hbm,
    nodes_ref, own_ref, diag_ref, out_ref, outgoing_ref, tiles_ref, cols_ref,
    count_ref, node_ref, row_ref, states_ref, sems,
):
    peers, slots = nodes_ref.shape
    pairs = [
        (states_hbm, states_ref), (node_hbm, node_ref), (count_hbm, count_ref),
        (row_hbm, row_ref), (diag_hbm, diag_ref), (cols_hbm, cols_ref),
        (tiles_hbm, tiles_ref),
    ]
    copies = [pltpu.make_async_copy(a, b, sems.at[i]) for i, (a, b) in enumerate(pairs)]
    for copy in copies:
        copy.start()
    for copy in copies[:3]:
        copy.wait()
    slot = lax.broadcasted_iota(jnp.int32, (1, slots), 1)
    nodes = jnp.concatenate(
        [
            jnp.where(slot < count_ref[0:1, o : o + 1], node_ref[0, o : o + 1], -1)
            for o in range(peers)
        ],
        axis=0,
    )
    nodes_ref[...] = nodes
    for k in range(out_ref.shape[1]):
        out_ref[:, k, :] = states_ref[:, k * LANES : (k + 1) * LANES]
    rows, current = ionic_rows([out_ref[i] for i in range(out_ref.shape[0])])
    for i, row in enumerate(rows):
        out_ref[i] = row
    outgoing_ref[...] = pick_current(current, nodes)
    for copy in copies[3:]:
        copy.wait()
    own_ref[...] = row_ref[0, 0:1]


def first_shares(
    chain, outgoing_ref, nodes_ref, row_ref, after_ref, before_ref, far_ref, diag_ref,
    maps_ref, blocks_ref, shares_ref,
):
    rows = [row_ref[...], after_ref[...], before_ref[...], far_ref[...]]
    maps = jnp.where(nodes_ref[...] < 0, -1, jnp.concatenate(rows, axis=0))
    maps_ref[...] = maps
    spread_current(outgoing_ref[...], maps, diag_ref[...], chain, shares_ref, blocks_ref)


def next_shares(
    chain, states_ref, e0, e1, e2, e3, nodes_ref, maps_ref, diag_ref, out_ref, blocks_ref, shares_ref
):
    nodes, maps = nodes_ref[...], maps_ref[...]
    feedback = feedback_of([e[...] for e in (e0, e1, e2, e3)], nodes, maps, states_ref.shape[1])
    rows = [states_ref[i] for i in range(states_ref.shape[0])]
    rows[0] = rows[0] + TIME_STEP * FEEDBACK_RATE * feedback
    rows, current = ionic_rows(rows)
    for i, row in enumerate(rows):
        out_ref[i] = row
    outgoing = pick_current(current, nodes)
    spread_current(outgoing, maps, diag_ref[...], chain, shares_ref, blocks_ref)


def last_feedback(states_ref, e0, e1, e2, e3, nodes_ref, maps_ref, out_ref, dense_ref):
    nodes, maps = nodes_ref[...], maps_ref[...]
    torso = e0.shape[0]
    estimates = [e0[...], e1[0:torso], e2[0:torso], e3[...]]
    feedback = feedback_of(estimates, nodes, maps, states_ref.shape[1])
    dense_ref[...] = states_ref[...]
    dense_ref[0] = states_ref[0] + TIME_STEP * FEEDBACK_RATE * feedback
    for k in range(states_ref.shape[1]):
        out_ref[:, k * LANES : (k + 1) * LANES] = dense_ref[:, k, :]


def sweep_one(
    chain, own_cols, other_cols, own_ref, other_ref, mine_ref, yours_ref, diag_ref,
    residual_ref, direction_ref, estimate_ref, window_ref, product_ref,
):
    torso = residual_ref.shape[0]
    forcing = TORSO_COUPLING * (mine_ref[...] + yours_ref[...])
    diag = diag_ref[...]
    residual = forcing[0:torso]
    direction = residual / (CHEB_THETA * diag)
    rims = [slice(torso + k * HALO, torso + (k + 1) * HALO) for k in range(4)]
    before = forcing[rims[0]] / (CHEB_THETA * mine_ref[rims[2]])
    after = forcing[rims[1]] / (CHEB_THETA * mine_ref[rims[3]])
    fill_window(chain, direction, before, after, window_ref)
    product(own_ref, other_ref, own_cols, other_cols, window_ref, product_ref)
    residual = residual - (diag * direction + product_ref[...])
    estimate = direction
    direction = KEEP[0] * direction + PULL[0] * (residual / diag)
    residual_ref[...] = residual
    direction_ref[...] = direction
    estimate_ref[...] = estimate + direction


def fill_window(chain, direction, before, after, window_ref):
    torso = direction.shape[0]
    here = lax.axis_index("dom")
    window_ref[0:HALO] = jnp.where(here > 0, before, 0.0)
    window_ref[HALO : HALO + torso] = direction
    window_ref[HALO + torso : 2 * HALO + torso] = jnp.where(here < chain - 1, after, 0.0)


def sweep_two(
    chain, last, own_cols, other_cols, own_ref, other_ref, before_ref, after_ref, direction_in,
    residual_in, estimate_in, diag_ref, *refs,
):
    estimate_ref, window_ref, product_ref = refs[0], refs[-2], refs[-1]
    torso = estimate_ref.shape[0]
    diag = diag_ref[...]
    direction = direction_in[...]
    fill_window(chain, direction, before_ref[...], after_ref[...], window_ref)
    product(own_ref, other_ref, own_cols, other_cols, window_ref, product_ref)
    residual = residual_in[...] - (diag * direction + product_ref[...])
    direction = KEEP[1] * direction + PULL[1] * (residual / diag)
    estimate = estimate_in[...] + direction
    estimate_ref[...] = estimate
    if last:
        final_ref, residual_ref, direction_ref, prev_ref, next_ref = refs[1:-2]
        final_ref[...] = estimate
        residual_ref[...] = residual
        direction_ref[...] = direction
        prev_ref[0:torso] = estimate
        prev_ref[torso : torso + HALO] = direction[0:HALO]
        next_ref[0:torso] = estimate
        next_ref[torso : torso + HALO] = direction[torso - HALO : torso]


def last_residual(
    chain, own_cols, other_cols, own_ref, other_ref, after_ref, before_ref, direction_in,
    residual_in, diag_ref, residual_ref, window_ref, product_ref,
):
    torso = residual_ref.shape[0]
    rim = slice(torso, torso + HALO)
    diag = diag_ref[...]
    direction = direction_in[...]
    fill_window(chain, direction, before_ref[rim], after_ref[rim], window_ref)
    product(own_ref, other_ref, own_cols, other_cols, window_ref, product_ref)
    residual_ref[...] = residual_in[...] - (diag * direction + product_ref[...])


def on_device(states, send_node, send_count, recv_row, columns, tile_values, diagonal):
    chain = lax.axis_size("dom")
    peers, slots = send_node.shape[1:]
    node_count = states.shape[1]
    heart = node_count // LANES
    torso = diagonal.shape[0] // LANES
    far = peer_offsets(chain)[3]

    def from_peer(value, offset):
        return lax.ppermute(value, "dom", [((i + offset) % chain, i) for i in range(chain)])

    def from_sibling(value):
        return lax.ppermute(value, "sub", [(0, 1), (1, 0)])

    def shape(*dims, dtype=F32):
        return jax.ShapeDtypeStruct(dims, dtype)

    dense = shape(states.shape[0], heart, LANES)
    field = shape(torso, LANES)
    packed = shape(torso + HALO, LANES)
    table = shape(peers, slots, dtype=jnp.int32)
    row = shape(1, slots, dtype=jnp.int32)
    blocks = shape(chain, 2 * torso, LANES)
    shares = (pltpu.VMEM(((chain + 2) * torso, LANES), F32),)
    work = (pltpu.VMEM((torso + 2 * HALO, LANES), F32), pltpu.VMEM(field.shape, F32))
    arrivals = (
        pltpu.VMEM(send_count.shape, jnp.int32),
        pltpu.VMEM(send_node.shape, jnp.int32),
        pltpu.VMEM(recv_row.shape, jnp.int32),
        pltpu.VMEM(states.shape, F32),
        pltpu.SemaphoreType.DMA((7,)),
    )

    got_after = from_peer(recv_row[0, 1:2], 1)
    got_before = from_peer(recv_row[0, 2:3], chain - 1)
    got_far = from_peer(recv_row[0, 3:4], far)
    other_tiles = from_sibling(tile_values)
    columns = columns.T
    nodes, own_rows, diag, states, outgoing, tiles, columns = call(
        begin,
        (
            table,
            row,
            field,
            dense,
            shape(peers, slots),
            shape(*tile_values.shape),
            shape(*columns.shape, dtype=jnp.int32),
        ),
        arrivals,
    )(in_specs=[HBM] * 7)(
        send_count, send_node, recv_row, diagonal.reshape(torso, LANES), states, tile_values,
        columns,
    )
    other_columns = from_sibling(columns)
    stored = (columns, other_columns, tiles, other_tiles)
    maps, parts = call(functools.partial(first_shares, chain), (table, blocks), shares)(
        in_specs=[VMEM] * 7
    )(outgoing, nodes, own_rows, got_after, got_before, got_far, diag)
    parts, stored = lax.optimization_barrier((parts, stored))
    for time_step in range(2):
        last = time_step == 1
        parts = lax.all_to_all(parts, "dom", split_axis=0, concat_axis=0, tiled=True)
        mine = jnp.sum(parts, axis=0)
        residual, direction, estimate = call(functools.partial(sweep_one, chain), (field,) * 3, work)(
            in_specs=[SMEM] * 2 + [VMEM] * 5
        )(*stored, mine, from_sibling(mine), diag)
        before = from_peer(direction[-HALO:], chain - 1)
        after = from_peer(direction[:HALO], 1)
        estimate, *rest = call(
            functools.partial(sweep_two, chain, last),
            (field,) * 4 + (packed,) * 2 if last else (field,),
            work,
        )(in_specs=[SMEM] * 2 + [VMEM] * 8)(
            *stored, before, after, direction, residual, estimate, diag
        )
        if not last:
            got_after, got_before = from_peer(estimate, 1), from_peer(estimate, chain - 1)
            got_far = from_peer(estimate, far)
            states, parts = call(
                functools.partial(next_shares, chain), (dense, blocks), shares
            )(in_specs=[VMEM] * 8)(
                states, estimate, got_after, got_before, got_far, nodes, maps, diag
            )
    potential, residual, direction, to_prev, to_next = rest
    got_after, got_before = from_peer(to_prev, 1), from_peer(to_next, chain - 1)
    got_far = from_peer(estimate, far)
    residual = call(functools.partial(last_residual, chain), field, work)(
        in_specs=[SMEM] * 2 + [VMEM] * 7
    )(*stored, got_after, got_before, direction, residual, diag)
    new_states = call(
        last_feedback, shape(*dense.shape[:1], node_count), (pltpu.VMEM(dense.shape, F32),)
    )(in_specs=[VMEM] * 7)(states, estimate, got_after, got_before, got_far, nodes, maps)
    return new_states, potential.reshape(-1), residual.reshape(-1)


def solution(mesh):
    placed = (
        P(None, ("case", "dom", "sub")),
        P(("case", "dom", "sub"), None, None),
        P(("case", "dom", "sub"), None),
        P(("case", "dom", "sub"), None, None),
        P(("case", "dom"), "sub"),
        P(("case", "dom"), "sub", None, None),
        P(("case", "dom")),
    )
    return jax.shard_map(
        on_device,
        mesh=mesh,
        in_specs=placed,
        out_specs=(P(None, ("case", "dom", "sub")), P(("case", "dom")), P(("case", "dom"))),
        check_vma=False,
    )
```

```python
import functools

import jax
import jax.numpy as jnp
from jax import lax
from jax.experimental import pallas as pl
from jax.experimental.pallas import tpu as pltpu
from jax.sharding import PartitionSpec as P

HALO = 2
SWEEPS = 3
LANES = 128

TIME_STEP = 0.02
NERNST_SCALE = 0.267
SODIUM_OUT = 1.4
POTASSIUM_OUT = 0.054
CALCIUM_OUT = 2000.0
COND_SODIUM = 8.0
COND_CALCIUM = 1.0
COND_TRANSIENT = 0.3
COND_RAPID = 0.2
COND_SLOW = 0.3
COND_INWARD = 2.0
COND_RELEASE = 3.0
MEMBRANE_RATE = 2.0
TORSO_COUPLING = 0.5
FEEDBACK_RATE = 5.0
CHEB_THETA = 1.0
CHEB_DELTA = 0.5
GATE_MIDPOINT = [-0.56, -0.7, -0.7, -0.08, -0.2, -0.3, 0.2, -0.28, -0.26, -0.88, 0.05, -0.8, -0.5]
GATE_STEEPNESS = [0.09, -0.07, -0.07, 0.07, -0.07, -0.09, 0.06, -0.05, 0.07, -0.24, 0.14, -0.1, 0.08]
TIME_BASE = [0.02, 0.3, 1.0, 0.1, 2.0, 0.5, 0.1, 1.0, 1.0, 0.5, 1.0, 0.05, 0.2]
TIME_PEAK = [0.1, 1.0, 3.0, 0.5, 5.0, 2.0, 0.3, 5.0, 3.0, 2.0, 4.0, 0.1, 1.0]

SIGMA = CHEB_THETA / CHEB_DELTA
KEEP, PULL = [], []
_ratio = 1.0 / SIGMA
for _ in range(SWEEPS - 1):
    _next = 1.0 / (2.0 * SIGMA - _ratio)
    KEEP.append(_next * _ratio)
    PULL.append(2.0 * _next / CHEB_DELTA)
    _ratio = _next

VMEM = pl.BlockSpec(memory_space=pltpu.VMEM)
SMEM = pl.BlockSpec(memory_space=pltpu.SMEM)
F32 = jnp.float32


def call(kernel, outs, scratch=(), limit=16, cost=4_000_000):
    return functools.partial(
        pl.pallas_call,
        kernel,
        out_shape=outs,
        out_specs=jax.tree.map(lambda _: VMEM, outs),
        scratch_shapes=list(scratch),
        compiler_params=pltpu.CompilerParams(vmem_limit_bytes=limit << 20),
        cost_estimate=pl.CostEstimate(flops=cost, bytes_accessed=1 << 18, transcendentals=0),
    )


def ionic_rows(rows):
    voltage, gating = rows[0], rows[1:14]
    sodium, potassium, calcium, reticulum, subspace = rows[14:19]
    moved = []
    for i, gate in enumerate(gating):
        shifted = voltage - GATE_MIDPOINT[i]
        steady = jax.nn.sigmoid(shifted / GATE_STEEPNESS[i])
        time_const = TIME_BASE[i] + TIME_PEAK[i] * jnp.exp(-jnp.square(shifted / 0.3))
        moved.append(steady + (gate - steady) * jnp.exp(-TIME_STEP / time_const))
    g = moved
    sodium_rev = NERNST_SCALE * jnp.log(SODIUM_OUT / sodium)
    potassium_rev = NERNST_SCALE * jnp.log(POTASSIUM_OUT / potassium)
    calcium_rev = 0.5 * NERNST_SCALE * jnp.log(CALCIUM_OUT / subspace)
    sodium_flow = COND_SODIUM * (g[0] * g[0] * g[0]) * g[1] * g[2] * (voltage - sodium_rev)
    calcium_flow = COND_CALCIUM * g[3] * g[4] * g[5] * (voltage - calcium_rev)
    potassium_cond = (
        COND_TRANSIENT * g[6] * g[7]
        + COND_RAPID * g[8] * g[9]
        + COND_SLOW * (g[10] * g[10])
        + COND_INWARD * g[11]
    )
    potassium_flow = potassium_cond * (voltage - potassium_rev)
    current = sodium_flow + calcium_flow + potassium_flow
    release = COND_RELEASE * g[12] * (reticulum - subspace) / (reticulum + subspace)
    sodium = sodium * jnp.exp(-0.5 * TIME_STEP * sodium_flow)
    potassium = potassium * jnp.exp(-0.5 * TIME_STEP * potassium_flow)
    calcium = calcium * jnp.exp(-0.5 * TIME_STEP * calcium_flow)
    subspace = subspace * jnp.exp(TIME_STEP * (release - 0.5 * calcium_flow))
    reticulum = reticulum * jnp.exp(-TIME_STEP * release)
    voltage = voltage - TIME_STEP * MEMBRANE_RATE * current
    return [voltage, *moved, sodium, potassium, calcium, reticulum, subspace], current


def pairs_of(index):
    chunks = [index[:, k : k + LANES] for k in range(0, index.shape[1], LANES)]
    return [jnp.concatenate(chunks[k : k + 2], axis=0) for k in range(0, len(chunks), 2)]


def gather(source, rows, index):
    peers = index.shape[0]
    out = []
    for pair in pairs_of(index):
        high, low = pair >> 7, pair & (LANES - 1)
        total = jnp.zeros(pair.shape, F32)
        for h in range(rows):
            picked = jnp.take_along_axis(source(h), low, axis=1)
            total = jnp.where(high == h, picked, total)
        out += [total[:peers], total[peers:]]
    return jnp.concatenate(out, axis=1)


def scatter(values, index, rows):
    slots = values.shape[1]
    high, low = index >> 7, index & (LANES - 1)
    first = values.astype(jnp.bfloat16).astype(F32)
    rest = values - first
    second = rest.astype(jnp.bfloat16).astype(F32)
    third = rest - second
    mine = lax.broadcasted_iota(jnp.int32, (rows, slots), 0) == high
    left = jnp.concatenate([jnp.where(mine, part, 0.0) for part in (first, second, third)], axis=0)
    spread = lax.broadcasted_iota(jnp.int32, (LANES, slots), 0) == low
    right = jnp.where(spread, 1.0, 0.0).astype(jnp.bfloat16)
    sums = lax.dot_general(
        left.astype(jnp.bfloat16), right, (((1,), (1,)), ((), ())), preferred_element_type=F32
    )
    return sums[:rows] + sums[rows : 2 * rows] + sums[2 * rows :]


def pick_current(current, nodes):
    rows, peers = current.shape[0], nodes.shape[0]
    return gather(
        lambda h: jnp.broadcast_to(current[h : h + 1], (2 * peers, LANES)), rows, nodes
    )


def is_even():
    return lax.rem(lax.axis_index("dom"), 2) == 0


def by_side(first, second):
    even = is_even()
    return jnp.where(even, first, second), jnp.where(even, second, first)


def spread_current(outgoing, maps, own_ref, first_ref, second_ref, far_ref):
    torso = own_ref.shape[0]
    own, after, before, far = (
        scatter(outgoing[o : o + 1], maps[o : o + 1], torso) for o in range(maps.shape[0])
    )
    even = is_even()
    own_ref[...] = own
    first_ref[...] = jnp.where(even, after, before)
    second_ref[...] = jnp.where(even, before, after)
    far_ref[...] = far


def feedback_of(estimates, nodes, maps, heart):
    peers = nodes.shape[0]
    torso = estimates[0].shape[0]

    def source(h):
        rows = [estimate[h : h + 1] for estimate in estimates]
        return jnp.concatenate(rows * 2, axis=0)

    returned = gather(source, torso, maps)
    total = jnp.zeros((heart, LANES), F32)
    for o in range(peers):
        total = total + scatter(returned[o : o + 1], nodes[o : o + 1], heart)
    return total


def product(own_ref, other_ref, own_cols, other_cols, window_ref, out_ref):
    tiles, slots = own_ref.shape[0], own_ref.shape[1]
    eye = lax.broadcasted_iota(jnp.int32, (LANES, LANES), 0) == lax.broadcasted_iota(
        jnp.int32, (LANES, LANES), 1
    )
    for t in range(tiles):
        total = None
        for ref, cols in ((own_ref, own_cols), (other_ref, other_cols)):
            for k in range(slots):
                term = ref[t, k] * window_ref[pl.ds(cols[k, t], 1), :]
                total = term if total is None else total + term
        column = jnp.sum(total, axis=1, keepdims=True)
        out_ref[t : t + 1, :] = jnp.sum(jnp.where(eye, column, 0.0), axis=0, keepdims=True)


def fetch(pairs, sems):
    copies = [pltpu.make_async_copy(a, b, sems.at[i]) for i, (a, b) in enumerate(pairs)]
    for copy in copies:
        copy.start()
    return copies


def begin(states_ref, nodes_ref, rows_ref, out_ref, outgoing_ref, own_rows):
    own_rows[...] = rows_ref[0, 0:1]
    for k in range(out_ref.shape[1]):
        out_ref[:, k, :] = states_ref[:, k * LANES : (k + 1) * LANES]
    rows, current = ionic_rows([out_ref[i] for i in range(out_ref.shape[0])])
    for i, row in enumerate(rows):
        out_ref[i] = row
    outgoing_ref[...] = pick_current(current, nodes_ref[...])


def bring(tiles_ref, cols_ref, diag_ref, own_ref, cols_out, diag_out, own_out):
    cols_out[...] = cols_ref[...]
    diag_out[...] = diag_ref[...]
    own_out[...] = own_ref[...]
    del tiles_ref


def first_shares(
    outgoing_ref, nodes_ref, own_rows, first_rows, second_rows, far_rows,
    maps_ref, own_ref, first_ref, second_ref, far_ref,
):
    after, before = by_side(first_rows[0], second_rows[0])
    rows = jnp.concatenate([own_rows[...], after[1:2], before[2:3], far_rows[0, 3:4]], axis=0)
    maps = jnp.where(nodes_ref[...] < 0, -1, rows)
    maps_ref[...] = maps
    spread_current(outgoing_ref[...], maps, own_ref, first_ref, second_ref, far_ref)


def next_shares(
    states_ref, own_estimate, first_estimate, second_estimate, far_estimate, nodes_ref, maps_ref,
    out_ref, own_ref, first_ref, second_ref, far_ref,
):
    nodes, maps = nodes_ref[...], maps_ref[...]
    after, before = by_side(first_estimate[...], second_estimate[...])
    estimates = [own_estimate[...], after, before, far_estimate[...]]
    feedback = feedback_of(estimates, nodes, maps, states_ref.shape[1])
    rows = [states_ref[i] for i in range(states_ref.shape[0])]
    rows[0] = rows[0] + TIME_STEP * FEEDBACK_RATE * feedback
    rows, current = ionic_rows(rows)
    for i, row in enumerate(rows):
        out_ref[i] = row
    outgoing = pick_current(current, nodes)
    spread_current(outgoing, maps, own_ref, first_ref, second_ref, far_ref)


def last_feedback(
    states_ref, own_estimate, first_estimate, second_estimate, far_estimate, nodes_ref, maps_ref,
    out_ref, dense_ref,
):
    nodes, maps = nodes_ref[...], maps_ref[...]
    torso = own_estimate.shape[0]
    after, before = by_side(first_estimate[0:torso], second_estimate[0:torso])
    estimates = [own_estimate[...], after, before, far_estimate[...]]
    feedback = feedback_of(estimates, nodes, maps, states_ref.shape[1])
    dense_ref[...] = states_ref[...]
    dense_ref[0] = states_ref[0] + TIME_STEP * FEEDBACK_RATE * feedback
    for k in range(states_ref.shape[1]):
        out_ref[:, k * LANES : (k + 1) * LANES] = dense_ref[:, k, :]


def fill_window(chain, direction, first, second, window_ref):
    torso = direction.shape[0]
    here = lax.axis_index("dom")
    after, before = by_side(first, second)
    window_ref[0:HALO] = jnp.where(here > 0, before[torso - HALO :], 0.0)
    window_ref[HALO : HALO + torso] = direction
    window_ref[HALO + torso : 2 * HALO + torso] = jnp.where(here < chain - 1, after[0:HALO], 0.0)


def sweep_one(
    chain, own_cols, other_cols, own_ref, other_ref, mine_ref, yours_ref, diag_ref,
    residual_ref, direction_ref, estimate_ref, window_ref, product_ref,
):
    torso = residual_ref.shape[0]
    total = mine_ref[...] + yours_ref[...]
    diag = diag_ref[...]
    residual = total[0:torso]
    direction = residual / (CHEB_THETA * diag)
    fill_window(chain, direction, total[torso : 2 * torso], total[2 * torso :], window_ref)
    product(own_ref, other_ref, own_cols, other_cols, window_ref, product_ref)
    residual = residual - (diag * direction + product_ref[...])
    estimate = direction
    direction = KEEP[0] * direction + PULL[0] * (residual / diag)
    residual_ref[...] = residual
    direction_ref[...] = direction
    estimate_ref[...] = estimate + direction


def sweep_two(
    chain, last, own_cols, other_cols, own_ref, other_ref, first_ref, second_ref, direction_in,
    residual_in, estimate_in, diag_ref, *refs,
):
    estimate_ref, window_ref, product_ref = refs[0], refs[-2], refs[-1]
    torso = estimate_ref.shape[0]
    diag = diag_ref[...]
    direction = direction_in[...]
    fill_window(chain, direction, first_ref[...], second_ref[...], window_ref)
    product(own_ref, other_ref, own_cols, other_cols, window_ref, product_ref)
    residual = residual_in[...] - (diag * direction + product_ref[...])
    direction = KEEP[1] * direction + PULL[1] * (residual / diag)
    estimate = estimate_in[...] + direction
    estimate_ref[...] = estimate
    if last:
        final_ref, residual_ref, packed_ref = refs[1:-2]
        final_ref[...] = estimate
        residual_ref[...] = residual
        packed_ref[0:torso] = estimate
        packed_ref[torso : 2 * torso] = direction


def last_residual(
    chain, own_cols, other_cols, own_ref, other_ref, first_ref, second_ref, packed_ref,
    residual_in, diag_ref, residual_ref, window_ref, product_ref,
):
    torso = residual_ref.shape[0]
    tail = slice(torso, 2 * torso)
    direction = packed_ref[tail]
    fill_window(chain, direction, first_ref[tail], second_ref[tail], window_ref)
    product(own_ref, other_ref, own_cols, other_cols, window_ref, product_ref)
    residual_ref[...] = residual_in[...] - (diag_ref[...] * direction + product_ref[...])


def on_device(states, send_node, send_count, recv_row, columns, tile_values, diagonal):
    chain = lax.axis_size("dom")
    peers, slots = send_node.shape[1:]
    node_count = states.shape[1]
    heart = node_count // LANES
    torso = diagonal.shape[0] // LANES

    def swap(value, partner):
        return lax.ppermute(value, "dom", [(i, partner(i) % chain) for i in range(chain)])

    def with_first(value):
        return swap(value, lambda i: i ^ 1)

    def with_second(value):
        return swap(value, lambda i: ((i + 1) ^ 1) - 1)

    def with_far(value):
        return swap(value, lambda i: i + chain // 2)

    def from_sibling(value):
        return lax.ppermute(value, "sub", [(0, 1), (1, 0)])

    def shape(*dims, dtype=F32):
        return jax.ShapeDtypeStruct(dims, dtype)

    dense = shape(states.shape[0], heart, LANES)
    field = shape(torso, LANES)
    packed = shape(2 * torso, LANES)
    table = shape(peers, slots, dtype=jnp.int32)
    work = (pltpu.VMEM((torso + 2 * HALO, LANES), F32), pltpu.VMEM((torso, LANES), F32))

    rows = [with_first(recv_row), with_second(recv_row), with_far(recv_row)]
    other_tiles = from_sibling(tile_values)
    live = jnp.arange(slots, dtype=jnp.int32)[None, :] < send_count[0][:, None]
    nodes = jnp.where(live, send_node[0], -1)
    row = shape(1, slots, dtype=jnp.int32)
    states, outgoing, own_rows = call(begin, (dense, shape(peers, slots), row))(
        in_specs=[VMEM] * 3
    )(states, nodes, recv_row)
    maps, own, *shares = call(first_shares, (table,) + (field,) * 4)(in_specs=[VMEM] * 6)(
        outgoing, nodes, own_rows, *rows
    )
    columns, diag, own = call(bring, (shape(*columns.shape[::-1], dtype=jnp.int32), field, field))(
        in_specs=[VMEM] * 4
    )(tile_values, columns.T, diagonal.reshape(torso, LANES), own)
    stored = (columns, from_sibling(columns), tile_values, other_tiles)
    for time_step in range(2):
        last = time_step == 1
        first, second, far = shares
        forcing = TORSO_COUPLING * (own + with_first(first) + with_second(second) + with_far(far))
        direction = forcing / (CHEB_THETA * diag)
        mine = jnp.concatenate([forcing, with_first(direction), with_second(direction)])
        residual, direction, estimate = call(
            functools.partial(sweep_one, chain), (field,) * 3, work
        )(in_specs=[SMEM] * 2 + [VMEM] * 5)(*stored, mine, from_sibling(mine), diag)
        estimate, *rest = call(
            functools.partial(sweep_two, chain, last),
            (field,) * 3 + (packed,) if last else (field,),
            work,
        )(in_specs=[SMEM] * 2 + [VMEM] * 8)(
            *stored, with_first(direction), with_second(direction), direction, residual, estimate,
            diag,
        )
        if not last:
            states, own, *shares = call(next_shares, (dense,) + (field,) * 4)(
                in_specs=[VMEM] * 7
            )(
                states, estimate, with_first(estimate), with_second(estimate), with_far(estimate),
                nodes, maps,
            )
    potential, residual, both = rest
    first, second = with_first(both), with_second(both)
    residual = call(functools.partial(last_residual, chain), field, work)(
        in_specs=[SMEM] * 2 + [VMEM] * 7
    )(*stored, first, second, both, residual, diag)
    new_states = call(
        last_feedback, shape(*dense.shape[:1], node_count), (pltpu.VMEM(dense.shape, F32),)
    )(in_specs=[VMEM] * 7)(states, estimate, first, second, with_far(estimate), nodes, maps)
    return new_states, potential.reshape(-1), residual.reshape(-1)


def solution(mesh):
    placed = (
        P(None, ("case", "dom", "sub")),
        P(("case", "dom", "sub"), None, None),
        P(("case", "dom", "sub"), None),
        P(("case", "dom", "sub"), None, None),
        P(("case", "dom"), "sub"),
        P(("case", "dom"), "sub", None, None),
        P(("case", "dom")),
    )
    return jax.shard_map(
        on_device,
        mesh=mesh,
        in_specs=placed,
        out_specs=(P(None, ("case", "dom", "sub")), P(("case", "dom")), P(("case", "dom"))),
        check_vma=False,
    )
```

```python
import functools

import jax
import jax.numpy as jnp
from jax import lax
from jax.experimental import pallas as pl
from jax.experimental.pallas import tpu as pltpu
from jax.sharding import PartitionSpec as P

HALO = 2
SWEEPS = 3
LANES = 128

TIME_STEP = 0.02
NERNST_SCALE = 0.267
SODIUM_OUT = 1.4
POTASSIUM_OUT = 0.054
CALCIUM_OUT = 2000.0
COND_SODIUM = 8.0
COND_CALCIUM = 1.0
COND_TRANSIENT = 0.3
COND_RAPID = 0.2
COND_SLOW = 0.3
COND_INWARD = 2.0
COND_RELEASE = 3.0
MEMBRANE_RATE = 2.0
TORSO_COUPLING = 0.5
FEEDBACK_RATE = 5.0
CHEB_THETA = 1.0
CHEB_DELTA = 0.5
GATE_MIDPOINT = [-0.56, -0.7, -0.7, -0.08, -0.2, -0.3, 0.2, -0.28, -0.26, -0.88, 0.05, -0.8, -0.5]
GATE_STEEPNESS = [0.09, -0.07, -0.07, 0.07, -0.07, -0.09, 0.06, -0.05, 0.07, -0.24, 0.14, -0.1, 0.08]
TIME_BASE = [0.02, 0.3, 1.0, 0.1, 2.0, 0.5, 0.1, 1.0, 1.0, 0.5, 1.0, 0.05, 0.2]
TIME_PEAK = [0.1, 1.0, 3.0, 0.5, 5.0, 2.0, 0.3, 5.0, 3.0, 2.0, 4.0, 0.1, 1.0]

SIGMA = CHEB_THETA / CHEB_DELTA
KEEP, PULL = [], []
_ratio = 1.0 / SIGMA
for _ in range(SWEEPS - 1):
    _next = 1.0 / (2.0 * SIGMA - _ratio)
    KEEP.append(_next * _ratio)
    PULL.append(2.0 * _next / CHEB_DELTA)
    _ratio = _next

VMEM = pl.BlockSpec(memory_space=pltpu.VMEM)
SMEM = pl.BlockSpec(memory_space=pltpu.SMEM)
F32 = jnp.float32


def call(kernel, outs, scratch=(), limit=16, cost=4_000_000):
    return functools.partial(
        pl.pallas_call,
        kernel,
        out_shape=outs,
        out_specs=jax.tree.map(lambda _: VMEM, outs),
        scratch_shapes=list(scratch),
        compiler_params=pltpu.CompilerParams(vmem_limit_bytes=limit << 20),
        cost_estimate=pl.CostEstimate(flops=cost, bytes_accessed=1 << 18, transcendentals=0),
    )


def ionic_rows(rows):
    voltage, gating = rows[0], rows[1:14]
    sodium, potassium, calcium, reticulum, subspace = rows[14:19]
    moved = []
    for i, gate in enumerate(gating):
        shifted = voltage - GATE_MIDPOINT[i]
        steady = jax.nn.sigmoid(shifted / GATE_STEEPNESS[i])
        time_const = TIME_BASE[i] + TIME_PEAK[i] * jnp.exp(-jnp.square(shifted / 0.3))
        moved.append(steady + (gate - steady) * jnp.exp(-TIME_STEP / time_const))
    g = moved
    sodium_rev = NERNST_SCALE * jnp.log(SODIUM_OUT / sodium)
    potassium_rev = NERNST_SCALE * jnp.log(POTASSIUM_OUT / potassium)
    calcium_rev = 0.5 * NERNST_SCALE * jnp.log(CALCIUM_OUT / subspace)
    sodium_flow = COND_SODIUM * (g[0] * g[0] * g[0]) * g[1] * g[2] * (voltage - sodium_rev)
    calcium_flow = COND_CALCIUM * g[3] * g[4] * g[5] * (voltage - calcium_rev)
    potassium_cond = (
        COND_TRANSIENT * g[6] * g[7]
        + COND_RAPID * g[8] * g[9]
        + COND_SLOW * (g[10] * g[10])
        + COND_INWARD * g[11]
    )
    potassium_flow = potassium_cond * (voltage - potassium_rev)
    current = sodium_flow + calcium_flow + potassium_flow
    release = COND_RELEASE * g[12] * (reticulum - subspace) / (reticulum + subspace)
    sodium = sodium * jnp.exp(-0.5 * TIME_STEP * sodium_flow)
    potassium = potassium * jnp.exp(-0.5 * TIME_STEP * potassium_flow)
    calcium = calcium * jnp.exp(-0.5 * TIME_STEP * calcium_flow)
    subspace = subspace * jnp.exp(TIME_STEP * (release - 0.5 * calcium_flow))
    reticulum = reticulum * jnp.exp(-TIME_STEP * release)
    voltage = voltage - TIME_STEP * MEMBRANE_RATE * current
    return [voltage, *moved, sodium, potassium, calcium, reticulum, subspace], current


def pairs_of(index):
    chunks = [index[:, k : k + LANES] for k in range(0, index.shape[1], LANES)]
    return [jnp.concatenate(chunks[k : k + 2], axis=0) for k in range(0, len(chunks), 2)]


def gather(source, rows, index):
    peers = index.shape[0]
    out = []
    for pair in pairs_of(index):
        high, low = pair >> 7, pair & (LANES - 1)
        total = jnp.zeros(pair.shape, F32)
        for h in range(rows):
            picked = jnp.take_along_axis(source(h), low, axis=1)
            total = jnp.where(high == h, picked, total)
        out += [total[:peers], total[peers:]]
    return jnp.concatenate(out, axis=1)


def scatter(values, index, rows):
    slots = values.shape[1]
    high, low = index >> 7, index & (LANES - 1)
    first = values.astype(jnp.bfloat16).astype(F32)
    rest = values - first
    second = rest.astype(jnp.bfloat16).astype(F32)
    third = rest - second
    mine = lax.broadcasted_iota(jnp.int32, (rows, slots), 0) == high
    left = jnp.concatenate([jnp.where(mine, part, 0.0) for part in (first, second, third)], axis=0)
    spread = lax.broadcasted_iota(jnp.int32, (LANES, slots), 0) == low
    right = jnp.where(spread, 1.0, 0.0).astype(jnp.bfloat16)
    sums = lax.dot_general(
        left.astype(jnp.bfloat16), right, (((1,), (1,)), ((), ())), preferred_element_type=F32
    )
    return sums[:rows] + sums[rows : 2 * rows] + sums[2 * rows :]


def pick_current(current, nodes):
    rows, peers = current.shape[0], nodes.shape[0]
    return gather(
        lambda h: jnp.broadcast_to(current[h : h + 1], (2 * peers, LANES)), rows, nodes
    )


def is_even():
    return lax.rem(lax.axis_index("dom"), 2) == 0


def by_side(first, second):
    even = is_even()
    return jnp.where(even, first, second), jnp.where(even, second, first)


def spread_current(outgoing, maps, own_ref, first_ref, second_ref, far_ref):
    torso = own_ref.shape[0]
    own, after, before, far = (
        scatter(outgoing[o : o + 1], maps[o : o + 1], torso) for o in range(maps.shape[0])
    )
    even = is_even()
    own_ref[...] = own
    first_ref[...] = jnp.where(even, after, before)
    second_ref[...] = jnp.where(even, before, after)
    far_ref[...] = far


def feedback_of(estimates, nodes, maps, heart):
    peers = nodes.shape[0]
    torso = estimates[0].shape[0]

    def source(h):
        rows = [estimate[h : h + 1] for estimate in estimates]
        return jnp.concatenate(rows * 2, axis=0)

    returned = gather(source, torso, maps)
    total = jnp.zeros((heart, LANES), F32)
    for o in range(peers):
        total = total + scatter(returned[o : o + 1], nodes[o : o + 1], heart)
    return total


def product(own_ref, other_ref, own_cols, other_cols, window_ref, out_ref):
    tiles, slots = own_ref.shape[0], own_ref.shape[1]
    eye = lax.broadcasted_iota(jnp.int32, (LANES, LANES), 0) == lax.broadcasted_iota(
        jnp.int32, (LANES, LANES), 1
    )
    for t in range(tiles):
        total = None
        for ref, cols in ((own_ref, own_cols), (other_ref, other_cols)):
            for k in range(slots):
                term = ref[t, k] * window_ref[pl.ds(cols[k, t], 1), :]
                total = term if total is None else total + term
        column = jnp.sum(total, axis=1, keepdims=True)
        out_ref[t : t + 1, :] = jnp.sum(jnp.where(eye, column, 0.0), axis=0, keepdims=True)


def fetch(pairs, sems):
    copies = [pltpu.make_async_copy(a, b, sems.at[i]) for i, (a, b) in enumerate(pairs)]
    for copy in copies:
        copy.start()
    return copies


def begin(states_ref, table_ref, out_ref, payload_ref):
    peers = table_ref.shape[0] // 2
    for k in range(out_ref.shape[1]):
        out_ref[:, k, :] = states_ref[:, k * LANES : (k + 1) * LANES]
    rows, current = ionic_rows([out_ref[i] for i in range(out_ref.shape[0])])
    for i, row in enumerate(rows):
        out_ref[i] = row
    payload_ref[0:peers] = pick_current(current, table_ref[0:peers])
    payload_ref[peers:] = table_ref[peers:].astype(F32)


def bring(tiles_ref, cols_ref, diag_ref, payload_ref, cols_out, diag_out, payload_out):
    cols_out[...] = cols_ref[...]
    diag_out[...] = diag_ref[...]
    payload_out[...] = payload_ref[...]
    del tiles_ref


def first_forcing(
    table_ref, own_ref, first_ref, second_ref, far_ref, diag_ref,
    maps_ref, forcing_ref, direction_ref,
):
    peers = table_ref.shape[0] // 2
    after, before = by_side(first_ref[...], second_ref[...])
    come = [own_ref[0:1], before[1:2], after[2:3], far_ref[3:4]]
    rows = [own_ref[peers : peers + 1], after[peers + 1 : peers + 2]]
    rows += [before[peers + 2 : peers + 3], far_ref[peers + 3 : peers + 4]]
    nodes = table_ref[0:peers]
    maps_ref[...] = jnp.where(nodes < 0, -1, jnp.concatenate(rows, axis=0).astype(jnp.int32))
    total = None
    for o in range(peers):
        part = scatter(come[o], table_ref[peers + o : peers + o + 1], forcing_ref.shape[0])
        total = part if total is None else total + part
    forcing = TORSO_COUPLING * total
    forcing_ref[...] = forcing
    direction_ref[...] = forcing / (CHEB_THETA * diag_ref[...])


def next_shares(
    states_ref, own_estimate, first_estimate, second_estimate, far_estimate, table_ref, maps_ref,
    out_ref, own_ref, first_ref, second_ref, far_ref,
):
    nodes, maps = table_ref[0 : table_ref.shape[0] // 2], maps_ref[...]
    after, before = by_side(first_estimate[...], second_estimate[...])
    estimates = [own_estimate[...], after, before, far_estimate[...]]
    feedback = feedback_of(estimates, nodes, maps, states_ref.shape[1])
    rows = [states_ref[i] for i in range(states_ref.shape[0])]
    rows[0] = rows[0] + TIME_STEP * FEEDBACK_RATE * feedback
    rows, current = ionic_rows(rows)
    for i, row in enumerate(rows):
        out_ref[i] = row
    outgoing = pick_current(current, nodes)
    spread_current(outgoing, maps, own_ref, first_ref, second_ref, far_ref)


def fill_window(chain, direction, first, second, window_ref):
    torso = direction.shape[0]
    here = lax.axis_index("dom")
    after, before = by_side(first, second)
    window_ref[0:HALO] = jnp.where(here > 0, before[torso - HALO :], 0.0)
    window_ref[HALO : HALO + torso] = direction
    window_ref[HALO + torso : 2 * HALO + torso] = jnp.where(here < chain - 1, after[0:HALO], 0.0)


def sweep_one(
    chain, own_cols, other_cols, own_ref, other_ref, mine_ref, yours_ref, diag_ref,
    residual_ref, direction_ref, estimate_ref, window_ref, product_ref,
):
    torso = residual_ref.shape[0]
    total = mine_ref[...] + yours_ref[...]
    diag = diag_ref[...]
    residual = total[0:torso]
    direction = residual / (CHEB_THETA * diag)
    fill_window(chain, direction, total[torso : 2 * torso], total[2 * torso :], window_ref)
    product(own_ref, other_ref, own_cols, other_cols, window_ref, product_ref)
    residual = residual - (diag * direction + product_ref[...])
    estimate = direction
    direction = KEEP[0] * direction + PULL[0] * (residual / diag)
    residual_ref[...] = residual
    direction_ref[...] = direction
    estimate_ref[...] = estimate + direction


def sweep_two(
    chain, last, own_cols, other_cols, own_ref, other_ref, first_ref, second_ref, direction_in,
    residual_in, estimate_in, diag_ref, *refs,
):
    estimate_ref, window_ref, product_ref = refs[0], refs[-2], refs[-1]
    torso = estimate_ref.shape[0]
    diag = diag_ref[...]
    direction = direction_in[...]
    fill_window(chain, direction, first_ref[...], second_ref[...], window_ref)
    product(own_ref, other_ref, own_cols, other_cols, window_ref, product_ref)
    residual = residual_in[...] - (diag * direction + product_ref[...])
    direction = KEEP[1] * direction + PULL[1] * (residual / diag)
    estimate = estimate_in[...] + direction
    estimate_ref[...] = estimate
    if last:
        residual_ref, packed_ref = refs[1:-2]
        residual_ref[...] = residual
        packed_ref[0:torso] = estimate
        packed_ref[torso : 2 * torso] = direction


def finish(
    chain, own_cols, other_cols, own_ref, other_ref, first_ref, second_ref, packed_ref, far_ref,
    residual_in, diag_ref, states_ref, table_ref, maps_ref,
    out_ref, potential_ref, residual_ref, window_ref, product_ref, dense_ref,
):
    torso = residual_ref.shape[0]
    peers = maps_ref.shape[0]
    head, tail = slice(0, torso), slice(torso, 2 * torso)
    estimate, direction = packed_ref[head], packed_ref[tail]
    potential_ref[...] = estimate
    after, before = by_side(first_ref[head], second_ref[head])
    feedback = feedback_of(
        [estimate, after, before, far_ref[...]], table_ref[0:peers], maps_ref[...],
        states_ref.shape[1],
    )
    dense_ref[...] = states_ref[...]
    dense_ref[0] = states_ref[0] + TIME_STEP * FEEDBACK_RATE * feedback
    for k in range(states_ref.shape[1]):
        out_ref[:, k * LANES : (k + 1) * LANES] = dense_ref[:, k, :]
    fill_window(chain, direction, first_ref[tail], second_ref[tail], window_ref)
    product(own_ref, other_ref, own_cols, other_cols, window_ref, product_ref)
    residual_ref[...] = residual_in[...] - (diag_ref[...] * direction + product_ref[...])


def on_device(states, send_node, send_count, recv_row, columns, tile_values, diagonal):
    chain = lax.axis_size("dom")
    peers, slots = send_node.shape[1:]
    node_count = states.shape[1]
    heart = node_count // LANES
    torso = diagonal.shape[0] // LANES

    def swap(value, partner):
        return lax.ppermute(value, "dom", [(i, partner(i) % chain) for i in range(chain)])

    def with_first(value):
        return swap(value, lambda i: i ^ 1)

    def with_second(value):
        return swap(value, lambda i: ((i + 1) ^ 1) - 1)

    def with_inner(value):
        ends = (0, chain - 1)
        return swap(value, lambda i: i if i in ends else ((i + 1) ^ 1) - 1)

    def with_far(value):
        return swap(value, lambda i: i + chain // 2)

    def from_sibling(value):
        return lax.ppermute(value, "sub", [(0, 1), (1, 0)])

    def shape(*dims, dtype=F32):
        return jax.ShapeDtypeStruct(dims, dtype)

    dense = shape(states.shape[0], heart, LANES)
    field = shape(torso, LANES)
    packed = shape(2 * torso, LANES)
    work = (pltpu.VMEM((torso + 2 * HALO, LANES), F32), pltpu.VMEM((torso, LANES), F32))

    other_tiles = from_sibling(tile_values)
    live = jnp.arange(slots, dtype=jnp.int32)[None, :] < send_count[0][:, None]
    table = jnp.concatenate([jnp.where(live, send_node[0], -1), recv_row[0]])
    states, payload = call(begin, (dense, shape(2 * peers, slots)))(in_specs=[VMEM] * 2)(
        states, table
    )
    columns, diag, own = call(
        bring, (shape(*columns.shape[::-1], dtype=jnp.int32), field, shape(2 * peers, slots))
    )(in_specs=[VMEM] * 4)(tile_values, columns.T, diagonal.reshape(torso, LANES), payload)
    stored = (columns, from_sibling(columns), tile_values, other_tiles)
    maps, forcing, direction = call(
        first_forcing, (shape(peers, slots, dtype=jnp.int32), field, field)
    )(in_specs=[VMEM] * 6)(
        table, own, with_first(payload), with_second(payload), with_far(payload), diag
    )
    for time_step in range(2):
        last = time_step == 1
        mine = jnp.concatenate([forcing, with_first(direction), with_inner(direction)])
        residual, direction, estimate = call(
            functools.partial(sweep_one, chain), (field,) * 3, work
        )(in_specs=[SMEM] * 2 + [VMEM] * 5)(*stored, mine, from_sibling(mine), diag)
        estimate, *rest = call(
            functools.partial(sweep_two, chain, last),
            (field,) * 2 + (packed,) if last else (field,),
            work,
        )(in_specs=[SMEM] * 2 + [VMEM] * 8)(
            *stored, with_first(direction), with_inner(direction), direction, residual, estimate,
            diag,
        )
        if not last:
            states, own, first, second, far = call(next_shares, (dense,) + (field,) * 4)(
                in_specs=[VMEM] * 7
            )(
                states, estimate, with_first(estimate), with_second(estimate), with_far(estimate),
                table, maps,
            )
            forcing = own + with_first(first) + with_second(second) + with_far(far)
            forcing = TORSO_COUPLING * forcing
            direction = forcing / (CHEB_THETA * diag)
    residual, both = rest
    new_states, potential, residual = call(
        functools.partial(finish, chain),
        (shape(*dense.shape[:1], node_count), field, field),
        work + (pltpu.VMEM(dense.shape, F32),),
    )(in_specs=[SMEM] * 2 + [VMEM] * 11)(
        *stored, with_first(both), with_second(both), both, with_far(estimate), residual, diag,
        states, table, maps,
    )
    return new_states, potential.reshape(-1), residual.reshape(-1)


def solution(mesh):
    placed = (
        P(None, ("case", "dom", "sub")),
        P(("case", "dom", "sub"), None, None),
        P(("case", "dom", "sub"), None),
        P(("case", "dom", "sub"), None, None),
        P(("case", "dom"), "sub"),
        P(("case", "dom"), "sub", None, None),
        P(("case", "dom")),
    )
    return jax.shard_map(
        on_device,
        mesh=mesh,
        in_specs=placed,
        out_specs=(P(None, ("case", "dom", "sub")), P(("case", "dom")), P(("case", "dom"))),
        check_vma=False,
    )
```

```python
import functools

import jax
import jax.numpy as jnp
from jax import lax
from jax.experimental import pallas as pl
from jax.experimental.pallas import tpu as pltpu
from jax.sharding import PartitionSpec as P

HALO = 2
SWEEPS = 3
LANES = 128

TIME_STEP = 0.02
NERNST_SCALE = 0.267
SODIUM_OUT = 1.4
POTASSIUM_OUT = 0.054
CALCIUM_OUT = 2000.0
COND_SODIUM = 8.0
COND_CALCIUM = 1.0
COND_TRANSIENT = 0.3
COND_RAPID = 0.2
COND_SLOW = 0.3
COND_INWARD = 2.0
COND_RELEASE = 3.0
MEMBRANE_RATE = 2.0
TORSO_COUPLING = 0.5
FEEDBACK_RATE = 5.0
CHEB_THETA = 1.0
CHEB_DELTA = 0.5
GATE_MIDPOINT = [-0.56, -0.7, -0.7, -0.08, -0.2, -0.3, 0.2, -0.28, -0.26, -0.88, 0.05, -0.8, -0.5]
GATE_STEEPNESS = [0.09, -0.07, -0.07, 0.07, -0.07, -0.09, 0.06, -0.05, 0.07, -0.24, 0.14, -0.1, 0.08]
TIME_BASE = [0.02, 0.3, 1.0, 0.1, 2.0, 0.5, 0.1, 1.0, 1.0, 0.5, 1.0, 0.05, 0.2]
TIME_PEAK = [0.1, 1.0, 3.0, 0.5, 5.0, 2.0, 0.3, 5.0, 3.0, 2.0, 4.0, 0.1, 1.0]

SIGMA = CHEB_THETA / CHEB_DELTA
KEEP, PULL = [], []
_ratio = 1.0 / SIGMA
for _ in range(SWEEPS - 1):
    _next = 1.0 / (2.0 * SIGMA - _ratio)
    KEEP.append(_next * _ratio)
    PULL.append(2.0 * _next / CHEB_DELTA)
    _ratio = _next

VMEM = pl.BlockSpec(memory_space=pltpu.VMEM)
SMEM = pl.BlockSpec(memory_space=pltpu.SMEM)
F32 = jnp.float32


def call(kernel, outs, scratch=(), limit=16, cost=4_000_000):
    return functools.partial(
        pl.pallas_call,
        kernel,
        out_shape=outs,
        out_specs=jax.tree.map(lambda _: VMEM, outs),
        scratch_shapes=list(scratch),
        compiler_params=pltpu.CompilerParams(vmem_limit_bytes=limit << 20),
        cost_estimate=pl.CostEstimate(flops=cost, bytes_accessed=1 << 18, transcendentals=0),
    )


def ionic_rows(rows):
    voltage, gating = rows[0], rows[1:14]
    sodium, potassium, calcium, reticulum, subspace = rows[14:19]
    moved = []
    for i, gate in enumerate(gating):
        shifted = voltage - GATE_MIDPOINT[i]
        steady = jax.nn.sigmoid(shifted / GATE_STEEPNESS[i])
        time_const = TIME_BASE[i] + TIME_PEAK[i] * jnp.exp(-jnp.square(shifted / 0.3))
        moved.append(steady + (gate - steady) * jnp.exp(-TIME_STEP / time_const))
    g = moved
    sodium_rev = NERNST_SCALE * jnp.log(SODIUM_OUT / sodium)
    potassium_rev = NERNST_SCALE * jnp.log(POTASSIUM_OUT / potassium)
    calcium_rev = 0.5 * NERNST_SCALE * jnp.log(CALCIUM_OUT / subspace)
    sodium_flow = COND_SODIUM * (g[0] * g[0] * g[0]) * g[1] * g[2] * (voltage - sodium_rev)
    calcium_flow = COND_CALCIUM * g[3] * g[4] * g[5] * (voltage - calcium_rev)
    potassium_cond = (
        COND_TRANSIENT * g[6] * g[7]
        + COND_RAPID * g[8] * g[9]
        + COND_SLOW * (g[10] * g[10])
        + COND_INWARD * g[11]
    )
    potassium_flow = potassium_cond * (voltage - potassium_rev)
    current = sodium_flow + calcium_flow + potassium_flow
    release = COND_RELEASE * g[12] * (reticulum - subspace) / (reticulum + subspace)
    sodium = sodium * jnp.exp(-0.5 * TIME_STEP * sodium_flow)
    potassium = potassium * jnp.exp(-0.5 * TIME_STEP * potassium_flow)
    calcium = calcium * jnp.exp(-0.5 * TIME_STEP * calcium_flow)
    subspace = subspace * jnp.exp(TIME_STEP * (release - 0.5 * calcium_flow))
    reticulum = reticulum * jnp.exp(-TIME_STEP * release)
    voltage = voltage - TIME_STEP * MEMBRANE_RATE * current
    return [voltage, *moved, sodium, potassium, calcium, reticulum, subspace], current


def pairs_of(index):
    chunks = [index[:, k : k + LANES] for k in range(0, index.shape[1], LANES)]
    return [jnp.concatenate(chunks[k : k + 2], axis=0) for k in range(0, len(chunks), 2)]


def gather(source, rows, index):
    peers = index.shape[0]
    out = []
    for pair in pairs_of(index):
        high, low = pair >> 7, pair & (LANES - 1)
        total = jnp.zeros(pair.shape, F32)
        for h in range(rows):
            picked = jnp.take_along_axis(source(h), low, axis=1)
            total = jnp.where(high == h, picked, total)
        out += [total[:peers], total[peers:]]
    return jnp.concatenate(out, axis=1)


def scatter(values, index, rows):
    slots = values.shape[1]
    high, low = index >> 7, index & (LANES - 1)
    first = values.astype(jnp.bfloat16).astype(F32)
    rest = values - first
    second = rest.astype(jnp.bfloat16).astype(F32)
    third = rest - second
    mine = lax.broadcasted_iota(jnp.int32, (rows, slots), 0) == high
    left = jnp.concatenate([jnp.where(mine, part, 0.0) for part in (first, second, third)], axis=0)
    spread = lax.broadcasted_iota(jnp.int32, (LANES, slots), 0) == low
    right = jnp.where(spread, 1.0, 0.0).astype(jnp.bfloat16)
    sums = lax.dot_general(
        left.astype(jnp.bfloat16), right, (((1,), (1,)), ((), ())), preferred_element_type=F32
    )
    return sums[:rows] + sums[rows : 2 * rows] + sums[2 * rows :]


def pick_current(current, nodes):
    rows, peers = current.shape[0], nodes.shape[0]
    return gather(
        lambda h: jnp.broadcast_to(current[h : h + 1], (2 * peers, LANES)), rows, nodes
    )


def is_even():
    return lax.rem(lax.axis_index("dom"), 2) == 0


def by_partner(mine, yours):
    zero = lax.axis_index("sub") == 0
    return jnp.where(zero, mine, yours), jnp.where(zero, yours, mine)


def by_side(first, second):
    even = is_even()
    return jnp.where(even, first, second), jnp.where(even, second, first)


def spread_current(outgoing, maps, own_ref, first_ref, second_ref, far_ref):
    torso = own_ref.shape[0]
    own, after, before, far = (
        scatter(outgoing[o : o + 1], maps[o : o + 1], torso) for o in range(maps.shape[0])
    )
    even = is_even()
    own_ref[...] = own
    first_ref[...] = jnp.where(even, after, before)
    second_ref[...] = jnp.where(even, before, after)
    far_ref[...] = far


def feedback_of(estimates, nodes, maps, heart):
    peers = nodes.shape[0]
    torso = estimates[0].shape[0]

    def source(h):
        rows = [estimate[h : h + 1] for estimate in estimates]
        return jnp.concatenate(rows * 2, axis=0)

    returned = gather(source, torso, maps)
    total = jnp.zeros((heart, LANES), F32)
    for o in range(peers):
        total = total + scatter(returned[o : o + 1], nodes[o : o + 1], heart)
    return total


def product(own_ref, other_ref, own_cols, other_cols, window_ref, out_ref):
    tiles, slots = own_ref.shape[0], own_ref.shape[1]
    eye = lax.broadcasted_iota(jnp.int32, (LANES, LANES), 0) == lax.broadcasted_iota(
        jnp.int32, (LANES, LANES), 1
    )
    for t in range(tiles):
        total = None
        for ref, cols in ((own_ref, own_cols), (other_ref, other_cols)):
            for k in range(slots):
                term = ref[t, k] * window_ref[pl.ds(cols[k, t], 1), :]
                total = term if total is None else total + term
        column = jnp.sum(total, axis=1, keepdims=True)
        out_ref[t : t + 1, :] = jnp.sum(jnp.where(eye, column, 0.0), axis=0, keepdims=True)


def fetch(pairs, sems):
    copies = [pltpu.make_async_copy(a, b, sems.at[i]) for i, (a, b) in enumerate(pairs)]
    for copy in copies:
        copy.start()
    return copies


def begin(states_ref, table_ref, out_ref, payload_ref, nodes_ref):
    peers, slots = nodes_ref.shape
    for k in range(out_ref.shape[1]):
        out_ref[:, k, :] = states_ref[:, k * LANES : (k + 1) * LANES]
    slot = lax.broadcasted_iota(jnp.int32, (peers, slots), 1)
    nodes = jnp.where(slot < table_ref[2 * peers :], table_ref[0:peers], -1)
    nodes_ref[...] = nodes
    rows, current = ionic_rows([out_ref[i] for i in range(out_ref.shape[0])])
    for i, row in enumerate(rows):
        out_ref[i] = row
    payload_ref[0:peers] = pick_current(current, nodes)
    payload_ref[peers:] = table_ref[peers : 2 * peers].astype(F32)


def bring(cols_ref, diag_ref, payload_ref, cols_out, diag_out, payload_out):
    cols_out[...] = cols_ref[...]
    diag_out[...] = diag_ref[...]
    payload_out[...] = payload_ref[...]


def bring_tiles(tiles_ref, direction_ref, direction_out):
    direction_out[...] = direction_ref[...]
    del tiles_ref


def first_forcing(
    nodes_ref, table_ref, own_ref, first_ref, second_ref, far_ref,
    maps_ref, forcing_ref,
):
    peers = nodes_ref.shape[0]
    after, before = by_side(first_ref[...], second_ref[...])
    come = [own_ref[0:1], before[1:2], after[2:3], far_ref[3:4]]
    rows = [own_ref[peers : peers + 1], after[peers + 1 : peers + 2]]
    rows += [before[peers + 2 : peers + 3], far_ref[peers + 3 : peers + 4]]
    maps_ref[...] = jnp.where(nodes_ref[...] < 0, -1, jnp.concatenate(rows, axis=0).astype(jnp.int32))
    total = None
    for o in range(peers):
        part = scatter(come[o], table_ref[peers + o : peers + o + 1], forcing_ref.shape[0])
        total = part if total is None else total + part
    forcing_ref[...] = TORSO_COUPLING * total


def next_shares(
    states_ref, own_estimate, first_estimate, second_estimate, far_estimate, nodes_ref, maps_ref,
    out_ref, own_ref, first_ref, second_ref, far_ref,
):
    nodes, maps = nodes_ref[...], maps_ref[...]
    after, before = by_side(first_estimate[...], second_estimate[...])
    estimates = [own_estimate[...], after, before, far_estimate[...]]
    feedback = feedback_of(estimates, nodes, maps, states_ref.shape[1])
    rows = [states_ref[i] for i in range(states_ref.shape[0])]
    rows[0] = rows[0] + TIME_STEP * FEEDBACK_RATE * feedback
    rows, current = ionic_rows(rows)
    for i, row in enumerate(rows):
        out_ref[i] = row
    outgoing = pick_current(current, nodes)
    spread_current(outgoing, maps, own_ref, first_ref, second_ref, far_ref)


def fill_window(chain, direction, first, second, window_ref):
    torso = direction.shape[0]
    here = lax.axis_index("dom")
    after, before = by_side(first, second)
    window_ref[0:HALO] = jnp.where(here > 0, before[torso - HALO :], 0.0)
    window_ref[HALO : HALO + torso] = direction
    window_ref[HALO + torso : 2 * HALO + torso] = jnp.where(here < chain - 1, after[0:HALO], 0.0)


def sweep_one(
    chain, own_cols, other_cols, own_ref, other_ref, mine_ref, yours_ref, forcing_ref,
    direction_in, diag_ref, residual_ref, direction_ref, estimate_ref, window_ref, product_ref,
):
    diag = diag_ref[...]
    direction = direction_in[...]
    first, second = by_partner(mine_ref[...], yours_ref[...])
    fill_window(chain, direction, first, second, window_ref)
    product(own_ref, other_ref, own_cols, other_cols, window_ref, product_ref)
    residual = forcing_ref[...] - (diag * direction + product_ref[...])
    estimate = direction
    direction = KEEP[0] * direction + PULL[0] * (residual / diag)
    residual_ref[...] = residual
    direction_ref[...] = direction
    estimate_ref[...] = estimate + direction


def sweep_two(
    chain, last, own_cols, other_cols, own_ref, other_ref, mine_ref, yours_ref, direction_in,
    residual_in, estimate_in, diag_ref, *refs,
):
    estimate_ref, window_ref, product_ref = refs[0], refs[-2], refs[-1]
    torso = estimate_ref.shape[0]
    diag = diag_ref[...]
    direction = direction_in[...]
    first, second = by_partner(mine_ref[...], yours_ref[...])
    fill_window(chain, direction, first, second, window_ref)
    product(own_ref, other_ref, own_cols, other_cols, window_ref, product_ref)
    residual = residual_in[...] - (diag * direction + product_ref[...])
    direction = KEEP[1] * direction + PULL[1] * (residual / diag)
    estimate = estimate_in[...] + direction
    estimate_ref[...] = estimate
    if last:
        residual_ref, packed_ref = refs[1:-2]
        residual_ref[...] = residual
        packed_ref[0:torso] = estimate
        packed_ref[torso : 2 * torso] = direction


def finish(
    chain, own_cols, other_cols, own_ref, other_ref, first_ref, second_ref, packed_ref, far_ref,
    residual_in, diag_ref, states_ref, nodes_ref, maps_ref,
    out_ref, potential_ref, residual_ref, window_ref, product_ref, dense_ref,
):
    torso = residual_ref.shape[0]
    head, tail = slice(0, torso), slice(torso, 2 * torso)
    estimate, direction = packed_ref[head], packed_ref[tail]
    potential_ref[...] = estimate
    after, before = by_side(first_ref[head], second_ref[head])
    feedback = feedback_of(
        [estimate, after, before, far_ref[...]], nodes_ref[...], maps_ref[...],
        states_ref.shape[1],
    )
    dense_ref[...] = states_ref[...]
    dense_ref[0] = states_ref[0] + TIME_STEP * FEEDBACK_RATE * feedback
    for k in range(states_ref.shape[1]):
        out_ref[:, k * LANES : (k + 1) * LANES] = dense_ref[:, k, :]
    fill_window(chain, direction, first_ref[tail], second_ref[tail], window_ref)
    product(own_ref, other_ref, own_cols, other_cols, window_ref, product_ref)
    residual_ref[...] = residual_in[...] - (diag_ref[...] * direction + product_ref[...])


def on_device(states, send_node, send_count, recv_row, columns, tile_values, diagonal):
    chain = lax.axis_size("dom")
    peers, slots = send_node.shape[1:]
    node_count = states.shape[1]
    heart = node_count // LANES
    torso = diagonal.shape[0] // LANES

    def swap(value, partner):
        return lax.ppermute(value, "dom", [(i, partner(i) % chain) for i in range(chain)])

    def with_first(value):
        return swap(value, lambda i: i ^ 1)

    def with_second(value):
        return swap(value, lambda i: ((i + 1) ^ 1) - 1)

    def with_either(value):
        pairs = [(2 * i, 2 * (i ^ 1)) for i in range(chain)]
        pairs += [(2 * i + 1, 2 * ((((i + 1) ^ 1) - 1) % chain) + 1) for i in range(chain)]
        return lax.ppermute(value, ("dom", "sub"), pairs)

    def with_far(value):
        return swap(value, lambda i: i + chain // 2)

    def from_sibling(value):
        return lax.ppermute(value, "sub", [(0, 1), (1, 0)])

    def shape(*dims, dtype=F32):
        return jax.ShapeDtypeStruct(dims, dtype)

    dense = shape(states.shape[0], heart, LANES)
    field = shape(torso, LANES)
    packed = shape(2 * torso, LANES)
    work = (pltpu.VMEM((torso + 2 * HALO, LANES), F32), pltpu.VMEM((torso, LANES), F32))

    other_tiles = from_sibling(tile_values)
    counts = jnp.broadcast_to(send_count[0][:, None], (peers, slots))
    table = jnp.concatenate([send_node[0], recv_row[0], counts])
    index = shape(peers, slots, dtype=jnp.int32)
    payload = shape(2 * peers, slots)
    states, payload, nodes = call(begin, (dense, payload, index))(in_specs=[VMEM] * 2)(
        states, table
    )
    columns, diag, own = call(
        bring, (shape(*columns.shape[::-1], dtype=jnp.int32), field, payload)
    )(in_specs=[VMEM] * 3)(columns.T, diagonal.reshape(torso, LANES), payload)
    stored = (columns, from_sibling(columns), tile_values, other_tiles)
    maps, forcing = call(first_forcing, (index, field))(in_specs=[VMEM] * 6)(
        nodes, table, own, with_first(payload), with_second(payload), with_far(payload)
    )
    for time_step in range(2):
        last = time_step == 1
        forcing = forcing + from_sibling(forcing)
        direction = forcing / (CHEB_THETA * diag)
        halo = with_either(direction)
        if not last:
            direction = call(bring_tiles, field)(in_specs=[VMEM] * 2)(tile_values, direction)
            halo, direction = lax.optimization_barrier((halo, direction))
        residual, direction, estimate = call(
            functools.partial(sweep_one, chain), (field,) * 3, work
        )(in_specs=[SMEM] * 2 + [VMEM] * 7)(
            *stored, halo, from_sibling(halo), forcing, direction, diag
        )
        halo = with_either(direction)
        estimate, *rest = call(
            functools.partial(sweep_two, chain, last),
            (field,) * 2 + (packed,) if last else (field,),
            work,
        )(in_specs=[SMEM] * 2 + [VMEM] * 8)(
            *stored, halo, from_sibling(halo), direction, residual, estimate, diag
        )
        if not last:
            states, own, first, second, far = call(next_shares, (dense,) + (field,) * 4)(
                in_specs=[VMEM] * 7
            )(
                states, estimate, with_first(estimate), with_second(estimate), with_far(estimate),
                nodes, maps,
            )
            forcing = own + with_first(first) + with_second(second) + with_far(far)
            forcing = TORSO_COUPLING * forcing
    residual, both = rest
    new_states, potential, residual = call(
        functools.partial(finish, chain),
        (shape(*dense.shape[:1], node_count), field, field),
        work + (pltpu.VMEM(dense.shape, F32),),
    )(in_specs=[SMEM] * 2 + [VMEM] * 11)(
        *stored, with_first(both), with_second(both), both, with_far(estimate), residual, diag,
        states, nodes, maps,
    )
    return new_states, potential.reshape(-1), residual.reshape(-1)


def solution(mesh):
    placed = (
        P(None, ("case", "dom", "sub")),
        P(("case", "dom", "sub"), None, None),
        P(("case", "dom", "sub"), None),
        P(("case", "dom", "sub"), None, None),
        P(("case", "dom"), "sub"),
        P(("case", "dom"), "sub", None, None),
        P(("case", "dom")),
    )
    return jax.shard_map(
        on_device,
        mesh=mesh,
        in_specs=placed,
        out_specs=(P(None, ("case", "dom", "sub")), P(("case", "dom")), P(("case", "dom"))),
        check_vma=False,
    )
```

```python
import functools

import jax
import jax.numpy as jnp
from jax import lax
from jax.experimental import pallas as pl
from jax.experimental.pallas import tpu as pltpu
from jax.sharding import PartitionSpec as P

HALO = 2
SWEEPS = 3
LANES = 128

TIME_STEP = 0.02
NERNST_SCALE = 0.267
SODIUM_OUT = 1.4
POTASSIUM_OUT = 0.054
CALCIUM_OUT = 2000.0
COND_SODIUM = 8.0
COND_CALCIUM = 1.0
COND_TRANSIENT = 0.3
COND_RAPID = 0.2
COND_SLOW = 0.3
COND_INWARD = 2.0
COND_RELEASE = 3.0
MEMBRANE_RATE = 2.0
TORSO_COUPLING = 0.5
FEEDBACK_RATE = 5.0
CHEB_THETA = 1.0
CHEB_DELTA = 0.5
GATE_MIDPOINT = [-0.56, -0.7, -0.7, -0.08, -0.2, -0.3, 0.2, -0.28, -0.26, -0.88, 0.05, -0.8, -0.5]
GATE_STEEPNESS = [0.09, -0.07, -0.07, 0.07, -0.07, -0.09, 0.06, -0.05, 0.07, -0.24, 0.14, -0.1, 0.08]
TIME_BASE = [0.02, 0.3, 1.0, 0.1, 2.0, 0.5, 0.1, 1.0, 1.0, 0.5, 1.0, 0.05, 0.2]
TIME_PEAK = [0.1, 1.0, 3.0, 0.5, 5.0, 2.0, 0.3, 5.0, 3.0, 2.0, 4.0, 0.1, 1.0]

SIGMA = CHEB_THETA / CHEB_DELTA
KEEP, PULL = [], []
_ratio = 1.0 / SIGMA
for _ in range(SWEEPS - 1):
    _next = 1.0 / (2.0 * SIGMA - _ratio)
    KEEP.append(_next * _ratio)
    PULL.append(2.0 * _next / CHEB_DELTA)
    _ratio = _next

VMEM = pl.BlockSpec(memory_space=pltpu.VMEM)
SMEM = pl.BlockSpec(memory_space=pltpu.SMEM)
F32 = jnp.float32


def call(kernel, outs, scratch=(), limit=16, cost=4_000_000):
    return functools.partial(
        pl.pallas_call,
        kernel,
        out_shape=outs,
        out_specs=jax.tree.map(lambda _: VMEM, outs),
        scratch_shapes=list(scratch),
        compiler_params=pltpu.CompilerParams(vmem_limit_bytes=limit << 20),
        cost_estimate=pl.CostEstimate(flops=cost, bytes_accessed=1 << 18, transcendentals=0),
    )


def ionic_rows(rows):
    voltage, gating = rows[0], rows[1:14]
    sodium, potassium, calcium, reticulum, subspace = rows[14:19]
    moved = []
    for i, gate in enumerate(gating):
        shifted = voltage - GATE_MIDPOINT[i]
        steady = jax.nn.sigmoid(shifted / GATE_STEEPNESS[i])
        time_const = TIME_BASE[i] + TIME_PEAK[i] * jnp.exp(-jnp.square(shifted / 0.3))
        moved.append(steady + (gate - steady) * jnp.exp(-TIME_STEP / time_const))
    g = moved
    sodium_rev = NERNST_SCALE * jnp.log(SODIUM_OUT / sodium)
    potassium_rev = NERNST_SCALE * jnp.log(POTASSIUM_OUT / potassium)
    calcium_rev = 0.5 * NERNST_SCALE * jnp.log(CALCIUM_OUT / subspace)
    sodium_flow = COND_SODIUM * (g[0] * g[0] * g[0]) * g[1] * g[2] * (voltage - sodium_rev)
    calcium_flow = COND_CALCIUM * g[3] * g[4] * g[5] * (voltage - calcium_rev)
    potassium_cond = (
        COND_TRANSIENT * g[6] * g[7]
        + COND_RAPID * g[8] * g[9]
        + COND_SLOW * (g[10] * g[10])
        + COND_INWARD * g[11]
    )
    potassium_flow = potassium_cond * (voltage - potassium_rev)
    current = sodium_flow + calcium_flow + potassium_flow
    release = COND_RELEASE * g[12] * (reticulum - subspace) / (reticulum + subspace)
    sodium = sodium * jnp.exp(-0.5 * TIME_STEP * sodium_flow)
    potassium = potassium * jnp.exp(-0.5 * TIME_STEP * potassium_flow)
    calcium = calcium * jnp.exp(-0.5 * TIME_STEP * calcium_flow)
    subspace = subspace * jnp.exp(TIME_STEP * (release - 0.5 * calcium_flow))
    reticulum = reticulum * jnp.exp(-TIME_STEP * release)
    voltage = voltage - TIME_STEP * MEMBRANE_RATE * current
    return [voltage, *moved, sodium, potassium, calcium, reticulum, subspace], current


def pairs_of(index):
    chunks = [index[:, k : k + LANES] for k in range(0, index.shape[1], LANES)]
    return [jnp.concatenate(chunks[k : k + 2], axis=0) for k in range(0, len(chunks), 2)]


def gather(source, rows, index):
    peers = index.shape[0]
    out = []
    for pair in pairs_of(index):
        high, low = pair >> 7, pair & (LANES - 1)
        total = jnp.zeros(pair.shape, F32)
        for h in range(rows):
            picked = jnp.take_along_axis(source(h), low, axis=1)
            total = jnp.where(high == h, picked, total)
        out += [total[:peers], total[peers:]]
    return jnp.concatenate(out, axis=1)


def scatter(values, index, rows):
    slots = values.shape[1]
    high, low = index >> 7, index & (LANES - 1)
    first = values.astype(jnp.bfloat16).astype(F32)
    rest = values - first
    second = rest.astype(jnp.bfloat16).astype(F32)
    third = rest - second
    mine = lax.broadcasted_iota(jnp.int32, (rows, slots), 0) == high
    left = jnp.concatenate([jnp.where(mine, part, 0.0) for part in (first, second, third)], axis=0)
    spread = lax.broadcasted_iota(jnp.int32, (LANES, slots), 0) == low
    right = jnp.where(spread, 1.0, 0.0).astype(jnp.bfloat16)
    sums = lax.dot_general(
        left.astype(jnp.bfloat16), right, (((1,), (1,)), ((), ())), preferred_element_type=F32
    )
    return sums[:rows] + sums[rows : 2 * rows] + sums[2 * rows :]


def pick_current(current, nodes):
    rows, peers = current.shape[0], nodes.shape[0]
    return gather(
        lambda h: jnp.broadcast_to(current[h : h + 1], (2 * peers, LANES)), rows, nodes
    )


def is_even():
    return lax.rem(lax.axis_index("dom"), 2) == 0


def by_partner(mine, yours):
    zero = lax.axis_index("sub") == 0
    return jnp.where(zero, mine, yours), jnp.where(zero, yours, mine)


def by_side(first, second):
    even = is_even()
    return jnp.where(even, first, second), jnp.where(even, second, first)


def spread_current(outgoing, maps, own_ref, first_ref, second_ref, far_ref):
    torso = own_ref.shape[0]
    own, after, before, far = (
        scatter(outgoing[o : o + 1], maps[o : o + 1], torso) for o in range(maps.shape[0])
    )
    even = is_even()
    own_ref[...] = own
    first_ref[...] = jnp.where(even, after, before)
    second_ref[...] = jnp.where(even, before, after)
    far_ref[...] = far


def feedback_of(estimates, nodes, maps, heart):
    peers = nodes.shape[0]
    torso = estimates[0].shape[0]

    def source(h):
        rows = [estimate[h : h + 1] for estimate in estimates]
        return jnp.concatenate(rows * 2, axis=0)

    returned = gather(source, torso, maps)
    total = jnp.zeros((heart, LANES), F32)
    for o in range(peers):
        total = total + scatter(returned[o : o + 1], nodes[o : o + 1], heart)
    return total


def product(own_ref, other_ref, own_cols, other_cols, window_ref, out_ref):
    tiles, slots = own_ref.shape[0], own_ref.shape[1]
    eye = lax.broadcasted_iota(jnp.int32, (LANES, LANES), 0) == lax.broadcasted_iota(
        jnp.int32, (LANES, LANES), 1
    )
    for t in range(tiles):
        total = None
        for ref, cols in ((own_ref, own_cols), (other_ref, other_cols)):
            for k in range(slots):
                term = ref[t, k] * window_ref[pl.ds(cols[k, t], 1), :]
                total = term if total is None else total + term
        column = jnp.sum(total, axis=1, keepdims=True)
        out_ref[t : t + 1, :] = jnp.sum(jnp.where(eye, column, 0.0), axis=0, keepdims=True)


def fetch(pairs, sems):
    copies = [pltpu.make_async_copy(a, b, sems.at[i]) for i, (a, b) in enumerate(pairs)]
    for copy in copies:
        copy.start()
    return copies


def begin(states_ref, table_ref, out_ref, payload_ref, nodes_ref):
    peers, slots = nodes_ref.shape
    for k in range(out_ref.shape[1]):
        out_ref[:, k, :] = states_ref[:, k * LANES : (k + 1) * LANES]
    nodes = table_ref[0:peers]
    nodes_ref[...] = nodes
    rows, current = ionic_rows([out_ref[i] for i in range(out_ref.shape[0])])
    for i, row in enumerate(rows):
        out_ref[i] = row
    payload_ref[0:peers] = pick_current(current, nodes)
    payload_ref[peers:] = table_ref[peers:].astype(F32)


def bring(cols_ref, diag_ref, payload_ref, cols_out, diag_out, payload_out):
    cols_out[...] = cols_ref[...]
    diag_out[...] = diag_ref[...]
    payload_out[...] = payload_ref[...]


def bring_tiles(tiles_ref, direction_ref, direction_out):
    direction_out[...] = direction_ref[...]
    del tiles_ref


def first_forcing(
    nodes_ref, table_ref, own_ref, first_ref, second_ref, far_ref,
    maps_ref, forcing_ref,
):
    peers = nodes_ref.shape[0]
    after, before = by_side(first_ref[...], second_ref[...])
    come = [own_ref[0:1], before[1:2], after[2:3], far_ref[3:4]]
    rows = [own_ref[peers : peers + 1], after[peers + 1 : peers + 2]]
    rows += [before[peers + 2 : peers + 3], far_ref[peers + 3 : peers + 4]]
    maps_ref[...] = jnp.where(nodes_ref[...] < 0, -1, jnp.concatenate(rows, axis=0).astype(jnp.int32))
    total = None
    for o in range(peers):
        part = scatter(come[o], table_ref[peers + o : peers + o + 1], forcing_ref.shape[0])
        total = part if total is None else total + part
    forcing_ref[...] = TORSO_COUPLING * total


def next_shares(
    states_ref, own_estimate, first_estimate, second_estimate, far_estimate, nodes_ref, maps_ref,
    out_ref, own_ref, first_ref, second_ref, far_ref,
):
    nodes, maps = nodes_ref[...], maps_ref[...]
    after, before = by_side(first_estimate[...], second_estimate[...])
    estimates = [own_estimate[...], after, before, far_estimate[...]]
    feedback = feedback_of(estimates, nodes, maps, states_ref.shape[1])
    rows = [states_ref[i] for i in range(states_ref.shape[0])]
    rows[0] = rows[0] + TIME_STEP * FEEDBACK_RATE * feedback
    rows, current = ionic_rows(rows)
    for i, row in enumerate(rows):
        out_ref[i] = row
    outgoing = pick_current(current, nodes)
    spread_current(outgoing, maps, own_ref, first_ref, second_ref, far_ref)


def fill_window(chain, direction, first, second, window_ref):
    torso = direction.shape[0]
    here = lax.axis_index("dom")
    after, before = by_side(first, second)
    window_ref[0:HALO] = jnp.where(here > 0, before[torso - HALO :], 0.0)
    window_ref[HALO : HALO + torso] = direction
    window_ref[HALO + torso : 2 * HALO + torso] = jnp.where(here < chain - 1, after[0:HALO], 0.0)


def sweep_one(
    chain, own_cols, other_cols, own_ref, other_ref, mine_ref, yours_ref, forcing_ref,
    direction_in, diag_ref, residual_ref, direction_ref, estimate_ref, window_ref, product_ref,
):
    diag = diag_ref[...]
    direction = direction_in[...]
    first, second = by_partner(mine_ref[...], yours_ref[...])
    fill_window(chain, direction, first, second, window_ref)
    product(own_ref, other_ref, own_cols, other_cols, window_ref, product_ref)
    residual = forcing_ref[...] - (diag * direction + product_ref[...])
    estimate = direction
    direction = KEEP[0] * direction + PULL[0] * (residual / diag)
    residual_ref[...] = residual
    direction_ref[...] = direction
    estimate_ref[...] = estimate + direction


def sweep_two(
    chain, last, own_cols, other_cols, own_ref, other_ref, mine_ref, yours_ref, direction_in,
    residual_in, estimate_in, diag_ref, *refs,
):
    estimate_ref, window_ref, product_ref = refs[0], refs[-2], refs[-1]
    torso = estimate_ref.shape[0]
    diag = diag_ref[...]
    direction = direction_in[...]
    first, second = by_partner(mine_ref[...], yours_ref[...])
    fill_window(chain, direction, first, second, window_ref)
    product(own_ref, other_ref, own_cols, other_cols, window_ref, product_ref)
    residual = residual_in[...] - (diag * direction + product_ref[...])
    direction = KEEP[1] * direction + PULL[1] * (residual / diag)
    estimate = estimate_in[...] + direction
    estimate_ref[...] = estimate
    if last:
        residual_ref, packed_ref = refs[1:-2]
        residual_ref[...] = residual
        packed_ref[0:torso] = estimate
        packed_ref[torso : 2 * torso] = direction


def finish(
    chain, own_cols, other_cols, own_ref, other_ref, first_ref, second_ref, packed_ref, far_ref,
    residual_in, diag_ref, states_ref, nodes_ref, maps_ref,
    out_ref, potential_ref, residual_ref, window_ref, product_ref, dense_ref,
):
    torso = residual_ref.shape[0]
    head, tail = slice(0, torso), slice(torso, 2 * torso)
    estimate, direction = packed_ref[head], packed_ref[tail]
    potential_ref[...] = estimate
    after, before = by_side(first_ref[head], second_ref[head])
    feedback = feedback_of(
        [estimate, after, before, far_ref[...]], nodes_ref[...], maps_ref[...],
        states_ref.shape[1],
    )
    dense_ref[...] = states_ref[...]
    dense_ref[0] = states_ref[0] + TIME_STEP * FEEDBACK_RATE * feedback
    for k in range(states_ref.shape[1]):
        out_ref[:, k * LANES : (k + 1) * LANES] = dense_ref[:, k, :]
    fill_window(chain, direction, first_ref[tail], second_ref[tail], window_ref)
    product(own_ref, other_ref, own_cols, other_cols, window_ref, product_ref)
    residual_ref[...] = residual_in[...] - (diag_ref[...] * direction + product_ref[...])


def on_device(states, send_node, send_count, recv_row, columns, tile_values, diagonal):
    chain = lax.axis_size("dom")
    peers, slots = send_node.shape[1:]
    node_count = states.shape[1]
    heart = node_count // LANES
    torso = diagonal.shape[0] // LANES

    def swap(value, partner):
        return lax.ppermute(value, "dom", [(i, partner(i) % chain) for i in range(chain)])

    def with_first(value):
        return swap(value, lambda i: i ^ 1)

    def with_second(value):
        return swap(value, lambda i: ((i + 1) ^ 1) - 1)

    def with_either(value):
        cases = lax.axis_size("case")
        ends = (0, chain - 1) if cases % 2 == 0 else ()
        pairs = []
        for case in range(cases):
            for i in range(chain):
                me = (case * chain + i) * 2
                pairs.append((me, (case * chain + (i ^ 1)) * 2))
                if i in ends:
                    pairs.append((me + 1, ((case ^ 1) * chain + i) * 2 + 1))
                else:
                    second = (((i + 1) ^ 1) - 1) % chain
                    pairs.append((me + 1, (case * chain + second) * 2 + 1))
        return lax.ppermute(value, ("case", "dom", "sub"), pairs)

    def with_far(value):
        return swap(value, lambda i: i + chain // 2)

    def from_sibling(value):
        return lax.ppermute(value, "sub", [(0, 1), (1, 0)])

    def shape(*dims, dtype=F32):
        return jax.ShapeDtypeStruct(dims, dtype)

    dense = shape(states.shape[0], heart, LANES)
    field = shape(torso, LANES)
    packed = shape(2 * torso, LANES)
    work = (pltpu.VMEM((torso + 2 * HALO, LANES), F32), pltpu.VMEM((torso, LANES), F32))

    other_tiles = from_sibling(tile_values)
    live = jnp.arange(slots, dtype=jnp.int32)[None, :] < send_count[0][:, None]
    table = jnp.concatenate([jnp.where(live, send_node[0], -1), recv_row[0]])
    index = shape(peers, slots, dtype=jnp.int32)
    payload = shape(2 * peers, slots)
    states, payload, nodes = call(begin, (dense, payload, index))(in_specs=[VMEM] * 2)(
        states, table
    )
    columns, diag, own = call(
        bring, (shape(*columns.shape[::-1], dtype=jnp.int32), field, payload)
    )(in_specs=[VMEM] * 3)(columns.T, diagonal.reshape(torso, LANES), payload)
    stored = (columns, from_sibling(columns), tile_values, other_tiles)
    maps, forcing = call(first_forcing, (index, field))(in_specs=[VMEM] * 6)(
        nodes, table, own, with_first(payload), with_second(payload), with_far(payload)
    )
    for time_step in range(2):
        last = time_step == 1
        forcing = forcing + from_sibling(forcing)
        direction = forcing / (CHEB_THETA * diag)
        halo = with_either(direction)
        if not last:
            direction = call(bring_tiles, field)(in_specs=[VMEM] * 2)(tile_values, direction)
            halo, direction = lax.optimization_barrier((halo, direction))
        residual, direction, estimate = call(
            functools.partial(sweep_one, chain), (field,) * 3, work
        )(in_specs=[SMEM] * 2 + [VMEM] * 7)(
            *stored, halo, from_sibling(halo), forcing, direction, diag
        )
        halo = with_either(direction)
        estimate, *rest = call(
            functools.partial(sweep_two, chain, last),
            (field,) * 2 + (packed,) if last else (field,),
            work,
        )(in_specs=[SMEM] * 2 + [VMEM] * 8)(
            *stored, halo, from_sibling(halo), direction, residual, estimate, diag
        )
        if not last:
            states, own, first, second, far = call(next_shares, (dense,) + (field,) * 4)(
                in_specs=[VMEM] * 7
            )(
                states, estimate, with_first(estimate), with_second(estimate), with_far(estimate),
                nodes, maps,
            )
            forcing = own + with_first(first) + with_second(second) + with_far(far)
            forcing = TORSO_COUPLING * forcing
    residual, both = rest
    new_states, potential, residual = call(
        functools.partial(finish, chain),
        (shape(*dense.shape[:1], node_count), field, field),
        work + (pltpu.VMEM(dense.shape, F32),),
    )(in_specs=[SMEM] * 2 + [VMEM] * 11)(
        *stored, with_first(both), with_second(both), both, with_far(estimate), residual, diag,
        states, nodes, maps,
    )
    return new_states, potential.reshape(-1), residual.reshape(-1)


def solution(mesh):
    placed = (
        P(None, ("case", "dom", "sub")),
        P(("case", "dom", "sub"), None, None),
        P(("case", "dom", "sub"), None),
        P(("case", "dom", "sub"), None, None),
        P(("case", "dom"), "sub"),
        P(("case", "dom"), "sub", None, None),
        P(("case", "dom")),
    )
    return jax.shard_map(
        on_device,
        mesh=mesh,
        in_specs=placed,
        out_specs=(P(None, ("case", "dom", "sub")), P(("case", "dom")), P(("case", "dom"))),
        check_vma=False,
    )
```

```python
import functools

import jax
import jax.numpy as jnp
from jax import lax
from jax.experimental import pallas as pl
from jax.experimental.pallas import tpu as pltpu
from jax.sharding import PartitionSpec as P

HALO = 2
SWEEPS = 3
LANES = 128

TIME_STEP = 0.02
NERNST_SCALE = 0.267
SODIUM_OUT = 1.4
POTASSIUM_OUT = 0.054
CALCIUM_OUT = 2000.0
COND_SODIUM = 8.0
COND_CALCIUM = 1.0
COND_TRANSIENT = 0.3
COND_RAPID = 0.2
COND_SLOW = 0.3
COND_INWARD = 2.0
COND_RELEASE = 3.0
MEMBRANE_RATE = 2.0
TORSO_COUPLING = 0.5
FEEDBACK_RATE = 5.0
CHEB_THETA = 1.0
CHEB_DELTA = 0.5
GATE_MIDPOINT = [-0.56, -0.7, -0.7, -0.08, -0.2, -0.3, 0.2, -0.28, -0.26, -0.88, 0.05, -0.8, -0.5]
GATE_STEEPNESS = [0.09, -0.07, -0.07, 0.07, -0.07, -0.09, 0.06, -0.05, 0.07, -0.24, 0.14, -0.1, 0.08]
TIME_BASE = [0.02, 0.3, 1.0, 0.1, 2.0, 0.5, 0.1, 1.0, 1.0, 0.5, 1.0, 0.05, 0.2]
TIME_PEAK = [0.1, 1.0, 3.0, 0.5, 5.0, 2.0, 0.3, 5.0, 3.0, 2.0, 4.0, 0.1, 1.0]

SIGMA = CHEB_THETA / CHEB_DELTA
KEEP, PULL = [], []
_ratio = 1.0 / SIGMA
for _ in range(SWEEPS - 1):
    _next = 1.0 / (2.0 * SIGMA - _ratio)
    KEEP.append(_next * _ratio)
    PULL.append(2.0 * _next / CHEB_DELTA)
    _ratio = _next

VMEM = pl.BlockSpec(memory_space=pltpu.VMEM)
F32 = jnp.float32


def call(kernel, outs, scratch=(), limit=16, cost=4_000_000):
    return functools.partial(
        pl.pallas_call,
        kernel,
        out_shape=outs,
        out_specs=jax.tree.map(lambda _: VMEM, outs),
        scratch_shapes=list(scratch),
        compiler_params=pltpu.CompilerParams(vmem_limit_bytes=limit << 20),
        cost_estimate=pl.CostEstimate(flops=cost, bytes_accessed=1 << 18, transcendentals=0),
    )


def ionic_rows(rows):
    voltage, gating = rows[0], rows[1:14]
    sodium, potassium, calcium, reticulum, subspace = rows[14:19]
    moved = []
    for i, gate in enumerate(gating):
        shifted = voltage - GATE_MIDPOINT[i]
        steady = jax.nn.sigmoid(shifted / GATE_STEEPNESS[i])
        time_const = TIME_BASE[i] + TIME_PEAK[i] * jnp.exp(-jnp.square(shifted / 0.3))
        moved.append(steady + (gate - steady) * jnp.exp(-TIME_STEP / time_const))
    g = moved
    sodium_rev = NERNST_SCALE * jnp.log(SODIUM_OUT / sodium)
    potassium_rev = NERNST_SCALE * jnp.log(POTASSIUM_OUT / potassium)
    calcium_rev = 0.5 * NERNST_SCALE * jnp.log(CALCIUM_OUT / subspace)
    sodium_flow = COND_SODIUM * (g[0] * g[0] * g[0]) * g[1] * g[2] * (voltage - sodium_rev)
    calcium_flow = COND_CALCIUM * g[3] * g[4] * g[5] * (voltage - calcium_rev)
    potassium_cond = (
        COND_TRANSIENT * g[6] * g[7]
        + COND_RAPID * g[8] * g[9]
        + COND_SLOW * (g[10] * g[10])
        + COND_INWARD * g[11]
    )
    potassium_flow = potassium_cond * (voltage - potassium_rev)
    current = sodium_flow + calcium_flow + potassium_flow
    release = COND_RELEASE * g[12] * (reticulum - subspace) / (reticulum + subspace)
    sodium = sodium * jnp.exp(-0.5 * TIME_STEP * sodium_flow)
    potassium = potassium * jnp.exp(-0.5 * TIME_STEP * potassium_flow)
    calcium = calcium * jnp.exp(-0.5 * TIME_STEP * calcium_flow)
    subspace = subspace * jnp.exp(TIME_STEP * (release - 0.5 * calcium_flow))
    reticulum = reticulum * jnp.exp(-TIME_STEP * release)
    voltage = voltage - TIME_STEP * MEMBRANE_RATE * current
    return [voltage, *moved, sodium, potassium, calcium, reticulum, subspace], current


def pairs_of(index):
    chunks = [index[:, k : k + LANES] for k in range(0, index.shape[1], LANES)]
    return [jnp.concatenate(chunks[k : k + 2], axis=0) for k in range(0, len(chunks), 2)]


def gather(source, rows, index):
    peers = index.shape[0]
    out = []
    for pair in pairs_of(index):
        high, low = pair >> 7, pair & (LANES - 1)
        total = jnp.zeros(pair.shape, F32)
        for h in range(rows):
            picked = jnp.take_along_axis(source(h), low, axis=1)
            total = jnp.where(high == h, picked, total)
        out += [total[:peers], total[peers:]]
    return jnp.concatenate(out, axis=1)


def three_parts(value):
    first = value.astype(jnp.bfloat16).astype(F32)
    rest = value - first
    second = rest.astype(jnp.bfloat16).astype(F32)
    return first, second, rest - second


def scatter(values, index, rows):
    slots = values.shape[1]
    high, low = index >> 7, index & (LANES - 1)
    mine = lax.broadcasted_iota(jnp.int32, (rows, slots), 0) == high
    left = jnp.concatenate([jnp.where(mine, part, 0.0) for part in three_parts(values)], axis=0)
    spread = lax.broadcasted_iota(jnp.int32, (LANES, slots), 0) == low
    right = jnp.where(spread, 1.0, 0.0).astype(jnp.bfloat16)
    sums = lax.dot_general(
        left.astype(jnp.bfloat16), right, (((1,), (1,)), ((), ())), preferred_element_type=F32
    )
    return sums[:rows] + sums[rows : 2 * rows] + sums[2 * rows :]


def pick_current(current, nodes):
    rows, peers = current.shape[0], nodes.shape[0]
    return gather(
        lambda h: jnp.broadcast_to(current[h : h + 1], (2 * peers, LANES)), rows, nodes
    )


def is_even():
    return lax.rem(lax.axis_index("dom"), 2) == 0


def by_partner(mine, yours):
    zero = lax.axis_index("sub") == 0
    return jnp.where(zero, mine, yours), jnp.where(zero, yours, mine)


def by_side(first, second):
    even = is_even()
    return jnp.where(even, first, second), jnp.where(even, second, first)


def spread_current(outgoing, maps, own_ref, first_ref, second_ref, far_ref):
    torso = own_ref.shape[0]
    own, after, before, far = (
        scatter(outgoing[o : o + 1], maps[o : o + 1], torso) for o in range(maps.shape[0])
    )
    even = is_even()
    own_ref[...] = own
    first_ref[...] = jnp.where(even, after, before)
    second_ref[...] = jnp.where(even, before, after)
    far_ref[...] = far


def feedback_of(estimates, nodes, maps, heart):
    peers = nodes.shape[0]
    torso = estimates[0].shape[0]

    def source(h):
        rows = [estimate[h : h + 1] for estimate in estimates]
        return jnp.concatenate(rows * 2, axis=0)

    returned = gather(source, torso, maps)
    total = jnp.zeros((heart, LANES), F32)
    for o in range(peers):
        total = total + scatter(returned[o : o + 1], nodes[o : o + 1], heart)
    return total


def product(own_ref, other_ref, pick_ref, window):
    tiles, slots = own_ref.shape[0], own_ref.shape[1]
    parts = jnp.concatenate(three_parts(window), axis=1).astype(jnp.bfloat16)
    picked = jnp.dot(pick_ref[...].astype(jnp.bfloat16), parts, preferred_element_type=F32)
    picked = picked[:, :LANES] + picked[:, LANES : 2 * LANES] + picked[:, 2 * LANES :]
    eye = lax.broadcasted_iota(jnp.int32, (LANES, LANES), 0) == lax.broadcasted_iota(
        jnp.int32, (LANES, LANES), 1
    )
    rows = []
    for t in range(tiles):
        total = None
        for k in range(2 * slots):
            tile = own_ref[t, k] if k < slots else other_ref[t, k - slots]
            term = tile * picked[k * tiles + t : k * tiles + t + 1]
            total = term if total is None else total + term
        column = jnp.sum(total, axis=1, keepdims=True)
        rows.append(jnp.sum(jnp.where(eye, column, 0.0), axis=0, keepdims=True))
    return jnp.concatenate(rows, axis=0)


def fetch(pairs, sems):
    copies = [pltpu.make_async_copy(a, b, sems.at[i]) for i, (a, b) in enumerate(pairs)]
    for copy in copies:
        copy.start()
    return copies


def begin(states_ref, table_ref, out_ref, payload_ref, nodes_ref):
    peers, slots = nodes_ref.shape
    for k in range(out_ref.shape[1]):
        out_ref[:, k, :] = states_ref[:, k * LANES : (k + 1) * LANES]
    slot = lax.broadcasted_iota(jnp.int32, (1, slots), 1)
    for o in range(peers):
        live = slot < table_ref[2 * peers : 2 * peers + 1, o : o + 1]
        nodes_ref[o : o + 1] = jnp.where(live, table_ref[o : o + 1], -1)
    rows, current = ionic_rows([out_ref[i] for i in range(out_ref.shape[0])])
    for i, row in enumerate(rows):
        out_ref[i] = row
    payload_ref[0:peers] = pick_current(current, nodes_ref[...])
    payload_ref[peers:] = table_ref[peers : 2 * peers].astype(F32)


def bring(cols_ref, diag_ref, payload_ref, cols_out, diag_out, payload_out):
    cols_out[...] = cols_ref[...]
    diag_out[...] = diag_ref[...]
    payload_out[...] = payload_ref[...]


def bring_tiles(tiles_ref, own_cols, other_cols, direction_ref, direction_out, pick_ref):
    direction_out[...] = direction_ref[...]
    slots, tiles = own_cols.shape
    eye = lax.broadcasted_iota(jnp.int32, (tiles, tiles), 0) == lax.broadcasted_iota(
        jnp.int32, (tiles, tiles), 1
    )
    place = lax.broadcasted_iota(jnp.int32, (tiles, pick_ref.shape[1]), 1)
    for k in range(2 * slots):
        row = own_cols[k : k + 1] if k < slots else other_cols[k - slots : k - slots + 1]
        column = jnp.sum(jnp.where(eye, row.astype(F32), 0.0), axis=1, keepdims=True)
        pick_ref[k * tiles : (k + 1) * tiles] = jnp.where(place == column.astype(jnp.int32), 1.0, 0.0)
    del tiles_ref


def first_forcing(
    nodes_ref, table_ref, own_ref, first_ref, far_ref, second_ref,
    maps_ref, forcing_ref,
):
    peers = nodes_ref.shape[0]
    after, before = by_side(first_ref[...], second_ref[...])
    come = [own_ref[0:1], before[1:2], after[2:3], far_ref[3:4]]
    rows = [own_ref[peers : peers + 1], after[peers + 1 : peers + 2]]
    rows += [before[peers + 2 : peers + 3], far_ref[peers + 3 : peers + 4]]
    maps_ref[...] = jnp.where(nodes_ref[...] < 0, -1, jnp.concatenate(rows, axis=0).astype(jnp.int32))
    total = None
    for o in range(peers):
        part = scatter(come[o], table_ref[peers + o : peers + o + 1], forcing_ref.shape[0])
        total = part if total is None else total + part
    forcing_ref[...] = TORSO_COUPLING * total


def next_shares(
    states_ref, own_estimate, first_estimate, far_estimate, second_estimate, nodes_ref, maps_ref,
    out_ref, own_ref, first_ref, second_ref, far_ref,
):
    nodes, maps = nodes_ref[...], maps_ref[...]
    after, before = by_side(first_estimate[...], second_estimate[...])
    estimates = [own_estimate[...], after, before, far_estimate[...]]
    feedback = feedback_of(estimates, nodes, maps, states_ref.shape[1])
    rows = [states_ref[i] for i in range(states_ref.shape[0])]
    rows[0] = rows[0] + TIME_STEP * FEEDBACK_RATE * feedback
    rows, current = ionic_rows(rows)
    for i, row in enumerate(rows):
        out_ref[i] = row
    outgoing = pick_current(current, nodes)
    spread_current(outgoing, maps, own_ref, first_ref, second_ref, far_ref)


def window_of(chain, direction, first, second):
    torso = direction.shape[0]
    here = lax.axis_index("dom")
    after, before = by_side(first, second)
    before = jnp.where(here > 0, before[torso - HALO :], 0.0)
    after = jnp.where(here < chain - 1, after[0:HALO], 0.0)
    filler = jnp.zeros((torso - 2 * HALO, LANES), F32)
    return jnp.concatenate([before, direction, after, filler], axis=0)


def sweep_one(
    chain, own_ref, other_ref, pick_ref, mine_ref, yours_ref, forcing_ref, direction_in, diag_ref,
    residual_ref, direction_ref, estimate_ref,
):
    diag = diag_ref[...]
    direction = direction_in[...]
    window = window_of(chain, direction, *by_partner(mine_ref[...], yours_ref[...]))
    moved = product(own_ref, other_ref, pick_ref, window)
    residual = forcing_ref[...] - (diag * direction + moved)
    estimate = direction
    direction = KEEP[0] * direction + PULL[0] * (residual / diag)
    residual_ref[...] = residual
    direction_ref[...] = direction
    estimate_ref[...] = estimate + direction


def sweep_two(
    chain, last, own_ref, other_ref, pick_ref, mine_ref, yours_ref, direction_in, residual_in,
    estimate_in, diag_ref, estimate_ref, *refs,
):
    torso = estimate_ref.shape[0]
    diag = diag_ref[...]
    direction = direction_in[...]
    window = window_of(chain, direction, *by_partner(mine_ref[...], yours_ref[...]))
    moved = product(own_ref, other_ref, pick_ref, window)
    residual = residual_in[...] - (diag * direction + moved)
    direction = KEEP[1] * direction + PULL[1] * (residual / diag)
    estimate = estimate_in[...] + direction
    if last:
        residual_ref, = refs
        residual_ref[...] = residual
        estimate_ref[0 : torso // 2] = estimate
        estimate_ref[torso // 2 :] = direction
    else:
        estimate_ref[...] = estimate


def finish(
    chain, own_ref, other_ref, pick_ref, packed_ref, first_ref, far_ref, second_ref, residual_in,
    diag_ref, states_ref, nodes_ref, maps_ref, out_ref, potential_ref, residual_ref, dense_ref,
):
    torso = residual_ref.shape[0]
    head, tail = slice(0, torso), slice(torso, 2 * torso)
    estimate, direction = packed_ref[head], packed_ref[tail]
    potential_ref[...] = estimate
    after, before = by_side(first_ref[head], second_ref[head])
    feedback = feedback_of(
        [estimate, after, before, far_ref[head]], nodes_ref[...], maps_ref[...],
        states_ref.shape[1],
    )
    dense_ref[...] = states_ref[...]
    dense_ref[0] = states_ref[0] + TIME_STEP * FEEDBACK_RATE * feedback
    for k in range(states_ref.shape[1]):
        out_ref[:, k * LANES : (k + 1) * LANES] = dense_ref[:, k, :]
    window = window_of(chain, direction, first_ref[tail], second_ref[tail])
    moved = product(own_ref, other_ref, pick_ref, window)
    residual_ref[...] = residual_in[...] - (diag_ref[...] * direction + moved)


def on_device(states, send_node, send_count, recv_row, columns, tile_values, diagonal):
    chain = lax.axis_size("dom")
    peers, slots = send_node.shape[1:]
    node_count = states.shape[1]
    heart = node_count // LANES
    torso = diagonal.shape[0] // LANES

    def swap(value, partner):
        return lax.ppermute(value, "dom", [(i, partner(i) % chain) for i in range(chain)])

    def with_first(value):
        return swap(value, lambda i: i ^ 1)

    def with_second(value):
        return swap(value, lambda i: ((i + 1) ^ 1) - 1)

    def with_either(value):
        cases = lax.axis_size("case")
        ends = (0, chain - 1) if cases % 2 == 0 else ()
        pairs = []
        for case in range(cases):
            for i in range(chain):
                me = (case * chain + i) * 2
                pairs.append((me, (case * chain + (i ^ 1)) * 2))
                if i in ends:
                    pairs.append((me + 1, ((case ^ 1) * chain + i) * 2 + 1))
                else:
                    second = (((i + 1) ^ 1) - 1) % chain
                    pairs.append((me + 1, (case * chain + second) * 2 + 1))
        return lax.ppermute(value, ("case", "dom", "sub"), pairs)

    def with_far(value):
        return swap(value, lambda i: i + chain // 2)

    def from_sibling(value):
        return lax.ppermute(value, "sub", [(0, 1), (1, 0)])

    def shape(*dims, dtype=F32):
        return jax.ShapeDtypeStruct(dims, dtype)

    dense = shape(states.shape[0], heart, LANES)
    field = shape(torso, LANES)
    packed = shape(2 * torso, LANES)
    other_tiles = from_sibling(tile_values)
    counts = jnp.pad(send_count, ((0, 0), (0, slots - peers)))
    table = jnp.concatenate([send_node[0], recv_row[0], counts])
    index = shape(peers, slots, dtype=jnp.int32)
    payload = shape(2 * peers, slots)
    states, payload, nodes = call(begin, (dense, payload, index))(in_specs=[VMEM] * 2)(
        states, table
    )
    columns, diag, own = call(
        bring, (shape(*columns.shape[::-1], dtype=jnp.int32), field, payload)
    )(in_specs=[VMEM] * 3)(columns.T, diagonal.reshape(torso, LANES), payload)
    first, far, second = with_first(payload), with_far(payload), with_second(payload)
    maps, forcing = call(first_forcing, (index, field))(in_specs=[VMEM] * 6)(
        nodes, table, own, first, far, second
    )
    for time_step in range(2):
        last = time_step == 1
        forcing = forcing + from_sibling(forcing)
        direction = forcing / (CHEB_THETA * diag)
        halo = with_either(direction)
        if not last:
            choices = 2 * columns.shape[0] * torso
            direction, pick = call(bring_tiles, (field, shape(choices, 2 * torso)))(
                in_specs=[VMEM] * 4
            )(tile_values, columns, from_sibling(columns), direction)
            halo, direction = lax.optimization_barrier((halo, direction))
            stored = (tile_values, other_tiles, pick)
        residual, direction, estimate = call(
            functools.partial(sweep_one, chain), (field,) * 3
        )(in_specs=[VMEM] * 8)(*stored, halo, from_sibling(halo), forcing, direction, diag)
        halo = with_either(direction)
        swept = call(
            functools.partial(sweep_two, chain, last), (packed, field) if last else field
        )(in_specs=[VMEM] * 9)(
            *stored, halo, from_sibling(halo), direction, residual, estimate, diag
        )
        estimate, residual = swept if last else (swept, None)
        first, far, second = with_first(estimate), with_far(estimate), with_second(estimate)
        if not last:
            states, own, *shares = call(next_shares, (dense,) + (field,) * 4)(
                in_specs=[VMEM] * 7
            )(states, estimate, first, far, second, nodes, maps)
            forcing = own + with_second(shares[1]) + with_far(shares[2]) + with_first(shares[0])
            forcing = TORSO_COUPLING * forcing
    new_states, potential, residual = call(
        functools.partial(finish, chain),
        (shape(*dense.shape[:1], node_count), field, field),
        (pltpu.VMEM(dense.shape, F32),),
    )(in_specs=[VMEM] * 12)(
        *stored, estimate, first, far, second, residual, diag, states, nodes, maps
    )
    return new_states, potential.reshape(-1), residual.reshape(-1)


def solution(mesh):
    placed = (
        P(None, ("case", "dom", "sub")),
        P(("case", "dom", "sub"), None, None),
        P(("case", "dom", "sub"), None),
        P(("case", "dom", "sub"), None, None),
        P(("case", "dom"), "sub"),
        P(("case", "dom"), "sub", None, None),
        P(("case", "dom")),
    )
    return jax.shard_map(
        on_device,
        mesh=mesh,
        in_specs=placed,
        out_specs=(P(None, ("case", "dom", "sub")), P(("case", "dom")), P(("case", "dom"))),
        check_vma=False,
    )
```

```python
import functools

import jax
import jax.numpy as jnp
from jax import lax
from jax.experimental import pallas as pl
from jax.experimental.pallas import tpu as pltpu
from jax.sharding import PartitionSpec as P

HALO = 2
SWEEPS = 3
LANES = 128

TIME_STEP = 0.02
NERNST_SCALE = 0.267
SODIUM_OUT = 1.4
POTASSIUM_OUT = 0.054
CALCIUM_OUT = 2000.0
COND_SODIUM = 8.0
COND_CALCIUM = 1.0
COND_TRANSIENT = 0.3
COND_RAPID = 0.2
COND_SLOW = 0.3
COND_INWARD = 2.0
COND_RELEASE = 3.0
MEMBRANE_RATE = 2.0
TORSO_COUPLING = 0.5
FEEDBACK_RATE = 5.0
CHEB_THETA = 1.0
CHEB_DELTA = 0.5
GATE_MIDPOINT = [-0.56, -0.7, -0.7, -0.08, -0.2, -0.3, 0.2, -0.28, -0.26, -0.88, 0.05, -0.8, -0.5]
GATE_STEEPNESS = [0.09, -0.07, -0.07, 0.07, -0.07, -0.09, 0.06, -0.05, 0.07, -0.24, 0.14, -0.1, 0.08]
TIME_BASE = [0.02, 0.3, 1.0, 0.1, 2.0, 0.5, 0.1, 1.0, 1.0, 0.5, 1.0, 0.05, 0.2]
TIME_PEAK = [0.1, 1.0, 3.0, 0.5, 5.0, 2.0, 0.3, 5.0, 3.0, 2.0, 4.0, 0.1, 1.0]

SIGMA = CHEB_THETA / CHEB_DELTA
KEEP, PULL = [], []
_ratio = 1.0 / SIGMA
for _ in range(SWEEPS - 1):
    _next = 1.0 / (2.0 * SIGMA - _ratio)
    KEEP.append(_next * _ratio)
    PULL.append(2.0 * _next / CHEB_DELTA)
    _ratio = _next

VMEM = pl.BlockSpec(memory_space=pltpu.VMEM)
F32 = jnp.float32


def call(kernel, outs, scratch=(), limit=16, cost=4_000_000):
    return functools.partial(
        pl.pallas_call,
        kernel,
        out_shape=outs,
        out_specs=jax.tree.map(lambda _: VMEM, outs),
        scratch_shapes=list(scratch),
        compiler_params=pltpu.CompilerParams(vmem_limit_bytes=limit << 20),
        cost_estimate=pl.CostEstimate(flops=cost, bytes_accessed=1 << 18, transcendentals=0),
    )


def ionic_rows(rows):
    voltage, gating = rows[0], rows[1:14]
    sodium, potassium, calcium, reticulum, subspace = rows[14:19]
    moved = []
    for i, gate in enumerate(gating):
        shifted = voltage - GATE_MIDPOINT[i]
        steady = jax.nn.sigmoid(shifted / GATE_STEEPNESS[i])
        time_const = TIME_BASE[i] + TIME_PEAK[i] * jnp.exp(-jnp.square(shifted / 0.3))
        moved.append(steady + (gate - steady) * jnp.exp(-TIME_STEP / time_const))
    g = moved
    sodium_rev = NERNST_SCALE * jnp.log(SODIUM_OUT / sodium)
    potassium_rev = NERNST_SCALE * jnp.log(POTASSIUM_OUT / potassium)
    calcium_rev = 0.5 * NERNST_SCALE * jnp.log(CALCIUM_OUT / subspace)
    sodium_flow = COND_SODIUM * (g[0] * g[0] * g[0]) * g[1] * g[2] * (voltage - sodium_rev)
    calcium_flow = COND_CALCIUM * g[3] * g[4] * g[5] * (voltage - calcium_rev)
    potassium_cond = (
        COND_TRANSIENT * g[6] * g[7]
        + COND_RAPID * g[8] * g[9]
        + COND_SLOW * (g[10] * g[10])
        + COND_INWARD * g[11]
    )
    potassium_flow = potassium_cond * (voltage - potassium_rev)
    current = sodium_flow + calcium_flow + potassium_flow
    release = COND_RELEASE * g[12] * (reticulum - subspace) / (reticulum + subspace)
    sodium = sodium * jnp.exp(-0.5 * TIME_STEP * sodium_flow)
    potassium = potassium * jnp.exp(-0.5 * TIME_STEP * potassium_flow)
    calcium = calcium * jnp.exp(-0.5 * TIME_STEP * calcium_flow)
    subspace = subspace * jnp.exp(TIME_STEP * (release - 0.5 * calcium_flow))
    reticulum = reticulum * jnp.exp(-TIME_STEP * release)
    voltage = voltage - TIME_STEP * MEMBRANE_RATE * current
    return [voltage, *moved, sodium, potassium, calcium, reticulum, subspace], current


def pairs_of(index):
    chunks = [index[:, k : k + LANES] for k in range(0, index.shape[1], LANES)]
    return [jnp.concatenate(chunks[k : k + 2], axis=0) for k in range(0, len(chunks), 2)]


def gather(source, rows, index):
    peers = index.shape[0]
    out = []
    for pair in pairs_of(index):
        high, low = pair >> 7, pair & (LANES - 1)
        total = jnp.zeros(pair.shape, F32)
        for h in range(rows):
            picked = jnp.take_along_axis(source(h), low, axis=1)
            total = jnp.where(high == h, picked, total)
        out += [total[:peers], total[peers:]]
    return jnp.concatenate(out, axis=1)


def three_parts(value):
    first = value.astype(jnp.bfloat16).astype(F32)
    rest = value - first
    second = rest.astype(jnp.bfloat16).astype(F32)
    return first, second, rest - second


def scatter(values, index, rows):
    slots = values.shape[1]
    high, low = index >> 7, index & (LANES - 1)
    mine = lax.broadcasted_iota(jnp.int32, (rows, slots), 0) == high
    left = jnp.concatenate([jnp.where(mine, part, 0.0) for part in three_parts(values)], axis=0)
    spread = lax.broadcasted_iota(jnp.int32, (LANES, slots), 0) == low
    right = jnp.where(spread, 1.0, 0.0).astype(jnp.bfloat16)
    sums = lax.dot_general(
        left.astype(jnp.bfloat16), right, (((1,), (1,)), ((), ())), preferred_element_type=F32
    )
    return sums[:rows] + sums[rows : 2 * rows] + sums[2 * rows :]


def pick_current(current, nodes):
    rows, peers = current.shape[0], nodes.shape[0]
    return gather(
        lambda h: jnp.broadcast_to(current[h : h + 1], (2 * peers, LANES)), rows, nodes
    )


def is_even():
    return lax.rem(lax.axis_index("dom"), 2) == 0


def meets_next():
    return is_even() == (lax.axis_index("sub") == 0)


def by_partner(mine, yours):
    zero = lax.axis_index("sub") == 0
    return jnp.where(zero, mine, yours), jnp.where(zero, yours, mine)


def by_side(first, second):
    even = is_even()
    return jnp.where(even, first, second), jnp.where(even, second, first)


def spread_current(outgoing, maps, own_ref, keep_ref, give_ref, far_ref):
    torso = own_ref.shape[0]
    own, after, before, far = (
        scatter(outgoing[o : o + 1], maps[o : o + 1], torso) for o in range(maps.shape[0])
    )
    ahead = meets_next()
    own_ref[...] = own
    keep_ref[...] = jnp.where(ahead, after, before)
    give_ref[...] = jnp.where(ahead, before, after)
    far_ref[...] = far


def feedback_of(estimates, nodes, maps, heart):
    peers = nodes.shape[0]
    torso = estimates[0].shape[0]

    def source(h):
        rows = [estimate[h : h + 1] for estimate in estimates]
        return jnp.concatenate(rows * 2, axis=0)

    returned = gather(source, torso, maps)
    total = jnp.zeros((heart, LANES), F32)
    for o in range(peers):
        total = total + scatter(returned[o : o + 1], nodes[o : o + 1], heart)
    return total


def product(own_ref, other_ref, pick_ref, window):
    tiles, slots = own_ref.shape[0], own_ref.shape[1]
    parts = jnp.concatenate(three_parts(window), axis=1).astype(jnp.bfloat16)
    picked = jnp.dot(pick_ref[...].astype(jnp.bfloat16), parts, preferred_element_type=F32)
    picked = picked[:, :LANES] + picked[:, LANES : 2 * LANES] + picked[:, 2 * LANES :]
    eye = lax.broadcasted_iota(jnp.int32, (LANES, LANES), 0) == lax.broadcasted_iota(
        jnp.int32, (LANES, LANES), 1
    )
    rows = []
    for t in range(tiles):
        total = None
        for k in range(2 * slots):
            tile = own_ref[t, k] if k < slots else other_ref[t, k - slots]
            term = tile * picked[k * tiles + t : k * tiles + t + 1]
            total = term if total is None else total + term
        column = jnp.sum(total, axis=1, keepdims=True)
        rows.append(jnp.sum(jnp.where(eye, column, 0.0), axis=0, keepdims=True))
    return jnp.concatenate(rows, axis=0)


def fetch(pairs, sems):
    copies = [pltpu.make_async_copy(a, b, sems.at[i]) for i, (a, b) in enumerate(pairs)]
    for copy in copies:
        copy.start()
    return copies


def begin(states_ref, table_ref, out_ref, payload_ref, nodes_ref):
    peers, slots = nodes_ref.shape
    for k in range(out_ref.shape[1]):
        out_ref[:, k, :] = states_ref[:, k * LANES : (k + 1) * LANES]
    slot = lax.broadcasted_iota(jnp.int32, (1, slots), 1)
    for o in range(peers):
        live = slot < table_ref[2 * peers : 2 * peers + 1, o : o + 1]
        nodes_ref[o : o + 1] = jnp.where(live, table_ref[o : o + 1], -1)
    rows, current = ionic_rows([out_ref[i] for i in range(out_ref.shape[0])])
    for i, row in enumerate(rows):
        out_ref[i] = row
    payload_ref[0:peers] = pick_current(current, nodes_ref[...])
    payload_ref[peers:] = table_ref[peers : 2 * peers].astype(F32)


def bring(cols_ref, diag_ref, payload_ref, cols_out, diag_out, payload_out):
    cols_out[...] = cols_ref[...]
    diag_out[...] = diag_ref[...]
    payload_out[...] = payload_ref[...]


def bring_tiles(tiles_ref, own_cols, other_cols, direction_ref, direction_out, pick_ref):
    direction_out[...] = direction_ref[...]
    slots, tiles = own_cols.shape
    eye = lax.broadcasted_iota(jnp.int32, (tiles, tiles), 0) == lax.broadcasted_iota(
        jnp.int32, (tiles, tiles), 1
    )
    place = lax.broadcasted_iota(jnp.int32, (tiles, pick_ref.shape[1]), 1)
    for k in range(2 * slots):
        row = own_cols[k : k + 1] if k < slots else other_cols[k - slots : k - slots + 1]
        column = jnp.sum(jnp.where(eye, row.astype(F32), 0.0), axis=1, keepdims=True)
        pick_ref[k * tiles : (k + 1) * tiles] = jnp.where(place == column.astype(jnp.int32), 1.0, 0.0)
    del tiles_ref


def first_forcing(
    nodes_ref, table_ref, own_ref, first_ref, far_ref, second_ref,
    maps_ref, forcing_ref,
):
    peers = nodes_ref.shape[0]
    after, before = by_side(first_ref[...], second_ref[...])
    come = [own_ref[0:1], before[1:2], after[2:3], far_ref[3:4]]
    rows = [own_ref[peers : peers + 1], after[peers + 1 : peers + 2]]
    rows += [before[peers + 2 : peers + 3], far_ref[peers + 3 : peers + 4]]
    maps_ref[...] = jnp.where(nodes_ref[...] < 0, -1, jnp.concatenate(rows, axis=0).astype(jnp.int32))
    total = None
    for o in range(peers):
        part = scatter(come[o], table_ref[peers + o : peers + o + 1], forcing_ref.shape[0])
        total = part if total is None else total + part
    forcing_ref[...] = TORSO_COUPLING * total


def next_shares(
    states_ref, own_estimate, far_estimate, mine_ref, yours_ref, nodes_ref, maps_ref,
    out_ref, own_ref, keep_ref, give_ref, far_ref,
):
    nodes, maps = nodes_ref[...], maps_ref[...]
    after, before = by_side(*by_partner(mine_ref[...], yours_ref[...]))
    estimates = [own_estimate[...], after, before, far_estimate[...]]
    feedback = feedback_of(estimates, nodes, maps, states_ref.shape[1])
    rows = [states_ref[i] for i in range(states_ref.shape[0])]
    rows[0] = rows[0] + TIME_STEP * FEEDBACK_RATE * feedback
    rows, current = ionic_rows(rows)
    for i, row in enumerate(rows):
        out_ref[i] = row
    outgoing = pick_current(current, nodes)
    spread_current(outgoing, maps, own_ref, keep_ref, give_ref, far_ref)


def window_of(chain, direction, first, second):
    torso = direction.shape[0]
    here = lax.axis_index("dom")
    after, before = by_side(first, second)
    before = jnp.where(here > 0, before[torso - HALO :], 0.0)
    after = jnp.where(here < chain - 1, after[0:HALO], 0.0)
    filler = jnp.zeros((torso - 2 * HALO, LANES), F32)
    return jnp.concatenate([before, direction, after, filler], axis=0)


def sweep_one(
    chain, own_ref, other_ref, pick_ref, mine_ref, yours_ref, forcing_ref, direction_in, diag_ref,
    residual_ref, direction_ref, estimate_ref,
):
    diag = diag_ref[...]
    direction = direction_in[...]
    window = window_of(chain, direction, *by_partner(mine_ref[...], yours_ref[...]))
    moved = product(own_ref, other_ref, pick_ref, window)
    residual = forcing_ref[...] - (diag * direction + moved)
    estimate = direction
    direction = KEEP[0] * direction + PULL[0] * (residual / diag)
    residual_ref[...] = residual
    direction_ref[...] = direction
    estimate_ref[...] = estimate + direction


def sweep_two(
    chain, last, own_ref, other_ref, pick_ref, mine_ref, yours_ref, direction_in, residual_in,
    estimate_in, diag_ref, estimate_ref, *refs,
):
    torso = estimate_ref.shape[0]
    diag = diag_ref[...]
    direction = direction_in[...]
    window = window_of(chain, direction, *by_partner(mine_ref[...], yours_ref[...]))
    moved = product(own_ref, other_ref, pick_ref, window)
    residual = residual_in[...] - (diag * direction + moved)
    direction = KEEP[1] * direction + PULL[1] * (residual / diag)
    estimate = estimate_in[...] + direction
    if last:
        residual_ref, = refs
        residual_ref[...] = residual
        estimate_ref[0 : torso // 2] = estimate
        estimate_ref[torso // 2 :] = direction
    else:
        estimate_ref[...] = estimate


def finish(
    chain, own_ref, other_ref, pick_ref, packed_ref, far_ref, mine_ref, yours_ref, residual_in,
    diag_ref, states_ref, nodes_ref, maps_ref, out_ref, potential_ref, residual_ref, dense_ref,
):
    torso = residual_ref.shape[0]
    head, tail = slice(0, torso), slice(torso, 2 * torso)
    estimate, direction = packed_ref[head], packed_ref[tail]
    potential_ref[...] = estimate
    first, second = by_partner(mine_ref[...], yours_ref[...])
    after, before = by_side(first[head], second[head])
    feedback = feedback_of(
        [estimate, after, before, far_ref[head]], nodes_ref[...], maps_ref[...],
        states_ref.shape[1],
    )
    dense_ref[...] = states_ref[...]
    dense_ref[0] = states_ref[0] + TIME_STEP * FEEDBACK_RATE * feedback
    for k in range(states_ref.shape[1]):
        out_ref[:, k * LANES : (k + 1) * LANES] = dense_ref[:, k, :]
    window = window_of(chain, direction, first[tail], second[tail])
    moved = product(own_ref, other_ref, pick_ref, window)
    residual_ref[...] = residual_in[...] - (diag_ref[...] * direction + moved)


def on_device(states, send_node, send_count, recv_row, columns, tile_values, diagonal):
    chain = lax.axis_size("dom")
    peers, slots = send_node.shape[1:]
    node_count = states.shape[1]
    heart = node_count // LANES
    torso = diagonal.shape[0] // LANES

    def swap(value, partner):
        return lax.ppermute(value, "dom", [(i, partner(i) % chain) for i in range(chain)])

    def with_first(value):
        return swap(value, lambda i: i ^ 1)

    def with_second(value):
        return swap(value, lambda i: ((i + 1) ^ 1) - 1)

    def with_either(value, closed):
        cases = lax.axis_size("case")
        ends = () if closed or cases % 2 else (0, chain - 1)
        pairs = []
        for case in range(cases):
            for i in range(chain):
                me = (case * chain + i) * 2
                pairs.append((me, (case * chain + (i ^ 1)) * 2))
                if i in ends:
                    pairs.append((me + 1, ((case ^ 1) * chain + i) * 2 + 1))
                else:
                    second = (((i + 1) ^ 1) - 1) % chain
                    pairs.append((me + 1, (case * chain + second) * 2 + 1))
        return lax.ppermute(value, ("case", "dom", "sub"), pairs)

    def with_far(value):
        return swap(value, lambda i: i + chain // 2)

    def from_sibling(value):
        return lax.ppermute(value, "sub", [(0, 1), (1, 0)])

    def shape(*dims, dtype=F32):
        return jax.ShapeDtypeStruct(dims, dtype)

    dense = shape(states.shape[0], heart, LANES)
    field = shape(torso, LANES)
    packed = shape(2 * torso, LANES)
    other_tiles = from_sibling(tile_values)
    counts = jnp.pad(send_count, ((0, 0), (0, slots - peers)))
    table = jnp.concatenate([send_node[0], recv_row[0], counts])
    index = shape(peers, slots, dtype=jnp.int32)
    payload = shape(2 * peers, slots)
    states, payload, nodes = call(begin, (dense, payload, index))(in_specs=[VMEM] * 2)(
        states, table
    )
    columns, diag, own = call(
        bring, (shape(*columns.shape[::-1], dtype=jnp.int32), field, payload)
    )(in_specs=[VMEM] * 3)(columns.T, diagonal.reshape(torso, LANES), payload)
    first, far, second = with_first(payload), with_far(payload), with_second(payload)
    maps, forcing = call(first_forcing, (index, field))(in_specs=[VMEM] * 6)(
        nodes, table, own, first, far, second
    )
    for time_step in range(2):
        last = time_step == 1
        forcing = forcing + from_sibling(forcing)
        direction = forcing / (CHEB_THETA * diag)
        halo = with_either(direction, False)
        if not last:
            choices = 2 * columns.shape[0] * torso
            direction, pick = call(bring_tiles, (field, shape(choices, 2 * torso)))(
                in_specs=[VMEM] * 4
            )(tile_values, columns, from_sibling(columns), direction)
            halo, direction = lax.optimization_barrier((halo, direction))
            stored = (tile_values, other_tiles, pick)
        residual, direction, estimate = call(
            functools.partial(sweep_one, chain), (field,) * 3
        )(in_specs=[VMEM] * 8)(*stored, halo, from_sibling(halo), forcing, direction, diag)
        halo = with_either(direction, False)
        swept = call(
            functools.partial(sweep_two, chain, last), (packed, field) if last else field
        )(in_specs=[VMEM] * 9)(
            *stored, halo, from_sibling(halo), direction, residual, estimate, diag
        )
        estimate, residual = swept if last else (swept, None)
        far = with_far(estimate)
        near = with_either(estimate, True)
        if not last:
            states, own, keep, give, away = call(next_shares, (dense,) + (field,) * 4)(
                in_specs=[VMEM] * 7
            )(states, estimate, far, near, from_sibling(near), nodes, maps)
            far = with_far(away)
            near = with_either(keep + from_sibling(give), True)
            forcing = TORSO_COUPLING * (own + far + near)
    new_states, potential, residual = call(
        functools.partial(finish, chain),
        (shape(*dense.shape[:1], node_count), field, field),
        (pltpu.VMEM(dense.shape, F32),),
    )(in_specs=[VMEM] * 12)(
        *stored, estimate, far, near, from_sibling(near), residual, diag, states, nodes, maps
    )
    return new_states, potential.reshape(-1), residual.reshape(-1)


def solution(mesh):
    placed = (
        P(None, ("case", "dom", "sub")),
        P(("case", "dom", "sub"), None, None),
        P(("case", "dom", "sub"), None),
        P(("case", "dom", "sub"), None, None),
        P(("case", "dom"), "sub"),
        P(("case", "dom"), "sub", None, None),
        P(("case", "dom")),
    )
    return jax.shard_map(
        on_device,
        mesh=mesh,
        in_specs=placed,
        out_specs=(P(None, ("case", "dom", "sub")), P(("case", "dom")), P(("case", "dom"))),
        check_vma=False,
    )
```

```python
import functools

import jax
import jax.numpy as jnp
from jax import lax
from jax.experimental import pallas as pl
from jax.experimental.pallas import tpu as pltpu
from jax.sharding import PartitionSpec as P

HALO = 2
SWEEPS = 3
LANES = 128

TIME_STEP = 0.02
NERNST_SCALE = 0.267
SODIUM_OUT = 1.4
POTASSIUM_OUT = 0.054
CALCIUM_OUT = 2000.0
COND_SODIUM = 8.0
COND_CALCIUM = 1.0
COND_TRANSIENT = 0.3
COND_RAPID = 0.2
COND_SLOW = 0.3
COND_INWARD = 2.0
COND_RELEASE = 3.0
MEMBRANE_RATE = 2.0
TORSO_COUPLING = 0.5
FEEDBACK_RATE = 5.0
CHEB_THETA = 1.0
CHEB_DELTA = 0.5
GATE_MIDPOINT = [-0.56, -0.7, -0.7, -0.08, -0.2, -0.3, 0.2, -0.28, -0.26, -0.88, 0.05, -0.8, -0.5]
GATE_STEEPNESS = [0.09, -0.07, -0.07, 0.07, -0.07, -0.09, 0.06, -0.05, 0.07, -0.24, 0.14, -0.1, 0.08]
TIME_BASE = [0.02, 0.3, 1.0, 0.1, 2.0, 0.5, 0.1, 1.0, 1.0, 0.5, 1.0, 0.05, 0.2]
TIME_PEAK = [0.1, 1.0, 3.0, 0.5, 5.0, 2.0, 0.3, 5.0, 3.0, 2.0, 4.0, 0.1, 1.0]

SIGMA = CHEB_THETA / CHEB_DELTA
KEEP, PULL = [], []
_ratio = 1.0 / SIGMA
for _ in range(SWEEPS - 1):
    _next = 1.0 / (2.0 * SIGMA - _ratio)
    KEEP.append(_next * _ratio)
    PULL.append(2.0 * _next / CHEB_DELTA)
    _ratio = _next

VMEM = pl.BlockSpec(memory_space=pltpu.VMEM)
F32 = jnp.float32


def call(kernel, outs, scratch=(), limit=16, cost=4_000_000):
    return functools.partial(
        pl.pallas_call,
        kernel,
        out_shape=outs,
        out_specs=jax.tree.map(lambda _: VMEM, outs),
        scratch_shapes=list(scratch),
        compiler_params=pltpu.CompilerParams(vmem_limit_bytes=limit << 20),
        cost_estimate=pl.CostEstimate(flops=cost, bytes_accessed=1 << 18, transcendentals=0),
    )


def ionic_rows(rows):
    voltage, gating = rows[0], rows[1:14]
    sodium, potassium, calcium, reticulum, subspace = rows[14:19]
    moved = []
    for i, gate in enumerate(gating):
        shifted = voltage - GATE_MIDPOINT[i]
        steady = jax.nn.sigmoid(shifted / GATE_STEEPNESS[i])
        time_const = TIME_BASE[i] + TIME_PEAK[i] * jnp.exp(-jnp.square(shifted / 0.3))
        moved.append(steady + (gate - steady) * jnp.exp(-TIME_STEP / time_const))
    g = moved
    sodium_rev = NERNST_SCALE * jnp.log(SODIUM_OUT / sodium)
    potassium_rev = NERNST_SCALE * jnp.log(POTASSIUM_OUT / potassium)
    calcium_rev = 0.5 * NERNST_SCALE * jnp.log(CALCIUM_OUT / subspace)
    sodium_flow = COND_SODIUM * (g[0] * g[0] * g[0]) * g[1] * g[2] * (voltage - sodium_rev)
    calcium_flow = COND_CALCIUM * g[3] * g[4] * g[5] * (voltage - calcium_rev)
    potassium_cond = (
        COND_TRANSIENT * g[6] * g[7]
        + COND_RAPID * g[8] * g[9]
        + COND_SLOW * (g[10] * g[10])
        + COND_INWARD * g[11]
    )
    potassium_flow = potassium_cond * (voltage - potassium_rev)
    current = sodium_flow + calcium_flow + potassium_flow
    release = COND_RELEASE * g[12] * (reticulum - subspace) / (reticulum + subspace)
    sodium = sodium * jnp.exp(-0.5 * TIME_STEP * sodium_flow)
    potassium = potassium * jnp.exp(-0.5 * TIME_STEP * potassium_flow)
    calcium = calcium * jnp.exp(-0.5 * TIME_STEP * calcium_flow)
    subspace = subspace * jnp.exp(TIME_STEP * (release - 0.5 * calcium_flow))
    reticulum = reticulum * jnp.exp(-TIME_STEP * release)
    voltage = voltage - TIME_STEP * MEMBRANE_RATE * current
    return [voltage, *moved, sodium, potassium, calcium, reticulum, subspace], current


def pairs_of(index):
    chunks = [index[:, k : k + LANES] for k in range(0, index.shape[1], LANES)]
    return [jnp.concatenate(chunks[k : k + 2], axis=0) for k in range(0, len(chunks), 2)]


def gather(source, rows, index):
    peers = index.shape[0]
    out = []
    for pair in pairs_of(index):
        high, low = pair >> 7, pair & (LANES - 1)
        total = jnp.zeros(pair.shape, F32)
        for h in range(rows):
            picked = jnp.take_along_axis(source(h), low, axis=1)
            total = jnp.where(high == h, picked, total)
        out += [total[:peers], total[peers:]]
    return jnp.concatenate(out, axis=1)


def three_parts(value):
    first = value.astype(jnp.bfloat16).astype(F32)
    rest = value - first
    second = rest.astype(jnp.bfloat16).astype(F32)
    return first, second, rest - second


def scatter(values, index, rows):
    slots = values.shape[1]
    high, low = index >> 7, index & (LANES - 1)
    mine = lax.broadcasted_iota(jnp.int32, (rows, slots), 0) == high
    left = jnp.concatenate([jnp.where(mine, part, 0.0) for part in three_parts(values)], axis=0)
    spread = lax.broadcasted_iota(jnp.int32, (LANES, slots), 0) == low
    right = jnp.where(spread, 1.0, 0.0).astype(jnp.bfloat16)
    sums = lax.dot_general(
        left.astype(jnp.bfloat16), right, (((1,), (1,)), ((), ())), preferred_element_type=F32
    )
    return sums[:rows] + sums[rows : 2 * rows] + sums[2 * rows :]


def pick_current(current, nodes):
    rows, peers = current.shape[0], nodes.shape[0]
    return gather(
        lambda h: jnp.broadcast_to(current[h : h + 1], (2 * peers, LANES)), rows, nodes
    )


def is_even():
    return lax.rem(lax.axis_index("dom"), 2) == 0


def by_sibling(mine, yours):
    ahead = lax.axis_index("sub") == 1
    return jnp.where(ahead, mine, yours), jnp.where(ahead, yours, mine)


def by_side(first, second):
    even = is_even()
    return jnp.where(even, first, second), jnp.where(even, second, first)


def spread_current(outgoing, maps, own_ref, keep_ref, give_ref, far_ref):
    torso = own_ref.shape[0]
    own, after, before, far = (
        scatter(outgoing[o : o + 1], maps[o : o + 1], torso) for o in range(maps.shape[0])
    )
    own_ref[...] = own
    keep_ref[...], give_ref[...] = by_sibling(after, before)
    far_ref[...] = far


def feedback_of(estimates, nodes, maps, heart):
    peers = nodes.shape[0]
    torso = estimates[0].shape[0]

    def source(h):
        rows = [estimate[h : h + 1] for estimate in estimates]
        return jnp.concatenate(rows * 2, axis=0)

    returned = gather(source, torso, maps)
    total = jnp.zeros((heart, LANES), F32)
    for o in range(peers):
        total = total + scatter(returned[o : o + 1], nodes[o : o + 1], heart)
    return total


def product(own_ref, other_ref, pick_ref, window):
    tiles, slots = own_ref.shape[0], own_ref.shape[1]
    parts = jnp.concatenate(three_parts(window), axis=1).astype(jnp.bfloat16)
    picked = jnp.dot(pick_ref[...].astype(jnp.bfloat16), parts, preferred_element_type=F32)
    picked = picked[:, :LANES] + picked[:, LANES : 2 * LANES] + picked[:, 2 * LANES :]
    eye = lax.broadcasted_iota(jnp.int32, (LANES, LANES), 0) == lax.broadcasted_iota(
        jnp.int32, (LANES, LANES), 1
    )
    rows = []
    for t in range(tiles):
        total = None
        for k in range(2 * slots):
            tile = own_ref[t, k] if k < slots else other_ref[t, k - slots]
            term = tile * picked[k * tiles + t : k * tiles + t + 1]
            total = term if total is None else total + term
        column = jnp.sum(total, axis=1, keepdims=True)
        rows.append(jnp.sum(jnp.where(eye, column, 0.0), axis=0, keepdims=True))
    return jnp.concatenate(rows, axis=0)


def fetch(pairs, sems):
    copies = [pltpu.make_async_copy(a, b, sems.at[i]) for i, (a, b) in enumerate(pairs)]
    for copy in copies:
        copy.start()
    return copies


def begin(states_ref, table_ref, out_ref, payload_ref, nodes_ref):
    peers, slots = nodes_ref.shape
    for k in range(out_ref.shape[1]):
        out_ref[:, k, :] = states_ref[:, k * LANES : (k + 1) * LANES]
    slot = lax.broadcasted_iota(jnp.int32, (1, slots), 1)
    for o in range(peers):
        live = slot < table_ref[2 * peers : 2 * peers + 1, o : o + 1]
        nodes_ref[o : o + 1] = jnp.where(live, table_ref[o : o + 1], -1)
    rows, current = ionic_rows([out_ref[i] for i in range(out_ref.shape[0])])
    for i, row in enumerate(rows):
        out_ref[i] = row
    payload_ref[0:peers] = pick_current(current, nodes_ref[...])
    payload_ref[peers:] = table_ref[peers : 2 * peers].astype(F32)


def bring(cols_ref, diag_ref, payload_ref, cols_out, diag_out, payload_out):
    cols_out[...] = cols_ref[...]
    diag_out[...] = diag_ref[...]
    payload_out[...] = payload_ref[...]


def bring_tiles(tiles_ref, own_cols, other_cols, direction_ref, direction_out, pick_ref):
    direction_out[...] = direction_ref[...]
    slots, tiles = own_cols.shape
    eye = lax.broadcasted_iota(jnp.int32, (tiles, tiles), 0) == lax.broadcasted_iota(
        jnp.int32, (tiles, tiles), 1
    )
    place = lax.broadcasted_iota(jnp.int32, (tiles, pick_ref.shape[1]), 1)
    for k in range(2 * slots):
        row = own_cols[k : k + 1] if k < slots else other_cols[k - slots : k - slots + 1]
        column = jnp.sum(jnp.where(eye, row.astype(F32), 0.0), axis=1, keepdims=True)
        pick_ref[k * tiles : (k + 1) * tiles] = jnp.where(place == column.astype(jnp.int32), 1.0, 0.0)
    del tiles_ref


def first_forcing(
    nodes_ref, table_ref, own_ref, first_ref, far_ref, second_ref,
    maps_ref, forcing_ref,
):
    peers = nodes_ref.shape[0]
    after, before = by_side(first_ref[...], second_ref[...])
    come = [own_ref[0:1], before[1:2], after[2:3], far_ref[3:4]]
    rows = [own_ref[peers : peers + 1], after[peers + 1 : peers + 2]]
    rows += [before[peers + 2 : peers + 3], far_ref[peers + 3 : peers + 4]]
    maps_ref[...] = jnp.where(nodes_ref[...] < 0, -1, jnp.concatenate(rows, axis=0).astype(jnp.int32))
    total = None
    for o in range(peers):
        part = scatter(come[o], table_ref[peers + o : peers + o + 1], forcing_ref.shape[0])
        total = part if total is None else total + part
    forcing_ref[...] = TORSO_COUPLING * total


def next_shares(
    states_ref, own_estimate, far_estimate, mine_ref, yours_ref, nodes_ref, maps_ref,
    out_ref, own_ref, keep_ref, give_ref, far_ref,
):
    nodes, maps = nodes_ref[...], maps_ref[...]
    after, before = by_sibling(mine_ref[...], yours_ref[...])
    estimates = [own_estimate[...], after, before, far_estimate[...]]
    feedback = feedback_of(estimates, nodes, maps, states_ref.shape[1])
    rows = [states_ref[i] for i in range(states_ref.shape[0])]
    rows[0] = rows[0] + TIME_STEP * FEEDBACK_RATE * feedback
    rows, current = ionic_rows(rows)
    for i, row in enumerate(rows):
        out_ref[i] = row
    outgoing = pick_current(current, nodes)
    spread_current(outgoing, maps, own_ref, keep_ref, give_ref, far_ref)


def window_of(chain, direction, mine, yours):
    torso = direction.shape[0]
    here = lax.axis_index("dom")
    after, before = by_sibling(mine, yours)
    before = jnp.where(here > 0, before[torso - HALO :], 0.0)
    after = jnp.where(here < chain - 1, after[0:HALO], 0.0)
    filler = jnp.zeros((torso - 2 * HALO, LANES), F32)
    return jnp.concatenate([before, direction, after, filler], axis=0)


def sweep_one(
    chain, own_ref, other_ref, pick_ref, mine_ref, yours_ref, forcing_ref, direction_in, diag_ref,
    residual_ref, direction_ref, estimate_ref,
):
    diag = diag_ref[...]
    direction = direction_in[...]
    window = window_of(chain, direction, mine_ref[...], yours_ref[...])
    moved = product(own_ref, other_ref, pick_ref, window)
    residual = forcing_ref[...] - (diag * direction + moved)
    estimate = direction
    direction = KEEP[0] * direction + PULL[0] * (residual / diag)
    residual_ref[...] = residual
    direction_ref[...] = direction
    estimate_ref[...] = estimate + direction


def sweep_two(
    chain, last, own_ref, other_ref, pick_ref, mine_ref, yours_ref, direction_in, residual_in,
    estimate_in, diag_ref, estimate_ref, *refs,
):
    torso = estimate_ref.shape[0]
    diag = diag_ref[...]
    direction = direction_in[...]
    window = window_of(chain, direction, mine_ref[...], yours_ref[...])
    moved = product(own_ref, other_ref, pick_ref, window)
    residual = residual_in[...] - (diag * direction + moved)
    direction = KEEP[1] * direction + PULL[1] * (residual / diag)
    estimate = estimate_in[...] + direction
    if last:
        residual_ref, = refs
        residual_ref[...] = residual
        estimate_ref[0 : torso // 2] = estimate
        estimate_ref[torso // 2 :] = direction
    else:
        estimate_ref[...] = estimate


def finish(
    chain, own_ref, other_ref, pick_ref, packed_ref, far_ref, mine_ref, yours_ref, residual_in,
    diag_ref, states_ref, nodes_ref, maps_ref, out_ref, potential_ref, residual_ref, dense_ref,
):
    torso = residual_ref.shape[0]
    head, tail = slice(0, torso), slice(torso, 2 * torso)
    estimate, direction = packed_ref[head], packed_ref[tail]
    potential_ref[...] = estimate
    after, before = by_sibling(mine_ref[head], yours_ref[head])
    feedback = feedback_of(
        [estimate, after, before, far_ref[head]], nodes_ref[...], maps_ref[...],
        states_ref.shape[1],
    )
    dense_ref[...] = states_ref[...]
    dense_ref[0] = states_ref[0] + TIME_STEP * FEEDBACK_RATE * feedback
    for k in range(states_ref.shape[1]):
        out_ref[:, k * LANES : (k + 1) * LANES] = dense_ref[:, k, :]
    window = window_of(chain, direction, mine_ref[tail], yours_ref[tail])
    moved = product(own_ref, other_ref, pick_ref, window)
    residual_ref[...] = residual_in[...] - (diag_ref[...] * direction + moved)


def on_device(states, send_node, send_count, recv_row, columns, tile_values, diagonal):
    chain = lax.axis_size("dom")
    peers, slots = send_node.shape[1:]
    node_count = states.shape[1]
    heart = node_count // LANES
    torso = diagonal.shape[0] // LANES

    def swap(value, partner):
        return lax.ppermute(value, "dom", [(i, partner(i) % chain) for i in range(chain)])

    def with_first(value):
        return swap(value, lambda i: i ^ 1)

    def with_second(value):
        return swap(value, lambda i: ((i + 1) ^ 1) - 1)

    def with_near(value, closed):
        cases = lax.axis_size("case")
        ring = 2 * chain
        pairs = []
        for case in range(cases):
            for me in range(ring):
                other = (me + 1 if me % 2 else me - 1) % ring
                beside = case
                if me in (0, ring - 1) and not closed and cases % 2 == 0:
                    other, beside = me, case ^ 1
                pairs.append((case * ring + me, beside * ring + other))
        return lax.ppermute(value, ("case", "dom", "sub"), pairs)

    def with_far(value):
        return swap(value, lambda i: i + chain // 2)

    def from_sibling(value):
        return lax.ppermute(value, "sub", [(0, 1), (1, 0)])

    def shape(*dims, dtype=F32):
        return jax.ShapeDtypeStruct(dims, dtype)

    dense = shape(states.shape[0], heart, LANES)
    field = shape(torso, LANES)
    packed = shape(2 * torso, LANES)
    other_tiles = from_sibling(tile_values)
    counts = jnp.pad(send_count, ((0, 0), (0, slots - peers)))
    table = jnp.concatenate([send_node[0], recv_row[0], counts])
    index = shape(peers, slots, dtype=jnp.int32)
    payload_shape = shape(2 * peers, slots)
    states, payload, nodes = call(begin, (dense, payload_shape, index))(in_specs=[VMEM] * 2)(
        states, table
    )
    columns, diag, own = call(
        bring, (shape(*columns.shape[::-1], dtype=jnp.int32), field, payload_shape)
    )(in_specs=[VMEM] * 3)(columns.T, diagonal.reshape(torso, LANES), payload)
    first, far, second = with_first(payload), with_far(payload), with_second(payload)
    second, other_columns = lax.optimization_barrier((second, from_sibling(columns)))
    maps, forcing = call(first_forcing, (index, field))(in_specs=[VMEM] * 6)(
        nodes, table, own, first, far, second
    )
    for time_step in range(2):
        last = time_step == 1
        forcing = forcing + from_sibling(forcing)
        direction = forcing / (CHEB_THETA * diag)
        halo = with_near(direction, False)
        if not last:
            choices = 2 * columns.shape[0] * torso
            direction, pick = call(bring_tiles, (field, shape(choices, 2 * torso)))(
                in_specs=[VMEM] * 4
            )(tile_values, columns, other_columns, direction)
            halo, direction = lax.optimization_barrier((halo, direction))
            stored = (tile_values, other_tiles, pick)
        residual, direction, estimate = call(
            functools.partial(sweep_one, chain), (field,) * 3
        )(in_specs=[VMEM] * 8)(*stored, halo, from_sibling(halo), forcing, direction, diag)
        halo = with_near(direction, False)
        swept = call(
            functools.partial(sweep_two, chain, last), (packed, field) if last else field
        )(in_specs=[VMEM] * 9)(
            *stored, halo, from_sibling(halo), direction, residual, estimate, diag
        )
        estimate, residual = swept if last else (swept, None)
        far = with_far(estimate)
        near = with_near(estimate, True)
        if not last:
            states, own, keep, give, away = call(next_shares, (dense,) + (field,) * 4)(
                in_specs=[VMEM] * 7
            )(states, estimate, far, near, from_sibling(near), nodes, maps)
            far = with_far(away)
            near = with_near(keep + from_sibling(give), True)
            forcing = TORSO_COUPLING * (own + far + near)
    new_states, potential, residual = call(
        functools.partial(finish, chain),
        (shape(*dense.shape[:1], node_count), field, field),
        (pltpu.VMEM(dense.shape, F32),),
    )(in_specs=[VMEM] * 12)(
        *stored, estimate, far, near, from_sibling(near), residual, diag, states, nodes, maps
    )
    return new_states, potential.reshape(-1), residual.reshape(-1)


def solution(mesh):
    placed = (
        P(None, ("case", "dom", "sub")),
        P(("case", "dom", "sub"), None, None),
        P(("case", "dom", "sub"), None),
        P(("case", "dom", "sub"), None, None),
        P(("case", "dom"), "sub"),
        P(("case", "dom"), "sub", None, None),
        P(("case", "dom")),
    )
    return jax.shard_map(
        on_device,
        mesh=mesh,
        in_specs=placed,
        out_specs=(P(None, ("case", "dom", "sub")), P(("case", "dom")), P(("case", "dom"))),
        check_vma=False,
    )
```

```python
import functools

import jax
import jax.numpy as jnp
from jax import lax
from jax.experimental import pallas as pl
from jax.experimental.pallas import tpu as pltpu
from jax.sharding import PartitionSpec as P

HALO = 2
SWEEPS = 3
LANES = 128

TIME_STEP = 0.02
NERNST_SCALE = 0.267
SODIUM_OUT = 1.4
POTASSIUM_OUT = 0.054
CALCIUM_OUT = 2000.0
COND_SODIUM = 8.0
COND_CALCIUM = 1.0
COND_TRANSIENT = 0.3
COND_RAPID = 0.2
COND_SLOW = 0.3
COND_INWARD = 2.0
COND_RELEASE = 3.0
MEMBRANE_RATE = 2.0
TORSO_COUPLING = 0.5
FEEDBACK_RATE = 5.0
CHEB_THETA = 1.0
CHEB_DELTA = 0.5
GATE_MIDPOINT = [-0.56, -0.7, -0.7, -0.08, -0.2, -0.3, 0.2, -0.28, -0.26, -0.88, 0.05, -0.8, -0.5]
GATE_STEEPNESS = [0.09, -0.07, -0.07, 0.07, -0.07, -0.09, 0.06, -0.05, 0.07, -0.24, 0.14, -0.1, 0.08]
TIME_BASE = [0.02, 0.3, 1.0, 0.1, 2.0, 0.5, 0.1, 1.0, 1.0, 0.5, 1.0, 0.05, 0.2]
TIME_PEAK = [0.1, 1.0, 3.0, 0.5, 5.0, 2.0, 0.3, 5.0, 3.0, 2.0, 4.0, 0.1, 1.0]

SIGMA = CHEB_THETA / CHEB_DELTA
KEEP, PULL = [], []
_ratio = 1.0 / SIGMA
for _ in range(SWEEPS - 1):
    _next = 1.0 / (2.0 * SIGMA - _ratio)
    KEEP.append(_next * _ratio)
    PULL.append(2.0 * _next / CHEB_DELTA)
    _ratio = _next

VMEM = pl.BlockSpec(memory_space=pltpu.VMEM)
F32 = jnp.float32


def call(kernel, outs, scratch=(), limit=16, cost=4_000_000):
    return functools.partial(
        pl.pallas_call,
        kernel,
        out_shape=outs,
        out_specs=jax.tree.map(lambda _: VMEM, outs),
        scratch_shapes=list(scratch),
        compiler_params=pltpu.CompilerParams(vmem_limit_bytes=limit << 20),
        cost_estimate=pl.CostEstimate(flops=cost, bytes_accessed=1 << 18, transcendentals=0),
    )


def ionic_rows(rows):
    voltage, gating = rows[0], rows[1:14]
    sodium, potassium, calcium, reticulum, subspace = rows[14:19]
    moved = []
    for i, gate in enumerate(gating):
        shifted = voltage - GATE_MIDPOINT[i]
        steady = jax.nn.sigmoid(shifted / GATE_STEEPNESS[i])
        time_const = TIME_BASE[i] + TIME_PEAK[i] * jnp.exp(-jnp.square(shifted / 0.3))
        moved.append(steady + (gate - steady) * jnp.exp(-TIME_STEP / time_const))
    g = moved
    sodium_rev = NERNST_SCALE * jnp.log(SODIUM_OUT / sodium)
    potassium_rev = NERNST_SCALE * jnp.log(POTASSIUM_OUT / potassium)
    calcium_rev = 0.5 * NERNST_SCALE * jnp.log(CALCIUM_OUT / subspace)
    sodium_flow = COND_SODIUM * (g[0] * g[0] * g[0]) * g[1] * g[2] * (voltage - sodium_rev)
    calcium_flow = COND_CALCIUM * g[3] * g[4] * g[5] * (voltage - calcium_rev)
    potassium_cond = (
        COND_TRANSIENT * g[6] * g[7]
        + COND_RAPID * g[8] * g[9]
        + COND_SLOW * (g[10] * g[10])
        + COND_INWARD * g[11]
    )
    potassium_flow = potassium_cond * (voltage - potassium_rev)
    current = sodium_flow + calcium_flow + potassium_flow
    release = COND_RELEASE * g[12] * (reticulum - subspace) / (reticulum + subspace)
    sodium = sodium * jnp.exp(-0.5 * TIME_STEP * sodium_flow)
    potassium = potassium * jnp.exp(-0.5 * TIME_STEP * potassium_flow)
    calcium = calcium * jnp.exp(-0.5 * TIME_STEP * calcium_flow)
    subspace = subspace * jnp.exp(TIME_STEP * (release - 0.5 * calcium_flow))
    reticulum = reticulum * jnp.exp(-TIME_STEP * release)
    voltage = voltage - TIME_STEP * MEMBRANE_RATE * current
    return [voltage, *moved, sodium, potassium, calcium, reticulum, subspace], current


def pairs_of(index):
    chunks = [index[:, k : k + LANES] for k in range(0, index.shape[1], LANES)]
    return [jnp.concatenate(chunks[k : k + 2], axis=0) for k in range(0, len(chunks), 2)]


def gather(source, rows, index):
    peers = index.shape[0]
    out = []
    for pair in pairs_of(index):
        high, low = pair >> 7, pair & (LANES - 1)
        total = jnp.zeros(pair.shape, F32)
        for h in range(rows):
            picked = jnp.take_along_axis(source(h), low, axis=1)
            total = jnp.where(high == h, picked, total)
        out += [total[:peers], total[peers:]]
    return jnp.concatenate(out, axis=1)


def three_parts(value):
    first = value.astype(jnp.bfloat16).astype(F32)
    rest = value - first
    second = rest.astype(jnp.bfloat16).astype(F32)
    return first, second, rest - second


def scatter(values, index, rows):
    slots = values.shape[1]
    high, low = index >> 7, index & (LANES - 1)
    mine = lax.broadcasted_iota(jnp.int32, (rows, slots), 0) == high
    left = jnp.concatenate([jnp.where(mine, part, 0.0) for part in three_parts(values)], axis=0)
    spread = lax.broadcasted_iota(jnp.int32, (LANES, slots), 0) == low
    right = jnp.where(spread, 1.0, 0.0).astype(jnp.bfloat16)
    sums = lax.dot_general(
        left.astype(jnp.bfloat16), right, (((1,), (1,)), ((), ())), preferred_element_type=F32
    )
    return sums[:rows] + sums[rows : 2 * rows] + sums[2 * rows :]


def pick_current(current, nodes):
    rows, peers = current.shape[0], nodes.shape[0]
    return gather(
        lambda h: jnp.broadcast_to(current[h : h + 1], (2 * peers, LANES)), rows, nodes
    )


def is_even():
    return lax.rem(lax.axis_index("dom"), 2) == 0


def meets_next():
    return is_even() == (lax.axis_index("sub") == 0)


def by_partner(mine, yours):
    zero = lax.axis_index("sub") == 0
    return jnp.where(zero, mine, yours), jnp.where(zero, yours, mine)


def by_side(first, second):
    even = is_even()
    return jnp.where(even, first, second), jnp.where(even, second, first)


def spread_current(outgoing, maps, own_ref, keep_ref, give_ref, far_ref):
    torso = own_ref.shape[0]
    own, after, before, far = (
        scatter(outgoing[o : o + 1], maps[o : o + 1], torso) for o in range(maps.shape[0])
    )
    ahead = meets_next()
    own_ref[...] = own
    keep_ref[...] = jnp.where(ahead, after, before)
    give_ref[...] = jnp.where(ahead, before, after)
    far_ref[...] = far


def feedback_of(estimates, nodes, maps, heart):
    peers = nodes.shape[0]
    torso = estimates[0].shape[0]

    def source(h):
        rows = [estimate[h : h + 1] for estimate in estimates]
        return jnp.concatenate(rows * 2, axis=0)

    returned = gather(source, torso, maps)
    total = jnp.zeros((heart, LANES), F32)
    for o in range(peers):
        total = total + scatter(returned[o : o + 1], nodes[o : o + 1], heart)
    return total


def product(own_ref, other_ref, pick_ref, window):
    tiles, slots = own_ref.shape[0], own_ref.shape[1]
    parts = jnp.concatenate(three_parts(window), axis=1).astype(jnp.bfloat16)
    picked = jnp.dot(pick_ref[...].astype(jnp.bfloat16), parts, preferred_element_type=F32)
    picked = picked[:, :LANES] + picked[:, LANES : 2 * LANES] + picked[:, 2 * LANES :]
    eye = lax.broadcasted_iota(jnp.int32, (LANES, LANES), 0) == lax.broadcasted_iota(
        jnp.int32, (LANES, LANES), 1
    )
    rows = []
    for t in range(tiles):
        total = None
        for k in range(2 * slots):
            tile = own_ref[t, k] if k < slots else other_ref[t, k - slots]
            term = tile * picked[k * tiles + t : k * tiles + t + 1]
            total = term if total is None else total + term
        column = jnp.sum(total, axis=1, keepdims=True)
        rows.append(jnp.sum(jnp.where(eye, column, 0.0), axis=0, keepdims=True))
    return jnp.concatenate(rows, axis=0)


def fetch(pairs, sems):
    copies = [pltpu.make_async_copy(a, b, sems.at[i]) for i, (a, b) in enumerate(pairs)]
    for copy in copies:
        copy.start()
    return copies


def begin(states_ref, table_ref, out_ref, payload_ref, nodes_ref):
    peers, slots = nodes_ref.shape
    for k in range(out_ref.shape[1]):
        out_ref[:, k, :] = states_ref[:, k * LANES : (k + 1) * LANES]
    slot = lax.broadcasted_iota(jnp.int32, (1, slots), 1)
    for o in range(peers):
        live = slot < table_ref[2 * peers : 2 * peers + 1, o : o + 1]
        nodes_ref[o : o + 1] = jnp.where(live, table_ref[o : o + 1], -1)
    rows, current = ionic_rows([out_ref[i] for i in range(out_ref.shape[0])])
    for i, row in enumerate(rows):
        out_ref[i] = row
    payload_ref[0:peers] = pick_current(current, nodes_ref[...])
    payload_ref[peers:] = table_ref[peers : 2 * peers].astype(F32)


def bring(cols_ref, diag_ref, payload_ref, cols_out, diag_out, payload_out):
    cols_out[...] = cols_ref[...]
    diag_out[...] = diag_ref[...]
    payload_out[...] = payload_ref[...]


def bring_tiles(tiles_ref, direction_ref, direction_out):
    direction_out[...] = direction_ref[...]
    del tiles_ref


def choose(own_cols, other_cols, pick_ref):
    slots, tiles = own_cols.shape
    eye = lax.broadcasted_iota(jnp.int32, (tiles, tiles), 0) == lax.broadcasted_iota(
        jnp.int32, (tiles, tiles), 1
    )
    place = lax.broadcasted_iota(jnp.int32, (tiles, pick_ref.shape[1]), 1)
    for k in range(2 * slots):
        row = own_cols[k : k + 1] if k < slots else other_cols[k - slots : k - slots + 1]
        column = jnp.sum(jnp.where(eye, row.astype(F32), 0.0), axis=1, keepdims=True)
        pick_ref[k * tiles : (k + 1) * tiles] = jnp.where(place == column.astype(jnp.int32), 1.0, 0.0)


def first_forcing(own_ref, sibling_ref, near_ref, far_ref, base_ref, give_ref, forcing_ref):
    peers = own_ref.shape[0] // 2
    ahead = meets_next()
    pairs = [(own_ref[0:1], own_ref[peers : peers + 1])]
    pairs.append((far_ref[3:4], own_ref[peers + 3 : peers + 4]))
    for k, mine in enumerate((own_ref, sibling_ref)):
        at = 2 * peers * k
        come = jnp.where(ahead, near_ref[at + 2 : at + 3], near_ref[at + 1 : at + 2])
        rows = jnp.where(ahead, mine[peers + 2 : peers + 3], mine[peers + 1 : peers + 2])
        pairs.append((come, rows))
    total = None
    for come, rows in pairs:
        part = scatter(come, rows.astype(jnp.int32), forcing_ref.shape[0])
        total = part if total is None else total + part
    forcing_ref[...] = TORSO_COUPLING * total
    keep, give = (
        jnp.where(ahead, near_ref[at + 1 : at + 2], near_ref[at + 2 : at + 3])
        for at in (peers, 3 * peers)
    )
    give_ref[...] = give
    base_ref[0:1] = own_ref[peers : peers + 1]
    base_ref[1:2] = keep
    base_ref[2:3] = far_ref[peers + 3 : peers + 4]


def complete(base_ref, got_ref, nodes_ref, maps_ref):
    ahead = meets_next()
    keep, got = base_ref[1:2], got_ref[...]
    after, before = jnp.where(ahead, keep, got), jnp.where(ahead, got, keep)
    rows = jnp.concatenate([base_ref[0:1], after, before, base_ref[2:3]], axis=0)
    maps_ref[...] = jnp.where(nodes_ref[...] < 0, -1, rows.astype(jnp.int32))


def next_shares(
    states_ref, own_estimate, far_estimate, mine_ref, yours_ref, nodes_ref, maps_ref,
    out_ref, own_ref, keep_ref, give_ref, far_ref,
):
    nodes, maps = nodes_ref[...], maps_ref[...]
    after, before = by_side(*by_partner(mine_ref[...], yours_ref[...]))
    estimates = [own_estimate[...], after, before, far_estimate[...]]
    feedback = feedback_of(estimates, nodes, maps, states_ref.shape[1])
    rows = [states_ref[i] for i in range(states_ref.shape[0])]
    rows[0] = rows[0] + TIME_STEP * FEEDBACK_RATE * feedback
    rows, current = ionic_rows(rows)
    for i, row in enumerate(rows):
        out_ref[i] = row
    outgoing = pick_current(current, nodes)
    spread_current(outgoing, maps, own_ref, keep_ref, give_ref, far_ref)


def window_of(chain, direction, first, second):
    torso = direction.shape[0]
    here = lax.axis_index("dom")
    after, before = by_side(first, second)
    before = jnp.where(here > 0, before[torso - HALO :], 0.0)
    after = jnp.where(here < chain - 1, after[0:HALO], 0.0)
    filler = jnp.zeros((torso - 2 * HALO, LANES), F32)
    return jnp.concatenate([before, direction, after, filler], axis=0)


def sweep_one(
    chain, own_ref, other_ref, pick_ref, mine_ref, yours_ref, forcing_ref, direction_in, diag_ref,
    residual_ref, direction_ref, estimate_ref,
):
    diag = diag_ref[...]
    direction = direction_in[...]
    window = window_of(chain, direction, *by_partner(mine_ref[...], yours_ref[...]))
    moved = product(own_ref, other_ref, pick_ref, window)
    residual = forcing_ref[...] - (diag * direction + moved)
    estimate = direction
    direction = KEEP[0] * direction + PULL[0] * (residual / diag)
    residual_ref[...] = residual
    direction_ref[...] = direction
    estimate_ref[...] = estimate + direction


def sweep_two(
    chain, last, own_ref, other_ref, pick_ref, mine_ref, yours_ref, direction_in, residual_in,
    estimate_in, diag_ref, estimate_ref, *refs,
):
    torso = estimate_ref.shape[0]
    diag = diag_ref[...]
    direction = direction_in[...]
    window = window_of(chain, direction, *by_partner(mine_ref[...], yours_ref[...]))
    moved = product(own_ref, other_ref, pick_ref, window)
    residual = residual_in[...] - (diag * direction + moved)
    direction = KEEP[1] * direction + PULL[1] * (residual / diag)
    estimate = estimate_in[...] + direction
    if last:
        residual_ref, = refs
        residual_ref[...] = residual
        estimate_ref[0 : torso // 2] = estimate
        estimate_ref[torso // 2 :] = direction
    else:
        estimate_ref[...] = estimate


def finish(
    chain, own_ref, other_ref, pick_ref, packed_ref, far_ref, mine_ref, yours_ref, residual_in,
    diag_ref, states_ref, nodes_ref, maps_ref, out_ref, potential_ref, residual_ref, dense_ref,
):
    torso = residual_ref.shape[0]
    head, tail = slice(0, torso), slice(torso, 2 * torso)
    estimate, direction = packed_ref[head], packed_ref[tail]
    potential_ref[...] = estimate
    first, second = by_partner(mine_ref[...], yours_ref[...])
    after, before = by_side(first[head], second[head])
    feedback = feedback_of(
        [estimate, after, before, far_ref[head]], nodes_ref[...], maps_ref[...],
        states_ref.shape[1],
    )
    dense_ref[...] = states_ref[...]
    dense_ref[0] = states_ref[0] + TIME_STEP * FEEDBACK_RATE * feedback
    for k in range(states_ref.shape[1]):
        out_ref[:, k * LANES : (k + 1) * LANES] = dense_ref[:, k, :]
    window = window_of(chain, direction, first[tail], second[tail])
    moved = product(own_ref, other_ref, pick_ref, window)
    residual_ref[...] = residual_in[...] - (diag_ref[...] * direction + moved)


def on_device(states, send_node, send_count, recv_row, columns, tile_values, diagonal):
    chain = lax.axis_size("dom")
    peers, slots = send_node.shape[1:]
    node_count = states.shape[1]
    heart = node_count // LANES
    torso = diagonal.shape[0] // LANES

    def with_far(value):
        return lax.ppermute(value, "dom", [(i, (i + chain // 2) % chain) for i in range(chain)])

    def with_either(value, closed):
        cases = lax.axis_size("case")
        ends = () if closed or cases % 2 else (0, chain - 1)
        pairs = []
        for case in range(cases):
            for i in range(chain):
                me = (case * chain + i) * 2
                pairs.append((me, (case * chain + (i ^ 1)) * 2))
                if i in ends:
                    pairs.append((me + 1, ((case ^ 1) * chain + i) * 2 + 1))
                else:
                    second = (((i + 1) ^ 1) - 1) % chain
                    pairs.append((me + 1, (case * chain + second) * 2 + 1))
        return lax.ppermute(value, ("case", "dom", "sub"), pairs)

    def from_sibling(value):
        return lax.ppermute(value, "sub", [(0, 1), (1, 0)])

    def shape(*dims, dtype=F32):
        return jax.ShapeDtypeStruct(dims, dtype)

    dense = shape(states.shape[0], heart, LANES)
    field = shape(torso, LANES)
    packed = shape(2 * torso, LANES)
    counts = jnp.pad(send_count, ((0, 0), (0, slots - peers)))
    table = jnp.concatenate([send_node[0], recv_row[0], counts])
    index = shape(peers, slots, dtype=jnp.int32)
    payload_shape = shape(2 * peers, slots)
    states, payload, nodes = call(begin, (dense, payload_shape, index))(in_specs=[VMEM] * 2)(
        states, table
    )
    beside = from_sibling(payload)
    tile_values, beside = lax.optimization_barrier((tile_values, beside))
    other_tiles = from_sibling(tile_values)
    far = with_far(payload)
    near = with_either(jnp.concatenate([payload, beside]), True)
    columns, diag, own = call(
        bring, (shape(*columns.shape[::-1], dtype=jnp.int32), field, payload_shape)
    )(in_specs=[VMEM] * 3)(columns.T, diagonal.reshape(torso, LANES), payload)
    base, give, forcing = call(first_forcing, (shape(3, slots), shape(1, slots), field))(
        in_specs=[VMEM] * 4
    )(own, beside, near, far)
    maps = call(complete, index)(in_specs=[VMEM] * 3)(base, from_sibling(give), nodes)
    for time_step in range(2):
        last = time_step == 1
        forcing = forcing + from_sibling(forcing)
        direction = forcing / (CHEB_THETA * diag)
        halo = with_either(direction, False)
        if not last:
            choices = 2 * columns.shape[0] * torso
            direction = call(bring_tiles, field)(in_specs=[VMEM] * 2)(tile_values, direction)
            pick = call(choose, shape(choices, 2 * torso))(in_specs=[VMEM] * 2)(
                columns, from_sibling(columns)
            )
            halo, direction = lax.optimization_barrier((halo, direction))
            stored = (tile_values, other_tiles, pick)
        residual, direction, estimate = call(
            functools.partial(sweep_one, chain), (field,) * 3
        )(in_specs=[VMEM] * 8)(*stored, halo, from_sibling(halo), forcing, direction, diag)
        halo = with_either(direction, False)
        swept = call(
            functools.partial(sweep_two, chain, last), (packed, field) if last else field
        )(in_specs=[VMEM] * 9)(
            *stored, halo, from_sibling(halo), direction, residual, estimate, diag
        )
        estimate, residual = swept if last else (swept, None)
        far = with_far(estimate)
        near = with_either(estimate, True)
        if not last:
            states, own, keep, give, away = call(next_shares, (dense,) + (field,) * 4)(
                in_specs=[VMEM] * 7
            )(states, estimate, far, near, from_sibling(near), nodes, maps)
            far = with_far(away)
            near = with_either(keep + from_sibling(give), True)
            forcing = TORSO_COUPLING * (own + far + near)
    new_states, potential, residual = call(
        functools.partial(finish, chain),
        (shape(*dense.shape[:1], node_count), field, field),
        (pltpu.VMEM(dense.shape, F32),),
    )(in_specs=[VMEM] * 12)(
        *stored, estimate, far, near, from_sibling(near), residual, diag, states, nodes, maps
    )
    return new_states, potential.reshape(-1), residual.reshape(-1)


def solution(mesh):
    placed = (
        P(None, ("case", "dom", "sub")),
        P(("case", "dom", "sub"), None, None),
        P(("case", "dom", "sub"), None),
        P(("case", "dom", "sub"), None, None),
        P(("case", "dom"), "sub"),
        P(("case", "dom"), "sub", None, None),
        P(("case", "dom")),
    )
    return jax.shard_map(
        on_device,
        mesh=mesh,
        in_specs=placed,
        out_specs=(P(None, ("case", "dom", "sub")), P(("case", "dom")), P(("case", "dom"))),
        check_vma=False,
    )
```

```python
import functools

import jax
import jax.numpy as jnp
from jax import lax
from jax.experimental import pallas as pl
from jax.experimental.pallas import tpu as pltpu
from jax.sharding import PartitionSpec as P

HALO = 2
SWEEPS = 3
LANES = 128

TIME_STEP = 0.02
NERNST_SCALE = 0.267
SODIUM_OUT = 1.4
POTASSIUM_OUT = 0.054
CALCIUM_OUT = 2000.0
COND_SODIUM = 8.0
COND_CALCIUM = 1.0
COND_TRANSIENT = 0.3
COND_RAPID = 0.2
COND_SLOW = 0.3
COND_INWARD = 2.0
COND_RELEASE = 3.0
MEMBRANE_RATE = 2.0
TORSO_COUPLING = 0.5
FEEDBACK_RATE = 5.0
CHEB_THETA = 1.0
CHEB_DELTA = 0.5
GATE_MIDPOINT = [-0.56, -0.7, -0.7, -0.08, -0.2, -0.3, 0.2, -0.28, -0.26, -0.88, 0.05, -0.8, -0.5]
GATE_STEEPNESS = [0.09, -0.07, -0.07, 0.07, -0.07, -0.09, 0.06, -0.05, 0.07, -0.24, 0.14, -0.1, 0.08]
TIME_BASE = [0.02, 0.3, 1.0, 0.1, 2.0, 0.5, 0.1, 1.0, 1.0, 0.5, 1.0, 0.05, 0.2]
TIME_PEAK = [0.1, 1.0, 3.0, 0.5, 5.0, 2.0, 0.3, 5.0, 3.0, 2.0, 4.0, 0.1, 1.0]

SIGMA = CHEB_THETA / CHEB_DELTA
KEEP, PULL = [], []
_ratio = 1.0 / SIGMA
for _ in range(SWEEPS - 1):
    _next = 1.0 / (2.0 * SIGMA - _ratio)
    KEEP.append(_next * _ratio)
    PULL.append(2.0 * _next / CHEB_DELTA)
    _ratio = _next

VMEM = pl.BlockSpec(memory_space=pltpu.VMEM)
F32 = jnp.float32


def call(kernel, outs, scratch=(), limit=16, cost=4_000_000):
    return functools.partial(
        pl.pallas_call,
        kernel,
        out_shape=outs,
        out_specs=jax.tree.map(lambda _: VMEM, outs),
        scratch_shapes=list(scratch),
        compiler_params=pltpu.CompilerParams(vmem_limit_bytes=limit << 20),
        cost_estimate=pl.CostEstimate(flops=cost, bytes_accessed=1 << 18, transcendentals=0),
    )


def ionic_rows(rows):
    voltage, gating = rows[0], rows[1:14]
    sodium, potassium, calcium, reticulum, subspace = rows[14:19]
    moved = []
    for i, gate in enumerate(gating):
        shifted = voltage - GATE_MIDPOINT[i]
        steady = jax.nn.sigmoid(shifted / GATE_STEEPNESS[i])
        time_const = TIME_BASE[i] + TIME_PEAK[i] * jnp.exp(-jnp.square(shifted / 0.3))
        moved.append(steady + (gate - steady) * jnp.exp(-TIME_STEP / time_const))
    g = moved
    sodium_rev = NERNST_SCALE * jnp.log(SODIUM_OUT / sodium)
    potassium_rev = NERNST_SCALE * jnp.log(POTASSIUM_OUT / potassium)
    calcium_rev = 0.5 * NERNST_SCALE * jnp.log(CALCIUM_OUT / subspace)
    sodium_flow = COND_SODIUM * (g[0] * g[0] * g[0]) * g[1] * g[2] * (voltage - sodium_rev)
    calcium_flow = COND_CALCIUM * g[3] * g[4] * g[5] * (voltage - calcium_rev)
    potassium_cond = (
        COND_TRANSIENT * g[6] * g[7]
        + COND_RAPID * g[8] * g[9]
        + COND_SLOW * (g[10] * g[10])
        + COND_INWARD * g[11]
    )
    potassium_flow = potassium_cond * (voltage - potassium_rev)
    current = sodium_flow + calcium_flow + potassium_flow
    release = COND_RELEASE * g[12] * (reticulum - subspace) / (reticulum + subspace)
    sodium = sodium * jnp.exp(-0.5 * TIME_STEP * sodium_flow)
    potassium = potassium * jnp.exp(-0.5 * TIME_STEP * potassium_flow)
    calcium = calcium * jnp.exp(-0.5 * TIME_STEP * calcium_flow)
    subspace = subspace * jnp.exp(TIME_STEP * (release - 0.5 * calcium_flow))
    reticulum = reticulum * jnp.exp(-TIME_STEP * release)
    voltage = voltage - TIME_STEP * MEMBRANE_RATE * current
    return [voltage, *moved, sodium, potassium, calcium, reticulum, subspace], current


def pairs_of(index):
    chunks = [index[:, k : k + LANES] for k in range(0, index.shape[1], LANES)]
    return [jnp.concatenate(chunks[k : k + 2], axis=0) for k in range(0, len(chunks), 2)]


def gather(source, rows, index):
    peers = index.shape[0]
    out = []
    for pair in pairs_of(index):
        high, low = pair >> 7, pair & (LANES - 1)
        total = jnp.zeros(pair.shape, F32)
        for h in range(rows):
            picked = jnp.take_along_axis(source(h), low, axis=1)
            total = jnp.where(high == h, picked, total)
        out += [total[:peers], total[peers:]]
    return jnp.concatenate(out, axis=1)


def three_parts(value):
    first = value.astype(jnp.bfloat16).astype(F32)
    rest = value - first
    second = rest.astype(jnp.bfloat16).astype(F32)
    return first, second, rest - second


def scatter(values, index, rows):
    slots = values.shape[1]
    high, low = index >> 7, index & (LANES - 1)
    mine = lax.broadcasted_iota(jnp.int32, (rows, slots), 0) == high
    left = jnp.concatenate([jnp.where(mine, part, 0.0) for part in three_parts(values)], axis=0)
    spread = lax.broadcasted_iota(jnp.int32, (LANES, slots), 0) == low
    right = jnp.where(spread, 1.0, 0.0).astype(jnp.bfloat16)
    sums = lax.dot_general(
        left.astype(jnp.bfloat16), right, (((1,), (1,)), ((), ())), preferred_element_type=F32
    )
    return sums[:rows] + sums[rows : 2 * rows] + sums[2 * rows :]


def pick_current(current, nodes):
    rows, peers = current.shape[0], nodes.shape[0]
    return gather(
        lambda h: jnp.broadcast_to(current[h : h + 1], (2 * peers, LANES)), rows, nodes
    )


def is_even():
    return lax.rem(lax.axis_index("dom"), 2) == 0


def meets_next():
    return is_even() == (lax.axis_index("sub") == 0)


def by_partner(mine, yours):
    zero = lax.axis_index("sub") == 0
    return jnp.where(zero, mine, yours), jnp.where(zero, yours, mine)


def by_side(first, second):
    even = is_even()
    return jnp.where(even, first, second), jnp.where(even, second, first)


def spread_current(outgoing, maps, own_ref, keep_ref, give_ref, far_ref):
    torso = own_ref.shape[0]
    own, after, before, far = (
        scatter(outgoing[o : o + 1], maps[o : o + 1], torso) for o in range(maps.shape[0])
    )
    ahead = meets_next()
    own_ref[...] = own
    keep_ref[...] = jnp.where(ahead, after, before)
    give_ref[...] = jnp.where(ahead, before, after)
    far_ref[...] = far


def feedback_of(estimates, nodes, maps, heart):
    peers = nodes.shape[0]
    torso = estimates[0].shape[0]

    def source(h):
        rows = [estimate[h : h + 1] for estimate in estimates]
        return jnp.concatenate(rows * 2, axis=0)

    returned = gather(source, torso, maps)
    total = jnp.zeros((heart, LANES), F32)
    for o in range(peers):
        total = total + scatter(returned[o : o + 1], nodes[o : o + 1], heart)
    return total


def product(own_ref, other_ref, pick_ref, window):
    tiles, slots = own_ref.shape[0], own_ref.shape[1]
    parts = jnp.concatenate(three_parts(window), axis=1).astype(jnp.bfloat16)
    picked = jnp.dot(pick_ref[...].astype(jnp.bfloat16), parts, preferred_element_type=F32)
    picked = picked[:, :LANES] + picked[:, LANES : 2 * LANES] + picked[:, 2 * LANES :]
    eye = lax.broadcasted_iota(jnp.int32, (LANES, LANES), 0) == lax.broadcasted_iota(
        jnp.int32, (LANES, LANES), 1
    )
    rows = []
    for t in range(tiles):
        total = None
        for k in range(2 * slots):
            tile = own_ref[t, k] if k < slots else other_ref[t, k - slots]
            term = tile * picked[k * tiles + t : k * tiles + t + 1]
            total = term if total is None else total + term
        column = jnp.sum(total, axis=1, keepdims=True)
        rows.append(jnp.sum(jnp.where(eye, column, 0.0), axis=0, keepdims=True))
    return jnp.concatenate(rows, axis=0)


def fetch(pairs, sems):
    copies = [pltpu.make_async_copy(a, b, sems.at[i]) for i, (a, b) in enumerate(pairs)]
    for copy in copies:
        copy.start()
    return copies


def begin(
    states_ref, table_ref, out_ref, nodes_ref, own_ref, keep_ref, give_ref, far_ref
):
    peers, slots = nodes_ref.shape
    for k in range(out_ref.shape[1]):
        out_ref[:, k, :] = states_ref[:, k * LANES : (k + 1) * LANES]
    slot = lax.broadcasted_iota(jnp.int32, (1, slots), 1)
    for o in range(peers):
        live = slot < table_ref[2 * peers : 2 * peers + 1, o : o + 1]
        nodes_ref[o : o + 1] = jnp.where(live, table_ref[o : o + 1], -1)
    rows, current = ionic_rows([out_ref[i] for i in range(out_ref.shape[0])])
    for i, row in enumerate(rows):
        out_ref[i] = row
    outgoing = pick_current(current, nodes_ref[...])
    incoming = table_ref[peers : 2 * peers].astype(F32)

    def pair(out, into):
        return jnp.concatenate([outgoing[out : out + 1], incoming[into : into + 1]], axis=0)

    to_next, to_prev = pair(1, 2), pair(2, 1)
    ahead = meets_next()
    own_ref[...] = pair(0, 0)
    keep_ref[...] = jnp.where(ahead, to_next, to_prev)
    give_ref[...] = jnp.where(ahead, to_prev, to_next)
    far_ref[...] = pair(3, 3)


def bring(cols_ref, diag_ref, own_ref, cols_out, diag_out, own_out):
    cols_out[...] = cols_ref[...]
    diag_out[...] = diag_ref[...]
    own_out[...] = own_ref[...]


def bring_tiles(tiles_ref, direction_ref, direction_out):
    direction_out[...] = direction_ref[...]
    del tiles_ref


def choose(own_cols, other_cols, pick_ref):
    slots, tiles = own_cols.shape
    eye = lax.broadcasted_iota(jnp.int32, (tiles, tiles), 0) == lax.broadcasted_iota(
        jnp.int32, (tiles, tiles), 1
    )
    place = lax.broadcasted_iota(jnp.int32, (tiles, pick_ref.shape[1]), 1)
    for k in range(2 * slots):
        row = own_cols[k : k + 1] if k < slots else other_cols[k - slots : k - slots + 1]
        column = jnp.sum(jnp.where(eye, row.astype(F32), 0.0), axis=1, keepdims=True)
        pick_ref[k * tiles : (k + 1) * tiles] = jnp.where(place == column.astype(jnp.int32), 1.0, 0.0)


def first_forcing(
    own_ref, keep_ref, got_ref, near_ref, to_far, far_ref, give_ref, forcing_ref
):
    total = None
    for come, rows in (
        (own_ref[0:1], own_ref[1:2]),
        (far_ref[0:1], to_far[1:2]),
        (near_ref[0:1], keep_ref[1:2]),
        (near_ref[2:3], got_ref[1:2]),
    ):
        part = scatter(come, rows.astype(jnp.int32), forcing_ref.shape[0])
        total = part if total is None else total + part
    forcing_ref[...] = TORSO_COUPLING * total
    give_ref[...] = near_ref[3:4]


def complete(own_ref, near_ref, far_ref, got_ref, nodes_ref, maps_ref):
    ahead = meets_next()
    keep, got = near_ref[1:2], got_ref[...]
    after, before = jnp.where(ahead, keep, got), jnp.where(ahead, got, keep)
    rows = jnp.concatenate([own_ref[1:2], after, before, far_ref[1:2]], axis=0)
    maps_ref[...] = jnp.where(nodes_ref[...] < 0, -1, rows.astype(jnp.int32))


def next_shares(
    states_ref, own_estimate, far_estimate, mine_ref, yours_ref, nodes_ref, maps_ref,
    out_ref, own_ref, keep_ref, give_ref, far_ref,
):
    nodes, maps = nodes_ref[...], maps_ref[...]
    after, before = by_side(*by_partner(mine_ref[...], yours_ref[...]))
    estimates = [own_estimate[...], after, before, far_estimate[...]]
    feedback = feedback_of(estimates, nodes, maps, states_ref.shape[1])
    rows = [states_ref[i] for i in range(states_ref.shape[0])]
    rows[0] = rows[0] + TIME_STEP * FEEDBACK_RATE * feedback
    rows, current = ionic_rows(rows)
    for i, row in enumerate(rows):
        out_ref[i] = row
    outgoing = pick_current(current, nodes)
    spread_current(outgoing, maps, own_ref, keep_ref, give_ref, far_ref)


def window_of(chain, direction, first, second):
    torso = direction.shape[0]
    here = lax.axis_index("dom")
    after, before = by_side(first, second)
    before = jnp.where(here > 0, before[torso - HALO :], 0.0)
    after = jnp.where(here < chain - 1, after[0:HALO], 0.0)
    filler = jnp.zeros((torso - 2 * HALO, LANES), F32)
    return jnp.concatenate([before, direction, after, filler], axis=0)


def sweep_one(
    chain, own_ref, other_ref, pick_ref, mine_ref, yours_ref, forcing_ref, direction_in, diag_ref,
    residual_ref, direction_ref, estimate_ref,
):
    diag = diag_ref[...]
    direction = direction_in[...]
    window = window_of(chain, direction, *by_partner(mine_ref[...], yours_ref[...]))
    moved = product(own_ref, other_ref, pick_ref, window)
    residual = forcing_ref[...] - (diag * direction + moved)
    estimate = direction
    direction = KEEP[0] * direction + PULL[0] * (residual / diag)
    residual_ref[...] = residual
    direction_ref[...] = direction
    estimate_ref[...] = estimate + direction


def sweep_two(
    chain, last, own_ref, other_ref, pick_ref, mine_ref, yours_ref, direction_in, residual_in,
    estimate_in, diag_ref, estimate_ref, *refs,
):
    torso = estimate_ref.shape[0]
    diag = diag_ref[...]
    direction = direction_in[...]
    window = window_of(chain, direction, *by_partner(mine_ref[...], yours_ref[...]))
    moved = product(own_ref, other_ref, pick_ref, window)
    residual = residual_in[...] - (diag * direction + moved)
    direction = KEEP[1] * direction + PULL[1] * (residual / diag)
    estimate = estimate_in[...] + direction
    if last:
        residual_ref, = refs
        residual_ref[...] = residual
        estimate_ref[0 : torso // 2] = estimate
        estimate_ref[torso // 2 :] = direction
    else:
        estimate_ref[...] = estimate


def finish(
    chain, own_ref, other_ref, pick_ref, packed_ref, far_ref, mine_ref, yours_ref, residual_in,
    diag_ref, states_ref, nodes_ref, maps_ref, out_ref, potential_ref, residual_ref, dense_ref,
):
    torso = residual_ref.shape[0]
    head, tail = slice(0, torso), slice(torso, 2 * torso)
    estimate, direction = packed_ref[head], packed_ref[tail]
    potential_ref[...] = estimate
    first, second = by_partner(mine_ref[...], yours_ref[...])
    after, before = by_side(first[head], second[head])
    feedback = feedback_of(
        [estimate, after, before, far_ref[head]], nodes_ref[...], maps_ref[...],
        states_ref.shape[1],
    )
    dense_ref[...] = states_ref[...]
    dense_ref[0] = states_ref[0] + TIME_STEP * FEEDBACK_RATE * feedback
    for k in range(states_ref.shape[1]):
        out_ref[:, k * LANES : (k + 1) * LANES] = dense_ref[:, k, :]
    window = window_of(chain, direction, first[tail], second[tail])
    moved = product(own_ref, other_ref, pick_ref, window)
    residual_ref[...] = residual_in[...] - (diag_ref[...] * direction + moved)


def on_device(states, send_node, send_count, recv_row, columns, tile_values, diagonal):
    chain = lax.axis_size("dom")
    peers, slots = send_node.shape[1:]
    node_count = states.shape[1]
    heart = node_count // LANES
    torso = diagonal.shape[0] // LANES

    def with_far(value):
        return lax.ppermute(value, "dom", [(i, (i + chain // 2) % chain) for i in range(chain)])

    def with_either(value, closed):
        cases = lax.axis_size("case")
        ends = () if closed or cases % 2 else (0, chain - 1)
        pairs = []
        for case in range(cases):
            for i in range(chain):
                me = (case * chain + i) * 2
                pairs.append((me, (case * chain + (i ^ 1)) * 2))
                if i in ends:
                    pairs.append((me + 1, ((case ^ 1) * chain + i) * 2 + 1))
                else:
                    second = (((i + 1) ^ 1) - 1) % chain
                    pairs.append((me + 1, (case * chain + second) * 2 + 1))
        return lax.ppermute(value, ("case", "dom", "sub"), pairs)

    def from_sibling(value):
        return lax.ppermute(value, "sub", [(0, 1), (1, 0)])

    def shape(*dims, dtype=F32):
        return jax.ShapeDtypeStruct(dims, dtype)

    dense = shape(states.shape[0], heart, LANES)
    field = shape(torso, LANES)
    packed = shape(2 * torso, LANES)
    counts = jnp.pad(send_count, ((0, 0), (0, slots - peers)))
    table = jnp.concatenate([send_node[0], recv_row[0], counts])
    index = shape(peers, slots, dtype=jnp.int32)
    double = shape(2, slots)
    states, nodes, own, keep, give, to_far = call(begin, (dense, index) + (double,) * 4)(
        in_specs=[VMEM] * 2
    )(states, table)
    got = from_sibling(give)
    tile_values, got = lax.optimization_barrier((tile_values, got))
    other_tiles = from_sibling(tile_values)
    far = with_far(to_far)
    near = with_either(jnp.concatenate([keep, got]), True)
    columns, diag, own = call(
        bring, (shape(*columns.shape[::-1], dtype=jnp.int32), field, double)
    )(in_specs=[VMEM] * 3)(columns.T, diagonal.reshape(torso, LANES), own)
    give, forcing = call(first_forcing, (shape(1, slots), field))(in_specs=[VMEM] * 6)(
        own, keep, got, near, to_far, far
    )
    maps = call(complete, index)(in_specs=[VMEM] * 5)(own, near, far, from_sibling(give), nodes)
    other_columns = from_sibling(columns)
    for time_step in range(2):
        last = time_step == 1
        others = from_sibling(forcing)
        if not last:
            others, other_columns = lax.optimization_barrier((others, other_columns))
        forcing = forcing + others
        direction = forcing / (CHEB_THETA * diag)
        halo = with_either(direction, False)
        if not last:
            choices = 2 * columns.shape[0] * torso
            direction = call(bring_tiles, field)(in_specs=[VMEM] * 2)(tile_values, direction)
            pick = call(choose, shape(choices, 2 * torso))(in_specs=[VMEM] * 2)(
                columns, other_columns
            )
            halo, direction = lax.optimization_barrier((halo, direction))
            stored = (tile_values, other_tiles, pick)
        residual, direction, estimate = call(
            functools.partial(sweep_one, chain), (field,) * 3
        )(in_specs=[VMEM] * 8)(*stored, halo, from_sibling(halo), forcing, direction, diag)
        halo = with_either(direction, False)
        swept = call(
            functools.partial(sweep_two, chain, last), (packed, field) if last else field
        )(in_specs=[VMEM] * 9)(
            *stored, halo, from_sibling(halo), direction, residual, estimate, diag
        )
        estimate, residual = swept if last else (swept, None)
        far = with_far(estimate)
        near = with_either(estimate, True)
        if not last:
            states, own, keep, give, away = call(next_shares, (dense,) + (field,) * 4)(
                in_specs=[VMEM] * 7
            )(states, estimate, far, near, from_sibling(near), nodes, maps)
            far = with_far(away)
            near = with_either(keep + from_sibling(give), True)
            forcing = TORSO_COUPLING * (own + far + near)
    new_states, potential, residual = call(
        functools.partial(finish, chain),
        (shape(*dense.shape[:1], node_count), field, field),
        (pltpu.VMEM(dense.shape, F32),),
    )(in_specs=[VMEM] * 12)(
        *stored, estimate, far, near, from_sibling(near), residual, diag, states, nodes, maps
    )
    return new_states, potential.reshape(-1), residual.reshape(-1)


def solution(mesh):
    placed = (
        P(None, ("case", "dom", "sub")),
        P(("case", "dom", "sub"), None, None),
        P(("case", "dom", "sub"), None),
        P(("case", "dom", "sub"), None, None),
        P(("case", "dom"), "sub"),
        P(("case", "dom"), "sub", None, None),
        P(("case", "dom")),
    )
    return jax.shard_map(
        on_device,
        mesh=mesh,
        in_specs=placed,
        out_specs=(P(None, ("case", "dom", "sub")), P(("case", "dom")), P(("case", "dom"))),
        check_vma=False,
    )
```

```python
import functools

import jax
import jax.numpy as jnp
from jax import lax
from jax.experimental import pallas as pl
from jax.experimental.pallas import tpu as pltpu
from jax.sharding import PartitionSpec as P

HALO = 2
SWEEPS = 3
LANES = 128

TIME_STEP = 0.02
NERNST_SCALE = 0.267
SODIUM_OUT = 1.4
POTASSIUM_OUT = 0.054
CALCIUM_OUT = 2000.0
COND_SODIUM = 8.0
COND_CALCIUM = 1.0
COND_TRANSIENT = 0.3
COND_RAPID = 0.2
COND_SLOW = 0.3
COND_INWARD = 2.0
COND_RELEASE = 3.0
MEMBRANE_RATE = 2.0
TORSO_COUPLING = 0.5
FEEDBACK_RATE = 5.0
CHEB_THETA = 1.0
CHEB_DELTA = 0.5
GATE_MIDPOINT = [-0.56, -0.7, -0.7, -0.08, -0.2, -0.3, 0.2, -0.28, -0.26, -0.88, 0.05, -0.8, -0.5]
GATE_STEEPNESS = [0.09, -0.07, -0.07, 0.07, -0.07, -0.09, 0.06, -0.05, 0.07, -0.24, 0.14, -0.1, 0.08]
TIME_BASE = [0.02, 0.3, 1.0, 0.1, 2.0, 0.5, 0.1, 1.0, 1.0, 0.5, 1.0, 0.05, 0.2]
TIME_PEAK = [0.1, 1.0, 3.0, 0.5, 5.0, 2.0, 0.3, 5.0, 3.0, 2.0, 4.0, 0.1, 1.0]

SIGMA = CHEB_THETA / CHEB_DELTA
KEEP, PULL = [], []
_ratio = 1.0 / SIGMA
for _ in range(SWEEPS - 1):
    _next = 1.0 / (2.0 * SIGMA - _ratio)
    KEEP.append(_next * _ratio)
    PULL.append(2.0 * _next / CHEB_DELTA)
    _ratio = _next

VMEM = pl.BlockSpec(memory_space=pltpu.VMEM)
F32 = jnp.float32


def call(kernel, outs, scratch=(), limit=16, cost=4_000_000):
    return functools.partial(
        pl.pallas_call,
        kernel,
        out_shape=outs,
        out_specs=jax.tree.map(lambda _: VMEM, outs),
        scratch_shapes=list(scratch),
        compiler_params=pltpu.CompilerParams(vmem_limit_bytes=limit << 20),
        cost_estimate=pl.CostEstimate(flops=cost, bytes_accessed=1 << 18, transcendentals=0),
    )


def ionic_rows(rows):
    voltage, gating = rows[0], rows[1:14]
    sodium, potassium, calcium, reticulum, subspace = rows[14:19]
    moved = []
    for i, gate in enumerate(gating):
        shifted = voltage - GATE_MIDPOINT[i]
        steady = jax.nn.sigmoid(shifted / GATE_STEEPNESS[i])
        time_const = TIME_BASE[i] + TIME_PEAK[i] * jnp.exp(-jnp.square(shifted / 0.3))
        moved.append(steady + (gate - steady) * jnp.exp(-TIME_STEP / time_const))
    g = moved
    sodium_rev = NERNST_SCALE * jnp.log(SODIUM_OUT / sodium)
    potassium_rev = NERNST_SCALE * jnp.log(POTASSIUM_OUT / potassium)
    calcium_rev = 0.5 * NERNST_SCALE * jnp.log(CALCIUM_OUT / subspace)
    sodium_flow = COND_SODIUM * (g[0] * g[0] * g[0]) * g[1] * g[2] * (voltage - sodium_rev)
    calcium_flow = COND_CALCIUM * g[3] * g[4] * g[5] * (voltage - calcium_rev)
    potassium_cond = (
        COND_TRANSIENT * g[6] * g[7]
        + COND_RAPID * g[8] * g[9]
        + COND_SLOW * (g[10] * g[10])
        + COND_INWARD * g[11]
    )
    potassium_flow = potassium_cond * (voltage - potassium_rev)
    current = sodium_flow + calcium_flow + potassium_flow
    release = COND_RELEASE * g[12] * (reticulum - subspace) / (reticulum + subspace)
    sodium = sodium * jnp.exp(-0.5 * TIME_STEP * sodium_flow)
    potassium = potassium * jnp.exp(-0.5 * TIME_STEP * potassium_flow)
    calcium = calcium * jnp.exp(-0.5 * TIME_STEP * calcium_flow)
    subspace = subspace * jnp.exp(TIME_STEP * (release - 0.5 * calcium_flow))
    reticulum = reticulum * jnp.exp(-TIME_STEP * release)
    voltage = voltage - TIME_STEP * MEMBRANE_RATE * current
    return [voltage, *moved, sodium, potassium, calcium, reticulum, subspace], current


def pairs_of(index):
    chunks = [index[:, k : k + LANES] for k in range(0, index.shape[1], LANES)]
    return [jnp.concatenate(chunks[k : k + 2], axis=0) for k in range(0, len(chunks), 2)]


def gather(source, rows, index):
    peers = index.shape[0]
    out = []
    for pair in pairs_of(index):
        high, low = pair >> 7, pair & (LANES - 1)
        total = jnp.zeros(pair.shape, F32)
        for h in range(rows):
            picked = jnp.take_along_axis(source(h), low, axis=1)
            total = jnp.where(high == h, picked, total)
        out += [total[:peers], total[peers:]]
    return jnp.concatenate(out, axis=1)


def three_parts(value):
    first = value.astype(jnp.bfloat16).astype(F32)
    rest = value - first
    second = rest.astype(jnp.bfloat16).astype(F32)
    return first, second, rest - second


def scatter(values, index, rows):
    slots = values.shape[1]
    high, low = index >> 7, index & (LANES - 1)
    mine = lax.broadcasted_iota(jnp.int32, (rows, slots), 0) == high
    left = jnp.concatenate([jnp.where(mine, part, 0.0) for part in three_parts(values)], axis=0)
    spread = lax.broadcasted_iota(jnp.int32, (LANES, slots), 0) == low
    right = jnp.where(spread, 1.0, 0.0).astype(jnp.bfloat16)
    sums = lax.dot_general(
        left.astype(jnp.bfloat16), right, (((1,), (1,)), ((), ())), preferred_element_type=F32
    )
    return sums[:rows] + sums[rows : 2 * rows] + sums[2 * rows :]


def pick_current(current, nodes):
    rows, peers = current.shape[0], nodes.shape[0]
    return gather(
        lambda h: jnp.broadcast_to(current[h : h + 1], (2 * peers, LANES)), rows, nodes
    )


def is_even():
    return lax.rem(lax.axis_index("dom"), 2) == 0


def meets_next():
    return is_even() == (lax.axis_index("sub") == 0)


def by_partner(mine, yours):
    zero = lax.axis_index("sub") == 0
    return jnp.where(zero, mine, yours), jnp.where(zero, yours, mine)


def by_side(first, second):
    even = is_even()
    return jnp.where(even, first, second), jnp.where(even, second, first)


def spread_current(outgoing, maps, own_ref, keep_ref, give_ref, far_ref):
    torso = own_ref.shape[0]
    own, after, before, far = (
        scatter(outgoing[o : o + 1], maps[o : o + 1], torso) for o in range(maps.shape[0])
    )
    ahead = meets_next()
    own_ref[...] = own
    keep_ref[...] = jnp.where(ahead, after, before)
    give_ref[...] = jnp.where(ahead, before, after)
    far_ref[...] = far


def feedback_of(estimates, nodes, maps, heart):
    peers = nodes.shape[0]
    torso = estimates[0].shape[0]

    def source(h):
        rows = [estimate[h : h + 1] for estimate in estimates]
        return jnp.concatenate(rows * 2, axis=0)

    returned = gather(source, torso, maps)
    total = jnp.zeros((heart, LANES), F32)
    for o in range(peers):
        total = total + scatter(returned[o : o + 1], nodes[o : o + 1], heart)
    return total


def tile_rows(count, slots, tile, pick, window):
    parts = jnp.concatenate(three_parts(window), axis=1).astype(jnp.bfloat16)
    picked = jnp.dot(pick.astype(jnp.bfloat16), parts, preferred_element_type=F32)
    picked = picked[:, :LANES] + picked[:, LANES : 2 * LANES] + picked[:, 2 * LANES :]
    eye = lax.broadcasted_iota(jnp.int32, (LANES, LANES), 0) == lax.broadcasted_iota(
        jnp.int32, (LANES, LANES), 1
    )
    rows = []
    for t in range(count):
        total = None
        for k in range(slots):
            term = tile(t, k) * picked[k * count + t : k * count + t + 1]
            total = term if total is None else total + term
        column = jnp.sum(total, axis=1, keepdims=True)
        rows.append(jnp.sum(jnp.where(eye, column, 0.0), axis=0, keepdims=True))
    return jnp.concatenate(rows, axis=0)


def product(own_ref, other_ref, pick_ref, window):
    tiles, slots = own_ref.shape[0], own_ref.shape[1]
    return tile_rows(
        tiles,
        2 * slots,
        lambda t, k: own_ref[t, k] if k < slots else other_ref[t, k - slots],
        pick_ref[...],
        window,
    )


def fetch(pairs, sems):
    copies = [pltpu.make_async_copy(a, b, sems.at[i]) for i, (a, b) in enumerate(pairs)]
    for copy in copies:
        copy.start()
    return copies


def begin(
    states_ref, table_ref, out_ref, nodes_ref, own_ref, keep_ref, give_ref, far_ref
):
    peers, slots = nodes_ref.shape
    for k in range(out_ref.shape[1]):
        out_ref[:, k, :] = states_ref[:, k * LANES : (k + 1) * LANES]
    slot = lax.broadcasted_iota(jnp.int32, (1, slots), 1)
    for o in range(peers):
        live = slot < table_ref[2 * peers : 2 * peers + 1, o : o + 1]
        nodes_ref[o : o + 1] = jnp.where(live, table_ref[o : o + 1], -1)
    rows, current = ionic_rows([out_ref[i] for i in range(out_ref.shape[0])])
    for i, row in enumerate(rows):
        out_ref[i] = row
    outgoing = pick_current(current, nodes_ref[...])
    incoming = table_ref[peers : 2 * peers].astype(F32)

    def pair(out, into):
        return jnp.concatenate([outgoing[out : out + 1], incoming[into : into + 1]], axis=0)

    to_next, to_prev = pair(1, 2), pair(2, 1)
    ahead = meets_next()
    own_ref[...] = pair(0, 0)
    keep_ref[...] = jnp.where(ahead, to_next, to_prev)
    give_ref[...] = jnp.where(ahead, to_prev, to_next)
    far_ref[...] = pair(3, 3)


def bring(cols_ref, diag_ref, own_ref, cols_out, diag_out, own_out):
    cols_out[...] = cols_ref[...]
    diag_out[...] = diag_ref[...]
    own_out[...] = own_ref[...]


def bring_tiles(tiles_ref, direction_ref, direction_out):
    direction_out[...] = direction_ref[...]
    del tiles_ref


def choose(own_cols, other_cols, pick_ref):
    slots, tiles = own_cols.shape
    eye = lax.broadcasted_iota(jnp.int32, (tiles, tiles), 0) == lax.broadcasted_iota(
        jnp.int32, (tiles, tiles), 1
    )
    place = lax.broadcasted_iota(jnp.int32, (tiles, pick_ref.shape[1]), 1)
    for k in range(2 * slots):
        row = own_cols[k : k + 1] if k < slots else other_cols[k - slots : k - slots + 1]
        column = jnp.sum(jnp.where(eye, row.astype(F32), 0.0), axis=1, keepdims=True)
        pick_ref[k * tiles : (k + 1) * tiles] = jnp.where(place == column.astype(jnp.int32), 1.0, 0.0)


def first_forcing(
    own_ref, keep_ref, got_ref, near_ref, to_far, far_ref, give_ref, forcing_ref
):
    total = None
    for come, rows in (
        (own_ref[0:1], own_ref[1:2]),
        (far_ref[0:1], to_far[1:2]),
        (near_ref[0:1], keep_ref[1:2]),
        (near_ref[2:3], got_ref[1:2]),
    ):
        part = scatter(come, rows.astype(jnp.int32), forcing_ref.shape[0])
        total = part if total is None else total + part
    forcing_ref[...] = TORSO_COUPLING * total
    give_ref[...] = near_ref[3:4]


def complete(own_ref, near_ref, far_ref, got_ref, nodes_ref, maps_ref):
    ahead = meets_next()
    keep, got = near_ref[1:2], got_ref[...]
    after, before = jnp.where(ahead, keep, got), jnp.where(ahead, got, keep)
    rows = jnp.concatenate([own_ref[1:2], after, before, far_ref[1:2]], axis=0)
    maps_ref[...] = jnp.where(nodes_ref[...] < 0, -1, rows.astype(jnp.int32))


def next_shares(
    states_ref, own_estimate, far_estimate, mine_ref, yours_ref, nodes_ref, maps_ref,
    out_ref, own_ref, keep_ref, give_ref, far_ref,
):
    nodes, maps = nodes_ref[...], maps_ref[...]
    after, before = by_side(*by_partner(mine_ref[...], yours_ref[...]))
    estimates = [own_estimate[...], after, before, far_estimate[...]]
    feedback = feedback_of(estimates, nodes, maps, states_ref.shape[1])
    rows = [states_ref[i] for i in range(states_ref.shape[0])]
    rows[0] = rows[0] + TIME_STEP * FEEDBACK_RATE * feedback
    rows, current = ionic_rows(rows)
    for i, row in enumerate(rows):
        out_ref[i] = row
    outgoing = pick_current(current, nodes)
    spread_current(outgoing, maps, own_ref, keep_ref, give_ref, far_ref)


def window_of(chain, direction, first, second):
    torso = direction.shape[0]
    here = lax.axis_index("dom")
    after, before = by_side(first, second)
    before = jnp.where(here > 0, before[torso - HALO :], 0.0)
    after = jnp.where(here < chain - 1, after[0:HALO], 0.0)
    filler = jnp.zeros((torso - 2 * HALO, LANES), F32)
    return jnp.concatenate([before, direction, after, filler], axis=0)


def sweep_one(
    chain, own_ref, other_ref, pick_ref, mine_ref, yours_ref, forcing_ref, direction_in, diag_ref,
    residual_ref, direction_ref, estimate_ref,
):
    diag = diag_ref[...]
    direction = direction_in[...]
    window = window_of(chain, direction, *by_partner(mine_ref[...], yours_ref[...]))
    moved = product(own_ref, other_ref, pick_ref, window)
    residual = forcing_ref[...] - (diag * direction + moved)
    estimate = direction
    direction = KEEP[0] * direction + PULL[0] * (residual / diag)
    residual_ref[...] = residual
    direction_ref[...] = direction
    estimate_ref[...] = estimate + direction


def sweep_two(
    chain, own_ref, other_ref, pick_ref, mine_ref, yours_ref, direction_in, residual_in,
    estimate_in, diag_ref, estimate_ref,
):
    diag = diag_ref[...]
    direction = direction_in[...]
    window = window_of(chain, direction, *by_partner(mine_ref[...], yours_ref[...]))
    moved = product(own_ref, other_ref, pick_ref, window)
    residual = residual_in[...] - (diag * direction + moved)
    direction = KEEP[1] * direction + PULL[1] * (residual / diag)
    estimate_ref[...] = estimate_in[...] + direction


def pack_border(own_ref, other_ref, pick_ref, diag_ref, out_ref, sems):
    tiles, slots = own_ref.shape[0], own_ref.shape[1]
    ahead = meets_next()
    first = jnp.where(ahead, tiles - HALO, 0)
    copies = []
    for j in range(HALO):
        for i, ref in enumerate((own_ref, other_ref)):
            at = (2 * j + i) * slots
            copy = pltpu.make_async_copy(
                ref.at[first + j], out_ref.at[pl.ds(at, slots)], sems.at[2 * j + i]
            )
            copy.start()
            copies.append(copy)
    last = 2 * HALO * slots
    out_ref[last] = jnp.zeros((LANES, LANES), F32)
    width = pick_ref.shape[1]
    for k in range(2 * slots):
        rows = pick_ref[k * tiles : (k + 1) * tiles]
        out_ref[last, k * HALO : (k + 1) * HALO, 0:width] = jnp.where(
            ahead, rows[tiles - HALO :], rows[:HALO]
        )
    at = 2 * slots * HALO
    out_ref[last, at : at + HALO] = jnp.where(ahead, diag_ref[tiles - HALO :], diag_ref[:HALO])
    for copy in copies:
        copy.wait()


def sweep_both(
    chain, own_ref, other_ref, pick_ref, mine_border, yours_border, mine_ref, yours_ref, mine_two,
    yours_two, forcing_ref, direction_ref, diag_ref, packed_ref, residual_ref,
):
    torso = diag_ref.shape[0]
    slots = 2 * own_ref.shape[1]
    here = lax.axis_index("dom")
    ahead = meets_next()
    diag = diag_ref[...]
    direction = direction_ref[...]
    after, before = by_side(*by_partner(mine_ref[...], yours_ref[...]))
    after = jnp.where(here < chain - 1, after, 0.0)
    before = jnp.where(here > 0, before, 0.0)
    low, high = by_partner(mine_two[...], yours_two[...])
    lower = lax.rem(here, 4) < 2
    beyond_after = jnp.where(here < chain - 2, jnp.where(lower, low, high)[:HALO], 0.0)
    beyond_before = jnp.where(here > 1, jnp.where(lower, high, low)[torso - HALO :], 0.0)
    filler = jnp.zeros((torso - 2 * HALO, LANES), F32)
    window = jnp.concatenate([before[torso - HALO :], direction, after[:HALO], filler], axis=0)
    window_after = jnp.concatenate([direction[torso - HALO :], after, beyond_after, filler], axis=0)
    window_before = jnp.concatenate([beyond_before, before, direction[:HALO], filler], axis=0)

    moved = product(own_ref, other_ref, pick_ref, window)
    residual = forcing_ref[...] - (diag * direction + moved)
    second = KEEP[0] * direction + PULL[0] * (residual / diag)
    rims = []
    for border, is_next in ((mine_border, ahead), (yours_border, jnp.logical_not(ahead))):
        last = HALO * slots
        moved = tile_rows(
            HALO,
            slots,
            lambda t, k, border=border: border[t * slots + k],
            border[last, 0 : slots * HALO, 0 : pick_ref.shape[1]],
            jnp.where(is_next, window_after, window_before),
        )
        rim_diag = border[last, slots * HALO : slots * HALO + HALO]
        rim = jnp.where(is_next, after[:HALO], before[torso - HALO :])
        left = CHEB_THETA * rim_diag * rim - (rim_diag * rim + moved)
        outside = jnp.where(is_next, here == chain - 1, here == 0)
        rims.append(jnp.where(outside, 0.0, KEEP[0] * rim + PULL[0] * (left / rim_diag)))
    rim_after = jnp.where(ahead, rims[0], rims[1])
    rim_before = jnp.where(ahead, rims[1], rims[0])

    window = jnp.concatenate([rim_before, second, rim_after, filler], axis=0)
    moved = product(own_ref, other_ref, pick_ref, window)
    residual = residual - (diag * second + moved)
    third = KEEP[1] * second + PULL[1] * (residual / diag)
    residual_ref[...] = residual
    packed_ref[0:torso] = direction + second + third
    packed_ref[torso:] = third


def finish(
    chain, own_ref, other_ref, pick_ref, packed_ref, far_ref, mine_ref, yours_ref, residual_in,
    diag_ref, states_ref, nodes_ref, maps_ref, out_ref, potential_ref, residual_ref, dense_ref,
):
    torso = residual_ref.shape[0]
    head, tail = slice(0, torso), slice(torso, 2 * torso)
    estimate, direction = packed_ref[head], packed_ref[tail]
    potential_ref[...] = estimate
    first, second = by_partner(mine_ref[...], yours_ref[...])
    after, before = by_side(first[head], second[head])
    feedback = feedback_of(
        [estimate, after, before, far_ref[head]], nodes_ref[...], maps_ref[...],
        states_ref.shape[1],
    )
    dense_ref[...] = states_ref[...]
    dense_ref[0] = states_ref[0] + TIME_STEP * FEEDBACK_RATE * feedback
    for k in range(states_ref.shape[1]):
        out_ref[:, k * LANES : (k + 1) * LANES] = dense_ref[:, k, :]
    window = window_of(chain, direction, first[tail], second[tail])
    moved = product(own_ref, other_ref, pick_ref, window)
    residual_ref[...] = residual_in[...] - (diag_ref[...] * direction + moved)


def on_device(states, send_node, send_count, recv_row, columns, tile_values, diagonal):
    chain = lax.axis_size("dom")
    peers, slots = send_node.shape[1:]
    node_count = states.shape[1]
    heart = node_count // LANES
    torso = diagonal.shape[0] // LANES

    def with_two(value):
        cases = lax.axis_size("case")
        pairs = []
        for case in range(cases):
            for i in range(chain):
                me = (case * chain + i) * 2
                pairs.append((me, (case * chain + (i ^ 2)) * 2))
                if i in (0, 1, chain - 2, chain - 1) and cases % 2 == 0:
                    pairs.append((me + 1, ((case ^ 1) * chain + i) * 2 + 1))
                else:
                    other = (((i - 2) ^ 2) + 2) % chain
                    pairs.append((me + 1, (case * chain + other) * 2 + 1))
        return lax.ppermute(value, ("case", "dom", "sub"), pairs)

    def with_far(value):
        return lax.ppermute(value, "dom", [(i, (i + chain // 2) % chain) for i in range(chain)])

    def with_either(value, closed):
        cases = lax.axis_size("case")
        ends = () if closed or cases % 2 else (0, chain - 1)
        pairs = []
        for case in range(cases):
            for i in range(chain):
                me = (case * chain + i) * 2
                pairs.append((me, (case * chain + (i ^ 1)) * 2))
                if i in ends:
                    pairs.append((me + 1, ((case ^ 1) * chain + i) * 2 + 1))
                else:
                    second = (((i + 1) ^ 1) - 1) % chain
                    pairs.append((me + 1, (case * chain + second) * 2 + 1))
        return lax.ppermute(value, ("case", "dom", "sub"), pairs)

    def from_sibling(value):
        return lax.ppermute(value, "sub", [(0, 1), (1, 0)])

    def shape(*dims, dtype=F32):
        return jax.ShapeDtypeStruct(dims, dtype)

    dense = shape(states.shape[0], heart, LANES)
    field = shape(torso, LANES)
    packed = shape(2 * torso, LANES)
    counts = jnp.pad(send_count, ((0, 0), (0, slots - peers)))
    table = jnp.concatenate([send_node[0], recv_row[0], counts])
    index = shape(peers, slots, dtype=jnp.int32)
    double = shape(2, slots)
    states, nodes, own, keep, give, to_far = call(begin, (dense, index) + (double,) * 4)(
        in_specs=[VMEM] * 2
    )(states, table)
    got = from_sibling(give)
    tile_values, got = lax.optimization_barrier((tile_values, got))
    other_tiles = from_sibling(tile_values)
    far = with_far(to_far)
    near = with_either(jnp.concatenate([keep, got]), True)
    columns, diag, own = call(
        bring, (shape(*columns.shape[::-1], dtype=jnp.int32), field, double)
    )(in_specs=[VMEM] * 3)(columns.T, diagonal.reshape(torso, LANES), own)
    give, forcing = call(first_forcing, (shape(1, slots), field))(in_specs=[VMEM] * 6)(
        own, keep, got, near, to_far, far
    )
    maps = call(complete, index)(in_specs=[VMEM] * 5)(own, near, far, from_sibling(give), nodes)
    other_columns = from_sibling(columns)
    others, other_columns = lax.optimization_barrier((from_sibling(forcing), other_columns))
    forcing = forcing + others
    direction = forcing / (CHEB_THETA * diag)
    halo = with_either(direction, False)
    direction = call(bring_tiles, field)(in_specs=[VMEM] * 2)(tile_values, direction)
    choices = 2 * columns.shape[0] * torso
    pick = call(choose, shape(choices, 2 * torso))(in_specs=[VMEM] * 2)(columns, other_columns)
    halo, direction = lax.optimization_barrier((halo, direction))
    stored = (tile_values, other_tiles, pick)
    residual, direction, estimate = call(functools.partial(sweep_one, chain), (field,) * 3)(
        in_specs=[VMEM] * 8
    )(*stored, halo, from_sibling(halo), forcing, direction, diag)
    halo = with_either(direction, False)
    slots_all = 2 * columns.shape[0]
    early, _ = lax.optimization_barrier((diag, halo))
    border = call(
        pack_border,
        shape(HALO * slots_all + 1, LANES, LANES),
        (pltpu.SemaphoreType.DMA((2 * HALO,)),),
    )(in_specs=[VMEM] * 4)(*stored, early)
    border = with_either(border, False)
    estimate = call(functools.partial(sweep_two, chain), field)(in_specs=[VMEM] * 9)(
        *stored, halo, from_sibling(halo), direction, residual, estimate, diag
    )
    far = with_far(estimate)
    near = with_either(estimate, True)
    states, own, keep, give, away = call(next_shares, (dense,) + (field,) * 4)(
        in_specs=[VMEM] * 7
    )(states, estimate, far, near, from_sibling(near), nodes, maps)

    far = with_far(away)
    near = with_either(keep + from_sibling(give), True)
    forcing = TORSO_COUPLING * (own + far + near)
    forcing = forcing + from_sibling(forcing)
    direction = forcing / (CHEB_THETA * diag)
    halo, two = with_either(direction, False), with_two(direction)
    border, _ = lax.optimization_barrier((border, direction))
    both, residual = call(functools.partial(sweep_both, chain), (packed, field))(
        in_specs=[VMEM] * 12
    )(
        *stored, border, from_sibling(border), halo, from_sibling(halo), two, from_sibling(two),
        forcing, direction, diag,
    )
    far = with_far(both)
    near = with_either(both, True)
    new_states, potential, residual = call(
        functools.partial(finish, chain),
        (shape(*dense.shape[:1], node_count), field, field),
        (pltpu.VMEM(dense.shape, F32),),
    )(in_specs=[VMEM] * 12)(
        *stored, both, far, near, from_sibling(near), residual, diag, states, nodes, maps
    )
    return new_states, potential.reshape(-1), residual.reshape(-1)


def solution(mesh):
    placed = (
        P(None, ("case", "dom", "sub")),
        P(("case", "dom", "sub"), None, None),
        P(("case", "dom", "sub"), None),
        P(("case", "dom", "sub"), None, None),
        P(("case", "dom"), "sub"),
        P(("case", "dom"), "sub", None, None),
        P(("case", "dom")),
    )
    return jax.shard_map(
        on_device,
        mesh=mesh,
        in_specs=placed,
        out_specs=(P(None, ("case", "dom", "sub")), P(("case", "dom")), P(("case", "dom"))),
        check_vma=False,
    )
```

```python
import functools

import jax
import jax.numpy as jnp
from jax import lax
from jax.experimental import pallas as pl
from jax.experimental.pallas import tpu as pltpu
from jax.sharding import PartitionSpec as P

HALO = 2
SWEEPS = 3
LANES = 128

TIME_STEP = 0.02
NERNST_SCALE = 0.267
SODIUM_OUT = 1.4
POTASSIUM_OUT = 0.054
CALCIUM_OUT = 2000.0
COND_SODIUM = 8.0
COND_CALCIUM = 1.0
COND_TRANSIENT = 0.3
COND_RAPID = 0.2
COND_SLOW = 0.3
COND_INWARD = 2.0
COND_RELEASE = 3.0
MEMBRANE_RATE = 2.0
TORSO_COUPLING = 0.5
FEEDBACK_RATE = 5.0
CHEB_THETA = 1.0
CHEB_DELTA = 0.5
GATE_MIDPOINT = [-0.56, -0.7, -0.7, -0.08, -0.2, -0.3, 0.2, -0.28, -0.26, -0.88, 0.05, -0.8, -0.5]
GATE_STEEPNESS = [0.09, -0.07, -0.07, 0.07, -0.07, -0.09, 0.06, -0.05, 0.07, -0.24, 0.14, -0.1, 0.08]
TIME_BASE = [0.02, 0.3, 1.0, 0.1, 2.0, 0.5, 0.1, 1.0, 1.0, 0.5, 1.0, 0.05, 0.2]
TIME_PEAK = [0.1, 1.0, 3.0, 0.5, 5.0, 2.0, 0.3, 5.0, 3.0, 2.0, 4.0, 0.1, 1.0]

SIGMA = CHEB_THETA / CHEB_DELTA
KEEP, PULL = [], []
_ratio = 1.0 / SIGMA
for _ in range(SWEEPS - 1):
    _next = 1.0 / (2.0 * SIGMA - _ratio)
    KEEP.append(_next * _ratio)
    PULL.append(2.0 * _next / CHEB_DELTA)
    _ratio = _next

VMEM = pl.BlockSpec(memory_space=pltpu.VMEM)
F32 = jnp.float32


def call(kernel, outs, scratch=(), limit=16, cost=4_000_000):
    return functools.partial(
        pl.pallas_call,
        kernel,
        out_shape=outs,
        out_specs=jax.tree.map(lambda _: VMEM, outs),
        scratch_shapes=list(scratch),
        compiler_params=pltpu.CompilerParams(vmem_limit_bytes=limit << 20),
        cost_estimate=pl.CostEstimate(flops=cost, bytes_accessed=1 << 18, transcendentals=0),
    )


def ionic_rows(rows):
    voltage, gating = rows[0], rows[1:14]
    sodium, potassium, calcium, reticulum, subspace = rows[14:19]
    moved = []
    for i, gate in enumerate(gating):
        shifted = voltage - GATE_MIDPOINT[i]
        steady = jax.nn.sigmoid(shifted / GATE_STEEPNESS[i])
        time_const = TIME_BASE[i] + TIME_PEAK[i] * jnp.exp(-jnp.square(shifted / 0.3))
        moved.append(steady + (gate - steady) * jnp.exp(-TIME_STEP / time_const))
    g = moved
    sodium_rev = NERNST_SCALE * jnp.log(SODIUM_OUT / sodium)
    potassium_rev = NERNST_SCALE * jnp.log(POTASSIUM_OUT / potassium)
    calcium_rev = 0.5 * NERNST_SCALE * jnp.log(CALCIUM_OUT / subspace)
    sodium_flow = COND_SODIUM * (g[0] * g[0] * g[0]) * g[1] * g[2] * (voltage - sodium_rev)
    calcium_flow = COND_CALCIUM * g[3] * g[4] * g[5] * (voltage - calcium_rev)
    potassium_cond = (
        COND_TRANSIENT * g[6] * g[7]
        + COND_RAPID * g[8] * g[9]
        + COND_SLOW * (g[10] * g[10])
        + COND_INWARD * g[11]
    )
    potassium_flow = potassium_cond * (voltage - potassium_rev)
    current = sodium_flow + calcium_flow + potassium_flow
    release = COND_RELEASE * g[12] * (reticulum - subspace) / (reticulum + subspace)
    sodium = sodium * jnp.exp(-0.5 * TIME_STEP * sodium_flow)
    potassium = potassium * jnp.exp(-0.5 * TIME_STEP * potassium_flow)
    calcium = calcium * jnp.exp(-0.5 * TIME_STEP * calcium_flow)
    subspace = subspace * jnp.exp(TIME_STEP * (release - 0.5 * calcium_flow))
    reticulum = reticulum * jnp.exp(-TIME_STEP * release)
    voltage = voltage - TIME_STEP * MEMBRANE_RATE * current
    return [voltage, *moved, sodium, potassium, calcium, reticulum, subspace], current


def pairs_of(index):
    chunks = [index[:, k : k + LANES] for k in range(0, index.shape[1], LANES)]
    return [jnp.concatenate(chunks[k : k + 2], axis=0) for k in range(0, len(chunks), 2)]


def gather(source, rows, index):
    peers = index.shape[0]
    out = []
    for pair in pairs_of(index):
        high, low = pair >> 7, pair & (LANES - 1)
        total = jnp.zeros(pair.shape, F32)
        for h in range(rows):
            picked = jnp.take_along_axis(source(h), low, axis=1)
            total = jnp.where(high == h, picked, total)
        out += [total[:peers], total[peers:]]
    return jnp.concatenate(out, axis=1)


def three_parts(value):
    first = value.astype(jnp.bfloat16).astype(F32)
    rest = value - first
    second = rest.astype(jnp.bfloat16).astype(F32)
    return first, second, rest - second


def scatter(values, index, rows):
    slots = values.shape[1]
    high, low = index >> 7, index & (LANES - 1)
    mine = lax.broadcasted_iota(jnp.int32, (rows, slots), 0) == high
    left = jnp.concatenate([jnp.where(mine, part, 0.0) for part in three_parts(values)], axis=0)
    spread = lax.broadcasted_iota(jnp.int32, (LANES, slots), 0) == low
    right = jnp.where(spread, 1.0, 0.0).astype(jnp.bfloat16)
    sums = lax.dot_general(
        left.astype(jnp.bfloat16), right, (((1,), (1,)), ((), ())), preferred_element_type=F32
    )
    return sums[:rows] + sums[rows : 2 * rows] + sums[2 * rows :]


def pick_current(current, nodes):
    rows, peers = current.shape[0], nodes.shape[0]
    return gather(
        lambda h: jnp.broadcast_to(current[h : h + 1], (2 * peers, LANES)), rows, nodes
    )


def is_even():
    return lax.rem(lax.axis_index("dom"), 2) == 0


def meets_next():
    return is_even() == (lax.axis_index("sub") == 0)


def by_partner(mine, yours):
    zero = lax.axis_index("sub") == 0
    return jnp.where(zero, mine, yours), jnp.where(zero, yours, mine)


def by_side(first, second):
    even = is_even()
    return jnp.where(even, first, second), jnp.where(even, second, first)


def spread_current(outgoing, maps, own_ref, keep_ref, give_ref, far_ref):
    torso = own_ref.shape[0]
    own, after, before, far = (
        scatter(outgoing[o : o + 1], maps[o : o + 1], torso) for o in range(maps.shape[0])
    )
    ahead = meets_next()
    own_ref[...] = own
    keep_ref[...] = jnp.where(ahead, after, before)
    give_ref[...] = jnp.where(ahead, before, after)
    far_ref[...] = far


def feedback_of(estimates, nodes, maps, heart):
    peers = nodes.shape[0]
    torso = estimates[0].shape[0]

    def source(h):
        rows = [estimate[h : h + 1] for estimate in estimates]
        return jnp.concatenate(rows * 2, axis=0)

    returned = gather(source, torso, maps)
    total = jnp.zeros((heart, LANES), F32)
    for o in range(peers):
        total = total + scatter(returned[o : o + 1], nodes[o : o + 1], heart)
    return total


def product(own_ref, other_ref, pick_ref, window):
    tiles, slots = own_ref.shape[0], own_ref.shape[1]
    parts = jnp.concatenate(three_parts(window), axis=1).astype(jnp.bfloat16)
    picked = jnp.dot(pick_ref[...].astype(jnp.bfloat16), parts, preferred_element_type=F32)
    picked = picked[:, :LANES] + picked[:, LANES : 2 * LANES] + picked[:, 2 * LANES :]
    eye = lax.broadcasted_iota(jnp.int32, (LANES, LANES), 0) == lax.broadcasted_iota(
        jnp.int32, (LANES, LANES), 1
    )
    rows = []
    for t in range(tiles):
        total = None
        for k in range(2 * slots):
            tile = own_ref[t, k] if k < slots else other_ref[t, k - slots]
            term = tile * picked[k * tiles + t : k * tiles + t + 1]
            total = term if total is None else total + term
        column = jnp.sum(total, axis=1, keepdims=True)
        rows.append(jnp.sum(jnp.where(eye, column, 0.0), axis=0, keepdims=True))
    return jnp.concatenate(rows, axis=0)


def fetch(pairs, sems):
    copies = [pltpu.make_async_copy(a, b, sems.at[i]) for i, (a, b) in enumerate(pairs)]
    for copy in copies:
        copy.start()
    return copies


def begin(
    states_ref, table_ref, out_ref, nodes_ref, own_ref, keep_ref, give_ref, far_ref
):
    peers, slots = nodes_ref.shape
    for k in range(out_ref.shape[1]):
        out_ref[:, k, :] = states_ref[:, k * LANES : (k + 1) * LANES]
    slot = lax.broadcasted_iota(jnp.int32, (1, slots), 1)
    for o in range(peers):
        live = slot < table_ref[2 * peers : 2 * peers + 1, o : o + 1]
        nodes_ref[o : o + 1] = jnp.where(live, table_ref[o : o + 1], -1)
    rows, current = ionic_rows([out_ref[i] for i in range(out_ref.shape[0])])
    for i, row in enumerate(rows):
        out_ref[i] = row
    outgoing = pick_current(current, nodes_ref[...])
    incoming = table_ref[peers : 2 * peers].astype(F32)

    def pair(out, into):
        return jnp.concatenate([outgoing[out : out + 1], incoming[into : into + 1]], axis=0)

    to_next, to_prev = pair(1, 2), pair(2, 1)
    ahead = meets_next()
    own_ref[...] = pair(0, 0)
    keep_ref[...] = jnp.where(ahead, to_next, to_prev)
    give_ref[...] = jnp.where(ahead, to_prev, to_next)
    far_ref[...] = pair(3, 3)


def bring(cols_ref, diag_ref, own_ref, cols_out, diag_out, own_out):
    cols_out[...] = cols_ref[...]
    diag_out[...] = diag_ref[...]
    own_out[...] = own_ref[...]


def bring_tiles(tiles_ref, direction_ref, direction_out):
    direction_out[...] = direction_ref[...]
    del tiles_ref


def choose(own_cols, other_cols, pick_ref):
    slots, tiles = own_cols.shape
    eye = lax.broadcasted_iota(jnp.int32, (tiles, tiles), 0) == lax.broadcasted_iota(
        jnp.int32, (tiles, tiles), 1
    )
    place = lax.broadcasted_iota(jnp.int32, (tiles, pick_ref.shape[1]), 1)
    for k in range(2 * slots):
        row = own_cols[k : k + 1] if k < slots else other_cols[k - slots : k - slots + 1]
        column = jnp.sum(jnp.where(eye, row.astype(F32), 0.0), axis=1, keepdims=True)
        pick_ref[k * tiles : (k + 1) * tiles] = jnp.where(place == column.astype(jnp.int32), 1.0, 0.0)


def first_forcing(
    own_ref, keep_ref, got_ref, near_ref, to_far, far_ref, give_ref, forcing_ref
):
    total = None
    for come, rows in (
        (own_ref[0:1], own_ref[1:2]),
        (far_ref[0:1], to_far[1:2]),
        (near_ref[0:1], keep_ref[1:2]),
        (near_ref[2:3], got_ref[1:2]),
    ):
        part = scatter(come, rows.astype(jnp.int32), forcing_ref.shape[0])
        total = part if total is None else total + part
    forcing_ref[...] = TORSO_COUPLING * total
    give_ref[...] = near_ref[3:4]


def complete(own_ref, near_ref, far_ref, got_ref, nodes_ref, maps_ref):
    ahead = meets_next()
    keep, got = near_ref[1:2], got_ref[...]
    after, before = jnp.where(ahead, keep, got), jnp.where(ahead, got, keep)
    rows = jnp.concatenate([own_ref[1:2], after, before, far_ref[1:2]], axis=0)
    maps_ref[...] = jnp.where(nodes_ref[...] < 0, -1, rows.astype(jnp.int32))


def next_shares(
    states_ref, own_estimate, far_estimate, mine_ref, yours_ref, nodes_ref, maps_ref,
    out_ref, own_ref, keep_ref, give_ref, far_ref,
):
    nodes, maps = nodes_ref[...], maps_ref[...]
    after, before = by_side(*by_partner(mine_ref[...], yours_ref[...]))
    estimates = [own_estimate[...], after, before, far_estimate[...]]
    feedback = feedback_of(estimates, nodes, maps, states_ref.shape[1])
    rows = [states_ref[i] for i in range(states_ref.shape[0])]
    rows[0] = rows[0] + TIME_STEP * FEEDBACK_RATE * feedback
    rows, current = ionic_rows(rows)
    for i, row in enumerate(rows):
        out_ref[i] = row
    outgoing = pick_current(current, nodes)
    spread_current(outgoing, maps, own_ref, keep_ref, give_ref, far_ref)


def window_of(chain, direction, first, second):
    torso = direction.shape[0]
    here = lax.axis_index("dom")
    after, before = by_side(first, second)
    before = jnp.where(here > 0, before[torso - HALO :], 0.0)
    after = jnp.where(here < chain - 1, after[0:HALO], 0.0)
    filler = jnp.zeros((torso - 2 * HALO, LANES), F32)
    return jnp.concatenate([before, direction, after, filler], axis=0)


def sweep_one(
    chain, own_ref, other_ref, pick_ref, mine_ref, yours_ref, forcing_ref, direction_in, diag_ref,
    residual_ref, direction_ref, estimate_ref,
):
    diag = diag_ref[...]
    direction = direction_in[...]
    window = window_of(chain, direction, *by_partner(mine_ref[...], yours_ref[...]))
    moved = product(own_ref, other_ref, pick_ref, window)
    residual = forcing_ref[...] - (diag * direction + moved)
    estimate = direction
    direction = KEEP[0] * direction + PULL[0] * (residual / diag)
    residual_ref[...] = residual
    direction_ref[...] = direction
    estimate_ref[...] = estimate + direction


def sweep_two(
    chain, last, own_ref, other_ref, pick_ref, mine_ref, yours_ref, direction_in, residual_in,
    estimate_in, diag_ref, estimate_ref, *refs,
):
    torso = estimate_ref.shape[0]
    diag = diag_ref[...]
    direction = direction_in[...]
    window = window_of(chain, direction, *by_partner(mine_ref[...], yours_ref[...]))
    moved = product(own_ref, other_ref, pick_ref, window)
    residual = residual_in[...] - (diag * direction + moved)
    direction = KEEP[1] * direction + PULL[1] * (residual / diag)
    estimate = estimate_in[...] + direction
    if last:
        residual_ref, = refs
        residual_ref[...] = residual
        estimate_ref[0 : torso // 2] = estimate
        estimate_ref[torso // 2 :] = direction
    else:
        estimate_ref[...] = estimate


def finish(
    chain, own_ref, other_ref, pick_ref, packed_ref, far_ref, mine_ref, yours_ref, residual_in,
    diag_ref, states_ref, nodes_ref, maps_ref, out_ref, potential_ref, residual_ref, dense_ref,
):
    torso = residual_ref.shape[0]
    head, tail = slice(0, torso), slice(torso, 2 * torso)
    estimate, direction = packed_ref[head], packed_ref[tail]
    potential_ref[...] = estimate
    first, second = by_partner(mine_ref[...], yours_ref[...])
    after, before = by_side(first[head], second[head])
    feedback = feedback_of(
        [estimate, after, before, far_ref[head]], nodes_ref[...], maps_ref[...],
        states_ref.shape[1],
    )
    dense_ref[...] = states_ref[...]
    dense_ref[0] = states_ref[0] + TIME_STEP * FEEDBACK_RATE * feedback
    for k in range(states_ref.shape[1]):
        out_ref[:, k * LANES : (k + 1) * LANES] = dense_ref[:, k, :]
    window = window_of(chain, direction, first[tail], second[tail])
    moved = product(own_ref, other_ref, pick_ref, window)
    residual_ref[...] = residual_in[...] - (diag_ref[...] * direction + moved)


def on_device(states, send_node, send_count, recv_row, columns, tile_values, diagonal):
    chain = lax.axis_size("dom")
    peers, slots = send_node.shape[1:]
    node_count = states.shape[1]
    heart = node_count // LANES
    torso = diagonal.shape[0] // LANES

    def with_far(value):
        return lax.ppermute(value, "dom", [(i, (i + chain // 2) % chain) for i in range(chain)])

    def with_either(value, closed):
        cases = lax.axis_size("case")
        ends = () if closed or cases % 2 else (0, chain - 1)
        pairs = []
        for case in range(cases):
            for i in range(chain):
                me = (case * chain + i) * 2
                pairs.append((me, (case * chain + (i ^ 1)) * 2))
                if i in ends:
                    pairs.append((me + 1, ((case ^ 1) * chain + i) * 2 + 1))
                else:
                    second = (((i + 1) ^ 1) - 1) % chain
                    pairs.append((me + 1, (case * chain + second) * 2 + 1))
        return lax.ppermute(value, ("case", "dom", "sub"), pairs)

    def from_sibling(value):
        return lax.ppermute(value, "sub", [(0, 1), (1, 0)])

    def shape(*dims, dtype=F32):
        return jax.ShapeDtypeStruct(dims, dtype)

    dense = shape(states.shape[0], heart, LANES)
    field = shape(torso, LANES)
    packed = shape(2 * torso, LANES)
    counts = jnp.pad(send_count, ((0, 0), (0, slots - peers)))
    table = jnp.concatenate([send_node[0], recv_row[0], counts])
    index = shape(peers, slots, dtype=jnp.int32)
    other_tiles = from_sibling(tile_values)
    double = shape(2, slots)
    states, nodes, own, keep, give, to_far = call(begin, (dense, index) + (double,) * 4)(
        in_specs=[VMEM] * 2
    )(states, table)
    got = from_sibling(give)
    far = with_far(to_far)
    near = with_either(jnp.concatenate([keep, got]), True)
    columns, diag, own = call(
        bring, (shape(*columns.shape[::-1], dtype=jnp.int32), field, double)
    )(in_specs=[VMEM] * 3)(columns.T, diagonal.reshape(torso, LANES), own)
    give, forcing = call(first_forcing, (shape(1, slots), field))(in_specs=[VMEM] * 6)(
        own, keep, got, near, to_far, far
    )
    maps = call(complete, index)(in_specs=[VMEM] * 5)(own, near, far, from_sibling(give), nodes)
    other_columns = from_sibling(columns)
    for time_step in range(2):
        last = time_step == 1
        others = from_sibling(forcing)
        if not last:
            others, other_columns = lax.optimization_barrier((others, other_columns))
        forcing = forcing + others
        direction = forcing / (CHEB_THETA * diag)
        halo = with_either(direction, False)
        if not last:
            choices = 2 * columns.shape[0] * torso
            direction = call(bring_tiles, field)(in_specs=[VMEM] * 2)(tile_values, direction)
            pick = call(choose, shape(choices, 2 * torso))(in_specs=[VMEM] * 2)(
                columns, other_columns
            )
            halo, direction = lax.optimization_barrier((halo, direction))
            stored = (tile_values, other_tiles, pick)
        residual, direction, estimate = call(
            functools.partial(sweep_one, chain), (field,) * 3
        )(in_specs=[VMEM] * 8)(*stored, halo, from_sibling(halo), forcing, direction, diag)
        halo = with_either(direction, False)
        swept = call(
            functools.partial(sweep_two, chain, last), (packed, field) if last else field
        )(in_specs=[VMEM] * 9)(
            *stored, halo, from_sibling(halo), direction, residual, estimate, diag
        )
        estimate, residual = swept if last else (swept, None)
        far = with_far(estimate)
        near = with_either(estimate, True)
        if not last:
            states, own, keep, give, away = call(next_shares, (dense,) + (field,) * 4)(
                in_specs=[VMEM] * 7
            )(states, estimate, far, near, from_sibling(near), nodes, maps)
            far = with_far(away)
            near = with_either(keep + from_sibling(give), True)
            forcing = TORSO_COUPLING * (own + far + near)
    new_states, potential, residual = call(
        functools.partial(finish, chain),
        (shape(*dense.shape[:1], node_count), field, field),
        (pltpu.VMEM(dense.shape, F32),),
    )(in_specs=[VMEM] * 12)(
        *stored, estimate, far, near, from_sibling(near), residual, diag, states, nodes, maps
    )
    return new_states, potential.reshape(-1), residual.reshape(-1)


def solution(mesh):
    placed = (
        P(None, ("case", "dom", "sub")),
        P(("case", "dom", "sub"), None, None),
        P(("case", "dom", "sub"), None),
        P(("case", "dom", "sub"), None, None),
        P(("case", "dom"), "sub"),
        P(("case", "dom"), "sub", None, None),
        P(("case", "dom")),
    )
    return jax.shard_map(
        on_device,
        mesh=mesh,
        in_specs=placed,
        out_specs=(P(None, ("case", "dom", "sub")), P(("case", "dom")), P(("case", "dom"))),
        check_vma=False,
    )
```

```python
import functools

import jax
import jax.numpy as jnp
from jax import lax
from jax.experimental import pallas as pl
from jax.experimental.pallas import tpu as pltpu
from jax.sharding import PartitionSpec as P

HALO = 2
SWEEPS = 3
LANES = 128

TIME_STEP = 0.02
NERNST_SCALE = 0.267
SODIUM_OUT = 1.4
POTASSIUM_OUT = 0.054
CALCIUM_OUT = 2000.0
COND_SODIUM = 8.0
COND_CALCIUM = 1.0
COND_TRANSIENT = 0.3
COND_RAPID = 0.2
COND_SLOW = 0.3
COND_INWARD = 2.0
COND_RELEASE = 3.0
MEMBRANE_RATE = 2.0
TORSO_COUPLING = 0.5
FEEDBACK_RATE = 5.0
CHEB_THETA = 1.0
CHEB_DELTA = 0.5
GATE_MIDPOINT = [-0.56, -0.7, -0.7, -0.08, -0.2, -0.3, 0.2, -0.28, -0.26, -0.88, 0.05, -0.8, -0.5]
GATE_STEEPNESS = [0.09, -0.07, -0.07, 0.07, -0.07, -0.09, 0.06, -0.05, 0.07, -0.24, 0.14, -0.1, 0.08]
TIME_BASE = [0.02, 0.3, 1.0, 0.1, 2.0, 0.5, 0.1, 1.0, 1.0, 0.5, 1.0, 0.05, 0.2]
TIME_PEAK = [0.1, 1.0, 3.0, 0.5, 5.0, 2.0, 0.3, 5.0, 3.0, 2.0, 4.0, 0.1, 1.0]

SIGMA = CHEB_THETA / CHEB_DELTA
KEEP, PULL = [], []
_ratio = 1.0 / SIGMA
for _ in range(SWEEPS - 1):
    _next = 1.0 / (2.0 * SIGMA - _ratio)
    KEEP.append(_next * _ratio)
    PULL.append(2.0 * _next / CHEB_DELTA)
    _ratio = _next

VMEM = pl.BlockSpec(memory_space=pltpu.VMEM)
F32 = jnp.float32


def call(kernel, outs, scratch=(), limit=16, cost=4_000_000):
    return functools.partial(
        pl.pallas_call,
        kernel,
        out_shape=outs,
        out_specs=jax.tree.map(lambda _: VMEM, outs),
        scratch_shapes=list(scratch),
        compiler_params=pltpu.CompilerParams(vmem_limit_bytes=limit << 20),
        cost_estimate=pl.CostEstimate(flops=cost, bytes_accessed=1 << 18, transcendentals=0),
    )


def ionic_rows(rows):
    voltage, gating = rows[0], rows[1:14]
    sodium, potassium, calcium, reticulum, subspace = rows[14:19]
    moved = []
    for i, gate in enumerate(gating):
        shifted = voltage - GATE_MIDPOINT[i]
        steady = jax.nn.sigmoid(shifted / GATE_STEEPNESS[i])
        time_const = TIME_BASE[i] + TIME_PEAK[i] * jnp.exp(-jnp.square(shifted / 0.3))
        moved.append(steady + (gate - steady) * jnp.exp(-TIME_STEP / time_const))
    g = moved
    sodium_rev = NERNST_SCALE * jnp.log(SODIUM_OUT / sodium)
    potassium_rev = NERNST_SCALE * jnp.log(POTASSIUM_OUT / potassium)
    calcium_rev = 0.5 * NERNST_SCALE * jnp.log(CALCIUM_OUT / subspace)
    sodium_flow = COND_SODIUM * (g[0] * g[0] * g[0]) * g[1] * g[2] * (voltage - sodium_rev)
    calcium_flow = COND_CALCIUM * g[3] * g[4] * g[5] * (voltage - calcium_rev)
    potassium_cond = (
        COND_TRANSIENT * g[6] * g[7]
        + COND_RAPID * g[8] * g[9]
        + COND_SLOW * (g[10] * g[10])
        + COND_INWARD * g[11]
    )
    potassium_flow = potassium_cond * (voltage - potassium_rev)
    current = sodium_flow + calcium_flow + potassium_flow
    release = COND_RELEASE * g[12] * (reticulum - subspace) / (reticulum + subspace)
    sodium = sodium * jnp.exp(-0.5 * TIME_STEP * sodium_flow)
    potassium = potassium * jnp.exp(-0.5 * TIME_STEP * potassium_flow)
    calcium = calcium * jnp.exp(-0.5 * TIME_STEP * calcium_flow)
    subspace = subspace * jnp.exp(TIME_STEP * (release - 0.5 * calcium_flow))
    reticulum = reticulum * jnp.exp(-TIME_STEP * release)
    voltage = voltage - TIME_STEP * MEMBRANE_RATE * current
    return [voltage, *moved, sodium, potassium, calcium, reticulum, subspace], current


def pairs_of(index):
    chunks = [index[:, k : k + LANES] for k in range(0, index.shape[1], LANES)]
    return [jnp.concatenate(chunks[k : k + 2], axis=0) for k in range(0, len(chunks), 2)]


def gather(source, rows, index):
    peers = index.shape[0]
    out = []
    for pair in pairs_of(index):
        high, low = pair >> 7, pair & (LANES - 1)
        total = jnp.zeros(pair.shape, F32)
        for h in range(rows):
            picked = jnp.take_along_axis(source(h), low, axis=1)
            total = jnp.where(high == h, picked, total)
        out += [total[:peers], total[peers:]]
    return jnp.concatenate(out, axis=1)


def three_parts(value):
    first = value.astype(jnp.bfloat16).astype(F32)
    rest = value - first
    second = rest.astype(jnp.bfloat16).astype(F32)
    return first, second, rest - second


def scatter(values, index, rows):
    slots = values.shape[1]
    high, low = index >> 7, index & (LANES - 1)
    mine = lax.broadcasted_iota(jnp.int32, (rows, slots), 0) == high
    left = jnp.concatenate([jnp.where(mine, part, 0.0) for part in three_parts(values)], axis=0)
    spread = lax.broadcasted_iota(jnp.int32, (LANES, slots), 0) == low
    right = jnp.where(spread, 1.0, 0.0).astype(jnp.bfloat16)
    sums = lax.dot_general(
        left.astype(jnp.bfloat16), right, (((1,), (1,)), ((), ())), preferred_element_type=F32
    )
    return sums[:rows] + sums[rows : 2 * rows] + sums[2 * rows :]


def pick_current(current, nodes):
    rows, peers = current.shape[0], nodes.shape[0]
    return gather(
        lambda h: jnp.broadcast_to(current[h : h + 1], (2 * peers, LANES)), rows, nodes
    )


def is_even():
    return lax.rem(lax.axis_index("dom"), 2) == 0


def meets_next():
    return is_even() == (lax.axis_index("sub") == 0)


def by_partner(mine, yours):
    zero = lax.axis_index("sub") == 0
    return jnp.where(zero, mine, yours), jnp.where(zero, yours, mine)


def by_side(first, second):
    even = is_even()
    return jnp.where(even, first, second), jnp.where(even, second, first)


def spread_current(outgoing, maps, own_ref, keep_ref, give_ref, far_ref):
    torso = own_ref.shape[0]
    own, after, before, far = (
        scatter(outgoing[o : o + 1], maps[o : o + 1], torso) for o in range(maps.shape[0])
    )
    ahead = meets_next()
    own_ref[...] = own
    keep_ref[...] = jnp.where(ahead, after, before)
    give_ref[...] = jnp.where(ahead, before, after)
    far_ref[...] = far


def feedback_of(estimates, nodes, maps, heart):
    peers = nodes.shape[0]
    torso = estimates[0].shape[0]

    def source(h):
        rows = [estimate[h : h + 1] for estimate in estimates]
        return jnp.concatenate(rows * 2, axis=0)

    returned = gather(source, torso, maps)
    total = jnp.zeros((heart, LANES), F32)
    for o in range(peers):
        total = total + scatter(returned[o : o + 1], nodes[o : o + 1], heart)
    return total


def product(own_ref, other_ref, pick_ref, window):
    tiles, slots = own_ref.shape[0], own_ref.shape[1]
    parts = jnp.concatenate(three_parts(window), axis=1).astype(jnp.bfloat16)
    picked = jnp.dot(pick_ref[...].astype(jnp.bfloat16), parts, preferred_element_type=F32)
    picked = picked[:, :LANES] + picked[:, LANES : 2 * LANES] + picked[:, 2 * LANES :]
    eye = lax.broadcasted_iota(jnp.int32, (LANES, LANES), 0) == lax.broadcasted_iota(
        jnp.int32, (LANES, LANES), 1
    )
    rows = []
    for t in range(tiles):
        total = None
        for k in range(2 * slots):
            tile = own_ref[t, k] if k < slots else other_ref[t, k - slots]
            term = tile * picked[k * tiles + t : k * tiles + t + 1]
            total = term if total is None else total + term
        column = jnp.sum(total, axis=1, keepdims=True)
        rows.append(jnp.sum(jnp.where(eye, column, 0.0), axis=0, keepdims=True))
    return jnp.concatenate(rows, axis=0)


def fetch(pairs, sems):
    copies = [pltpu.make_async_copy(a, b, sems.at[i]) for i, (a, b) in enumerate(pairs)]
    for copy in copies:
        copy.start()
    return copies


def begin(
    states_ref, table_ref, out_ref, nodes_ref, own_ref, keep_ref, give_ref, far_ref
):
    peers, slots = nodes_ref.shape
    for k in range(out_ref.shape[1]):
        out_ref[:, k, :] = states_ref[:, k * LANES : (k + 1) * LANES]
    slot = lax.broadcasted_iota(jnp.int32, (1, slots), 1)
    for o in range(peers):
        live = slot < table_ref[2 * peers : 2 * peers + 1, o : o + 1]
        nodes_ref[o : o + 1] = jnp.where(live, table_ref[o : o + 1], -1)
    rows, current = ionic_rows([out_ref[i] for i in range(out_ref.shape[0])])
    for i, row in enumerate(rows):
        out_ref[i] = row
    outgoing = pick_current(current, nodes_ref[...])
    incoming = table_ref[peers : 2 * peers].astype(F32)

    def pair(out, into):
        return jnp.concatenate([outgoing[out : out + 1], incoming[into : into + 1]], axis=0)

    to_next, to_prev = pair(1, 2), pair(2, 1)
    ahead = meets_next()
    own_ref[...] = pair(0, 0)
    keep_ref[...] = jnp.where(ahead, to_next, to_prev)
    give_ref[...] = jnp.where(ahead, to_prev, to_next)
    far_ref[...] = jnp.zeros_like(far_ref)
    far_ref[0:2] = pair(3, 3)


def bring(cols_ref, diag_ref, own_ref, cols_out, diag_out, own_out):
    cols_out[...] = cols_ref[...]
    diag_out[...] = diag_ref[...]
    own_out[...] = own_ref[...]


def bring_tiles(tiles_ref, direction_ref, direction_out):
    direction_out[...] = direction_ref[...]
    del tiles_ref


def choose(own_cols, other_cols, pick_ref):
    slots, tiles = own_cols.shape
    eye = lax.broadcasted_iota(jnp.int32, (tiles, tiles), 0) == lax.broadcasted_iota(
        jnp.int32, (tiles, tiles), 1
    )
    place = lax.broadcasted_iota(jnp.int32, (tiles, pick_ref.shape[1]), 1)
    for k in range(2 * slots):
        row = own_cols[k : k + 1] if k < slots else other_cols[k - slots : k - slots + 1]
        column = jnp.sum(jnp.where(eye, row.astype(F32), 0.0), axis=1, keepdims=True)
        pick_ref[k * tiles : (k + 1) * tiles] = jnp.where(place == column.astype(jnp.int32), 1.0, 0.0)


def first_forcing(
    own_ref, far_ref, near_ref, keep_ref, got_ref, to_far, give_ref, forcing_ref
):
    total = None
    for come, rows in (
        (own_ref[0:1], own_ref[1:2]),
        (far_ref[0:1], to_far[1:2]),
        (near_ref[0:1], keep_ref[1:2]),
        (near_ref[2:3], got_ref[1:2]),
    ):
        part = scatter(come, rows.astype(jnp.int32), forcing_ref.shape[0])
        total = part if total is None else total + part
    forcing_ref[...] = TORSO_COUPLING * total
    give_ref[...] = near_ref[3:4]


def complete(own_ref, near_ref, far_ref, got_ref, nodes_ref, maps_ref):
    ahead = meets_next()
    keep, got = near_ref[1:2], got_ref[...]
    after, before = jnp.where(ahead, keep, got), jnp.where(ahead, got, keep)
    rows = jnp.concatenate([own_ref[1:2], after, before, far_ref[1:2]], axis=0)
    maps_ref[...] = jnp.where(nodes_ref[...] < 0, -1, rows.astype(jnp.int32))


def next_shares(
    states_ref, own_estimate, far_estimate, mine_ref, yours_ref, nodes_ref, maps_ref,
    out_ref, own_ref, keep_ref, give_ref, far_ref,
):
    nodes, maps = nodes_ref[...], maps_ref[...]
    after, before = by_side(*by_partner(mine_ref[...], yours_ref[...]))
    estimates = [own_estimate[...], after, before, far_estimate[...]]
    feedback = feedback_of(estimates, nodes, maps, states_ref.shape[1])
    rows = [states_ref[i] for i in range(states_ref.shape[0])]
    rows[0] = rows[0] + TIME_STEP * FEEDBACK_RATE * feedback
    rows, current = ionic_rows(rows)
    for i, row in enumerate(rows):
        out_ref[i] = row
    outgoing = pick_current(current, nodes)
    spread_current(outgoing, maps, own_ref, keep_ref, give_ref, far_ref)


def window_of(chain, direction, first, second):
    torso = direction.shape[0]
    here = lax.axis_index("dom")
    after, before = by_side(first, second)
    before = jnp.where(here > 0, before[torso - HALO :], 0.0)
    after = jnp.where(here < chain - 1, after[0:HALO], 0.0)
    filler = jnp.zeros((torso - 2 * HALO, LANES), F32)
    return jnp.concatenate([before, direction, after, filler], axis=0)


def sweep_one(
    chain, own_ref, other_ref, pick_ref, mine_ref, yours_ref, forcing_ref, direction_in, diag_ref,
    residual_ref, direction_ref, estimate_ref,
):
    diag = diag_ref[...]
    direction = direction_in[...]
    window = window_of(chain, direction, *by_partner(mine_ref[...], yours_ref[...]))
    moved = product(own_ref, other_ref, pick_ref, window)
    residual = forcing_ref[...] - (diag * direction + moved)
    estimate = direction
    direction = KEEP[0] * direction + PULL[0] * (residual / diag)
    residual_ref[...] = residual
    direction_ref[...] = direction
    estimate_ref[...] = estimate + direction


def sweep_two(
    chain, last, own_ref, other_ref, pick_ref, mine_ref, yours_ref, direction_in, residual_in,
    estimate_in, diag_ref, estimate_ref, *refs,
):
    torso = estimate_ref.shape[0]
    diag = diag_ref[...]
    direction = direction_in[...]
    window = window_of(chain, direction, *by_partner(mine_ref[...], yours_ref[...]))
    moved = product(own_ref, other_ref, pick_ref, window)
    residual = residual_in[...] - (diag * direction + moved)
    direction = KEEP[1] * direction + PULL[1] * (residual / diag)
    estimate = estimate_in[...] + direction
    if last:
        residual_ref, = refs
        residual_ref[...] = residual
        estimate_ref[0 : torso // 2] = estimate
        estimate_ref[torso // 2 :] = direction
    else:
        estimate_ref[...] = estimate


def finish(
    chain, own_ref, other_ref, pick_ref, packed_ref, far_ref, mine_ref, yours_ref, residual_in,
    diag_ref, states_ref, nodes_ref, maps_ref, out_ref, potential_ref, residual_ref, dense_ref,
):
    torso = residual_ref.shape[0]
    head, tail = slice(0, torso), slice(torso, 2 * torso)
    estimate, direction = packed_ref[head], packed_ref[tail]
    potential_ref[...] = estimate
    first, second = by_partner(mine_ref[...], yours_ref[...])
    after, before = by_side(first[head], second[head])
    feedback = feedback_of(
        [estimate, after, before, far_ref[head]], nodes_ref[...], maps_ref[...],
        states_ref.shape[1],
    )
    dense_ref[...] = states_ref[...]
    dense_ref[0] = states_ref[0] + TIME_STEP * FEEDBACK_RATE * feedback
    for k in range(states_ref.shape[1]):
        out_ref[:, k * LANES : (k + 1) * LANES] = dense_ref[:, k, :]
    window = window_of(chain, direction, first[tail], second[tail])
    moved = product(own_ref, other_ref, pick_ref, window)
    residual_ref[...] = residual_in[...] - (diag_ref[...] * direction + moved)


def on_device(states, send_node, send_count, recv_row, columns, tile_values, diagonal):
    chain = lax.axis_size("dom")
    peers, slots = send_node.shape[1:]
    node_count = states.shape[1]
    heart = node_count // LANES
    torso = diagonal.shape[0] // LANES

    def with_far(value):
        return lax.ppermute(value, "dom", [(i, (i + chain // 2) % chain) for i in range(chain)])

    def with_either(value, closed):
        cases = lax.axis_size("case")
        ends = () if closed or cases % 2 else (0, chain - 1)
        pairs = []
        for case in range(cases):
            for i in range(chain):
                me = (case * chain + i) * 2
                pairs.append((me, (case * chain + (i ^ 1)) * 2))
                if i in ends:
                    pairs.append((me + 1, ((case ^ 1) * chain + i) * 2 + 1))
                else:
                    second = (((i + 1) ^ 1) - 1) % chain
                    pairs.append((me + 1, (case * chain + second) * 2 + 1))
        return lax.ppermute(value, ("case", "dom", "sub"), pairs)

    def from_sibling(value):
        return lax.ppermute(value, "sub", [(0, 1), (1, 0)])

    def shape(*dims, dtype=F32):
        return jax.ShapeDtypeStruct(dims, dtype)

    dense = shape(states.shape[0], heart, LANES)
    field = shape(torso, LANES)
    packed = shape(2 * torso, LANES)
    counts = jnp.pad(send_count, ((0, 0), (0, slots - peers)))
    table = jnp.concatenate([send_node[0], recv_row[0], counts])
    index = shape(peers, slots, dtype=jnp.int32)
    other_tiles = from_sibling(tile_values)
    double = shape(2, slots)
    states, nodes, own, keep, give, to_far = call(begin, (dense, index) + (double,) * 3 + (shape(8, slots),))(
        in_specs=[VMEM] * 2
    )(states, table)
    got = from_sibling(give)
    far = with_far(to_far)
    near = with_either(jnp.concatenate([keep, got]), True)
    columns, diag, own = call(
        bring, (shape(*columns.shape[::-1], dtype=jnp.int32), field, double)
    )(in_specs=[VMEM] * 3)(columns.T, diagonal.reshape(torso, LANES), own)
    give, forcing = call(first_forcing, (shape(1, slots), field))(in_specs=[VMEM] * 6)(
        own, far, near, keep, got, to_far
    )
    maps = call(complete, index)(in_specs=[VMEM] * 5)(own, near, far, from_sibling(give), nodes)
    other_columns = from_sibling(columns)
    for time_step in range(2):
        last = time_step == 1
        others = from_sibling(forcing)
        if not last:
            others, other_columns = lax.optimization_barrier((others, other_columns))
        forcing = forcing + others
        direction = forcing / (CHEB_THETA * diag)
        halo = with_either(direction, False)
        if not last:
            choices = 2 * columns.shape[0] * torso
            direction = call(bring_tiles, field)(in_specs=[VMEM] * 2)(tile_values, direction)
            pick = call(choose, shape(choices, 2 * torso))(in_specs=[VMEM] * 2)(
                columns, other_columns
            )
            halo, direction = lax.optimization_barrier((halo, direction))
            stored = (tile_values, other_tiles, pick)
        residual, direction, estimate = call(
            functools.partial(sweep_one, chain), (field,) * 3
        )(in_specs=[VMEM] * 8)(*stored, halo, from_sibling(halo), forcing, direction, diag)
        halo = with_either(direction, False)
        swept = call(
            functools.partial(sweep_two, chain, last), (packed, field) if last else field
        )(in_specs=[VMEM] * 9)(
            *stored, halo, from_sibling(halo), direction, residual, estimate, diag
        )
        estimate, residual = swept if last else (swept, None)
        far = with_far(estimate)
        near = with_either(estimate, True)
        if not last:
            states, own, keep, give, away = call(next_shares, (dense,) + (field,) * 4)(
                in_specs=[VMEM] * 7
            )(states, estimate, far, near, from_sibling(near), nodes, maps)
            far = with_far(away)
            near = with_either(keep + from_sibling(give), True)
            forcing = TORSO_COUPLING * (own + far + near)
    new_states, potential, residual = call(
        functools.partial(finish, chain),
        (shape(*dense.shape[:1], node_count), field, field),
        (pltpu.VMEM(dense.shape, F32),),
    )(in_specs=[VMEM] * 12)(
        *stored, estimate, far, near, from_sibling(near), residual, diag, states, nodes, maps
    )
    return new_states, potential.reshape(-1), residual.reshape(-1)


def solution(mesh):
    placed = (
        P(None, ("case", "dom", "sub")),
        P(("case", "dom", "sub"), None, None),
        P(("case", "dom", "sub"), None),
        P(("case", "dom", "sub"), None, None),
        P(("case", "dom"), "sub"),
        P(("case", "dom"), "sub", None, None),
        P(("case", "dom")),
    )
    return jax.shard_map(
        on_device,
        mesh=mesh,
        in_specs=placed,
        out_specs=(P(None, ("case", "dom", "sub")), P(("case", "dom")), P(("case", "dom"))),
        check_vma=False,
    )
```

```python
import functools

import jax
import jax.numpy as jnp
from jax import lax
from jax.experimental import pallas as pl
from jax.experimental.pallas import tpu as pltpu
from jax.sharding import PartitionSpec as P

HALO = 2
SWEEPS = 3
LANES = 128

TIME_STEP = 0.02
NERNST_SCALE = 0.267
SODIUM_OUT = 1.4
POTASSIUM_OUT = 0.054
CALCIUM_OUT = 2000.0
COND_SODIUM = 8.0
COND_CALCIUM = 1.0
COND_TRANSIENT = 0.3
COND_RAPID = 0.2
COND_SLOW = 0.3
COND_INWARD = 2.0
COND_RELEASE = 3.0
MEMBRANE_RATE = 2.0
TORSO_COUPLING = 0.5
FEEDBACK_RATE = 5.0
CHEB_THETA = 1.0
CHEB_DELTA = 0.5
GATE_MIDPOINT = [-0.56, -0.7, -0.7, -0.08, -0.2, -0.3, 0.2, -0.28, -0.26, -0.88, 0.05, -0.8, -0.5]
GATE_STEEPNESS = [0.09, -0.07, -0.07, 0.07, -0.07, -0.09, 0.06, -0.05, 0.07, -0.24, 0.14, -0.1, 0.08]
TIME_BASE = [0.02, 0.3, 1.0, 0.1, 2.0, 0.5, 0.1, 1.0, 1.0, 0.5, 1.0, 0.05, 0.2]
TIME_PEAK = [0.1, 1.0, 3.0, 0.5, 5.0, 2.0, 0.3, 5.0, 3.0, 2.0, 4.0, 0.1, 1.0]

SIGMA = CHEB_THETA / CHEB_DELTA
KEEP, PULL = [], []
_ratio = 1.0 / SIGMA
for _ in range(SWEEPS - 1):
    _next = 1.0 / (2.0 * SIGMA - _ratio)
    KEEP.append(_next * _ratio)
    PULL.append(2.0 * _next / CHEB_DELTA)
    _ratio = _next

VMEM = pl.BlockSpec(memory_space=pltpu.VMEM)
F32 = jnp.float32


def call(kernel, outs, scratch=(), limit=16, cost=4_000_000):
    return functools.partial(
        pl.pallas_call,
        kernel,
        out_shape=outs,
        out_specs=jax.tree.map(lambda _: VMEM, outs),
        scratch_shapes=list(scratch),
        compiler_params=pltpu.CompilerParams(vmem_limit_bytes=limit << 20),
        cost_estimate=pl.CostEstimate(flops=cost, bytes_accessed=1 << 18, transcendentals=0),
    )


def ionic_rows(rows):
    voltage, gating = rows[0], rows[1:14]
    sodium, potassium, calcium, reticulum, subspace = rows[14:19]
    moved = []
    for i, gate in enumerate(gating):
        shifted = voltage - GATE_MIDPOINT[i]
        steady = jax.nn.sigmoid(shifted / GATE_STEEPNESS[i])
        time_const = TIME_BASE[i] + TIME_PEAK[i] * jnp.exp(-jnp.square(shifted / 0.3))
        moved.append(steady + (gate - steady) * jnp.exp(-TIME_STEP / time_const))
    g = moved
    sodium_rev = NERNST_SCALE * jnp.log(SODIUM_OUT / sodium)
    potassium_rev = NERNST_SCALE * jnp.log(POTASSIUM_OUT / potassium)
    calcium_rev = 0.5 * NERNST_SCALE * jnp.log(CALCIUM_OUT / subspace)
    sodium_flow = COND_SODIUM * (g[0] * g[0] * g[0]) * g[1] * g[2] * (voltage - sodium_rev)
    calcium_flow = COND_CALCIUM * g[3] * g[4] * g[5] * (voltage - calcium_rev)
    potassium_cond = (
        COND_TRANSIENT * g[6] * g[7]
        + COND_RAPID * g[8] * g[9]
        + COND_SLOW * (g[10] * g[10])
        + COND_INWARD * g[11]
    )
    potassium_flow = potassium_cond * (voltage - potassium_rev)
    current = sodium_flow + calcium_flow + potassium_flow
    release = COND_RELEASE * g[12] * (reticulum - subspace) / (reticulum + subspace)
    sodium = sodium * jnp.exp(-0.5 * TIME_STEP * sodium_flow)
    potassium = potassium * jnp.exp(-0.5 * TIME_STEP * potassium_flow)
    calcium = calcium * jnp.exp(-0.5 * TIME_STEP * calcium_flow)
    subspace = subspace * jnp.exp(TIME_STEP * (release - 0.5 * calcium_flow))
    reticulum = reticulum * jnp.exp(-TIME_STEP * release)
    voltage = voltage - TIME_STEP * MEMBRANE_RATE * current
    return [voltage, *moved, sodium, potassium, calcium, reticulum, subspace], current


def pairs_of(index):
    chunks = [index[:, k : k + LANES] for k in range(0, index.shape[1], LANES)]
    return [jnp.concatenate(chunks[k : k + 2], axis=0) for k in range(0, len(chunks), 2)]


def gather(source, rows, index):
    peers = index.shape[0]
    out = []
    for pair in pairs_of(index):
        high, low = pair >> 7, pair & (LANES - 1)
        total = jnp.zeros(pair.shape, F32)
        for h in range(rows):
            picked = jnp.take_along_axis(source(h), low, axis=1)
            total = jnp.where(high == h, picked, total)
        out += [total[:peers], total[peers:]]
    return jnp.concatenate(out, axis=1)


def three_parts(value):
    first = value.astype(jnp.bfloat16).astype(F32)
    rest = value - first
    second = rest.astype(jnp.bfloat16).astype(F32)
    return first, second, rest - second


def low_table(index):
    spread = lax.broadcasted_iota(jnp.int32, (LANES, index.shape[1]), 0) == (index & (LANES - 1))
    return jnp.where(spread, 1.0, 0.0).astype(jnp.bfloat16)


def scatter(values, index, rows, table=None):
    slots = values.shape[1]
    high = index >> 7
    mine = lax.broadcasted_iota(jnp.int32, (rows, slots), 0) == high
    left = jnp.concatenate([jnp.where(mine, part, 0.0) for part in three_parts(values)], axis=0)
    right = low_table(index) if table is None else table
    sums = lax.dot_general(
        left.astype(jnp.bfloat16), right, (((1,), (1,)), ((), ())), preferred_element_type=F32
    )
    return sums[:rows] + sums[rows : 2 * rows] + sums[2 * rows :]


def pick_current(current, nodes):
    rows, peers = current.shape[0], nodes.shape[0]
    return gather(
        lambda h: jnp.broadcast_to(current[h : h + 1], (2 * peers, LANES)), rows, nodes
    )


def is_even():
    return lax.rem(lax.axis_index("dom"), 2) == 0


def meets_next():
    return is_even() == (lax.axis_index("sub") == 0)


def by_partner(mine, yours):
    zero = lax.axis_index("sub") == 0
    return jnp.where(zero, mine, yours), jnp.where(zero, yours, mine)


def by_side(first, second):
    even = is_even()
    return jnp.where(even, first, second), jnp.where(even, second, first)


def spread_current(outgoing, maps, maps_low, own_ref, keep_ref, give_ref, far_ref):
    torso = own_ref.shape[0]
    own, after, before, far = (
        scatter(outgoing[o : o + 1], maps[o : o + 1], torso, maps_low[o]) for o in range(maps.shape[0])
    )
    ahead = meets_next()
    own_ref[...] = own
    keep_ref[...] = jnp.where(ahead, after, before)
    give_ref[...] = jnp.where(ahead, before, after)
    far_ref[...] = far


def feedback_of(estimates, nodes, nodes_low, maps, heart):
    peers = nodes.shape[0]
    torso = estimates[0].shape[0]

    def source(h):
        rows = [estimate[h : h + 1] for estimate in estimates]
        return jnp.concatenate(rows * 2, axis=0)

    returned = gather(source, torso, maps)
    total = jnp.zeros((heart, LANES), F32)
    for o in range(peers):
        total = total + scatter(returned[o : o + 1], nodes[o : o + 1], heart, nodes_low[o])
    return total


def product(own_ref, other_ref, pick_ref, window):
    tiles, slots = own_ref.shape[0], own_ref.shape[1]
    parts = jnp.concatenate(three_parts(window), axis=1).astype(jnp.bfloat16)
    picked = jnp.dot(pick_ref[...].astype(jnp.bfloat16), parts, preferred_element_type=F32)
    picked = picked[:, :LANES] + picked[:, LANES : 2 * LANES] + picked[:, 2 * LANES :]
    eye = lax.broadcasted_iota(jnp.int32, (LANES, LANES), 0) == lax.broadcasted_iota(
        jnp.int32, (LANES, LANES), 1
    )
    rows = []
    for t in range(tiles):
        total = None
        for k in range(2 * slots):
            tile = own_ref[t, k] if k < slots else other_ref[t, k - slots]
            term = tile * picked[k * tiles + t : k * tiles + t + 1]
            total = term if total is None else total + term
        column = jnp.sum(total, axis=1, keepdims=True)
        rows.append(jnp.sum(jnp.where(eye, column, 0.0), axis=0, keepdims=True))
    return jnp.concatenate(rows, axis=0)


def fetch(pairs, sems):
    copies = [pltpu.make_async_copy(a, b, sems.at[i]) for i, (a, b) in enumerate(pairs)]
    for copy in copies:
        copy.start()
    return copies


def begin(
    states_ref, table_ref, out_ref, nodes_ref, own_ref, keep_ref, give_ref, far_ref
):
    peers, slots = nodes_ref.shape
    for k in range(out_ref.shape[1]):
        out_ref[:, k, :] = states_ref[:, k * LANES : (k + 1) * LANES]
    slot = lax.broadcasted_iota(jnp.int32, (1, slots), 1)
    for o in range(peers):
        live = slot < table_ref[2 * peers : 2 * peers + 1, o : o + 1]
        nodes_ref[o : o + 1] = jnp.where(live, table_ref[o : o + 1], -1)
    rows, current = ionic_rows([out_ref[i] for i in range(out_ref.shape[0])])
    for i, row in enumerate(rows):
        out_ref[i] = row
    outgoing = pick_current(current, nodes_ref[...])
    incoming = table_ref[peers : 2 * peers].astype(F32)

    def pair(out, into):
        return jnp.concatenate([outgoing[out : out + 1], incoming[into : into + 1]], axis=0)

    to_next, to_prev = pair(1, 2), pair(2, 1)
    ahead = meets_next()
    own_ref[...] = pair(0, 0)
    keep_ref[...] = jnp.where(ahead, to_next, to_prev)
    give_ref[...] = jnp.where(ahead, to_prev, to_next)
    far_ref[...] = jnp.zeros_like(far_ref)
    far_ref[0:2] = pair(3, 3)


def bring(cols_ref, diag_ref, own_ref, cols_out, diag_out, own_out):
    cols_out[...] = cols_ref[...]
    diag_out[...] = diag_ref[...]
    own_out[...] = own_ref[...]


def bring_tiles(tiles_ref, direction_ref, direction_out):
    direction_out[...] = direction_ref[...]
    del tiles_ref


def choose(own_cols, other_cols, pick_ref):
    slots, tiles = own_cols.shape
    eye = lax.broadcasted_iota(jnp.int32, (tiles, tiles), 0) == lax.broadcasted_iota(
        jnp.int32, (tiles, tiles), 1
    )
    place = lax.broadcasted_iota(jnp.int32, (tiles, pick_ref.shape[1]), 1)
    for k in range(2 * slots):
        row = own_cols[k : k + 1] if k < slots else other_cols[k - slots : k - slots + 1]
        column = jnp.sum(jnp.where(eye, row.astype(F32), 0.0), axis=1, keepdims=True)
        pick_ref[k * tiles : (k + 1) * tiles] = jnp.where(place == column.astype(jnp.int32), 1.0, 0.0)


def first_forcing(
    own_ref, far_ref, near_ref, keep_ref, got_ref, to_far, give_ref, forcing_ref
):
    total = None
    for come, rows in (
        (own_ref[0:1], own_ref[1:2]),
        (far_ref[0:1], to_far[1:2]),
        (near_ref[0:1], keep_ref[1:2]),
        (near_ref[2:3], got_ref[1:2]),
    ):
        part = scatter(come, rows.astype(jnp.int32), forcing_ref.shape[0])
        total = part if total is None else total + part
    forcing_ref[...] = TORSO_COUPLING * total
    give_ref[...] = near_ref[3:4]


def complete(own_ref, near_ref, far_ref, got_ref, nodes_ref, maps_ref):
    ahead = meets_next()
    keep, got = near_ref[1:2], got_ref[...]
    after, before = jnp.where(ahead, keep, got), jnp.where(ahead, got, keep)
    rows = jnp.concatenate([own_ref[1:2], after, before, far_ref[1:2]], axis=0)
    maps_ref[...] = jnp.where(nodes_ref[...] < 0, -1, rows.astype(jnp.int32))


def spell(index_ref, low_ref):
    for o in range(index_ref.shape[0]):
        low_ref[o] = low_table(index_ref[o : o + 1])


def next_shares(
    states_ref, own_estimate, far_estimate, mine_ref, yours_ref, nodes_ref, maps_ref,
    nodes_low, maps_low, out_ref, own_ref, keep_ref, give_ref, far_ref,
):
    nodes, maps = nodes_ref[...], maps_ref[...]
    after, before = by_side(*by_partner(mine_ref[...], yours_ref[...]))
    estimates = [own_estimate[...], after, before, far_estimate[...]]
    feedback = feedback_of(estimates, nodes, nodes_low, maps, states_ref.shape[1])
    rows = [states_ref[i] for i in range(states_ref.shape[0])]
    rows[0] = rows[0] + TIME_STEP * FEEDBACK_RATE * feedback
    rows, current = ionic_rows(rows)
    for i, row in enumerate(rows):
        out_ref[i] = row
    outgoing = pick_current(current, nodes)
    spread_current(outgoing, maps, maps_low, own_ref, keep_ref, give_ref, far_ref)


def window_of(chain, direction, first, second):
    torso = direction.shape[0]
    here = lax.axis_index("dom")
    after, before = by_side(first, second)
    before = jnp.where(here > 0, before[torso - HALO :], 0.0)
    after = jnp.where(here < chain - 1, after[0:HALO], 0.0)
    filler = jnp.zeros((torso - 2 * HALO, LANES), F32)
    return jnp.concatenate([before, direction, after, filler], axis=0)


def sweep_one(
    chain, own_ref, other_ref, pick_ref, mine_ref, yours_ref, forcing_ref, direction_in, diag_ref,
    residual_ref, direction_ref, estimate_ref,
):
    diag = diag_ref[...]
    direction = direction_in[...]
    window = window_of(chain, direction, *by_partner(mine_ref[...], yours_ref[...]))
    moved = product(own_ref, other_ref, pick_ref, window)
    residual = forcing_ref[...] - (diag * direction + moved)
    estimate = direction
    direction = KEEP[0] * direction + PULL[0] * (residual / diag)
    residual_ref[...] = residual
    direction_ref[...] = direction
    estimate_ref[...] = estimate + direction


def sweep_two(
    chain, last, own_ref, other_ref, pick_ref, mine_ref, yours_ref, direction_in, residual_in,
    estimate_in, diag_ref, estimate_ref, *refs,
):
    torso = estimate_ref.shape[0]
    diag = diag_ref[...]
    direction = direction_in[...]
    window = window_of(chain, direction, *by_partner(mine_ref[...], yours_ref[...]))
    moved = product(own_ref, other_ref, pick_ref, window)
    residual = residual_in[...] - (diag * direction + moved)
    direction = KEEP[1] * direction + PULL[1] * (residual / diag)
    estimate = estimate_in[...] + direction
    if last:
        residual_ref, = refs
        residual_ref[...] = residual
        estimate_ref[0 : torso // 2] = estimate
        estimate_ref[torso // 2 :] = direction
    else:
        estimate_ref[...] = estimate


def finish(
    chain, own_ref, other_ref, pick_ref, packed_ref, far_ref, mine_ref, yours_ref, residual_in,
    diag_ref, states_ref, nodes_ref, nodes_low, maps_ref, out_ref, potential_ref, residual_ref, dense_ref,
):
    torso = residual_ref.shape[0]
    head, tail = slice(0, torso), slice(torso, 2 * torso)
    estimate, direction = packed_ref[head], packed_ref[tail]
    potential_ref[...] = estimate
    first, second = by_partner(mine_ref[...], yours_ref[...])
    after, before = by_side(first[head], second[head])
    feedback = feedback_of(
        [estimate, after, before, far_ref[head]], nodes_ref[...], nodes_low, maps_ref[...],
        states_ref.shape[1],
    )
    dense_ref[...] = states_ref[...]
    dense_ref[0] = states_ref[0] + TIME_STEP * FEEDBACK_RATE * feedback
    for k in range(states_ref.shape[1]):
        out_ref[:, k * LANES : (k + 1) * LANES] = dense_ref[:, k, :]
    window = window_of(chain, direction, first[tail], second[tail])
    moved = product(own_ref, other_ref, pick_ref, window)
    residual_ref[...] = residual_in[...] - (diag_ref[...] * direction + moved)


def on_device(states, send_node, send_count, recv_row, columns, tile_values, diagonal):
    chain = lax.axis_size("dom")
    peers, slots = send_node.shape[1:]
    node_count = states.shape[1]
    heart = node_count // LANES
    torso = diagonal.shape[0] // LANES

    def with_far(value):
        return lax.ppermute(value, "dom", [(i, (i + chain // 2) % chain) for i in range(chain)])

    def with_either(value, closed):
        cases = lax.axis_size("case")
        ends = () if closed or cases % 2 else (0, chain - 1)
        pairs = []
        for case in range(cases):
            for i in range(chain):
                me = (case * chain + i) * 2
                pairs.append((me, (case * chain + (i ^ 1)) * 2))
                if i in ends:
                    pairs.append((me + 1, ((case ^ 1) * chain + i) * 2 + 1))
                else:
                    second = (((i + 1) ^ 1) - 1) % chain
                    pairs.append((me + 1, (case * chain + second) * 2 + 1))
        return lax.ppermute(value, ("case", "dom", "sub"), pairs)

    def from_sibling(value):
        return lax.ppermute(value, "sub", [(0, 1), (1, 0)])

    def shape(*dims, dtype=F32):
        return jax.ShapeDtypeStruct(dims, dtype)

    dense = shape(states.shape[0], heart, LANES)
    field = shape(torso, LANES)
    packed = shape(2 * torso, LANES)
    counts = jnp.pad(send_count, ((0, 0), (0, slots - peers)))
    table = jnp.concatenate([send_node[0], recv_row[0], counts])
    index = shape(peers, slots, dtype=jnp.int32)
    other_tiles = from_sibling(tile_values)
    double = shape(2, slots)
    states, nodes, own, keep, give, to_far = call(begin, (dense, index) + (double,) * 3 + (shape(8, slots),))(
        in_specs=[VMEM] * 2
    )(states, table)
    got = from_sibling(give)
    far = with_far(to_far)
    near = with_either(jnp.concatenate([keep, got]), True)
    columns, diag, own = call(
        bring, (shape(*columns.shape[::-1], dtype=jnp.int32), field, double)
    )(in_specs=[VMEM] * 3)(columns.T, diagonal.reshape(torso, LANES), own)
    give, forcing = call(first_forcing, (shape(1, slots), field))(in_specs=[VMEM] * 6)(
        own, far, near, keep, got, to_far
    )
    maps = call(complete, index)(in_specs=[VMEM] * 5)(own, near, far, from_sibling(give), nodes)
    other_columns = from_sibling(columns)
    low = shape(peers, LANES, slots, dtype=jnp.bfloat16)
    nodes_low = call(spell, low)(in_specs=[VMEM])(nodes)
    maps_low = call(spell, low)(in_specs=[VMEM])(maps)
    for time_step in range(2):
        last = time_step == 1
        others = from_sibling(forcing)
        if not last:
            others, other_columns = lax.optimization_barrier((others, other_columns))
        forcing = forcing + others
        direction = forcing / (CHEB_THETA * diag)
        halo = with_either(direction, False)
        if not last:
            choices = 2 * columns.shape[0] * torso
            direction = call(bring_tiles, field)(in_specs=[VMEM] * 2)(tile_values, direction)
            pick = call(choose, shape(choices, 2 * torso))(in_specs=[VMEM] * 2)(
                columns, other_columns
            )
            halo, direction = lax.optimization_barrier((halo, direction))
            stored = (tile_values, other_tiles, pick)
        residual, direction, estimate = call(
            functools.partial(sweep_one, chain), (field,) * 3
        )(in_specs=[VMEM] * 8)(*stored, halo, from_sibling(halo), forcing, direction, diag)
        halo = with_either(direction, False)
        yours = from_sibling(halo)
        if not last:
            yours, maps = lax.optimization_barrier((yours, maps))
        swept = call(
            functools.partial(sweep_two, chain, last), (packed, field) if last else field
        )(in_specs=[VMEM] * 9)(
            *stored, halo, yours, direction, residual, estimate, diag
        )
        estimate, residual = swept if last else (swept, None)
        far = with_far(estimate)
        near = with_either(estimate, True)
        if not last:
            states, own, keep, give, away = call(next_shares, (dense,) + (field,) * 4)(
                in_specs=[VMEM] * 9
            )(states, estimate, far, near, from_sibling(near), nodes, maps, nodes_low, maps_low)
            far = with_far(away)
            near = with_either(keep + from_sibling(give), True)
            forcing = TORSO_COUPLING * (own + far + near)
    new_states, potential, residual = call(
        functools.partial(finish, chain),
        (shape(*dense.shape[:1], node_count), field, field),
        (pltpu.VMEM(dense.shape, F32),),
    )(in_specs=[VMEM] * 13)(
        *stored, estimate, far, near, from_sibling(near), residual, diag, states, nodes, nodes_low, maps
    )
    return new_states, potential.reshape(-1), residual.reshape(-1)


def solution(mesh):
    placed = (
        P(None, ("case", "dom", "sub")),
        P(("case", "dom", "sub"), None, None),
        P(("case", "dom", "sub"), None),
        P(("case", "dom", "sub"), None, None),
        P(("case", "dom"), "sub"),
        P(("case", "dom"), "sub", None, None),
        P(("case", "dom")),
    )
    return jax.shard_map(
        on_device,
        mesh=mesh,
        in_specs=placed,
        out_specs=(P(None, ("case", "dom", "sub")), P(("case", "dom")), P(("case", "dom"))),
        check_vma=False,
    )
```

```python
import functools

import jax
import jax.numpy as jnp
from jax import lax
from jax.experimental import pallas as pl
from jax.experimental.pallas import tpu as pltpu
from jax.sharding import PartitionSpec as P

HALO = 2
SWEEPS = 3
LANES = 128

TIME_STEP = 0.02
NERNST_SCALE = 0.267
SODIUM_OUT = 1.4
POTASSIUM_OUT = 0.054
CALCIUM_OUT = 2000.0
COND_SODIUM = 8.0
COND_CALCIUM = 1.0
COND_TRANSIENT = 0.3
COND_RAPID = 0.2
COND_SLOW = 0.3
COND_INWARD = 2.0
COND_RELEASE = 3.0
MEMBRANE_RATE = 2.0
TORSO_COUPLING = 0.5
FEEDBACK_RATE = 5.0
CHEB_THETA = 1.0
CHEB_DELTA = 0.5
GATE_MIDPOINT = [-0.56, -0.7, -0.7, -0.08, -0.2, -0.3, 0.2, -0.28, -0.26, -0.88, 0.05, -0.8, -0.5]
GATE_STEEPNESS = [0.09, -0.07, -0.07, 0.07, -0.07, -0.09, 0.06, -0.05, 0.07, -0.24, 0.14, -0.1, 0.08]
TIME_BASE = [0.02, 0.3, 1.0, 0.1, 2.0, 0.5, 0.1, 1.0, 1.0, 0.5, 1.0, 0.05, 0.2]
TIME_PEAK = [0.1, 1.0, 3.0, 0.5, 5.0, 2.0, 0.3, 5.0, 3.0, 2.0, 4.0, 0.1, 1.0]

SIGMA = CHEB_THETA / CHEB_DELTA
KEEP, PULL = [], []
_ratio = 1.0 / SIGMA
for _ in range(SWEEPS - 1):
    _next = 1.0 / (2.0 * SIGMA - _ratio)
    KEEP.append(_next * _ratio)
    PULL.append(2.0 * _next / CHEB_DELTA)
    _ratio = _next

VMEM = pl.BlockSpec(memory_space=pltpu.VMEM)
F32 = jnp.float32


def call(kernel, outs, scratch=(), limit=16, cost=4_000_000):
    return functools.partial(
        pl.pallas_call,
        kernel,
        out_shape=outs,
        out_specs=jax.tree.map(lambda _: VMEM, outs),
        scratch_shapes=list(scratch),
        compiler_params=pltpu.CompilerParams(vmem_limit_bytes=limit << 20),
        cost_estimate=pl.CostEstimate(flops=cost, bytes_accessed=1 << 18, transcendentals=0),
    )


def ionic_rows(rows):
    voltage, gating = rows[0], rows[1:14]
    sodium, potassium, calcium, reticulum, subspace = rows[14:19]
    moved = []
    for i, gate in enumerate(gating):
        shifted = voltage - GATE_MIDPOINT[i]
        steady = jax.nn.sigmoid(shifted / GATE_STEEPNESS[i])
        time_const = TIME_BASE[i] + TIME_PEAK[i] * jnp.exp(-jnp.square(shifted / 0.3))
        moved.append(steady + (gate - steady) * jnp.exp(-TIME_STEP / time_const))
    g = moved
    sodium_rev = NERNST_SCALE * jnp.log(SODIUM_OUT / sodium)
    potassium_rev = NERNST_SCALE * jnp.log(POTASSIUM_OUT / potassium)
    calcium_rev = 0.5 * NERNST_SCALE * jnp.log(CALCIUM_OUT / subspace)
    sodium_flow = COND_SODIUM * (g[0] * g[0] * g[0]) * g[1] * g[2] * (voltage - sodium_rev)
    calcium_flow = COND_CALCIUM * g[3] * g[4] * g[5] * (voltage - calcium_rev)
    potassium_cond = (
        COND_TRANSIENT * g[6] * g[7]
        + COND_RAPID * g[8] * g[9]
        + COND_SLOW * (g[10] * g[10])
        + COND_INWARD * g[11]
    )
    potassium_flow = potassium_cond * (voltage - potassium_rev)
    current = sodium_flow + calcium_flow + potassium_flow
    release = COND_RELEASE * g[12] * (reticulum - subspace) / (reticulum + subspace)
    sodium = sodium * jnp.exp(-0.5 * TIME_STEP * sodium_flow)
    potassium = potassium * jnp.exp(-0.5 * TIME_STEP * potassium_flow)
    calcium = calcium * jnp.exp(-0.5 * TIME_STEP * calcium_flow)
    subspace = subspace * jnp.exp(TIME_STEP * (release - 0.5 * calcium_flow))
    reticulum = reticulum * jnp.exp(-TIME_STEP * release)
    voltage = voltage - TIME_STEP * MEMBRANE_RATE * current
    return [voltage, *moved, sodium, potassium, calcium, reticulum, subspace], current


def pairs_of(index):
    chunks = [index[:, k : k + LANES] for k in range(0, index.shape[1], LANES)]
    return [jnp.concatenate(chunks[k : k + 2], axis=0) for k in range(0, len(chunks), 2)]


def gather(source, rows, index):
    peers = index.shape[0]
    out = []
    for pair in pairs_of(index):
        high, low = pair >> 7, pair & (LANES - 1)
        total = jnp.zeros(pair.shape, F32)
        for h in range(rows):
            picked = jnp.take_along_axis(source(h), low, axis=1)
            total = jnp.where(high == h, picked, total)
        out += [total[:peers], total[peers:]]
    return jnp.concatenate(out, axis=1)


def three_parts(value):
    first = value.astype(jnp.bfloat16).astype(F32)
    rest = value - first
    second = rest.astype(jnp.bfloat16).astype(F32)
    return first, second, rest - second


def scatter(values, index, rows):
    slots = values.shape[1]
    high, low = index >> 7, index & (LANES - 1)
    mine = lax.broadcasted_iota(jnp.int32, (rows, slots), 0) == high
    parts = [jnp.where(mine, part, 0.0) for part in three_parts(values)]
    pieces = jnp.concatenate(parts + [jnp.zeros((rows, slots), F32)], axis=0)
    spread = lax.broadcasted_iota(jnp.int32, (LANES, slots), 0) == low
    return lax.dot_general(
        jnp.where(spread, 1.0, 0.0).astype(jnp.bfloat16),
        pieces.astype(jnp.bfloat16),
        (((1,), (1,)), ((), ())),
        preferred_element_type=F32,
    )


def turned(sums, rows):
    whole = sums[0] if len(sums) == 1 else jnp.concatenate(sums, axis=1)
    if whole.shape[1] < LANES:
        filler = jnp.zeros((LANES, LANES - whole.shape[1]), F32)
        whole = jnp.concatenate([whole, filler], axis=1)
    whole = whole.T
    out = []
    for at in range(0, 4 * rows * len(sums), 4 * rows):
        first, second, third = (whole[at + k * rows : at + (k + 1) * rows] for k in range(3))
        out.append(first + second + third)
    return out


def pick_current(current, nodes):
    rows, peers = current.shape[0], nodes.shape[0]
    return gather(
        lambda h: jnp.broadcast_to(current[h : h + 1], (2 * peers, LANES)), rows, nodes
    )


def is_even():
    return lax.rem(lax.axis_index("dom"), 2) == 0


def meets_next():
    return is_even() == (lax.axis_index("sub") == 0)


def by_partner(mine, yours):
    zero = lax.axis_index("sub") == 0
    return jnp.where(zero, mine, yours), jnp.where(zero, yours, mine)


def by_side(first, second):
    even = is_even()
    return jnp.where(even, first, second), jnp.where(even, second, first)


def spread_current(outgoing, maps, own_ref, keep_ref, give_ref, far_ref):
    torso = own_ref.shape[0]
    own, after, before, far = turned(
        [scatter(outgoing[o : o + 1], maps[o : o + 1], torso) for o in range(maps.shape[0])], torso
    )
    ahead = meets_next()
    own_ref[...] = own
    keep_ref[...] = jnp.where(ahead, after, before)
    give_ref[...] = jnp.where(ahead, before, after)
    far_ref[...] = far


def feedback_of(estimates, nodes, maps, heart):
    peers = nodes.shape[0]
    torso = estimates[0].shape[0]

    def source(h):
        rows = [estimate[h : h + 1] for estimate in estimates]
        return jnp.concatenate(rows * 2, axis=0)

    returned = gather(source, torso, maps)
    total = None
    for o in range(peers):
        part = scatter(returned[o : o + 1], nodes[o : o + 1], heart)
        total = part if total is None else total + part
    return turned([total], heart)[0]


def product(own_ref, other_ref, pick_ref, window):
    tiles, slots = own_ref.shape[0], own_ref.shape[1]
    parts = jnp.concatenate(three_parts(window), axis=1).astype(jnp.bfloat16)
    picked = jnp.dot(pick_ref[...].astype(jnp.bfloat16), parts, preferred_element_type=F32)
    picked = picked[:, :LANES] + picked[:, LANES : 2 * LANES] + picked[:, 2 * LANES :]
    eye = lax.broadcasted_iota(jnp.int32, (LANES, LANES), 0) == lax.broadcasted_iota(
        jnp.int32, (LANES, LANES), 1
    )
    rows = []
    for t in range(tiles):
        total = None
        for k in range(2 * slots):
            tile = own_ref[t, k] if k < slots else other_ref[t, k - slots]
            term = tile * picked[k * tiles + t : k * tiles + t + 1]
            total = term if total is None else total + term
        column = jnp.sum(total, axis=1, keepdims=True)
        rows.append(jnp.sum(jnp.where(eye, column, 0.0), axis=0, keepdims=True))
    return jnp.concatenate(rows, axis=0)


def fetch(pairs, sems):
    copies = [pltpu.make_async_copy(a, b, sems.at[i]) for i, (a, b) in enumerate(pairs)]
    for copy in copies:
        copy.start()
    return copies


def begin(
    states_ref, table_ref, out_ref, nodes_ref, own_ref, keep_ref, give_ref, far_ref
):
    peers, slots = nodes_ref.shape
    for k in range(out_ref.shape[1]):
        out_ref[:, k, :] = states_ref[:, k * LANES : (k + 1) * LANES]
    slot = lax.broadcasted_iota(jnp.int32, (1, slots), 1)
    for o in range(peers):
        live = slot < table_ref[2 * peers : 2 * peers + 1, o : o + 1]
        nodes_ref[o : o + 1] = jnp.where(live, table_ref[o : o + 1], -1)
    rows, current = ionic_rows([out_ref[i] for i in range(out_ref.shape[0])])
    for i, row in enumerate(rows):
        out_ref[i] = row
    outgoing = pick_current(current, nodes_ref[...])
    incoming = table_ref[peers : 2 * peers].astype(F32)

    def pair(out, into):
        return jnp.concatenate([outgoing[out : out + 1], incoming[into : into + 1]], axis=0)

    to_next, to_prev = pair(1, 2), pair(2, 1)
    ahead = meets_next()
    own_ref[...] = pair(0, 0)
    keep_ref[...] = jnp.where(ahead, to_next, to_prev)
    give_ref[...] = jnp.where(ahead, to_prev, to_next)
    far_ref[...] = jnp.zeros_like(far_ref)
    far_ref[0:2] = pair(3, 3)


def bring(cols_ref, diag_ref, own_ref, cols_out, diag_out, own_out):
    cols_out[...] = cols_ref[...]
    diag_out[...] = diag_ref[...]
    own_out[...] = own_ref[...]


def bring_tiles(tiles_ref, direction_ref, direction_out):
    direction_out[...] = direction_ref[...]
    del tiles_ref


def choose(own_cols, other_cols, pick_ref):
    slots, tiles = own_cols.shape
    eye = lax.broadcasted_iota(jnp.int32, (tiles, tiles), 0) == lax.broadcasted_iota(
        jnp.int32, (tiles, tiles), 1
    )
    place = lax.broadcasted_iota(jnp.int32, (tiles, pick_ref.shape[1]), 1)
    for k in range(2 * slots):
        row = own_cols[k : k + 1] if k < slots else other_cols[k - slots : k - slots + 1]
        column = jnp.sum(jnp.where(eye, row.astype(F32), 0.0), axis=1, keepdims=True)
        pick_ref[k * tiles : (k + 1) * tiles] = jnp.where(place == column.astype(jnp.int32), 1.0, 0.0)


def first_forcing(
    own_ref, far_ref, near_ref, keep_ref, got_ref, to_far, give_ref, forcing_ref
):
    total = None
    for come, rows in (
        (own_ref[0:1], own_ref[1:2]),
        (far_ref[0:1], to_far[1:2]),
        (near_ref[0:1], keep_ref[1:2]),
        (near_ref[2:3], got_ref[1:2]),
    ):
        part = scatter(come, rows.astype(jnp.int32), forcing_ref.shape[0])
        total = part if total is None else total + part
    forcing_ref[...] = TORSO_COUPLING * turned([total], forcing_ref.shape[0])[0]
    give_ref[...] = near_ref[3:4]


def complete(own_ref, near_ref, far_ref, got_ref, nodes_ref, maps_ref):
    ahead = meets_next()
    keep, got = near_ref[1:2], got_ref[...]
    after, before = jnp.where(ahead, keep, got), jnp.where(ahead, got, keep)
    rows = jnp.concatenate([own_ref[1:2], after, before, far_ref[1:2]], axis=0)
    maps_ref[...] = jnp.where(nodes_ref[...] < 0, -1, rows.astype(jnp.int32))


def next_shares(
    states_ref, own_estimate, far_estimate, mine_ref, yours_ref, nodes_ref, maps_ref,
    out_ref, own_ref, keep_ref, give_ref, far_ref,
):
    nodes, maps = nodes_ref[...], maps_ref[...]
    after, before = by_side(*by_partner(mine_ref[...], yours_ref[...]))
    estimates = [own_estimate[...], after, before, far_estimate[...]]
    feedback = feedback_of(estimates, nodes, maps, states_ref.shape[1])
    rows = [states_ref[i] for i in range(states_ref.shape[0])]
    rows[0] = rows[0] + TIME_STEP * FEEDBACK_RATE * feedback
    rows, current = ionic_rows(rows)
    for i, row in enumerate(rows):
        out_ref[i] = row
    outgoing = pick_current(current, nodes)
    spread_current(outgoing, maps, own_ref, keep_ref, give_ref, far_ref)


def window_of(chain, direction, first, second):
    torso = direction.shape[0]
    here = lax.axis_index("dom")
    after, before = by_side(first, second)
    before = jnp.where(here > 0, before[torso - HALO :], 0.0)
    after = jnp.where(here < chain - 1, after[0:HALO], 0.0)
    filler = jnp.zeros((torso - 2 * HALO, LANES), F32)
    return jnp.concatenate([before, direction, after, filler], axis=0)


def sweep_one(
    chain, own_ref, other_ref, pick_ref, mine_ref, yours_ref, forcing_ref, direction_in, diag_ref,
    residual_ref, direction_ref, estimate_ref,
):
    diag = diag_ref[...]
    direction = direction_in[...]
    window = window_of(chain, direction, *by_partner(mine_ref[...], yours_ref[...]))
    moved = product(own_ref, other_ref, pick_ref, window)
    residual = forcing_ref[...] - (diag * direction + moved)
    estimate = direction
    direction = KEEP[0] * direction + PULL[0] * (residual / diag)
    residual_ref[...] = residual
    direction_ref[...] = direction
    estimate_ref[...] = estimate + direction


def sweep_two(
    chain, last, own_ref, other_ref, pick_ref, mine_ref, yours_ref, direction_in, residual_in,
    estimate_in, diag_ref, estimate_ref, *refs,
):
    torso = estimate_ref.shape[0]
    diag = diag_ref[...]
    direction = direction_in[...]
    window = window_of(chain, direction, *by_partner(mine_ref[...], yours_ref[...]))
    moved = product(own_ref, other_ref, pick_ref, window)
    residual = residual_in[...] - (diag * direction + moved)
    direction = KEEP[1] * direction + PULL[1] * (residual / diag)
    estimate = estimate_in[...] + direction
    if last:
        residual_ref, = refs
        residual_ref[...] = residual
        estimate_ref[0 : torso // 2] = estimate
        estimate_ref[torso // 2 :] = direction
    else:
        estimate_ref[...] = estimate


def finish(
    chain, own_ref, other_ref, pick_ref, packed_ref, far_ref, mine_ref, yours_ref, residual_in,
    diag_ref, states_ref, nodes_ref, maps_ref, out_ref, potential_ref, residual_ref, dense_ref,
):
    torso = residual_ref.shape[0]
    head, tail = slice(0, torso), slice(torso, 2 * torso)
    estimate, direction = packed_ref[head], packed_ref[tail]
    potential_ref[...] = estimate
    first, second = by_partner(mine_ref[...], yours_ref[...])
    after, before = by_side(first[head], second[head])
    feedback = feedback_of(
        [estimate, after, before, far_ref[head]], nodes_ref[...], maps_ref[...],
        states_ref.shape[1],
    )
    dense_ref[...] = states_ref[...]
    dense_ref[0] = states_ref[0] + TIME_STEP * FEEDBACK_RATE * feedback
    for k in range(states_ref.shape[1]):
        out_ref[:, k * LANES : (k + 1) * LANES] = dense_ref[:, k, :]
    window = window_of(chain, direction, first[tail], second[tail])
    moved = product(own_ref, other_ref, pick_ref, window)
    residual_ref[...] = residual_in[...] - (diag_ref[...] * direction + moved)


def on_device(states, send_node, send_count, recv_row, columns, tile_values, diagonal):
    chain = lax.axis_size("dom")
    peers, slots = send_node.shape[1:]
    node_count = states.shape[1]
    heart = node_count // LANES
    torso = diagonal.shape[0] // LANES

    def with_far(value):
        return lax.ppermute(value, "dom", [(i, (i + chain // 2) % chain) for i in range(chain)])

    def with_either(value, closed):
        cases = lax.axis_size("case")
        ends = () if closed or cases % 2 else (0, chain - 1)
        pairs = []
        for case in range(cases):
            for i in range(chain):
                me = (case * chain + i) * 2
                pairs.append((me, (case * chain + (i ^ 1)) * 2))
                if i in ends:
                    pairs.append((me + 1, ((case ^ 1) * chain + i) * 2 + 1))
                else:
                    second = (((i + 1) ^ 1) - 1) % chain
                    pairs.append((me + 1, (case * chain + second) * 2 + 1))
        return lax.ppermute(value, ("case", "dom", "sub"), pairs)

    def from_sibling(value):
        return lax.ppermute(value, "sub", [(0, 1), (1, 0)])

    def shape(*dims, dtype=F32):
        return jax.ShapeDtypeStruct(dims, dtype)

    dense = shape(states.shape[0], heart, LANES)
    field = shape(torso, LANES)
    packed = shape(2 * torso, LANES)
    counts = jnp.pad(send_count, ((0, 0), (0, slots - peers)))
    table = jnp.concatenate([send_node[0], recv_row[0], counts])
    index = shape(peers, slots, dtype=jnp.int32)
    other_tiles = from_sibling(tile_values)
    double = shape(2, slots)
    states, nodes, own, keep, give, to_far = call(begin, (dense, index) + (double,) * 3 + (shape(8, slots),))(
        in_specs=[VMEM] * 2
    )(states, table)
    got = from_sibling(give)
    far = with_far(to_far)
    near = with_either(jnp.concatenate([keep, got]), True)
    columns, diag, own = call(
        bring, (shape(*columns.shape[::-1], dtype=jnp.int32), field, double)
    )(in_specs=[VMEM] * 3)(columns.T, diagonal.reshape(torso, LANES), own)
    give, forcing = call(first_forcing, (shape(1, slots), field))(in_specs=[VMEM] * 6)(
        own, far, near, keep, got, to_far
    )
    maps = call(complete, index)(in_specs=[VMEM] * 5)(own, near, far, from_sibling(give), nodes)
    other_columns = from_sibling(columns)
    for time_step in range(2):
        last = time_step == 1
        others = from_sibling(forcing)
        if not last:
            others, other_columns = lax.optimization_barrier((others, other_columns))
        forcing = forcing + others
        direction = forcing / (CHEB_THETA * diag)
        halo = with_either(direction, False)
        if not last:
            choices = 2 * columns.shape[0] * torso
            direction = call(bring_tiles, field)(in_specs=[VMEM] * 2)(tile_values, direction)
            pick = call(choose, shape(choices, 2 * torso))(in_specs=[VMEM] * 2)(
                columns, other_columns
            )
            halo, direction = lax.optimization_barrier((halo, direction))
            stored = (tile_values, other_tiles, pick)
        residual, direction, estimate = call(
            functools.partial(sweep_one, chain), (field,) * 3
        )(in_specs=[VMEM] * 8)(*stored, halo, from_sibling(halo), forcing, direction, diag)
        halo = with_either(direction, False)
        swept = call(
            functools.partial(sweep_two, chain, last), (packed, field) if last else field
        )(in_specs=[VMEM] * 9)(
            *stored, halo, from_sibling(halo), direction, residual, estimate, diag
        )
        estimate, residual = swept if last else (swept, None)
        far = with_far(estimate)
        near = with_either(estimate, True)
        if not last:
            states, own, keep, give, away = call(next_shares, (dense,) + (field,) * 4)(
                in_specs=[VMEM] * 7
            )(states, estimate, far, near, from_sibling(near), nodes, maps)
            far = with_far(away)
            near = with_either(keep + from_sibling(give), True)
            forcing = TORSO_COUPLING * (own + far + near)
    new_states, potential, residual = call(
        functools.partial(finish, chain),
        (shape(*dense.shape[:1], node_count), field, field),
        (pltpu.VMEM(dense.shape, F32),),
    )(in_specs=[VMEM] * 12)(
        *stored, estimate, far, near, from_sibling(near), residual, diag, states, nodes, maps
    )
    return new_states, potential.reshape(-1), residual.reshape(-1)


def solution(mesh):
    placed = (
        P(None, ("case", "dom", "sub")),
        P(("case", "dom", "sub"), None, None),
        P(("case", "dom", "sub"), None),
        P(("case", "dom", "sub"), None, None),
        P(("case", "dom"), "sub"),
        P(("case", "dom"), "sub", None, None),
        P(("case", "dom")),
    )
    return jax.shard_map(
        on_device,
        mesh=mesh,
        in_specs=placed,
        out_specs=(P(None, ("case", "dom", "sub")), P(("case", "dom")), P(("case", "dom"))),
        check_vma=False,
    )
```

```python
import functools

import jax
import jax.numpy as jnp
from jax import lax
from jax.experimental import pallas as pl
from jax.experimental.pallas import tpu as pltpu
from jax.sharding import PartitionSpec as P

HALO = 2
SWEEPS = 3
LANES = 128

TIME_STEP = 0.02
NERNST_SCALE = 0.267
SODIUM_OUT = 1.4
POTASSIUM_OUT = 0.054
CALCIUM_OUT = 2000.0
COND_SODIUM = 8.0
COND_CALCIUM = 1.0
COND_TRANSIENT = 0.3
COND_RAPID = 0.2
COND_SLOW = 0.3
COND_INWARD = 2.0
COND_RELEASE = 3.0
MEMBRANE_RATE = 2.0
TORSO_COUPLING = 0.5
FEEDBACK_RATE = 5.0
CHEB_THETA = 1.0
CHEB_DELTA = 0.5
GATE_MIDPOINT = [-0.56, -0.7, -0.7, -0.08, -0.2, -0.3, 0.2, -0.28, -0.26, -0.88, 0.05, -0.8, -0.5]
GATE_STEEPNESS = [0.09, -0.07, -0.07, 0.07, -0.07, -0.09, 0.06, -0.05, 0.07, -0.24, 0.14, -0.1, 0.08]
TIME_BASE = [0.02, 0.3, 1.0, 0.1, 2.0, 0.5, 0.1, 1.0, 1.0, 0.5, 1.0, 0.05, 0.2]
TIME_PEAK = [0.1, 1.0, 3.0, 0.5, 5.0, 2.0, 0.3, 5.0, 3.0, 2.0, 4.0, 0.1, 1.0]

SIGMA = CHEB_THETA / CHEB_DELTA
KEEP, PULL = [], []
_ratio = 1.0 / SIGMA
for _ in range(SWEEPS - 1):
    _next = 1.0 / (2.0 * SIGMA - _ratio)
    KEEP.append(_next * _ratio)
    PULL.append(2.0 * _next / CHEB_DELTA)
    _ratio = _next

VMEM = pl.BlockSpec(memory_space=pltpu.VMEM)
F32 = jnp.float32


def call(kernel, outs, scratch=(), limit=16, cost=4_000_000):
    return functools.partial(
        pl.pallas_call,
        kernel,
        out_shape=outs,
        out_specs=jax.tree.map(lambda _: VMEM, outs),
        scratch_shapes=list(scratch),
        compiler_params=pltpu.CompilerParams(vmem_limit_bytes=limit << 20),
        cost_estimate=pl.CostEstimate(flops=cost, bytes_accessed=1 << 18, transcendentals=0),
    )


def ionic_rows(rows):
    voltage, gating = rows[0], rows[1:14]
    sodium, potassium, calcium, reticulum, subspace = rows[14:19]
    moved = []
    for i, gate in enumerate(gating):
        shifted = voltage - GATE_MIDPOINT[i]
        steady = jax.nn.sigmoid(shifted / GATE_STEEPNESS[i])
        time_const = TIME_BASE[i] + TIME_PEAK[i] * jnp.exp(-jnp.square(shifted / 0.3))
        moved.append(steady + (gate - steady) * jnp.exp(-TIME_STEP / time_const))
    g = moved
    sodium_rev = NERNST_SCALE * jnp.log(SODIUM_OUT / sodium)
    potassium_rev = NERNST_SCALE * jnp.log(POTASSIUM_OUT / potassium)
    calcium_rev = 0.5 * NERNST_SCALE * jnp.log(CALCIUM_OUT / subspace)
    sodium_flow = COND_SODIUM * (g[0] * g[0] * g[0]) * g[1] * g[2] * (voltage - sodium_rev)
    calcium_flow = COND_CALCIUM * g[3] * g[4] * g[5] * (voltage - calcium_rev)
    potassium_cond = (
        COND_TRANSIENT * g[6] * g[7]
        + COND_RAPID * g[8] * g[9]
        + COND_SLOW * (g[10] * g[10])
        + COND_INWARD * g[11]
    )
    potassium_flow = potassium_cond * (voltage - potassium_rev)
    current = sodium_flow + calcium_flow + potassium_flow
    release = COND_RELEASE * g[12] * (reticulum - subspace) / (reticulum + subspace)
    sodium = sodium * jnp.exp(-0.5 * TIME_STEP * sodium_flow)
    potassium = potassium * jnp.exp(-0.5 * TIME_STEP * potassium_flow)
    calcium = calcium * jnp.exp(-0.5 * TIME_STEP * calcium_flow)
    subspace = subspace * jnp.exp(TIME_STEP * (release - 0.5 * calcium_flow))
    reticulum = reticulum * jnp.exp(-TIME_STEP * release)
    voltage = voltage - TIME_STEP * MEMBRANE_RATE * current
    return [voltage, *moved, sodium, potassium, calcium, reticulum, subspace], current


def pairs_of(index):
    chunks = [index[:, k : k + LANES] for k in range(0, index.shape[1], LANES)]
    return [jnp.concatenate(chunks[k : k + 2], axis=0) for k in range(0, len(chunks), 2)]


def gather(source, rows, index):
    peers = index.shape[0]
    out = []
    for pair in pairs_of(index):
        high, low = pair >> 7, pair & (LANES - 1)
        total = jnp.zeros(pair.shape, F32)
        for h in range(rows):
            picked = jnp.take_along_axis(source(h), low, axis=1)
            total = jnp.where(high == h, picked, total)
        out += [total[:peers], total[peers:]]
    return jnp.concatenate(out, axis=1)


def two_parts(value):
    first = value.astype(jnp.bfloat16).astype(F32)
    return first, value - first


def scatter(values, index, rows):
    slots = values.shape[1]
    high, low = index >> 7, index & (LANES - 1)
    mine = lax.broadcasted_iota(jnp.int32, (rows, slots), 0) == high
    left = jnp.concatenate([jnp.where(mine, part, 0.0) for part in two_parts(values)], axis=0)
    spread = lax.broadcasted_iota(jnp.int32, (LANES, slots), 0) == low
    right = jnp.where(spread, 1.0, 0.0).astype(jnp.bfloat16)
    sums = lax.dot_general(
        left.astype(jnp.bfloat16), right, (((1,), (1,)), ((), ())), preferred_element_type=F32
    )
    return sums[:rows] + sums[rows:]


def pick_current(current, nodes):
    rows, peers = current.shape[0], nodes.shape[0]
    return gather(
        lambda h: jnp.broadcast_to(current[h : h + 1], (2 * peers, LANES)), rows, nodes
    )


def is_even():
    return lax.rem(lax.axis_index("dom"), 2) == 0


def meets_next():
    return is_even() == (lax.axis_index("sub") == 0)


def by_partner(mine, yours):
    zero = lax.axis_index("sub") == 0
    return jnp.where(zero, mine, yours), jnp.where(zero, yours, mine)


def by_side(first, second):
    even = is_even()
    return jnp.where(even, first, second), jnp.where(even, second, first)


def spread_current(outgoing, maps, own_ref, keep_ref, give_ref, far_ref):
    torso = own_ref.shape[0]
    own, after, before, far = (
        scatter(outgoing[o : o + 1], maps[o : o + 1], torso) for o in range(maps.shape[0])
    )
    ahead = meets_next()
    own_ref[...] = own
    keep_ref[...] = jnp.where(ahead, after, before)
    give_ref[...] = jnp.where(ahead, before, after)
    far_ref[...] = far


def feedback_of(estimates, nodes, maps, heart):
    peers = nodes.shape[0]
    torso = estimates[0].shape[0]

    def source(h):
        rows = [estimate[h : h + 1] for estimate in estimates]
        return jnp.concatenate(rows * 2, axis=0)

    returned = gather(source, torso, maps)
    total = jnp.zeros((heart, LANES), F32)
    for o in range(peers):
        total = total + scatter(returned[o : o + 1], nodes[o : o + 1], heart)
    return total


def product(own_ref, other_ref, pick_ref, window):
    tiles, slots = own_ref.shape[0], own_ref.shape[1]
    parts = jnp.concatenate(two_parts(window), axis=1).astype(jnp.bfloat16)
    picked = jnp.dot(pick_ref[...].astype(jnp.bfloat16), parts, preferred_element_type=F32)
    picked = picked[:, :LANES] + picked[:, LANES:]
    eye = lax.broadcasted_iota(jnp.int32, (LANES, LANES), 0) == lax.broadcasted_iota(
        jnp.int32, (LANES, LANES), 1
    )
    rows = []
    for t in range(tiles):
        total = None
        for k in range(2 * slots):
            tile = own_ref[t, k] if k < slots else other_ref[t, k - slots]
            term = tile * picked[k * tiles + t : k * tiles + t + 1]
            total = term if total is None else total + term
        column = jnp.sum(total, axis=1, keepdims=True)
        rows.append(jnp.sum(jnp.where(eye, column, 0.0), axis=0, keepdims=True))
    return jnp.concatenate(rows, axis=0)


def fetch(pairs, sems):
    copies = [pltpu.make_async_copy(a, b, sems.at[i]) for i, (a, b) in enumerate(pairs)]
    for copy in copies:
        copy.start()
    return copies


def begin(
    states_ref, table_ref, out_ref, nodes_ref, own_ref, keep_ref, give_ref, far_ref
):
    peers, slots = nodes_ref.shape
    for k in range(out_ref.shape[1]):
        out_ref[:, k, :] = states_ref[:, k * LANES : (k + 1) * LANES]
    slot = lax.broadcasted_iota(jnp.int32, (1, slots), 1)
    for o in range(peers):
        live = slot < table_ref[2 * peers : 2 * peers + 1, o : o + 1]
        nodes_ref[o : o + 1] = jnp.where(live, table_ref[o : o + 1], -1)
    rows, current = ionic_rows([out_ref[i] for i in range(out_ref.shape[0])])
    for i, row in enumerate(rows):
        out_ref[i] = row
    outgoing = pick_current(current, nodes_ref[...])
    incoming = table_ref[peers : 2 * peers].astype(F32)

    def pair(out, into):
        return jnp.concatenate([outgoing[out : out + 1], incoming[into : into + 1]], axis=0)

    to_next, to_prev = pair(1, 2), pair(2, 1)
    ahead = meets_next()
    own_ref[...] = pair(0, 0)
    keep_ref[...] = jnp.where(ahead, to_next, to_prev)
    give_ref[...] = jnp.where(ahead, to_prev, to_next)
    far_ref[...] = jnp.zeros_like(far_ref)
    far_ref[0:2] = pair(3, 3)


def bring(cols_ref, diag_ref, own_ref, cols_out, diag_out, own_out):
    cols_out[...] = cols_ref[...]
    diag_out[...] = diag_ref[...]
    own_out[...] = own_ref[...]


def bring_tiles(tiles_ref, direction_ref, direction_out):
    direction_out[...] = direction_ref[...]
    del tiles_ref


def choose(own_cols, other_cols, pick_ref):
    slots, tiles = own_cols.shape
    eye = lax.broadcasted_iota(jnp.int32, (tiles, tiles), 0) == lax.broadcasted_iota(
        jnp.int32, (tiles, tiles), 1
    )
    place = lax.broadcasted_iota(jnp.int32, (tiles, pick_ref.shape[1]), 1)
    for k in range(2 * slots):
        row = own_cols[k : k + 1] if k < slots else other_cols[k - slots : k - slots + 1]
        column = jnp.sum(jnp.where(eye, row.astype(F32), 0.0), axis=1, keepdims=True)
        pick_ref[k * tiles : (k + 1) * tiles] = jnp.where(place == column.astype(jnp.int32), 1.0, 0.0)


def first_forcing(
    own_ref, far_ref, near_ref, keep_ref, got_ref, to_far, give_ref, forcing_ref
):
    total = None
    for come, rows in (
        (own_ref[0:1], own_ref[1:2]),
        (far_ref[0:1], to_far[1:2]),
        (near_ref[0:1], keep_ref[1:2]),
        (near_ref[2:3], got_ref[1:2]),
    ):
        part = scatter(come, rows.astype(jnp.int32), forcing_ref.shape[0])
        total = part if total is None else total + part
    forcing_ref[...] = TORSO_COUPLING * total
    give_ref[...] = near_ref[3:4]


def complete(own_ref, near_ref, far_ref, got_ref, nodes_ref, maps_ref):
    ahead = meets_next()
    keep, got = near_ref[1:2], got_ref[...]
    after, before = jnp.where(ahead, keep, got), jnp.where(ahead, got, keep)
    rows = jnp.concatenate([own_ref[1:2], after, before, far_ref[1:2]], axis=0)
    maps_ref[...] = jnp.where(nodes_ref[...] < 0, -1, rows.astype(jnp.int32))


def next_shares(
    states_ref, own_estimate, far_estimate, mine_ref, yours_ref, nodes_ref, maps_ref,
    out_ref, own_ref, keep_ref, give_ref, far_ref,
):
    nodes, maps = nodes_ref[...], maps_ref[...]
    after, before = by_side(*by_partner(mine_ref[...], yours_ref[...]))
    estimates = [own_estimate[...], after, before, far_estimate[...]]
    feedback = feedback_of(estimates, nodes, maps, states_ref.shape[1])
    rows = [states_ref[i] for i in range(states_ref.shape[0])]
    rows[0] = rows[0] + TIME_STEP * FEEDBACK_RATE * feedback
    rows, current = ionic_rows(rows)
    for i, row in enumerate(rows):
        out_ref[i] = row
    outgoing = pick_current(current, nodes)
    spread_current(outgoing, maps, own_ref, keep_ref, give_ref, far_ref)


def window_of(chain, direction, first, second):
    torso = direction.shape[0]
    here = lax.axis_index("dom")
    after, before = by_side(first, second)
    before = jnp.where(here > 0, before[torso - HALO :], 0.0)
    after = jnp.where(here < chain - 1, after[0:HALO], 0.0)
    filler = jnp.zeros((torso - 2 * HALO, LANES), F32)
    return jnp.concatenate([before, direction, after, filler], axis=0)


def sweep_one(
    chain, own_ref, other_ref, pick_ref, mine_ref, yours_ref, forcing_ref, direction_in, diag_ref,
    residual_ref, direction_ref, estimate_ref,
):
    diag = diag_ref[...]
    direction = direction_in[...]
    window = window_of(chain, direction, *by_partner(mine_ref[...], yours_ref[...]))
    moved = product(own_ref, other_ref, pick_ref, window)
    residual = forcing_ref[...] - (diag * direction + moved)
    estimate = direction
    direction = KEEP[0] * direction + PULL[0] * (residual / diag)
    residual_ref[...] = residual
    direction_ref[...] = direction
    estimate_ref[...] = estimate + direction


def sweep_two(
    chain, last, own_ref, other_ref, pick_ref, mine_ref, yours_ref, direction_in, residual_in,
    estimate_in, diag_ref, estimate_ref, *refs,
):
    torso = estimate_ref.shape[0]
    diag = diag_ref[...]
    direction = direction_in[...]
    window = window_of(chain, direction, *by_partner(mine_ref[...], yours_ref[...]))
    moved = product(own_ref, other_ref, pick_ref, window)
    residual = residual_in[...] - (diag * direction + moved)
    direction = KEEP[1] * direction + PULL[1] * (residual / diag)
    estimate = estimate_in[...] + direction
    if last:
        residual_ref, = refs
        residual_ref[...] = residual
        estimate_ref[0 : torso // 2] = estimate
        estimate_ref[torso // 2 :] = direction
    else:
        estimate_ref[...] = estimate


def finish(
    chain, own_ref, other_ref, pick_ref, packed_ref, far_ref, mine_ref, yours_ref, residual_in,
    diag_ref, states_ref, nodes_ref, maps_ref, out_ref, potential_ref, residual_ref, dense_ref,
):
    torso = residual_ref.shape[0]
    head, tail = slice(0, torso), slice(torso, 2 * torso)
    estimate, direction = packed_ref[head], packed_ref[tail]
    potential_ref[...] = estimate
    first, second = by_partner(mine_ref[...], yours_ref[...])
    after, before = by_side(first[head], second[head])
    feedback = feedback_of(
        [estimate, after, before, far_ref[head]], nodes_ref[...], maps_ref[...],
        states_ref.shape[1],
    )
    dense_ref[...] = states_ref[...]
    dense_ref[0] = states_ref[0] + TIME_STEP * FEEDBACK_RATE * feedback
    for k in range(states_ref.shape[1]):
        out_ref[:, k * LANES : (k + 1) * LANES] = dense_ref[:, k, :]
    window = window_of(chain, direction, first[tail], second[tail])
    moved = product(own_ref, other_ref, pick_ref, window)
    residual_ref[...] = residual_in[...] - (diag_ref[...] * direction + moved)


def on_device(states, send_node, send_count, recv_row, columns, tile_values, diagonal):
    chain = lax.axis_size("dom")
    peers, slots = send_node.shape[1:]
    node_count = states.shape[1]
    heart = node_count // LANES
    torso = diagonal.shape[0] // LANES

    def with_far(value):
        return lax.ppermute(value, "dom", [(i, (i + chain // 2) % chain) for i in range(chain)])

    def with_either(value, closed):
        cases = lax.axis_size("case")
        ends = () if closed or cases % 2 else (0, chain - 1)
        pairs = []
        for case in range(cases):
            for i in range(chain):
                me = (case * chain + i) * 2
                pairs.append((me, (case * chain + (i ^ 1)) * 2))
                if i in ends:
                    pairs.append((me + 1, ((case ^ 1) * chain + i) * 2 + 1))
                else:
                    second = (((i + 1) ^ 1) - 1) % chain
                    pairs.append((me + 1, (case * chain + second) * 2 + 1))
        return lax.ppermute(value, ("case", "dom", "sub"), pairs)

    def from_sibling(value):
        return lax.ppermute(value, "sub", [(0, 1), (1, 0)])

    def shape(*dims, dtype=F32):
        return jax.ShapeDtypeStruct(dims, dtype)

    dense = shape(states.shape[0], heart, LANES)
    field = shape(torso, LANES)
    packed = shape(2 * torso, LANES)
    counts = jnp.pad(send_count, ((0, 0), (0, slots - peers)))
    table = jnp.concatenate([send_node[0], recv_row[0], counts])
    index = shape(peers, slots, dtype=jnp.int32)
    other_tiles = from_sibling(tile_values)
    double = shape(2, slots)
    states, nodes, own, keep, give, to_far = call(begin, (dense, index) + (double,) * 3 + (shape(8, slots),))(
        in_specs=[VMEM] * 2
    )(states, table)
    got = from_sibling(give)
    far = with_far(to_far)
    near = with_either(jnp.concatenate([keep, got]), True)
    columns, diag, own = call(
        bring, (shape(*columns.shape[::-1], dtype=jnp.int32), field, double)
    )(in_specs=[VMEM] * 3)(columns.T, diagonal.reshape(torso, LANES), own)
    give, forcing = call(first_forcing, (shape(1, slots), field))(in_specs=[VMEM] * 6)(
        own, far, near, keep, got, to_far
    )
    maps = call(complete, index)(in_specs=[VMEM] * 5)(own, near, far, from_sibling(give), nodes)
    other_columns = from_sibling(columns)
    for time_step in range(2):
        last = time_step == 1
        others = from_sibling(forcing)
        if not last:
            others, other_columns = lax.optimization_barrier((others, other_columns))
        forcing = forcing + others
        direction = forcing / (CHEB_THETA * diag)
        halo = with_either(direction, False)
        if not last:
            choices = 2 * columns.shape[0] * torso
            direction = call(bring_tiles, field)(in_specs=[VMEM] * 2)(tile_values, direction)
            pick = call(choose, shape(choices, 2 * torso))(in_specs=[VMEM] * 2)(
                columns, other_columns
            )
            halo, direction = lax.optimization_barrier((halo, direction))
            stored = (tile_values, other_tiles, pick)
        residual, direction, estimate = call(
            functools.partial(sweep_one, chain), (field,) * 3
        )(in_specs=[VMEM] * 8)(*stored, halo, from_sibling(halo), forcing, direction, diag)
        halo = with_either(direction, False)
        swept = call(
            functools.partial(sweep_two, chain, last), (packed, field) if last else field
        )(in_specs=[VMEM] * 9)(
            *stored, halo, from_sibling(halo), direction, residual, estimate, diag
        )
        estimate, residual = swept if last else (swept, None)
        far = with_far(estimate)
        near = with_either(estimate, True)
        if not last:
            states, own, keep, give, away = call(next_shares, (dense,) + (field,) * 4)(
                in_specs=[VMEM] * 7
            )(states, estimate, far, near, from_sibling(near), nodes, maps)
            far = with_far(away)
            near = with_either(keep + from_sibling(give), True)
            forcing = TORSO_COUPLING * (own + far + near)
    new_states, potential, residual = call(
        functools.partial(finish, chain),
        (shape(*dense.shape[:1], node_count), field, field),
        (pltpu.VMEM(dense.shape, F32),),
    )(in_specs=[VMEM] * 12)(
        *stored, estimate, far, near, from_sibling(near), residual, diag, states, nodes, maps
    )
    return new_states, potential.reshape(-1), residual.reshape(-1)


def solution(mesh):
    placed = (
        P(None, ("case", "dom", "sub")),
        P(("case", "dom", "sub"), None, None),
        P(("case", "dom", "sub"), None),
        P(("case", "dom", "sub"), None, None),
        P(("case", "dom"), "sub"),
        P(("case", "dom"), "sub", None, None),
        P(("case", "dom")),
    )
    return jax.shard_map(
        on_device,
        mesh=mesh,
        in_specs=placed,
        out_specs=(P(None, ("case", "dom", "sub")), P(("case", "dom")), P(("case", "dom"))),
        check_vma=False,
    )
```

```python
import functools

import jax
import jax.numpy as jnp
from jax import lax
from jax.experimental import pallas as pl
from jax.experimental.pallas import tpu as pltpu
from jax.sharding import PartitionSpec as P

HALO = 2
SWEEPS = 3
LANES = 128

TIME_STEP = 0.02
NERNST_SCALE = 0.267
SODIUM_OUT = 1.4
POTASSIUM_OUT = 0.054
CALCIUM_OUT = 2000.0
COND_SODIUM = 8.0
COND_CALCIUM = 1.0
COND_TRANSIENT = 0.3
COND_RAPID = 0.2
COND_SLOW = 0.3
COND_INWARD = 2.0
COND_RELEASE = 3.0
MEMBRANE_RATE = 2.0
TORSO_COUPLING = 0.5
FEEDBACK_RATE = 5.0
CHEB_THETA = 1.0
CHEB_DELTA = 0.5
GATE_MIDPOINT = [-0.56, -0.7, -0.7, -0.08, -0.2, -0.3, 0.2, -0.28, -0.26, -0.88, 0.05, -0.8, -0.5]
GATE_STEEPNESS = [0.09, -0.07, -0.07, 0.07, -0.07, -0.09, 0.06, -0.05, 0.07, -0.24, 0.14, -0.1, 0.08]
TIME_BASE = [0.02, 0.3, 1.0, 0.1, 2.0, 0.5, 0.1, 1.0, 1.0, 0.5, 1.0, 0.05, 0.2]
TIME_PEAK = [0.1, 1.0, 3.0, 0.5, 5.0, 2.0, 0.3, 5.0, 3.0, 2.0, 4.0, 0.1, 1.0]

SIGMA = CHEB_THETA / CHEB_DELTA
KEEP, PULL = [], []
_ratio = 1.0 / SIGMA
for _ in range(SWEEPS - 1):
    _next = 1.0 / (2.0 * SIGMA - _ratio)
    KEEP.append(_next * _ratio)
    PULL.append(2.0 * _next / CHEB_DELTA)
    _ratio = _next

VMEM = pl.BlockSpec(memory_space=pltpu.VMEM)
F32 = jnp.float32


def call(kernel, outs, scratch=(), limit=16, cost=4_000_000):
    return functools.partial(
        pl.pallas_call,
        kernel,
        out_shape=outs,
        out_specs=jax.tree.map(lambda _: VMEM, outs),
        scratch_shapes=list(scratch),
        compiler_params=pltpu.CompilerParams(vmem_limit_bytes=limit << 20),
        cost_estimate=pl.CostEstimate(flops=cost, bytes_accessed=1 << 18, transcendentals=0),
    )


def ionic_rows(rows):
    voltage, gating = rows[0], rows[1:14]
    sodium, potassium, calcium, reticulum, subspace = rows[14:19]
    moved = []
    for i, gate in enumerate(gating):
        shifted = voltage - GATE_MIDPOINT[i]
        steady = jax.nn.sigmoid(shifted / GATE_STEEPNESS[i])
        time_const = TIME_BASE[i] + TIME_PEAK[i] * jnp.exp(-jnp.square(shifted / 0.3))
        moved.append(steady + (gate - steady) * jnp.exp(-TIME_STEP / time_const))
    g = moved
    sodium_rev = NERNST_SCALE * jnp.log(SODIUM_OUT / sodium)
    potassium_rev = NERNST_SCALE * jnp.log(POTASSIUM_OUT / potassium)
    calcium_rev = 0.5 * NERNST_SCALE * jnp.log(CALCIUM_OUT / subspace)
    sodium_flow = COND_SODIUM * (g[0] * g[0] * g[0]) * g[1] * g[2] * (voltage - sodium_rev)
    calcium_flow = COND_CALCIUM * g[3] * g[4] * g[5] * (voltage - calcium_rev)
    potassium_cond = (
        COND_TRANSIENT * g[6] * g[7]
        + COND_RAPID * g[8] * g[9]
        + COND_SLOW * (g[10] * g[10])
        + COND_INWARD * g[11]
    )
    potassium_flow = potassium_cond * (voltage - potassium_rev)
    current = sodium_flow + calcium_flow + potassium_flow
    release = COND_RELEASE * g[12] * (reticulum - subspace) / (reticulum + subspace)
    sodium = sodium * jnp.exp(-0.5 * TIME_STEP * sodium_flow)
    potassium = potassium * jnp.exp(-0.5 * TIME_STEP * potassium_flow)
    calcium = calcium * jnp.exp(-0.5 * TIME_STEP * calcium_flow)
    subspace = subspace * jnp.exp(TIME_STEP * (release - 0.5 * calcium_flow))
    reticulum = reticulum * jnp.exp(-TIME_STEP * release)
    voltage = voltage - TIME_STEP * MEMBRANE_RATE * current
    return [voltage, *moved, sodium, potassium, calcium, reticulum, subspace], current


def pairs_of(index):
    chunks = [index[:, k : k + LANES] for k in range(0, index.shape[1], LANES)]
    return [jnp.concatenate(chunks[k : k + 2], axis=0) for k in range(0, len(chunks), 2)]


def gather(source, rows, index):
    peers = index.shape[0]
    out = []
    for pair in pairs_of(index):
        high, low = pair >> 7, pair & (LANES - 1)
        total = jnp.zeros(pair.shape, F32)
        for h in range(rows):
            picked = jnp.take_along_axis(source(h), low, axis=1)
            total = jnp.where(high == h, picked, total)
        out += [total[:peers], total[peers:]]
    return jnp.concatenate(out, axis=1)


def three_parts(value):
    first = value.astype(jnp.bfloat16).astype(F32)
    rest = value - first
    second = rest.astype(jnp.bfloat16).astype(F32)
    return first, second, rest - second


def scatter(values, index, rows):
    slots = values.shape[1]
    high, low = index >> 7, index & (LANES - 1)
    mine = lax.broadcasted_iota(jnp.int32, (rows, slots), 0) == high
    left = jnp.concatenate([jnp.where(mine, part, 0.0) for part in three_parts(values)], axis=0)
    spread = lax.broadcasted_iota(jnp.int32, (LANES, slots), 0) == low
    right = jnp.where(spread, 1.0, 0.0).astype(jnp.bfloat16)
    sums = lax.dot_general(
        left.astype(jnp.bfloat16), right, (((1,), (1,)), ((), ())), preferred_element_type=F32
    )
    return sums[:rows] + sums[rows : 2 * rows] + sums[2 * rows :]


def pick_current(current, nodes):
    rows, peers = current.shape[0], nodes.shape[0]
    return gather(
        lambda h: jnp.broadcast_to(current[h : h + 1], (2 * peers, LANES)), rows, nodes
    )


def is_even():
    return lax.rem(lax.axis_index("dom"), 2) == 0


def meets_next():
    return is_even() == (lax.axis_index("sub") == 0)


def by_partner(mine, yours):
    zero = lax.axis_index("sub") == 0
    return jnp.where(zero, mine, yours), jnp.where(zero, yours, mine)


def by_side(first, second):
    even = is_even()
    return jnp.where(even, first, second), jnp.where(even, second, first)


def spread_current(outgoing, maps, own_ref, keep_ref, give_ref, far_ref):
    torso = own_ref.shape[0]
    own, after, before, far = (
        scatter(outgoing[o : o + 1], maps[o : o + 1], torso) for o in range(maps.shape[0])
    )
    ahead = meets_next()
    own_ref[...] = own
    keep_ref[...] = jnp.where(ahead, after, before)
    give_ref[...] = jnp.where(ahead, before, after)
    far_ref[...] = far


def feedback_of(estimates, nodes, maps, heart):
    peers = nodes.shape[0]
    torso = estimates[0].shape[0]

    def source(h):
        rows = [estimate[h : h + 1] for estimate in estimates]
        return jnp.concatenate(rows * 2, axis=0)

    returned = gather(source, torso, maps)
    total = jnp.zeros((heart, LANES), F32)
    for o in range(peers):
        total = total + scatter(returned[o : o + 1], nodes[o : o + 1], heart)
    return total


def product(own_ref, other_ref, pick_ref, window):
    tiles, slots = own_ref.shape[0], own_ref.shape[1]
    parts = jnp.concatenate(three_parts(window), axis=1).astype(jnp.bfloat16)
    picked = jnp.dot(pick_ref[...].astype(jnp.bfloat16), parts, preferred_element_type=F32)
    picked = picked[:, :LANES] + picked[:, LANES : 2 * LANES] + picked[:, 2 * LANES :]
    eye = lax.broadcasted_iota(jnp.int32, (LANES, LANES), 0) == lax.broadcasted_iota(
        jnp.int32, (LANES, LANES), 1
    )
    rows = []
    for t in range(tiles):
        total = None
        for k in range(2 * slots):
            tile = own_ref[t, k] if k < slots else other_ref[t, k - slots]
            term = tile * picked[k * tiles + t : k * tiles + t + 1]
            total = term if total is None else total + term
        column = jnp.sum(total, axis=1, keepdims=True)
        rows.append(jnp.sum(jnp.where(eye, column, 0.0), axis=0, keepdims=True))
    return jnp.concatenate(rows, axis=0)


def fetch(pairs, sems):
    copies = [pltpu.make_async_copy(a, b, sems.at[i]) for i, (a, b) in enumerate(pairs)]
    for copy in copies:
        copy.start()
    return copies


def begin(
    states_ref, table_ref, out_ref, nodes_ref, own_ref, keep_ref, give_ref, far_ref
):
    peers, slots = nodes_ref.shape
    for k in range(out_ref.shape[1]):
        out_ref[:, k, :] = states_ref[:, k * LANES : (k + 1) * LANES]
    slot = lax.broadcasted_iota(jnp.int32, (1, slots), 1)
    for o in range(peers):
        live = slot < table_ref[2 * peers : 2 * peers + 1, o : o + 1]
        nodes_ref[o : o + 1] = jnp.where(live, table_ref[o : o + 1], -1)
    rows, current = ionic_rows([out_ref[i] for i in range(out_ref.shape[0])])
    for i, row in enumerate(rows):
        out_ref[i] = row
    outgoing = pick_current(current, nodes_ref[...])
    incoming = table_ref[peers : 2 * peers].astype(F32)

    def pair(out, into):
        return jnp.concatenate([outgoing[out : out + 1], incoming[into : into + 1]], axis=0)

    to_next, to_prev = pair(1, 2), pair(2, 1)
    ahead = meets_next()
    own_ref[...] = pair(0, 0)
    keep_ref[...] = jnp.where(ahead, to_next, to_prev)
    give_ref[...] = jnp.where(ahead, to_prev, to_next)
    far_ref[...] = jnp.zeros_like(far_ref)
    far_ref[0:2] = pair(3, 3)


def bring(cols_ref, diag_ref, own_ref, cols_out, diag_out, own_out):
    cols_out[...] = cols_ref[...]
    diag_out[...] = diag_ref[...]
    own_out[...] = own_ref[...]


def bring_tiles(tiles_ref, direction_ref, direction_out):
    direction_out[...] = direction_ref[...]
    del tiles_ref


def choose(own_cols, other_cols, pick_ref):
    slots, tiles = own_cols.shape
    eye = lax.broadcasted_iota(jnp.int32, (tiles, tiles), 0) == lax.broadcasted_iota(
        jnp.int32, (tiles, tiles), 1
    )
    place = lax.broadcasted_iota(jnp.int32, (tiles, pick_ref.shape[1]), 1)
    for k in range(2 * slots):
        row = own_cols[k : k + 1] if k < slots else other_cols[k - slots : k - slots + 1]
        column = jnp.sum(jnp.where(eye, row.astype(F32), 0.0), axis=1, keepdims=True)
        pick_ref[k * tiles : (k + 1) * tiles] = jnp.where(place == column.astype(jnp.int32), 1.0, 0.0)


def first_forcing(
    own_ref, far_ref, near_ref, keep_ref, got_ref, to_far, give_ref, forcing_ref
):
    total = None
    for come, rows in (
        (own_ref[0:1], own_ref[1:2]),
        (far_ref[0:1], to_far[1:2]),
        (near_ref[0:1], keep_ref[1:2]),
        (near_ref[2:3], got_ref[1:2]),
    ):
        part = scatter(come, rows.astype(jnp.int32), forcing_ref.shape[0])
        total = part if total is None else total + part
    forcing_ref[...] = TORSO_COUPLING * total
    give_ref[...] = near_ref[3:4]


def complete(own_ref, near_ref, far_ref, got_ref, nodes_ref, maps_ref):
    ahead = meets_next()
    keep, got = near_ref[1:2], got_ref[...]
    after, before = jnp.where(ahead, keep, got), jnp.where(ahead, got, keep)
    rows = jnp.concatenate([own_ref[1:2], after, before, far_ref[1:2]], axis=0)
    maps_ref[...] = jnp.where(nodes_ref[...] < 0, -1, rows.astype(jnp.int32))


def next_shares(
    states_ref, own_estimate, far_estimate, mine_ref, yours_ref, nodes_ref, maps_ref,
    out_ref, own_ref, keep_ref, give_ref, far_ref,
):
    nodes, maps = nodes_ref[...], maps_ref[...]
    after, before = by_side(*by_partner(mine_ref[...], yours_ref[...]))
    estimates = [own_estimate[...], after, before, far_estimate[...]]
    feedback = feedback_of(estimates, nodes, maps, states_ref.shape[1])
    rows = [states_ref[i] for i in range(states_ref.shape[0])]
    rows[0] = rows[0] + TIME_STEP * FEEDBACK_RATE * feedback
    rows, current = ionic_rows(rows)
    for i, row in enumerate(rows):
        out_ref[i] = row
    outgoing = pick_current(current, nodes)
    spread_current(outgoing, maps, own_ref, keep_ref, give_ref, far_ref)


def window_of(chain, direction, first, second):
    torso = direction.shape[0]
    here = lax.axis_index("dom")
    after, before = by_side(first, second)
    before = jnp.where(here > 0, before[torso - HALO :], 0.0)
    after = jnp.where(here < chain - 1, after[0:HALO], 0.0)
    filler = jnp.zeros((torso - 2 * HALO, LANES), F32)
    return jnp.concatenate([before, direction, after, filler], axis=0)


def sweep_one(
    chain, own_ref, other_ref, pick_ref, mine_ref, yours_ref, forcing_ref, direction_in, diag_ref,
    residual_ref, direction_ref, estimate_ref,
):
    diag = diag_ref[...]
    direction = direction_in[...]
    window = window_of(chain, direction, *by_partner(mine_ref[...], yours_ref[...]))
    moved = product(own_ref, other_ref, pick_ref, window)
    residual = forcing_ref[...] - (diag * direction + moved)
    estimate = direction
    direction = KEEP[0] * direction + PULL[0] * (residual / diag)
    residual_ref[...] = residual
    direction_ref[...] = direction
    estimate_ref[...] = estimate + direction


def sweep_two(
    chain, last, own_ref, other_ref, pick_ref, mine_ref, yours_ref, direction_in, residual_in,
    estimate_in, diag_ref, estimate_ref, *refs,
):
    torso = estimate_ref.shape[0]
    diag = diag_ref[...]
    direction = direction_in[...]
    window = window_of(chain, direction, *by_partner(mine_ref[...], yours_ref[...]))
    moved = product(own_ref, other_ref, pick_ref, window)
    residual = residual_in[...] - (diag * direction + moved)
    direction = KEEP[1] * direction + PULL[1] * (residual / diag)
    estimate = estimate_in[...] + direction
    if last:
        residual_ref, = refs
        residual_ref[...] = residual
        estimate_ref[0 : torso // 2] = estimate
        estimate_ref[torso // 2 :] = direction
    else:
        estimate_ref[...] = estimate


def finish(
    chain, own_ref, other_ref, pick_ref, packed_ref, far_ref, mine_ref, yours_ref, residual_in,
    diag_ref, states_ref, nodes_ref, maps_ref, out_ref, potential_ref, residual_ref, dense_ref,
):
    torso = residual_ref.shape[0]
    head, tail = slice(0, torso), slice(torso, 2 * torso)
    estimate, direction = packed_ref[head], packed_ref[tail]
    potential_ref[...] = estimate
    first, second = by_partner(mine_ref[...], yours_ref[...])
    after, before = by_side(first[head], second[head])
    feedback = feedback_of(
        [estimate, after, before, far_ref[head]], nodes_ref[...], maps_ref[...],
        states_ref.shape[1],
    )
    dense_ref[...] = states_ref[...]
    dense_ref[0] = states_ref[0] + TIME_STEP * FEEDBACK_RATE * feedback
    for k in range(states_ref.shape[1]):
        out_ref[:, k * LANES : (k + 1) * LANES] = dense_ref[:, k, :]
    window = window_of(chain, direction, first[tail], second[tail])
    moved = product(own_ref, other_ref, pick_ref, window)
    residual_ref[...] = residual_in[...] - (diag_ref[...] * direction + moved)


def on_device(states, send_node, send_count, recv_row, columns, tile_values, diagonal):
    chain = lax.axis_size("dom")
    peers, slots = send_node.shape[1:]
    node_count = states.shape[1]
    heart = node_count // LANES
    torso = diagonal.shape[0] // LANES

    def with_far(value):
        return lax.ppermute(value, "dom", [(i, (i + chain // 2) % chain) for i in range(chain)])

    def with_either(value, closed):
        cases = lax.axis_size("case")
        ends = () if closed or cases % 2 else (0, chain - 1)
        pairs = []
        for case in range(cases):
            for i in range(chain):
                me = (case * chain + i) * 2
                pairs.append((me, (case * chain + (i ^ 1)) * 2))
                if i in ends:
                    pairs.append((me + 1, ((case ^ 1) * chain + i) * 2 + 1))
                else:
                    second = (((i + 1) ^ 1) - 1) % chain
                    pairs.append((me + 1, (case * chain + second) * 2 + 1))
        return lax.ppermute(value, ("case", "dom", "sub"), pairs)

    def from_sibling(value):
        return lax.ppermute(value, "sub", [(0, 1), (1, 0)])

    def shape(*dims, dtype=F32):
        return jax.ShapeDtypeStruct(dims, dtype)

    dense = shape(states.shape[0], heart, LANES)
    field = shape(torso, LANES)
    packed = shape(2 * torso, LANES)
    counts = jnp.pad(send_count, ((0, 0), (0, slots - peers)))
    table = jnp.concatenate([send_node[0], recv_row[0], counts])
    index = shape(peers, slots, dtype=jnp.int32)
    other_tiles = from_sibling(tile_values)
    double = shape(2, slots)
    states, nodes, own, keep, give, to_far = call(begin, (dense, index) + (double,) * 3 + (shape(8, slots),))(
        in_specs=[VMEM] * 2
    )(states, table)
    got = from_sibling(give)
    far = with_far(to_far)
    near = with_either(jnp.concatenate([keep, got]), True)
    columns, diag, own = call(
        bring, (shape(*columns.shape[::-1], dtype=jnp.int32), field, double)
    )(in_specs=[VMEM] * 3)(columns.T, diagonal.reshape(torso, LANES), own)
    near, other_columns = lax.optimization_barrier((near, from_sibling(columns)))
    give, forcing = call(first_forcing, (shape(1, slots), field))(in_specs=[VMEM] * 6)(
        own, far, near, keep, got, to_far
    )
    maps = call(complete, index)(in_specs=[VMEM] * 5)(own, near, far, from_sibling(give), nodes)
    for time_step in range(2):
        last = time_step == 1
        others = from_sibling(forcing)
        forcing = forcing + others
        direction = forcing / (CHEB_THETA * diag)
        halo = with_either(direction, False)
        if not last:
            choices = 2 * columns.shape[0] * torso
            direction = call(bring_tiles, field)(in_specs=[VMEM] * 2)(tile_values, direction)
            pick = call(choose, shape(choices, 2 * torso))(in_specs=[VMEM] * 2)(
                columns, other_columns
            )
            halo, direction = lax.optimization_barrier((halo, direction))
            stored = (tile_values, other_tiles, pick)
        residual, direction, estimate = call(
            functools.partial(sweep_one, chain), (field,) * 3
        )(in_specs=[VMEM] * 8)(*stored, halo, from_sibling(halo), forcing, direction, diag)
        halo = with_either(direction, False)
        swept = call(
            functools.partial(sweep_two, chain, last), (packed, field) if last else field
        )(in_specs=[VMEM] * 9)(
            *stored, halo, from_sibling(halo), direction, residual, estimate, diag
        )
        estimate, residual = swept if last else (swept, None)
        far = with_far(estimate)
        near = with_either(estimate, True)
        if not last:
            states, own, keep, give, away = call(next_shares, (dense,) + (field,) * 4)(
                in_specs=[VMEM] * 7
            )(states, estimate, far, near, from_sibling(near), nodes, maps)
            far = with_far(away)
            near = with_either(keep + from_sibling(give), True)
            forcing = TORSO_COUPLING * (own + far + near)
    new_states, potential, residual = call(
        functools.partial(finish, chain),
        (shape(*dense.shape[:1], node_count), field, field),
        (pltpu.VMEM(dense.shape, F32),),
    )(in_specs=[VMEM] * 12)(
        *stored, estimate, far, near, from_sibling(near), residual, diag, states, nodes, maps
    )
    return new_states, potential.reshape(-1), residual.reshape(-1)


def solution(mesh):
    placed = (
        P(None, ("case", "dom", "sub")),
        P(("case", "dom", "sub"), None, None),
        P(("case", "dom", "sub"), None),
        P(("case", "dom", "sub"), None, None),
        P(("case", "dom"), "sub"),
        P(("case", "dom"), "sub", None, None),
        P(("case", "dom")),
    )
    return jax.shard_map(
        on_device,
        mesh=mesh,
        in_specs=placed,
        out_specs=(P(None, ("case", "dom", "sub")), P(("case", "dom")), P(("case", "dom"))),
        check_vma=False,
    )
```
